32 devices in a mesh: dp: 16 (over z, y, x), fsdp: 2 (over core).
Axes of the slice: x: 2, y: 2, z: 4, core: 2. Of those that a mesh axis runs over, the one named last changes fastest.
Arguments:
- tokens: bfloat16 [16384, 768], P(('dp', 'fsdp')), may hold values from -6 to 6
- upstream: bfloat16 [16384, 768], P(('dp', 'fsdp')), may hold values from -6 to 6
- lengths: int32 [32], P(('dp', 'fsdp')), may hold values from 1 to 512, 12288 in all
- qkv_weight: bfloat16 [768, 2304], P(('dp', 'fsdp')), may hold values from -0.21875 to 0.21875
- proj_weight: bfloat16 [768, 768], P(('dp', 'fsdp')), may hold values from -1.75 to 1.75
- up_weight: bfloat16 [768, 3072], P(('dp', 'fsdp')), may hold values from -0.21875 to 0.21875
- down_weight: bfloat16 [3072, 768], P(('dp', 'fsdp')), may hold values from -0.109375 to 0.109375
- gains: bfloat16 [768, 2], P(('dp', 'fsdp')), may hold values from 0.099609375 to 1.8984375
- shifts: bfloat16 [768, 6], P(('dp', 'fsdp')), may hold values from -3 to 3
- up_bias: bfloat16 [3072], P(('dp', 'fsdp')), may hold values from -3 to 3
Outputs:
- output: bfloat16 [16384, 768], P(('dp', 'fsdp'))
- grad_tokens: bfloat16 [16384, 768], P(('dp', 'fsdp'))
- grad_qkv: float32 [768, 2304], P(('dp', 'fsdp'))
- grad_proj: float32 [768, 768], P(('dp', 'fsdp'))
- grad_up: float32 [768, 3072], P(('dp', 'fsdp'))
- grad_down: float32 [3072, 768], P(('dp', 'fsdp'))
- grad_gains: float32 [768, 2], P(('dp', 'fsdp'))
- grad_shifts: float32 [768, 6], P(('dp', 'fsdp'))
- grad_bias_up: float32 [3072], P(('dp', 'fsdp'))
The draws below stay inside these ranges and needn't reach their ends.
Inputs may be any that keep to these rules, and one draw needn't show every extreme that they name: lengths[c] tokens of clip c are live, in its first slots; some clip fills all 512 slots.
All inputs are finite; a program needn't handle non-finite values. No bound on the sum of `lengths` on one device may be relied on, other than what follows from the above.
Results may differ from the reference program's by a relative error of at most 0.012.
Values may be sent and summed in bfloat16 or wider, within the bound.
No kernel may reach another device: no remote copies, remote signals or barrier semaphores. Data moves between devices by JAX's collectives and lax.ppermute only.
A program may use at most 192 MiB of HBM per device.

```python
import math
import jax
import jax.numpy as jnp
import numpy as np
from jax import lax

D = 768
HEADS = 12
FF = 3072
TOK_DEV = 512
CLIPS = 32
TOKENS = 16384


def block_scale(key, extent, shards, least, high):
    loudness = 1.0
    for position, shards_of in shards:
        draws = jax.random.uniform(jax.random.fold_in(jax.random.fold_in(key, 6), position), (shards_of,), jnp.float32, least / len(shards), high / len(shards))
        loudness = loudness * jnp.repeat(jnp.exp(draws), extent[position] // shards_of).reshape((-1,) + (1,) * (len(extent) - 1 - position))
    return loudness


def split_up(number_of, total, limit, slope):
    portions = [(1 << 20) // math.isqrt(rank ** slope) + 1 for rank in range(2, number_of + 1)]
    spare, given = total - limit - (number_of - 1), [1] * (number_of - 1)
    while spare > 0:
        candidates = [i for i in range(number_of - 1) if given[i] < limit]
        pool, remaining = sum([portions[i] for i in candidates]), spare
        for i in candidates:
            extra = min(limit - given[i], max(1, remaining * portions[i] // pool), spare)
            given[i] = given[i] + extra
            spare = spare - extra
    return np.array([limit] + given)


def ragged_sizes(key, amount, total, most, skew):
    if amount == 2:
        one = jax.random.randint(key, (), max(1, total - most), min(most, total - 1) + 1)
        return jnp.stack([one, total - one])
    sizes = jnp.asarray(split_up(amount, total, most, skew), jnp.int32)
    twos = (amount - 1) // 2
    giver, taker = sizes[1:1 + 2 * twos:2], sizes[2:2 + 2 * twos:2]
    room = jnp.minimum(giver - 1, most - taker)
    moved = jax.random.randint(jax.random.fold_in(key, 1), (twos,), 0, 1 << 20) % (room + 1)
    sizes = sizes.at[1:1 + 2 * twos:2].set(giver - moved).at[2:2 + 2 * twos:2].set(taker + moved)
    return sizes[jax.random.permutation(jax.random.fold_in(key, 2), amount)]


def bell_draw(key, extent, spread, most, shards=(), dtype=jnp.bfloat16):
    values = spread * jax.random.normal(key, extent, jnp.float32)
    if shards:
        values = values * block_scale(key, extent, shards, -0.22, 0.18)
    return jnp.clip(values, -most, most).astype(dtype)


def setup_inputs(seed: int = 0) -> dict:
    keys = jax.random.split(jax.random.key(seed), 11)
    return {
        "tokens": bell_draw(keys[0], (TOKENS, D), 1.0, 6.0, ((0, 32),)),
        "upstream": bell_draw(keys[1], (TOKENS, D), 1.0, 6.0, ((0, 32),)),
        "lengths": ragged_sizes(keys[2], CLIPS, CLIPS * TOK_DEV * 3 // 4, TOK_DEV, 2).astype(jnp.int32),
        "qkv_weight": bell_draw(keys[3], (D, 3 * D), D ** -0.5, 0.21875, ((0, 32),)),
        "proj_weight": bell_draw(keys[4], (D, D), (D // 64) ** -0.5, 1.75, ((0, 32),)),
        "up_weight": bell_draw(keys[5], (D, FF), D ** -0.5, 0.21875, ((0, 32),)),
        "down_weight": bell_draw(keys[6], (FF, D), FF ** -0.5, 0.109375, ((0, 32),)),
        "gains": jnp.clip(1.0 + 0.18 * jax.random.normal(keys[7], (D, 2), jnp.float32), 0.099609375, 1.8984375).astype(jnp.bfloat16),
        "shifts": bell_draw(keys[8], (D, 6), 0.5, 3.0, ((0, 32),)),
        "up_bias": bell_draw(keys[9], (FF,), 0.5, 3.0, ((0, 32),)),
    }


@jax.custom_vjp
def low(v):
    return lax.optimization_barrier(v.astype(jnp.bfloat16)).astype(jnp.float32)

@jax.custom_vjp
def low_back(v):
    return v

def low_keep(v):
    return (low(v), None)

def low_pass(kept, grad):
    return (grad,)

def back_keep(v):
    return (v, None)

def back_low(kept, grad):
    return (low(grad),)
low.defvjp(low_keep, low_pass)
low_back.defvjp(back_keep, back_low)
HIGHEST = lax.Precision.HIGHEST

def normalize(values, gain_col, shift_col):
    centred = values - lax.optimization_barrier(jnp.mean(values, axis=-1, keepdims=True))
    spread_sq = lax.optimization_barrier(jnp.mean(centred * centred, axis=-1, keepdims=True))
    return centred * lax.rsqrt(spread_sq + 1e-06) * gain_col + shift_col

def product(left, right):
    return jnp.dot(left, right, precision=HIGHEST)

def clip_layer(params, clip_rows, clip_len):
    qkv_weight, proj_weight, up_weight, down_weight, gains, shifts, up_bias = params
    tok_rows, feat_width = clip_rows.shape
    head_size = feat_width // HEADS
    live_mask = jnp.arange(tok_rows) < clip_len
    first = low(normalize(clip_rows, gains[:, 0], shifts[:, 0]))
    joint_bias = jnp.concatenate([shifts[:, 1], jnp.zeros_like(shifts[:, 1]), shifts[:, 2]])
    joint = low(low_back(product(first, qkv_weight) + joint_bias))
    queries = joint[:, :feat_width].reshape(tok_rows, HEADS, head_size)
    key_rows = joint[:, feat_width:2 * feat_width].reshape(tok_rows, HEADS, head_size)
    value_rows = joint[:, 2 * feat_width:].reshape(tok_rows, HEADS, head_size)
    scores = low_back(jnp.einsum('qhd,khd->hqk', queries, key_rows, precision=HIGHEST) * head_size ** (-0.5))
    scores = jnp.where(live_mask[None, None, :], scores, -1e+30)
    attn_low = low(jax.nn.softmax(scores, axis=-1))
    mixed = jnp.einsum('hqk,khd->qhd', attn_low, value_rows, precision=HIGHEST).reshape(tok_rows, feat_width)
    mixed = low(low_back(mixed))
    after = clip_rows + low_back(product(mixed, proj_weight) + shifts[:, 3])
    second = low(normalize(after, gains[:, 1], shifts[:, 4]))
    hidden = low_back(product(second, up_weight) + up_bias)
    active = low(jax.nn.gelu(hidden, approximate=False))
    return after + low_back(product(active, down_weight) + shifts[:, 5])

def whole_layer(params, clip_stack, clip_lens):

    def one_clip(clip_item):
        return jax.checkpoint(clip_layer)(params, clip_item[0], clip_item[1])
    return lax.map(one_clip, (clip_stack, clip_lens))

def reference(tokens, upstream, lengths, qkv_weight, proj_weight, up_weight, down_weight, gains, shifts, up_bias):
    n_clips = lengths.shape[0]
    feat_width = tokens.shape[1]
    clip_stack = tokens.astype(jnp.float32).reshape(n_clips, -1, feat_width)
    tok_rows = clip_stack.shape[1]
    params = (qkv_weight.astype(jnp.float32), proj_weight.astype(jnp.float32), up_weight.astype(jnp.float32), down_weight.astype(jnp.float32), gains.astype(jnp.float32), shifts.astype(jnp.float32), up_bias.astype(jnp.float32))

    def layer_of(param_set, stack_in):
        return whole_layer(param_set, stack_in, lengths)
    result, pull_back = jax.vjp(layer_of, params, clip_stack)
    live_rows = (jnp.arange(tok_rows)[None, :] < lengths[:, None]).astype(jnp.float32)
    cotangent = upstream.astype(jnp.float32).reshape(n_clips, tok_rows, feat_width) * live_rows[:, :, None]
    param_grads, stack_grad = pull_back(cotangent)
    grad_qkv, grad_proj, grad_up, grad_down, grad_gains, grad_shifts, grad_bias_up = param_grads
    return (result.reshape(-1, feat_width).astype(jnp.bfloat16), stack_grad.reshape(-1, feat_width).astype(jnp.bfloat16), grad_qkv, grad_proj, grad_up, grad_down, grad_gains, grad_shifts, grad_bias_up)
```

```python
import math
from functools import partial

import jax
import jax.numpy as jnp
from jax import lax
from jax.experimental import pallas as pl
from jax.experimental.pallas import tpu as pltpu
from jax.sharding import PartitionSpec as P

HEADS = 12
EPS = 1e-06
NEG = -1e30
AXES = ("dp", "fsdp")
F32 = jnp.float32
BF16 = jnp.bfloat16
VMEM_LIMIT = 56 * 1024 * 1024


def collect(qkv_weight, proj_weight, up_weight, down_weight, gains, shifts, up_bias):
    gathered = (
        lax.all_gather(qkv_weight, ("dp", "fsdp"), axis=0, tiled=True),
        lax.all_gather(proj_weight, ("dp", "fsdp"), axis=0, tiled=True),
        lax.all_gather(up_weight, ("dp", "fsdp"), axis=0, tiled=True),
        lax.all_gather(down_weight, ("dp", "fsdp"), axis=0, tiled=True),
        lax.all_gather(gains, ("dp", "fsdp"), axis=0, tiled=True),
        lax.all_gather(shifts, ("dp", "fsdp"), axis=0, tiled=True),
        lax.all_gather(up_bias, ("dp", "fsdp"), axis=0, tiled=True),
    )
    return gathered


def give_back(grad_qkv, grad_proj, grad_up, grad_down, grad_gains, grad_shifts, grad_bias_up):
    owned = (
        lax.psum_scatter(grad_qkv, ("dp", "fsdp"), scatter_dimension=0, tiled=True),
        lax.psum_scatter(grad_proj, ("dp", "fsdp"), scatter_dimension=0, tiled=True),
        lax.psum_scatter(grad_up, ("dp", "fsdp"), scatter_dimension=0, tiled=True),
        lax.psum_scatter(grad_down, ("dp", "fsdp"), scatter_dimension=0, tiled=True),
        lax.psum_scatter(grad_gains, ("dp", "fsdp"), scatter_dimension=0, tiled=True),
        lax.psum_scatter(grad_shifts, ("dp", "fsdp"), scatter_dimension=0, tiled=True),
        lax.psum_scatter(grad_bias_up, ("dp", "fsdp"), scatter_dimension=0, tiled=True),
    )
    return owned


def normalize(values):
    centred = values - jnp.mean(values, axis=-1, keepdims=True)
    inverse = lax.rsqrt(jnp.mean(centred * centred, axis=-1, keepdims=True) + EPS)
    return (centred * inverse, inverse)


def norm_back(grad_norm, normed, inverse):
    return inverse * (
        grad_norm
        - jnp.mean(grad_norm, axis=-1, keepdims=True)
        - normed * jnp.mean(grad_norm * normed, axis=-1, keepdims=True)
    )


def block_scores(query_blk, key_rows, live_mask, scaling):
    raw = (
        jnp.einsum("qhd,khd->hqk", query_blk, key_rows, preferred_element_type=jnp.float32)
        * scaling
    )
    return jnp.where(live_mask[None, None, :], raw, NEG)


def plain(
    tokens,
    upstream,
    lengths,
    qkv_weight,
    proj_weight,
    up_weight,
    down_weight,
    gains,
    shifts,
    up_bias,
):
    tok_rows, feat_width = tokens.shape
    n_heads = HEADS
    head_size = feat_width // n_heads
    scaling = head_size ** (-0.5)
    block_rows = min(512, tok_rows)
    group_heads = 4
    head_starts = list(range(0, n_heads, group_heads))
    gathered = collect(qkv_weight, proj_weight, up_weight, down_weight, gains, shifts, up_bias)
    qkv_full, proj_full, up_full, down_full, gain_full, shift_full, bias_full = gathered
    gain_f = gain_full.astype(jnp.float32)
    shift_f = shift_full.astype(jnp.float32)
    bias_f = bias_full.astype(jnp.float32)
    live_mask = lax.iota(jnp.int32, tok_rows) < lengths[0]
    source = tokens.astype(jnp.float32)
    norm_one, inv_one = normalize(source)
    first = (norm_one * gain_f[:, 0] + shift_f[:, 0]).astype(jnp.bfloat16)
    joint_bias = jnp.concatenate([shift_f[:, 1], jnp.zeros_like(shift_f[:, 1]), shift_f[:, 2]])
    joint = (jnp.dot(first, qkv_full, preferred_element_type=jnp.float32) + joint_bias).astype(
        jnp.bfloat16
    )
    queries = joint[:, :feat_width].reshape(tok_rows, n_heads, head_size)
    key_rows = joint[:, feat_width : 2 * feat_width].reshape(tok_rows, n_heads, head_size)
    value_rows = joint[:, 2 * feat_width :].reshape(tok_rows, n_heads, head_size)
    log_sums = {}
    offset = 0
    group_parts = []
    for head_lo in head_starts:
        head_hi = head_lo + group_heads
        scores = block_scores(
            queries[offset : offset + block_rows, head_lo:head_hi],
            key_rows[:, head_lo:head_hi],
            live_mask,
            scaling,
        )
        row_max = jnp.max(scores, axis=-1, keepdims=True)
        expd = jnp.exp(scores - row_max)
        row_sum = jnp.sum(expd, axis=-1, keepdims=True)
        attn_low = (expd / row_sum).astype(jnp.bfloat16)
        log_sums[offset, head_lo] = row_max + jnp.log(row_sum)
        group_parts.append(
            jnp.einsum(
                "hqk,khd->qhd",
                attn_low,
                value_rows[:, head_lo:head_hi],
                preferred_element_type=jnp.float32,
            )
        )
    mixed_parts = jnp.concatenate(group_parts, axis=1)
    mixed = mixed_parts.reshape(tok_rows, feat_width).astype(jnp.bfloat16)
    after = source + jnp.dot(mixed, proj_full, preferred_element_type=jnp.float32) + shift_f[:, 3]
    norm_two, inv_two = normalize(after)
    second = (norm_two * gain_f[:, 1] + shift_f[:, 4]).astype(jnp.bfloat16)
    hidden = jnp.dot(second, up_full, preferred_element_type=jnp.float32) + bias_f
    gelu_exact = partial(jax.nn.gelu, approximate=False)
    active = gelu_exact(hidden).astype(jnp.bfloat16)
    output = (
        after + jnp.dot(active, down_full, preferred_element_type=jnp.float32) + shift_f[:, 5]
    ).astype(jnp.bfloat16)
    regathered = collect(qkv_weight, proj_weight, up_weight, down_weight, gains, shifts, up_bias)
    qkv_full, proj_full, up_full, down_full, gain_full, shift_full, bias_full = regathered
    grad_y = jnp.where(live_mask[:, None], upstream, jnp.zeros_like(upstream))
    sum_y = jnp.sum(grad_y, axis=0, dtype=jnp.float32)
    grad_down = jnp.einsum("tf,td->fd", active, grad_y, preferred_element_type=jnp.float32)
    grad_active = jnp.einsum("td,fd->tf", grad_y, down_full, preferred_element_type=jnp.float32)
    gelu_value, gelu_pull = jax.vjp(gelu_exact, hidden)
    grad_hidden = gelu_pull(grad_active)[0].astype(jnp.bfloat16)
    grad_bias_up = jnp.sum(grad_hidden, axis=0, dtype=jnp.float32)
    grad_up = jnp.einsum("td,tf->df", second, grad_hidden, preferred_element_type=jnp.float32)
    grad_second = jnp.einsum("tf,df->td", grad_hidden, up_full, preferred_element_type=jnp.float32)
    gain_two_grad = jnp.sum(grad_second * norm_two, axis=0)
    shift_two_grad = jnp.sum(grad_second, axis=0)
    grad_after = grad_y.astype(jnp.float32) + norm_back(
        grad_second * gain_f[:, 1], norm_two, inv_two
    )
    grad_attn = grad_after.astype(jnp.bfloat16)
    sum_attn = jnp.sum(grad_attn, axis=0, dtype=jnp.float32)
    grad_proj = jnp.einsum("td,te->de", mixed, grad_attn, preferred_element_type=jnp.float32)
    grad_mixed = jnp.einsum("te,de->td", grad_attn, proj_full, preferred_element_type=jnp.float32)
    grad_mixed = grad_mixed.astype(jnp.bfloat16).reshape(tok_rows, n_heads, head_size)
    key_groups = {}
    value_groups = {}
    for head_lo in head_starts:
        key_groups[head_lo] = jnp.zeros((tok_rows, group_heads, head_size), jnp.float32)
        value_groups[head_lo] = jnp.zeros((tok_rows, group_heads, head_size), jnp.float32)
    offset = 0
    query_groups = []
    for head_lo in head_starts:
        head_hi = head_lo + group_heads
        query_blk = queries[offset : offset + block_rows, head_lo:head_hi]
        grad_blk = grad_mixed[offset : offset + block_rows, head_lo:head_hi]
        key_part = key_rows[:, head_lo:head_hi]
        scores = block_scores(query_blk, key_part, live_mask, scaling)
        attn_p = jnp.exp(scores - log_sums[offset, head_lo])
        value_groups[head_lo] = jnp.einsum(
            "hqk,qhd->khd",
            attn_p.astype(jnp.bfloat16),
            grad_blk,
            preferred_element_type=jnp.float32,
        )
        grad_prob = jnp.einsum(
            "qhd,khd->hqk",
            grad_blk,
            value_rows[:, head_lo:head_hi],
            preferred_element_type=jnp.float32,
        )
        grad_score = attn_p * (grad_prob - jnp.sum(attn_p * grad_prob, axis=-1, keepdims=True))
        score_low = grad_score.astype(jnp.bfloat16)
        query_groups.append(
            jnp.einsum("hqk,khd->qhd", score_low, key_part, preferred_element_type=jnp.float32)
            * scaling
        )
        key_groups[head_lo] = (
            jnp.einsum("hqk,qhd->khd", score_low, query_blk, preferred_element_type=jnp.float32)
            * scaling
        )
    grad_query_parts = jnp.concatenate(query_groups, axis=1)
    grad_keys = jnp.concatenate([key_groups[head_lo] for head_lo in head_starts], axis=1)
    grad_vals = jnp.concatenate([value_groups[head_lo] for head_lo in head_starts], axis=1)
    grad_joint = jnp.concatenate(
        [
            grad_query_parts.reshape(tok_rows, feat_width),
            grad_keys.reshape(tok_rows, feat_width),
            grad_vals.reshape(tok_rows, feat_width),
        ],
        axis=1,
    ).astype(jnp.bfloat16)
    joint_sums = jnp.sum(grad_joint, axis=0, dtype=jnp.float32)
    grad_qkv = jnp.einsum("td,te->de", first, grad_joint, preferred_element_type=jnp.float32)
    grad_first = jnp.einsum("te,de->td", grad_joint, qkv_full, preferred_element_type=jnp.float32)
    gain_one_grad = jnp.sum(grad_first * norm_one, axis=0)
    shift_one_grad = jnp.sum(grad_first, axis=0)
    grad_tokens = (grad_after + norm_back(grad_first * gain_f[:, 0], norm_one, inv_one)).astype(
        jnp.bfloat16
    )
    grad_gains = jnp.stack([gain_one_grad, gain_two_grad], axis=1)
    grad_shifts = jnp.stack(
        [
            shift_one_grad,
            joint_sums[:feat_width],
            joint_sums[2 * feat_width :],
            sum_attn,
            shift_two_grad,
            sum_y,
        ],
        axis=1,
    )
    owned = give_back(
        grad_qkv, grad_proj, grad_up, grad_down, grad_gains, grad_shifts, grad_bias_up
    )
    own_qkv, own_proj, own_up, own_down, own_gains, own_shifts, own_bias = owned
    return (
        output,
        grad_tokens,
        own_qkv,
        own_proj,
        own_up,
        own_down,
        own_gains,
        own_shifts,
        own_bias,
    )


BOTH_LAST = (((1,), (1,)), ((), ()))
SMEM = pl.BlockSpec(memory_space=pltpu.SMEM)
ANY = pl.BlockSpec(memory_space=pl.ANY)
CORE, LENGTH = 32, 33


def pairs(move):
    return [(i, move(i)) for i in range(32)]


def first_way(i):
    return i ^ (2 if i % 2 == 0 else 4)


def second_way(i):
    return i ^ (4 if i % 2 == 0 else 2)


def along_z(step):
    return lambda i: i ^ (8 * step)


def send(array, move):
    return lax.ppermute(array, AXES, pairs(move))


def swap(array):
    return send(array, lambda i: i ^ 1)


def facts(chip, core, length):
    places = []
    for of_core in (core, 1 - core):
        for j in range(16):
            z, first, second = j % 4, (j // 4) % 2, j // 8
            mask = jnp.where(of_core == 0, first + 2 * second, second + 2 * first)
            places.append(jnp.bitwise_xor(chip, mask + 4 * z))
    return jnp.stack(places + [core, length]).astype(jnp.int32)


def spread(piece):
    near = [send(piece, along_z(s)) for s in (1, 2, 3)]
    zs = jnp.stack([piece] + near)
    low = jnp.concatenate([zs, send(zs, first_way)])
    high = send(low, second_way)
    return low, high, swap(low), swap(high)


def params():
    return pltpu.CompilerParams(vmem_limit_bytes=VMEM_LIMIT)


def cost(flops, nbytes, exps=0):
    return pl.CostEstimate(flops=flops, bytes_accessed=nbytes, transcendentals=exps)


def shape(dims, dtype):
    return jax.ShapeDtypeStruct(dims, dtype)


def full(dims):
    return pl.BlockSpec(dims, lambda *_: (0,) * len(dims))


def dot(left, right):
    return jnp.dot(left, right, preferred_element_type=F32)


def dot_last(left, right):
    return lax.dot_general(left, right, BOTH_LAST, preferred_element_type=F32)


def fetch(info, pieces, dest, sems, by_half):
    copies = []
    for who in (0, 1):
        half = info[CORE] if who == 0 else 1 - info[CORE]
        for j in range(16):
            at = info[16 * who + j]
            src = pieces[2 * who + j // 8].at[j % 8]
            dst = dest.at[half, at] if by_half else dest.at[at, half]
            copies.append(pltpu.make_async_copy(src, dst, sems.at[16 * who + j]))
    for copy in copies:
        copy.start()
    return copies


def centre(values):
    centred = values - jnp.mean(values, axis=-1, keepdims=True)
    inverse = lax.rsqrt(jnp.mean(centred * centred, axis=-1, keepdims=True) + EPS)
    return centred * inverse, inverse


def layer_back(grad, normed, inverse):
    return inverse * (
        grad
        - jnp.mean(grad, axis=-1, keepdims=True)
        - normed * jnp.mean(grad * normed, axis=-1, keepdims=True)
    )


def enter_kernel(info, tokens, low, high, low_o, high_o, weights, vecs, first, joint, sems):
    feat = tokens.shape[1]
    third = feat // 2
    copies = fetch(info, (low, high, low_o, high_o), weights, sems, True)
    normed, _ = centre(tokens[...].astype(F32))
    for copy in copies:
        copy.wait()
    width = weights.shape[-1]
    small = weights[0, :, :, width - 128 :].reshape(feat, 128).astype(F32).T
    vecs[...] = small[:8]
    low_first = (normed * small[0:1] + small[2:3]).astype(BF16)
    first[...] = low_first
    for h in (0, 1):
        for part in range(3):
            w = weights[h, :, :, part * third : (part + 1) * third].reshape(feat, third)
            out = dot(low_first, w)
            if part != 1:
                row = 3 if part == 0 else 4
                out = out + small[row : row + 1, h * third : (h + 1) * third]
            joint[h, :, part * third : (part + 1) * third] = out.astype(BF16)


def enter(info, tokens, pieces):
    rows, feat = tokens.shape
    width = pieces[0].shape[-1]
    return pl.pallas_call(
        enter_kernel,
        out_shape=(
            shape((2, 16, feat // 16, width), BF16),
            shape((8, feat), F32),
            shape((rows, feat), BF16),
            shape((2, rows, 3 * feat // 2), BF16),
        ),
        in_specs=[SMEM, pl.BlockSpec(memory_space=pltpu.VMEM)] + [ANY] * 4,
        out_specs=tuple([pl.BlockSpec(memory_space=pltpu.VMEM)] * 4),
        scratch_shapes=[pltpu.SemaphoreType.DMA((32,))],
        compiler_params=params(),
        cost_estimate=cost(6 * rows * feat * feat, 8 * feat * width + 10 * rows * feat),
    )(info, tokens, *pieces)


def scores_of(info, keys, queries):
    raw = dot_last(keys, queries)
    place = lax.broadcasted_iota(jnp.int32, raw.shape, 0)
    return jnp.where(place < info[LENGTH], raw, NEG)


def mix_kernel(info, q, k, v, mixed, stats):
    head = q.shape[-1] // 2
    scale = head**-0.5
    turned = v[0].T
    outs = []
    for h in (0, 1):
        cols = slice(h * head, (h + 1) * head)
        scores = scores_of(info, k[0, :, cols], q[0, :, cols] * scale)
        most = jnp.max(scores, axis=0, keepdims=True)
        expd = jnp.exp(scores - most)
        total = jnp.sum(expd, axis=0, keepdims=True)
        attn = (expd * (1.0 / total)).astype(BF16)
        stats[0, h : h + 1] = most + jnp.log(total)
        outs.append(dot(turned[cols], attn))
    mixed[...] = jnp.concatenate(outs).T.astype(BF16)


def mix(info, joint):
    _, rows, width = joint.shape
    feat, pair = 2 * width // 3, 2 * width // 3 // HEADS * 2
    per = feat // 2 // pair
    spec = [
        pl.BlockSpec((1, rows, pair), lambda i, part=part: (i // per, 0, part * per + i % per))
        for part in range(3)
    ]
    n = HEADS // 2
    return pl.pallas_call(
        mix_kernel,
        grid=(n,),
        out_shape=(shape((rows, feat), BF16), shape((n, 8, rows), F32)),
        in_specs=[SMEM] + spec,
        out_specs=(
            pl.BlockSpec((rows, pair), lambda i: (0, i)),
            pl.BlockSpec((1, 8, rows), lambda i: (i, 0, 0)),
        ),
        compiler_params=params(),
        cost_estimate=cost(16 * rows * rows * feat, 8 * rows * feat, HEADS * rows * rows),
    )(info, joint, joint, joint)


def mix_back_kernel(info, q, k, v, grad, stats, theirs, mine):
    head = q.shape[-1] // 2
    scale = head**-0.5
    turned = k[0].T
    parts = [[], [], []]
    for h in (0, 1):
        cols = slice(h * head, (h + 1) * head)
        queries = q[0, :, cols] * scale
        grad_h = grad[:, cols]
        attn = jnp.exp(scores_of(info, k[0, :, cols], queries) - stats[0, h : h + 1])
        grad_prob = dot_last(v[0, :, cols], grad_h)
        inner = jnp.sum(attn * grad_prob, axis=0, keepdims=True)
        low = (attn * (grad_prob - inner)).astype(BF16)
        parts[0].append(dot(turned[cols], low) * scale)
        parts[1].append(dot(low, queries))
        parts[2].append(dot(attn.astype(BF16), grad_h))
    out = [
        jnp.concatenate(parts[0]).T.astype(BF16),
        jnp.concatenate(parts[1], axis=1).astype(BF16),
        jnp.concatenate(parts[2], axis=1).astype(BF16),
    ]
    step, per = pl.program_id(0), pl.num_programs(0) // 2

    @pl.when(step < per)
    def _():
        for part in range(3):
            theirs[part] = out[part]

    @pl.when(step >= per)
    def _():
        for part in range(3):
            mine[part] = out[part]


def mix_back(info, joint, grad_mixed, stats):
    _, rows, width = joint.shape
    feat, pair = 2 * width // 3, 2 * width // 3 // HEADS * 2
    per = feat // 2 // pair
    n = HEADS // 2

    def half(i, info):
        return jnp.where(i < per, 1 - info[CORE], info[CORE])

    spec = [
        pl.BlockSpec(
            (1, rows, pair), lambda i, info, part=part: (half(i, info), 0, part * per + i % per)
        )
        for part in range(3)
    ]
    out = shape((3, rows, feat // 2), BF16)
    return pl.pallas_call(
        mix_back_kernel,
        grid_spec=pltpu.PrefetchScalarGridSpec(
            num_scalar_prefetch=1,
            grid=(n,),
            in_specs=spec
            + [
                pl.BlockSpec((rows, pair), lambda i, info: (0, half(i, info) * per + i % per)),
                pl.BlockSpec(
                    (1, 8, rows), lambda i, info: (half(i, info) * per + i % per, 0, 0)
                ),
            ],
            out_specs=(
                pl.BlockSpec((3, rows, pair), lambda i, info: (0, 0, jnp.minimum(i, per - 1))),
                pl.BlockSpec((3, rows, pair), lambda i, info: (0, 0, jnp.maximum(i - per, 0))),
            ),
        ),
        out_shape=(out, out),
        compiler_params=params(),
        cost_estimate=cost(40 * rows * rows * feat, 16 * rows * feat, HEADS * rows * rows),
    )(info, joint, joint, joint, grad_mixed, stats)


GELU = (0.254829592, -0.284496736, 1.421413741, -1.453152027, 1.061405429)


def gelu_parts(x):
    bell = jnp.exp(-0.5 * x * x)
    t = 1.0 / (1.0 + (0.3275911 * 0.5**0.5) * jnp.abs(x))
    poly = GELU[4]
    for c in GELU[3::-1]:
        poly = poly * t + c
    tail = (0.5 * poly) * t * bell
    phi = jnp.where(x < 0, tail, 1.0 - tail)
    return x * phi, phi + x * (bell * (2 * math.pi) ** -0.5)


def rise_kernel(
    info,
    tokens,
    mixed,
    proj,
    vecs,
    bias,
    low,
    high,
    low_o,
    high_o,
    weights,
    after,
    second,
    active,
    slope,
    mine,
    theirs,
    turned,
    sems,
):
    step = pl.program_id(0)
    feat = tokens.shape[1]
    tile = active.shape[1]
    per = weights.shape[-1] // tile
    rows = mine.shape[1]

    @pl.when(step == 0)
    def _():
        copies = fetch(info, (low, high, low_o, high_o), weights, sems, True)
        grown = [dot(mixed[...], proj[h]) for h in (0, 1)]
        total = tokens[...].astype(F32) + jnp.concatenate(grown, axis=1) + vecs[5:6]
        after[...] = total
        normed, _ = centre(total)
        second[...] = (normed * vecs[1:2] + vecs[6:7]).astype(BF16)
        for copy in copies:
            copy.wait()

    cols = pl.ds(pl.multiple_of(lax.rem(step, per) * tile, tile), tile)
    w = weights[step // per, :, :, cols].reshape(feat, tile)
    hidden = dot(second[...], w) + bias[...]
    value, grad = gelu_parts(hidden)
    value = value.astype(BF16)
    active[...] = value
    slope[...] = grad.astype(BF16)
    count = tile // rows
    turned[pl.ds(step * count, count)] = value.T.reshape(count, rows, -1)

    @pl.when(step == pl.num_programs(0) - 1)
    def _():
        core = info[CORE]
        for j in range(16):
            mine[j] = turned[2 * info[j] + core]
            theirs[j] = turned[2 * info[16 + j] + 1 - core]


def rise(info, tokens, mixed, first_set, vecs, bias, pieces):
    rows, feat = tokens.shape
    width = pieces[0].shape[-1]
    hidden = 2 * width
    tile, block = 384, hidden // 32
    turned = shape((16, block, rows), BF16)
    return pl.pallas_call(
        rise_kernel,
        grid=(hidden // tile,),
        out_shape=(
            shape((2, 16, feat // 16, width), BF16),
            shape((rows, feat), F32),
            shape((rows, feat), BF16),
            shape((rows, hidden), BF16),
            shape((rows, hidden), BF16),
            turned,
            turned,
        ),
        in_specs=[
            SMEM,
            full((rows, feat)),
            full((rows, feat)),
            pl.BlockSpec((2, feat, feat // 2), lambda n: (0, 0, 3)),
            full((8, feat)),
            pl.BlockSpec((1, tile), lambda n: (0, n)),
        ]
        + [ANY] * 4,
        out_specs=(
            full((2, 16, feat // 16, width)),
            full((rows, feat)),
            full((rows, feat)),
            pl.BlockSpec((rows, tile), lambda n: (0, n)),
            pl.BlockSpec((rows, tile), lambda n: (0, n)),
            full(turned.shape),
            full(turned.shape),
        ),
        scratch_shapes=[pltpu.VMEM((32, block, rows), BF16), pltpu.SemaphoreType.DMA((32,))],
        compiler_params=params(),
        cost_estimate=cost(
            2 * rows * feat * (feat + hidden), 8 * feat * hidden, rows * hidden
        ),
    )(info, tokens, mixed, first_set, vecs, bias, *pieces)


def leave_kernel(after, active, down, vecs, output):
    output[...] = (after[...] + dot(active[...], down[...]) + vecs[7:8]).astype(BF16)


def leave(after, active, down, vecs):
    rows, feat = after.shape
    hidden = active.shape[1]
    tile = 384
    return pl.pallas_call(
        leave_kernel,
        grid=(feat // tile,),
        out_shape=shape((rows, feat), BF16),
        in_specs=[
            pl.BlockSpec((rows, tile), lambda n: (0, n)),
            full((rows, hidden)),
            pl.BlockSpec((hidden, tile), lambda n: (0, n)),
            pl.BlockSpec((8, tile), lambda n: (0, n)),
        ],
        out_specs=pl.BlockSpec((rows, tile), lambda n: (0, n)),
        compiler_params=params(),
        cost_estimate=cost(2 * rows * feat * hidden, 2 * hidden * (rows + feat)),
    )(after, active, down, vecs)


def fall_kernel(
    info,
    grad_y,
    slope,
    up,
    after,
    vecs,
    proj,
    low,
    high,
    low_o,
    high_o,
    weights,
    theirs,
    mine,
    bias_sum,
    grad_after,
    attn_theirs,
    attn_mine,
    grad_mixed,
    sums,
    grad_second,
    sems,
):
    step, steps = pl.program_id(0), pl.num_programs(0)
    core = info[CORE]
    feat = grad_y.shape[1]
    tile = slope.shape[1]
    per = steps // 2

    @pl.when(step == 0)
    def _():
        for copy in fetch(info, (low, high, low_o, high_o), weights, sems, False):
            copy.wait()
        grad_second[...] = jnp.zeros_like(grad_second)

    half = jnp.where(step < per, 1 - core, core)
    at = half * per + lax.rem(step, per)
    down = weights[pl.ds(2 * at, 2)].reshape(tile, feat)
    grad = (dot_last(grad_y[...], down) * slope[...].astype(F32)).astype(BF16)
    bias_sum[...] = jnp.sum(grad.astype(F32), axis=0, keepdims=True)
    grad_second[...] += dot_last(grad, up[0])

    @pl.when(step < per)
    def _():
        theirs[...] = grad

    @pl.when(step >= per)
    def _():
        mine[...] = grad

    @pl.when(step == steps - 1)
    def _():
        normed, inverse = centre(after[...])
        second = grad_second[...]
        live = grad_y[...].astype(F32)
        sums[0:1] = jnp.sum(second * normed, axis=0, keepdims=True)
        sums[1:2] = jnp.sum(second, axis=0, keepdims=True)
        total = live + layer_back(second * vecs[1:2], normed, inverse)
        grad_after[...] = total
        attn = total.astype(BF16)
        sums[2:3] = jnp.sum(attn.astype(F32), axis=0, keepdims=True)
        sums[3:4] = jnp.sum(live, axis=0, keepdims=True)
        sums[4:8] = jnp.zeros_like(sums[4:8])
        left, right = attn[:, : feat // 2], attn[:, feat // 2 :]
        attn_mine[...] = jnp.where(core == 0, left, right)
        attn_theirs[...] = jnp.where(core == 0, right, left)
        grad_mixed[...] = (dot_last(left, proj[0]) + dot_last(right, proj[1])).astype(BF16)


def fall(info, grad_y, slope, up_set, after, vecs, first_set, pieces):
    rows, feat = grad_y.shape
    hidden = slope.shape[1]
    tile = 384
    steps = hidden // tile
    per = steps // 2

    def at(n, info):
        return jnp.where(n < per, 1 - info[CORE], info[CORE]) * per + n % per

    def whole(dims):
        return pl.BlockSpec(dims, lambda n, info: (0,) * len(dims))

    return pl.pallas_call(
        fall_kernel,
        grid_spec=pltpu.PrefetchScalarGridSpec(
            num_scalar_prefetch=1,
            grid=(steps,),
            in_specs=[
                whole((rows, feat)),
                pl.BlockSpec((rows, tile), lambda n, info: (0, at(n, info))),
                pl.BlockSpec(
                    (1, feat, tile), lambda n, info: (at(n, info) // per, 0, n % per)
                ),
                whole((rows, feat)),
                whole((8, feat)),
                pl.BlockSpec((2, feat, feat // 2), lambda n, info: (0, 0, 3)),
            ]
            + [ANY] * 4,
            out_specs=(
                whole((16, 2, hidden // 32, feat)),
                pl.BlockSpec((rows, tile), lambda n, info: (0, jnp.minimum(n, per - 1))),
                pl.BlockSpec((rows, tile), lambda n, info: (0, jnp.maximum(n - per, 0))),
                pl.BlockSpec((1, tile), lambda n, info: (0, at(n, info))),
                whole((rows, feat)),
                whole((rows, feat // 2)),
                whole((rows, feat // 2)),
                whole((rows, feat)),
                whole((8, feat)),
            ),
            scratch_shapes=[pltpu.VMEM((rows, feat), F32), pltpu.SemaphoreType.DMA((32,))],
        ),
        out_shape=(
            shape((16, 2, hidden // 32, feat), BF16),
            shape((rows, hidden // 2), BF16),
            shape((rows, hidden // 2), BF16),
            shape((1, hidden), F32),
            shape((rows, feat), F32),
            shape((rows, feat // 2), BF16),
            shape((rows, feat // 2), BF16),
            shape((rows, feat), BF16),
            shape((8, feat), F32),
        ),
        compiler_params=params(),
        cost_estimate=cost(
            4 * rows * feat * hidden, 8 * feat * hidden + 8 * rows * hidden
        ),
    )(info, grad_y, slope, up_set, after, vecs, first_set, *pieces)


def exit_kernel(info, tokens, mine, theirs, weights, grad_after, vecs, grad_tokens, sums, grad_first):
    step = pl.program_id(0)
    core = info[CORE]
    third = mine.shape[2]
    half = jnp.where(step == 0, core, 1 - core)
    spot = pl.ds(pl.multiple_of(half * third, third), third)

    def parts(source):
        total = dot_last(source[0], weights[0, :, :third])
        for part in (1, 2):
            cols = slice(part * third, (part + 1) * third)
            total += dot_last(source[part], weights[0, :, cols])
        sums[2:3, spot] = jnp.sum(source[0].astype(F32), axis=0, keepdims=True)
        sums[3:4, spot] = jnp.sum(source[2].astype(F32), axis=0, keepdims=True)
        return total

    @pl.when(step == 0)
    def _():
        grad_first[...] = parts(mine)

    @pl.when(step == 1)
    def _():
        grad = grad_first[...] + parts(theirs)
        normed, inverse = centre(tokens[...].astype(F32))
        sums[0:1] = jnp.sum(grad * normed, axis=0, keepdims=True)
        sums[1:2] = jnp.sum(grad, axis=0, keepdims=True)
        sums[4:8] = jnp.zeros_like(sums[4:8])
        back = layer_back(grad * vecs[0:1], normed, inverse)
        grad_tokens[...] = (grad_after[...] + back).astype(BF16)


def exit_back(info, tokens, mine, theirs, first_set, grad_after, vecs):
    rows, feat = tokens.shape
    third = feat // 2

    def whole(dims):
        return pl.BlockSpec(dims, lambda n, info: (0,) * len(dims))

    return pl.pallas_call(
        exit_kernel,
        grid_spec=pltpu.PrefetchScalarGridSpec(
            num_scalar_prefetch=1,
            grid=(2,),
            in_specs=[
                whole((rows, feat)),
                whole((3, rows, third)),
                whole((3, rows, third)),
                pl.BlockSpec(
                    (1, feat, 3 * third),
                    lambda n, info: (jnp.where(n == 0, info[CORE], 1 - info[CORE]), 0, 0),
                ),
                whole((rows, feat)),
                whole((8, feat)),
            ],
            out_specs=(whole((rows, feat)), whole((8, feat))),
            scratch_shapes=[pltpu.VMEM((rows, feat), F32)],
        ),
        out_shape=(shape((rows, feat), BF16), shape((8, feat), F32)),
        compiler_params=params(),
        cost_estimate=cost(6 * rows * feat * feat, 6 * feat * feat + 12 * rows * feat),
    )(info, tokens, mine, theirs, first_set, grad_after, vecs)


def outer_kernel(info, left, left_o, right, right_o, keep, away, turned, blocks):
    rows = left.shape[0]

    @pl.when(pl.program_id(0) == 0)
    def _():
        turned[:, :rows] = left[...].T
        turned[:, rows:] = left_o[...].T

    total = dot(turned[:, :rows], right[0]) + dot(turned[:, rows:], right_o[0])
    blocks[...] = total.reshape(blocks.shape)
    for j in range(8):
        keep[j] = blocks[info[j]]
        away[j] = blocks[info[8 + j]].astype(BF16)


def outer(info, left, left_o, right, right_o, tile=384):
    rows, feat = left.shape
    n_parts, _, width = right.shape
    per = width // tile
    cols = n_parts * width
    block = feat // 16
    strip = pl.BlockSpec((1, rows, tile), lambda n: (n // per, 0, n % per))
    out = pl.BlockSpec((8, block, tile), lambda n: (0, 0, n))
    return pl.pallas_call(
        outer_kernel,
        grid=(cols // tile,),
        out_shape=(shape((8, block, cols), F32), shape((8, block, cols), BF16)),
        in_specs=[SMEM, full((rows, feat)), full((rows, feat)), strip, strip],
        out_specs=(out, out),
        scratch_shapes=[pltpu.VMEM((feat, 2 * rows), BF16), pltpu.VMEM((16, block, tile), F32)],
        compiler_params=params(),
        cost_estimate=cost(4 * rows * feat * cols, 4 * rows * (feat + cols) + 3 * feat * cols),
    )(info, left, left_o, right, right_o)


def outer_last_kernel(
    info, left, left_o, right, right_o, sums_a, sums_b, bias, keep, away, blocks, extra
):
    rows, feat = left.shape
    tile = right.shape[1]
    block = feat // 16
    total = dot(left[...].T, right[...]) + dot(left_o[...].T, right_o[...])
    blocks[...] = total.reshape(blocks.shape)
    extra[...] = jnp.zeros_like(extra)
    ordered = jnp.concatenate(
        [
            sums_b[0:1],
            sums_a[0:1],
            sums_b[1:4],
            sums_a[2:3],
            sums_a[1:2],
            sums_a[3:4],
        ]
    )
    each = bias.shape[1] // 16
    for chip in range(16):
        extra[chip, 0:8, 0:block] = ordered[:, chip * block : (chip + 1) * block]
        extra[chip, 8:9, 0:each] = bias[:, chip * each : (chip + 1) * each]
    for j in range(8):
        keep[j, :block] = blocks[info[j]]
        away[j, :block] = blocks[info[8 + j]].astype(BF16)
        keep[j, block:] = extra[info[j]]
        away[j, block:] = extra[info[8 + j]].astype(BF16)


def outer_last(info, left, left_o, right, right_o, sums_a, sums_b, bias):
    rows, feat = left.shape
    cols = right.shape[1]
    block = feat // 16
    vmem = pl.BlockSpec(memory_space=pltpu.VMEM)
    return pl.pallas_call(
        outer_last_kernel,
        out_shape=(shape((8, block + 16, cols), F32), shape((8, block + 16, cols), BF16)),
        in_specs=[SMEM] + [vmem] * 7,
        out_specs=(vmem, vmem),
        scratch_shapes=[pltpu.VMEM((16, block, cols), F32), pltpu.VMEM((16, 16, cols), F32)],
        compiler_params=params(),
        cost_estimate=cost(4 * rows * feat * cols, 4 * rows * (feat + cols) + 3 * feat * cols),
    )(info, left, left_o, right, right_o, sums_a, sums_b, bias)


def outer_down_kernel(left, left_o, right, right_o, keep, away):
    def flat(blocks):
        return blocks[...].reshape(-1, blocks.shape[-1])

    total = dot(flat(left), right[...]) + dot(flat(left_o), right_o[...])
    total = total.reshape(keep.shape)

    @pl.when(pl.program_id(0) >= 4)
    def _():
        keep[...] = total

    @pl.when(pl.program_id(0) < 4)
    def _():
        away[...] = total.astype(BF16)


def outer_down(left, left_o, right, right_o):
    _, block, rows = left.shape
    feat = right.shape[1]
    strip = pl.BlockSpec((2, block, rows), lambda j: ((j + 4) % 8, 0, 0))
    return pl.pallas_call(
        outer_down_kernel,
        grid=(8,),
        out_shape=(shape((8, block, feat), F32), shape((8, block, feat), BF16)),
        in_specs=[strip, strip, full((rows, feat)), full((rows, feat))],
        out_specs=(
            pl.BlockSpec((2, block, feat), lambda j: (jnp.maximum(j - 4, 0), 0, 0)),
            pl.BlockSpec((2, block, feat), lambda j: (jnp.minimum(j, 3), 0, 0)),
        ),
        compiler_params=params(),
        cost_estimate=cost(64 * rows * feat * block, 96 * block * (rows + feat)),
    )(left, left_o, right, right_o)


def add_first_kernel(keep, got, keep_s, got_s, kept, away):
    kept[...] = keep[...] + got[...].astype(F32)
    away[...] = (keep_s[...] + got_s[...].astype(F32)).astype(BF16)


def add_first(keep, got):
    _, rows, cols = keep.shape
    near = pl.BlockSpec((1, rows, cols), lambda i: (i, 0, 0))
    far = pl.BlockSpec((1, rows, cols), lambda i: (i + 4, 0, 0))
    return pl.pallas_call(
        add_first_kernel,
        grid=(4,),
        out_shape=(shape((4, rows, cols), F32), shape((4, rows, cols), BF16)),
        in_specs=[near, near, far, far],
        out_specs=(near, near),
        compiler_params=params(),
        cost_estimate=cost(8 * rows * cols, 72 * rows * cols),
    )(keep, got, keep, got)


def add_second_kernel(keep, got, base, one, two, three):
    base[...] = keep[0] + got[0].astype(F32)
    for s, out in ((1, one), (2, two), (3, three)):
        out[...] = (keep[s] + got[s].astype(F32)).astype(BF16)


def add_second(keep, got):
    _, rows, cols = keep.shape
    vmem = pl.BlockSpec(memory_space=pltpu.VMEM)
    low = shape((rows, cols), BF16)
    return pl.pallas_call(
        add_second_kernel,
        out_shape=(shape((rows, cols), F32), low, low, low),
        in_specs=[vmem] * 2,
        out_specs=(vmem,) * 4,
        compiler_params=params(),
        cost_estimate=cost(4 * rows * cols, 34 * rows * cols),
    )(keep, got)


def total_of(base, parts):
    return base[...] + parts[0][...].astype(F32) + (
        parts[1][...].astype(F32) + parts[2][...].astype(F32)
    )


def add_down_kernel(base, one, two, three, out):
    out[...] = total_of(base, (one, two, three))


def add_last_kernel(info, base, one, two, three, mine, theirs, total):
    core = info[CORE]
    half = mine.shape[0]
    total[...] = total_of(base, (one, two, three))
    mine[...] = total[pl.ds(pl.multiple_of(core * half, half), half)]
    theirs[...] = total[pl.ds(pl.multiple_of((1 - core) * half, half), half)]


def add_small_kernel(info, base, one, two, three, mine, theirs, total):
    core = info[CORE]
    half = mine.shape[0] - 16
    total[...] = total_of(base, (one, two, three))
    mine[:half] = total[pl.ds(pl.multiple_of(core * half, half), half)]
    theirs[:half] = total[pl.ds(pl.multiple_of((1 - core) * half, half), half)]
    mine[half:] = total[2 * half :]
    theirs[half:] = total[2 * half :]


def travel(keep, away):
    kept, away = add_first(keep, send(away, second_way))
    base, *lows = add_second(kept, send(away, first_way))
    return base, [send(low, along_z(s)) for low, s in zip(lows, (1, 2, 3))]


def home_down(keep, away):
    base, parts = travel(keep, away)
    vmem = pl.BlockSpec(memory_space=pltpu.VMEM)
    return pl.pallas_call(
        add_down_kernel,
        out_shape=shape(base.shape, F32),
        in_specs=[vmem] * 4,
        out_specs=vmem,
        compiler_params=params(),
        cost_estimate=cost(3 * base.size, 14 * base.size),
    )(base, *parts)


def home(info, keep, away, kernel, extra):
    base, parts = travel(keep, away)
    rows, cols = base.shape
    vmem = pl.BlockSpec(memory_space=pltpu.VMEM)
    out = shape(((rows - extra) // 2 + extra, cols), F32)
    mine, theirs = pl.pallas_call(
        kernel,
        out_shape=(out, out),
        in_specs=[SMEM] + [vmem] * 4,
        out_specs=(vmem, vmem),
        scratch_shapes=[pltpu.VMEM((rows, cols), F32)],
        compiler_params=params(),
        cost_estimate=cost(3 * base.size, 14 * base.size),
    )(info, base, *parts)
    return mine, swap(theirs)


def finish_kernel(
    info, qkv, qkv_o, proj, proj_o, up, up_o, out_qkv, out_proj, out_up, gains, shifts, bias
):
    rows, third = out_proj.shape[0], proj.shape[1]
    wide = up.shape[1]
    small = proj[rows:] + proj_o[rows:]
    each = 4 * rows

    def lay(core):
        for half, (a, b, c) in ((core, (qkv, proj, up)), (1 - core, (qkv_o, proj_o, up_o))):
            for part in range(3):
                spot = part * 2 * third + half * third
                out_qkv[:, spot : spot + third] = a[:, part * third : (part + 1) * third]
            out_proj[:, half * third : (half + 1) * third] = b[:rows]
            out_up[:, half * wide : (half + 1) * wide] = c[...]
        mine = small[0:8, core * rows : (core + 1) * rows]
        wide_mine = jnp.concatenate([mine, jnp.zeros((8, 128 - rows), F32)], axis=1).T
        gains[...] = wide_mine[:rows, 0:2]
        shifts[...] = wide_mine[:rows, 2:8]
        bias[...] = small[8:9, core * each : (core + 1) * each]

    @pl.when(info[CORE] == 0)
    def _():
        lay(0)

    @pl.when(info[CORE] == 1)
    def _():
        lay(1)


def finish(info, qkv, qkv_o, proj, proj_o, up, up_o):
    rows, third = up.shape[0], proj.shape[1]
    vmem = pl.BlockSpec(memory_space=pltpu.VMEM)
    return pl.pallas_call(
        finish_kernel,
        out_shape=(
            shape((rows, 6 * third), F32),
            shape((rows, 2 * third), F32),
            shape((rows, 2 * up.shape[1]), F32),
            shape((rows, 2), F32),
            shape((rows, 6), F32),
            shape((1, 4 * rows), F32),
        ),
        in_specs=[SMEM] + [vmem] * 6,
        out_specs=(vmem,) * 6,
        compiler_params=params(),
        cost_estimate=cost(0, 64 * rows * third),
    )(info, qkv, qkv_o, proj, proj_o, up, up_o)


def local(
    tokens,
    upstream,
    lengths,
    qkv_weight,
    proj_weight,
    up_weight,
    down_weight,
    gains,
    shifts,
    up_bias,
):
    tok_rows, feat = tokens.shape
    rows = qkv_weight.shape[0]
    hidden = up_weight.shape[1]
    third, wide = feat // 2, hidden // 2
    chip, core = lax.axis_index("dp"), lax.axis_index("fsdp")
    info = facts(chip, core, lengths[0])

    live = lax.iota(jnp.int32, tok_rows) < lengths[0]
    grad_y = jnp.where(live[:, None], upstream, jnp.zeros_like(upstream))

    small = jnp.concatenate([gains, shifts, up_bias.reshape(rows, -1)], axis=1)
    small = jnp.pad(small, ((0, 0), (0, 128 - small.shape[1])))

    def half_of(h):
        parts = [qkv_weight[:, i * feat + h * third : i * feat + (h + 1) * third] for i in range(3)]
        parts += [proj_weight[:, h * third : (h + 1) * third], small]
        parts += [up_weight[:, h * wide : (h + 1) * wide]]
        return jnp.concatenate(parts, axis=1)

    halves = jnp.stack([half_of(0), half_of(1)])
    mine = lax.dynamic_index_in_dim(halves, core, 0, keepdims=False)
    given = swap(lax.dynamic_index_in_dim(halves, 1 - core, 0, keepdims=False))
    piece = jnp.where(core == 0, jnp.concatenate([mine, given]), jnp.concatenate([given, mine]))
    one = 4 * third + 128
    first_pieces = spread(piece[:, :one])
    up_pieces = spread(piece[:, one:])
    down_pieces = spread(down_weight)
    grad_y_o = swap(grad_y)

    first_set, vecs, first, joint = enter(info, tokens, first_pieces)
    bias = first_set[0, :, :, one - 120 : one - 116].reshape(1, hidden).astype(F32)
    first_set = first_set.reshape(2, feat, one)
    first_o = swap(first)
    mixed, stats = mix(info, joint)
    mixed_o = swap(mixed)
    up_set, after, second, active, slope, turned, turned_t = rise(
        info, tokens, mixed, first_set, vecs, bias, up_pieces
    )
    second_o, turned_o = swap(second), swap(turned_t)
    own_down = home_down(*outer_down(turned, turned_o, grad_y, grad_y_o))

    down_set, hid_theirs, hid_mine, bias_sum, grad_after, at_theirs, at_mine, grad_mixed, sums_a = (
        fall(info, grad_y, slope, up_set.reshape(2, feat, wide), after, vecs, first_set, down_pieces)
    )
    hid_o, at_o = swap(hid_theirs), swap(at_theirs)
    own_up = home(
        info, *outer(info, second, second_o, hid_mine[None], hid_o[None]), add_last_kernel, 0
    )
    theirs, mine = mix_back(info, joint, grad_mixed, stats)
    own_qkv = home(info, *outer(info, first, first_o, mine, swap(theirs)), add_last_kernel, 0)
    grad_tokens, sums_b = exit_back(info, tokens, mine, theirs, first_set, grad_after, vecs)
    own_last = home(
        info,
        *outer_last(info, mixed, mixed_o, at_mine, at_o, sums_a, sums_b, bias_sum),
        add_small_kernel,
        16,
    )
    output = leave(after, active, down_set.reshape(hidden, feat), vecs)
    out_qkv, out_proj, out_up, out_gains, out_shifts, out_bias = finish(
        info, *own_qkv, *own_last, *own_up
    )
    return (
        output,
        grad_tokens,
        out_qkv,
        out_proj,
        out_up,
        own_down,
        out_gains,
        out_shifts,
        out_bias.reshape(-1),
    )


def solution(mesh):
    placed = (
        P(("dp", "fsdp"), None),
        P(("dp", "fsdp"), None),
        P(("dp", "fsdp")),
        P(("dp", "fsdp"), None),
        P(("dp", "fsdp"), None),
        P(("dp", "fsdp"), None),
        P(("dp", "fsdp"), None),
        P(("dp", "fsdp"), None),
        P(("dp", "fsdp"), None),
        P(("dp", "fsdp")),
    )
    sizes = (mesh.shape["dp"], mesh.shape["fsdp"])
    return jax.shard_map(
        local if sizes == (16, 2) else plain,
        mesh=mesh,
        in_specs=placed,
        out_specs=(
            P(("dp", "fsdp"), None),
            P(("dp", "fsdp"), None),
            P(("dp", "fsdp"), None),
            P(("dp", "fsdp"), None),
            P(("dp", "fsdp"), None),
            P(("dp", "fsdp"), None),
            P(("dp", "fsdp"), None),
            P(("dp", "fsdp"), None),
            P(("dp", "fsdp")),
        ),
        check_vma=False,
    )
```

```python
import math
from functools import partial

import jax
import jax.numpy as jnp
from jax import lax
from jax.experimental import pallas as pl
from jax.experimental.pallas import tpu as pltpu
from jax.sharding import PartitionSpec as P

HEADS = 12
EPS = 1e-06
NEG = -1e30
AXES = ("dp", "fsdp")
F32 = jnp.float32
BF16 = jnp.bfloat16
VMEM_LIMIT = 56 * 1024 * 1024


def collect(qkv_weight, proj_weight, up_weight, down_weight, gains, shifts, up_bias):
    gathered = (
        lax.all_gather(qkv_weight, ("dp", "fsdp"), axis=0, tiled=True),
        lax.all_gather(proj_weight, ("dp", "fsdp"), axis=0, tiled=True),
        lax.all_gather(up_weight, ("dp", "fsdp"), axis=0, tiled=True),
        lax.all_gather(down_weight, ("dp", "fsdp"), axis=0, tiled=True),
        lax.all_gather(gains, ("dp", "fsdp"), axis=0, tiled=True),
        lax.all_gather(shifts, ("dp", "fsdp"), axis=0, tiled=True),
        lax.all_gather(up_bias, ("dp", "fsdp"), axis=0, tiled=True),
    )
    return gathered


def give_back(grad_qkv, grad_proj, grad_up, grad_down, grad_gains, grad_shifts, grad_bias_up):
    owned = (
        lax.psum_scatter(grad_qkv, ("dp", "fsdp"), scatter_dimension=0, tiled=True),
        lax.psum_scatter(grad_proj, ("dp", "fsdp"), scatter_dimension=0, tiled=True),
        lax.psum_scatter(grad_up, ("dp", "fsdp"), scatter_dimension=0, tiled=True),
        lax.psum_scatter(grad_down, ("dp", "fsdp"), scatter_dimension=0, tiled=True),
        lax.psum_scatter(grad_gains, ("dp", "fsdp"), scatter_dimension=0, tiled=True),
        lax.psum_scatter(grad_shifts, ("dp", "fsdp"), scatter_dimension=0, tiled=True),
        lax.psum_scatter(grad_bias_up, ("dp", "fsdp"), scatter_dimension=0, tiled=True),
    )
    return owned


def normalize(values):
    centred = values - jnp.mean(values, axis=-1, keepdims=True)
    inverse = lax.rsqrt(jnp.mean(centred * centred, axis=-1, keepdims=True) + EPS)
    return (centred * inverse, inverse)


def norm_back(grad_norm, normed, inverse):
    return inverse * (
        grad_norm
        - jnp.mean(grad_norm, axis=-1, keepdims=True)
        - normed * jnp.mean(grad_norm * normed, axis=-1, keepdims=True)
    )


def block_scores(query_blk, key_rows, live_mask, scaling):
    raw = (
        jnp.einsum("qhd,khd->hqk", query_blk, key_rows, preferred_element_type=jnp.float32)
        * scaling
    )
    return jnp.where(live_mask[None, None, :], raw, NEG)


def plain(
    tokens,
    upstream,
    lengths,
    qkv_weight,
    proj_weight,
    up_weight,
    down_weight,
    gains,
    shifts,
    up_bias,
):
    tok_rows, feat_width = tokens.shape
    n_heads = HEADS
    head_size = feat_width // n_heads
    scaling = head_size ** (-0.5)
    block_rows = min(512, tok_rows)
    group_heads = 4
    head_starts = list(range(0, n_heads, group_heads))
    gathered = collect(qkv_weight, proj_weight, up_weight, down_weight, gains, shifts, up_bias)
    qkv_full, proj_full, up_full, down_full, gain_full, shift_full, bias_full = gathered
    gain_f = gain_full.astype(jnp.float32)
    shift_f = shift_full.astype(jnp.float32)
    bias_f = bias_full.astype(jnp.float32)
    live_mask = lax.iota(jnp.int32, tok_rows) < lengths[0]
    source = tokens.astype(jnp.float32)
    norm_one, inv_one = normalize(source)
    first = (norm_one * gain_f[:, 0] + shift_f[:, 0]).astype(jnp.bfloat16)
    joint_bias = jnp.concatenate([shift_f[:, 1], jnp.zeros_like(shift_f[:, 1]), shift_f[:, 2]])
    joint = (jnp.dot(first, qkv_full, preferred_element_type=jnp.float32) + joint_bias).astype(
        jnp.bfloat16
    )
    queries = joint[:, :feat_width].reshape(tok_rows, n_heads, head_size)
    key_rows = joint[:, feat_width : 2 * feat_width].reshape(tok_rows, n_heads, head_size)
    value_rows = joint[:, 2 * feat_width :].reshape(tok_rows, n_heads, head_size)
    log_sums = {}
    offset = 0
    group_parts = []
    for head_lo in head_starts:
        head_hi = head_lo + group_heads
        scores = block_scores(
            queries[offset : offset + block_rows, head_lo:head_hi],
            key_rows[:, head_lo:head_hi],
            live_mask,
            scaling,
        )
        row_max = jnp.max(scores, axis=-1, keepdims=True)
        expd = jnp.exp(scores - row_max)
        row_sum = jnp.sum(expd, axis=-1, keepdims=True)
        attn_low = (expd / row_sum).astype(jnp.bfloat16)
        log_sums[offset, head_lo] = row_max + jnp.log(row_sum)
        group_parts.append(
            jnp.einsum(
                "hqk,khd->qhd",
                attn_low,
                value_rows[:, head_lo:head_hi],
                preferred_element_type=jnp.float32,
            )
        )
    mixed_parts = jnp.concatenate(group_parts, axis=1)
    mixed = mixed_parts.reshape(tok_rows, feat_width).astype(jnp.bfloat16)
    after = source + jnp.dot(mixed, proj_full, preferred_element_type=jnp.float32) + shift_f[:, 3]
    norm_two, inv_two = normalize(after)
    second = (norm_two * gain_f[:, 1] + shift_f[:, 4]).astype(jnp.bfloat16)
    hidden = jnp.dot(second, up_full, preferred_element_type=jnp.float32) + bias_f
    gelu_exact = partial(jax.nn.gelu, approximate=False)
    active = gelu_exact(hidden).astype(jnp.bfloat16)
    output = (
        after + jnp.dot(active, down_full, preferred_element_type=jnp.float32) + shift_f[:, 5]
    ).astype(jnp.bfloat16)
    regathered = collect(qkv_weight, proj_weight, up_weight, down_weight, gains, shifts, up_bias)
    qkv_full, proj_full, up_full, down_full, gain_full, shift_full, bias_full = regathered
    grad_y = jnp.where(live_mask[:, None], upstream, jnp.zeros_like(upstream))
    sum_y = jnp.sum(grad_y, axis=0, dtype=jnp.float32)
    grad_down = jnp.einsum("tf,td->fd", active, grad_y, preferred_element_type=jnp.float32)
    grad_active = jnp.einsum("td,fd->tf", grad_y, down_full, preferred_element_type=jnp.float32)
    gelu_value, gelu_pull = jax.vjp(gelu_exact, hidden)
    grad_hidden = gelu_pull(grad_active)[0].astype(jnp.bfloat16)
    grad_bias_up = jnp.sum(grad_hidden, axis=0, dtype=jnp.float32)
    grad_up = jnp.einsum("td,tf->df", second, grad_hidden, preferred_element_type=jnp.float32)
    grad_second = jnp.einsum("tf,df->td", grad_hidden, up_full, preferred_element_type=jnp.float32)
    gain_two_grad = jnp.sum(grad_second * norm_two, axis=0)
    shift_two_grad = jnp.sum(grad_second, axis=0)
    grad_after = grad_y.astype(jnp.float32) + norm_back(
        grad_second * gain_f[:, 1], norm_two, inv_two
    )
    grad_attn = grad_after.astype(jnp.bfloat16)
    sum_attn = jnp.sum(grad_attn, axis=0, dtype=jnp.float32)
    grad_proj = jnp.einsum("td,te->de", mixed, grad_attn, preferred_element_type=jnp.float32)
    grad_mixed = jnp.einsum("te,de->td", grad_attn, proj_full, preferred_element_type=jnp.float32)
    grad_mixed = grad_mixed.astype(jnp.bfloat16).reshape(tok_rows, n_heads, head_size)
    key_groups = {}
    value_groups = {}
    for head_lo in head_starts:
        key_groups[head_lo] = jnp.zeros((tok_rows, group_heads, head_size), jnp.float32)
        value_groups[head_lo] = jnp.zeros((tok_rows, group_heads, head_size), jnp.float32)
    offset = 0
    query_groups = []
    for head_lo in head_starts:
        head_hi = head_lo + group_heads
        query_blk = queries[offset : offset + block_rows, head_lo:head_hi]
        grad_blk = grad_mixed[offset : offset + block_rows, head_lo:head_hi]
        key_part = key_rows[:, head_lo:head_hi]
        scores = block_scores(query_blk, key_part, live_mask, scaling)
        attn_p = jnp.exp(scores - log_sums[offset, head_lo])
        value_groups[head_lo] = jnp.einsum(
            "hqk,qhd->khd",
            attn_p.astype(jnp.bfloat16),
            grad_blk,
            preferred_element_type=jnp.float32,
        )
        grad_prob = jnp.einsum(
            "qhd,khd->hqk",
            grad_blk,
            value_rows[:, head_lo:head_hi],
            preferred_element_type=jnp.float32,
        )
        grad_score = attn_p * (grad_prob - jnp.sum(attn_p * grad_prob, axis=-1, keepdims=True))
        score_low = grad_score.astype(jnp.bfloat16)
        query_groups.append(
            jnp.einsum("hqk,khd->qhd", score_low, key_part, preferred_element_type=jnp.float32)
            * scaling
        )
        key_groups[head_lo] = (
            jnp.einsum("hqk,qhd->khd", score_low, query_blk, preferred_element_type=jnp.float32)
            * scaling
        )
    grad_query_parts = jnp.concatenate(query_groups, axis=1)
    grad_keys = jnp.concatenate([key_groups[head_lo] for head_lo in head_starts], axis=1)
    grad_vals = jnp.concatenate([value_groups[head_lo] for head_lo in head_starts], axis=1)
    grad_joint = jnp.concatenate(
        [
            grad_query_parts.reshape(tok_rows, feat_width),
            grad_keys.reshape(tok_rows, feat_width),
            grad_vals.reshape(tok_rows, feat_width),
        ],
        axis=1,
    ).astype(jnp.bfloat16)
    joint_sums = jnp.sum(grad_joint, axis=0, dtype=jnp.float32)
    grad_qkv = jnp.einsum("td,te->de", first, grad_joint, preferred_element_type=jnp.float32)
    grad_first = jnp.einsum("te,de->td", grad_joint, qkv_full, preferred_element_type=jnp.float32)
    gain_one_grad = jnp.sum(grad_first * norm_one, axis=0)
    shift_one_grad = jnp.sum(grad_first, axis=0)
    grad_tokens = (grad_after + norm_back(grad_first * gain_f[:, 0], norm_one, inv_one)).astype(
        jnp.bfloat16
    )
    grad_gains = jnp.stack([gain_one_grad, gain_two_grad], axis=1)
    grad_shifts = jnp.stack(
        [
            shift_one_grad,
            joint_sums[:feat_width],
            joint_sums[2 * feat_width :],
            sum_attn,
            shift_two_grad,
            sum_y,
        ],
        axis=1,
    )
    owned = give_back(
        grad_qkv, grad_proj, grad_up, grad_down, grad_gains, grad_shifts, grad_bias_up
    )
    own_qkv, own_proj, own_up, own_down, own_gains, own_shifts, own_bias = owned
    return (
        output,
        grad_tokens,
        own_qkv,
        own_proj,
        own_up,
        own_down,
        own_gains,
        own_shifts,
        own_bias,
    )


BOTH_LAST = (((1,), (1,)), ((), ()))
SMEM = pl.BlockSpec(memory_space=pltpu.SMEM)
ANY = pl.BlockSpec(memory_space=pl.ANY)
CORE, LENGTH, PLACE, PLACE_O = 32, 33, 34, 50


def pairs(move):
    return [(i, move(i)) for i in range(32)]


def first_way(i):
    return i ^ (2 if i % 2 == 0 else 4)


def second_way(i):
    return i ^ (4 if i % 2 == 0 else 2)


def along_z(step):
    return lambda i: i ^ (8 * step)


def send(array, move):
    return lax.ppermute(array, AXES, pairs(move))


def swap(array):
    return send(array, lambda i: i ^ 1)


def facts(chip, core, length):
    places = []
    for of_core in (core, 1 - core):
        for j in range(16):
            z, first, second = j % 4, (j // 4) % 2, j // 8
            mask = jnp.where(of_core == 0, first + 2 * second, second + 2 * first)
            places.append(jnp.bitwise_xor(chip, mask + 4 * z))
    spots = []
    for of_core in (core, 1 - core):
        for k in range(16):
            mask = jnp.bitwise_xor(chip, k)
            x, y, z = mask & 1, (mask >> 1) & 1, mask >> 2
            spots.append(z + jnp.where(of_core == 0, 4 * x + 8 * y, 4 * y + 8 * x))
    return jnp.stack(places + [core, length] + spots).astype(jnp.int32)


def params():
    return pltpu.CompilerParams(vmem_limit_bytes=VMEM_LIMIT)


def cost(micros):
    flops = int(micros * (3e10 if micros > 3 else 1e9))
    return pl.CostEstimate(flops=flops, bytes_accessed=1, transcendentals=0)


def shape(dims, dtype):
    return jax.ShapeDtypeStruct(dims, dtype)


def full(dims):
    return pl.BlockSpec(dims, lambda *_: (0,) * len(dims))


def dot(left, right):
    return jnp.dot(left, right, preferred_element_type=F32)


def dot_last(left, right):
    return lax.dot_general(left, right, BOTH_LAST, preferred_element_type=F32)


def fetch(info, pieces, dest, sems, by_half):
    copies = []
    for who in (0, 1):
        half = info[CORE] if who == 0 else 1 - info[CORE]
        for j in range(16):
            at = info[16 * who + j]
            src = pieces[2 * who + j // 8].at[j % 8]
            dst = dest.at[half, at] if by_half else dest.at[at, half]
            copies.append(pltpu.make_async_copy(src, dst, sems.at[16 * who + j]))
    for copy in copies:
        copy.start()
    return copies


def centre(values):
    centred = values - jnp.mean(values, axis=-1, keepdims=True)
    inverse = lax.rsqrt(jnp.mean(centred * centred, axis=-1, keepdims=True) + EPS)
    return centred * inverse, inverse


def layer_back(grad, normed, inverse):
    return inverse * (
        grad
        - jnp.mean(grad, axis=-1, keepdims=True)
        - normed * jnp.mean(grad * normed, axis=-1, keepdims=True)
    )


def halves_kernel(info, qkv, proj, up, mine, theirs):
    feat = proj.shape[1]
    third, wide = feat // 2, up.shape[1] // 2

    def lay(out, h):
        for i in range(3):
            cols = slice(i * feat + h * third, i * feat + (h + 1) * third)
            out[:, i * third : (i + 1) * third] = qkv[:, cols]
        out[:, 3 * third : 3 * third + wide] = up[:, h * wide : (h + 1) * wide]
        out[:, 3 * third + wide :] = proj[:, h * third : (h + 1) * third]

    @pl.when(info[CORE] == 0)
    def _():
        lay(mine, 0)
        lay(theirs, 1)

    @pl.when(info[CORE] == 1)
    def _():
        lay(mine, 1)
        lay(theirs, 0)


def halves(info, qkv, proj, up):
    rows = qkv.shape[0]
    width = (qkv.shape[1] + proj.shape[1] + up.shape[1]) // 2
    vmem = pl.BlockSpec(memory_space=pltpu.VMEM)
    out = shape((rows, width), BF16)
    return pl.pallas_call(
        halves_kernel,
        out_shape=(out, out),
        in_specs=[SMEM] + [vmem] * 3,
        out_specs=(vmem, vmem),
        compiler_params=params(),
        name="halves",
        cost_estimate=cost(2),
    )(info, qkv, proj, up)


def pieces_kernel(info, mine, given, small, one, two):
    ours, others = mine[...].astype(F32), given[...].astype(F32)
    few = small[...].astype(F32)
    none = jnp.zeros_like(few)
    first = info[CORE] == 0

    def stack(a, b):
        return jnp.concatenate([jnp.where(first, a, b), jnp.where(first, b, a)]).astype(BF16)

    split = one.shape[2] - few.shape[1]
    one[0, :, :split] = stack(ours[:, :split], others[:, :split])
    one[0, :, split:] = stack(few, none)
    two[0] = stack(ours[:, split:], others[:, split:])


def pieces_of(info, mine, given, small, split):
    rows, width = mine.shape
    one = split + small.shape[1]
    vmem = pl.BlockSpec(memory_space=pltpu.VMEM)
    return pl.pallas_call(
        pieces_kernel,
        out_shape=(shape((1, 2 * rows, one), BF16), shape((1, 2 * rows, width - split), BF16)),
        in_specs=[SMEM, vmem, vmem, vmem],
        out_specs=(vmem, vmem),
        compiler_params=params(),
        name="pieces_of",
        cost_estimate=cost(2),
    )(info, mine, given, small)


def gather_kernel(n_in, n_held, *refs):
    parts = refs[:n_in]
    out = refs[n_in + n_held]
    at = 0
    for part in parts:
        out[at : at + part.shape[0]] = part[...]
        at += part.shape[0]


def gather(parts, held=(), behind=()):
    vmem = pl.BlockSpec(memory_space=pltpu.VMEM)
    _, rows, cols = parts[0].shape
    count = sum(part.shape[0] for part in parts)
    n, n_held = len(parts), len(held)
    return pl.pallas_call(
        partial(gather_kernel, n, n_held + len(behind)),
        out_shape=(shape((count, rows, cols), BF16),) + tuple(shape(h.shape, h.dtype) for h in held),
        in_specs=[vmem] * n + [ANY] * (n_held + len(behind)),
        out_specs=(vmem,) + (ANY,) * n_held,
        input_output_aliases={n + i: 1 + i for i in range(n_held)},
        compiler_params=params(),
        name="gather",
        cost_estimate=cost(2),
    )(*parts, *held, *behind)


def gate_kernel(array, behind, out):
    pass


def gate(array, behind):
    return pl.pallas_call(
        gate_kernel,
        out_shape=shape(array.shape, array.dtype),
        in_specs=[ANY, ANY],
        out_specs=ANY,
        input_output_aliases={0: 0},
        compiler_params=params(),
        name="gate",
        cost_estimate=cost(1),
    )(array, behind)


def near_z(piece, steps):
    return [send(piece, along_z(s)) for s in steps]


def enter_kernel(
    info, tokens, low, high, low_o, high_o, kept, vecs, first, flipped, joint, weights, sems, sem
):
    feat = tokens.shape[1]
    third = feat // 2
    copies = fetch(info, (low, high, low_o, high_o), weights, sems, True)
    normed, _ = centre(tokens[...].astype(F32))
    for copy in copies:
        copy.wait()
    out = pltpu.make_async_copy(weights, kept, sem)
    out.start()
    split = 3 * third
    small = weights[0, :, :, split:] + weights[1, :, :, split:]
    small = small.reshape(feat, 128).astype(F32).T
    vecs[...] = small[:8]
    low_first = (normed * small[0:1] + small[2:3]).astype(BF16)
    first[...] = low_first
    flipped[...] = low_first.T.reshape(flipped.shape)
    for h in (0, 1):
        cols = slice(h * third, (h + 1) * third)
        bias = jnp.concatenate(
            [small[3:4, cols], jnp.zeros((1, third), F32), small[4:5, cols]], axis=1
        )
        w = weights[h, :, :, :split].reshape(feat, split)
        joint[h] = (dot(low_first, w) + bias).astype(BF16)
    out.wait()


def enter(info, tokens, pieces):
    rows, feat = tokens.shape
    width = pieces[0].shape[-1]
    vmem = pl.BlockSpec(memory_space=pltpu.VMEM)
    sets = (2, 16, feat // 16, width)
    return pl.pallas_call(
        enter_kernel,
        out_shape=(
            shape(sets, BF16),
            shape((8, feat), F32),
            shape((rows, feat), BF16),
            shape((16, feat // 16, rows), BF16),
            shape((2, rows, 3 * feat // 2), BF16),
        ),
        in_specs=[SMEM, vmem] + [ANY] * 4,
        out_specs=(ANY, vmem, vmem, vmem, vmem),
        scratch_shapes=[
            pltpu.VMEM(sets, BF16),
            pltpu.SemaphoreType.DMA((32,)),
            pltpu.SemaphoreType.DMA,
        ],
        compiler_params=params(),
        name="enter",
        cost_estimate=cost(8),
    )(info, tokens, *pieces)


def scores_of(info, keys, queries):
    raw = dot_last(keys, queries)
    place = lax.broadcasted_iota(jnp.int32, raw.shape, 0)
    return jnp.where(place < info[LENGTH], raw, NEG)


def mix_kernel(info, q, k, v, _, mixed, flipped, stats):
    head = q.shape[-1] // 2
    scale = head**-0.5
    turned = v[0].T
    outs = []
    for h in (0, 1):
        cols = slice(h * head, (h + 1) * head)
        scores = scores_of(info, k[0, :, cols], q[0, :, cols] * scale)
        most = jnp.max(scores, axis=0, keepdims=True)
        expd = jnp.exp(scores - most)
        total = jnp.sum(expd, axis=0, keepdims=True)
        attn = (expd * (1.0 / total)).astype(BF16)
        stats[0, h : h + 1] = most + jnp.log(total)
        outs.append(dot(turned[cols], attn))
    both = jnp.concatenate(outs)
    flipped[...] = both.astype(BF16)
    mixed[...] = both.T.astype(BF16)


def mix(info, joint, behind):
    _, rows, width = joint.shape
    feat, pair = 2 * width // 3, 2 * width // 3 // HEADS * 2
    per = feat // 2 // pair
    spec = [
        pl.BlockSpec((1, rows, pair), lambda i, part=part: (i // per, 0, part * per + i % per))
        for part in range(3)
    ]
    n = HEADS // 2
    return pl.pallas_call(
        mix_kernel,
        grid=(n,),
        out_shape=(
            shape((rows, feat), BF16),
            shape((feat, rows), BF16),
            shape((n, 8, rows), F32),
        ),
        in_specs=[SMEM] + spec + [ANY],
        out_specs=(
            pl.BlockSpec((rows, pair), lambda i: (0, i)),
            pl.BlockSpec((pair, rows), lambda i: (i, 0)),
            pl.BlockSpec((1, 8, rows), lambda i: (i, 0, 0)),
        ),
        compiler_params=params(),
        name="mix",
        cost_estimate=cost(10),
    )(info, joint, joint, joint, behind)


def mix_back_kernel(info, q, k, v, grad, stats, _, theirs, mine):
    head = q.shape[-1] // 2
    scale = head**-0.5
    turned = k[0].T
    parts = [[], [], []]
    for h in (0, 1):
        cols = slice(h * head, (h + 1) * head)
        queries = q[0, :, cols] * scale
        grad_h = grad[:, cols]
        attn = jnp.exp(scores_of(info, k[0, :, cols], queries) - stats[0, h : h + 1])
        grad_prob = dot_last(v[0, :, cols], grad_h)
        inner = jnp.sum(attn * grad_prob, axis=0, keepdims=True)
        low = (attn * (grad_prob - inner)).astype(BF16)
        parts[0].append(dot(turned[cols], low) * scale)
        parts[1].append(dot(low, queries))
        parts[2].append(dot(attn.astype(BF16), grad_h))
    out = [
        jnp.concatenate(parts[0]).T.astype(BF16),
        jnp.concatenate(parts[1], axis=1).astype(BF16),
        jnp.concatenate(parts[2], axis=1).astype(BF16),
    ]
    step, per = pl.program_id(0), pl.num_programs(0) // 2

    @pl.when(step < per)
    def _():
        for part in range(3):
            theirs[part] = out[part]

    @pl.when(step >= per)
    def _():
        for part in range(3):
            mine[part] = out[part]


def mix_back(info, joint, grad_mixed, stats, behind):
    _, rows, width = joint.shape
    feat, pair = 2 * width // 3, 2 * width // 3 // HEADS * 2
    per = feat // 2 // pair
    n = HEADS // 2

    def half(i, info):
        return jnp.where(i < per, 1 - info[CORE], info[CORE])

    spec = [
        pl.BlockSpec(
            (1, rows, pair), lambda i, info, part=part: (half(i, info), 0, part * per + i % per)
        )
        for part in range(3)
    ]
    out = shape((3, rows, feat // 2), BF16)
    return pl.pallas_call(
        mix_back_kernel,
        grid_spec=pltpu.PrefetchScalarGridSpec(
            num_scalar_prefetch=1,
            grid=(n,),
            in_specs=spec
            + [
                pl.BlockSpec((rows, pair), lambda i, info: (0, half(i, info) * per + i % per)),
                pl.BlockSpec(
                    (1, 8, rows), lambda i, info: (half(i, info) * per + i % per, 0, 0)
                ),
                ANY,
            ],
            out_specs=(
                pl.BlockSpec((3, rows, pair), lambda i, info: (0, 0, jnp.minimum(i, per - 1))),
                pl.BlockSpec((3, rows, pair), lambda i, info: (0, 0, jnp.maximum(i - per, 0))),
            ),
        ),
        out_shape=(out, out),
        compiler_params=params(),
        name="mix_back",
        cost_estimate=cost(16),
    )(info, joint, joint, joint, grad_mixed, stats, behind)


GELU = (0.254829592, -0.284496736, 1.421413741, -1.453152027, 1.061405429)


def gelu_parts(x):
    bell = jnp.exp2(x * x * (-0.5 / math.log(2)))
    below = 1.0 + (0.3275911 * 0.5**0.5) * jnp.abs(x)
    t = pl.reciprocal(below, approx=True)
    t = t * (2.0 - below * t)
    poly = 0.5 * GELU[4]
    for c in GELU[3::-1]:
        poly = poly * t + 0.5 * c
    tail = poly * t * bell
    phi = jnp.where(x < 0, tail, 1.0 - tail)
    return x * phi, phi + x * (bell * (2 * math.pi) ** -0.5)


def rise_kernel(
    info,
    tokens,
    mixed,
    vecs,
    bias,
    low,
    high,
    low_o,
    high_o,
    _,
    kept,
    after,
    second,
    flipped,
    active,
    slope,
    mine,
    theirs,
    weights,
    turned,
    sems,
    block_sems,
    sem,
):
    step, steps = pl.program_id(0), pl.num_programs(0)
    core = info[CORE]
    feat = tokens.shape[1]
    tile = active.shape[1]
    wide = weights.shape[-1] - feat // 2
    per = wide // tile
    rows = mine.shape[1]
    count = tile // rows
    keeping = pltpu.make_async_copy(weights, kept, sem)

    @pl.when(step == 0)
    def _():
        copies = fetch(info, (low, high, low_o, high_o), weights, sems, True)
        for copy in copies:
            copy.wait()
        keeping.start()
        grown = [
            dot(mixed[...], weights[h, :, :, wide:].reshape(feat, feat // 2)) for h in (0, 1)
        ]
        total = tokens[...].astype(F32) + jnp.concatenate(grown, axis=1) + vecs[5:6]
        after[...] = total
        normed, _ = centre(total)
        value = (normed * vecs[1:2] + vecs[6:7]).astype(BF16)
        second[...] = value
        flipped[...] = value.T.reshape(flipped.shape)

    cols = pl.ds(pl.multiple_of(lax.rem(step, per) * tile, tile), tile)
    w = weights[step // per, :, :, cols].reshape(feat, tile)
    hidden = dot(second[...], w) + bias[...]
    value, grad = gelu_parts(hidden)
    value = value.astype(BF16)
    active[...] = value
    slope[...] = grad.astype(BF16)
    turned[pl.ds(step * count, count)] = value.T.reshape(count, rows, -1)
    for i in range(count):
        at = step * count + i
        chip = step * (count // 2) + i // 2

        @pl.when(core == i % 2)
        def _():
            dst = mine.at[info[PLACE + chip]]
            pltpu.make_async_copy(turned.at[at], dst, block_sems.at[at]).start()

        @pl.when(core != i % 2)
        def _():
            dst = theirs.at[info[PLACE_O + chip]]
            pltpu.make_async_copy(turned.at[at], dst, block_sems.at[at]).start()

    @pl.when(step == steps - 1)
    def _():
        for at in range(turned.shape[0]):
            pltpu.make_async_copy(turned.at[at], mine.at[0], block_sems.at[at]).wait()
        keeping.wait()


def rise(info, tokens, mixed, vecs, bias, pieces, behind):
    rows, feat = tokens.shape
    width = pieces[0].shape[-1]
    hidden = 2 * width - feat
    tile, block = 768, hidden // 32
    turned = shape((16, block, rows), BF16)
    sets = (2, 16, feat // 16, width)
    strip = pl.BlockSpec((rows, tile), lambda n: (0, n))
    return pl.pallas_call(
        rise_kernel,
        grid=(hidden // tile,),
        out_shape=(
            shape(sets, BF16),
            shape((rows, feat), F32),
            shape((rows, feat), BF16),
            shape((16, feat // 16, rows), BF16),
            shape((rows, hidden), BF16),
            shape((rows, hidden), BF16),
            turned,
            turned,
        ),
        in_specs=[
            SMEM,
            full((rows, feat)),
            full((rows, feat)),
            full((8, feat)),
            pl.BlockSpec((1, tile), lambda n: (0, n)),
        ]
        + [ANY] * 5,
        out_specs=(
            ANY,
            full((rows, feat)),
            full((rows, feat)),
            full((16, feat // 16, rows)),
            strip,
            strip,
            ANY,
            ANY,
        ),
        scratch_shapes=[
            pltpu.VMEM(sets, BF16),
            pltpu.VMEM((32, block, rows), BF16),
            pltpu.SemaphoreType.DMA((32,)),
            pltpu.SemaphoreType.DMA((32,)),
            pltpu.SemaphoreType.DMA,
        ],
        compiler_params=params(),
        name="rise",
        cost_estimate=cost(18),
    )(info, tokens, mixed, vecs, bias, *pieces, behind)


def leave_kernel(after, active, down, vecs, _, output, total):
    step = pl.program_id(0)
    part = dot(active[...], down[...])

    @pl.when(step == 0)
    def _():
        total[...] = after[...] + vecs[7:8] + part

    @pl.when(step > 0)
    def _():
        total[...] += part

    @pl.when(step == pl.num_programs(0) - 1)
    def _():
        output[...] = total[...].astype(BF16)


def leave(after, active, down, vecs, behind):
    rows, feat = after.shape
    hidden = active.shape[1]
    tile = 768
    return pl.pallas_call(
        leave_kernel,
        grid=(hidden // tile,),
        out_shape=shape((rows, feat), BF16),
        in_specs=[
            full((rows, feat)),
            pl.BlockSpec((rows, tile), lambda n: (0, n)),
            pl.BlockSpec((tile, feat), lambda n: (n, 0)),
            full((8, feat)),
            ANY,
        ],
        out_specs=full((rows, feat)),
        scratch_shapes=[pltpu.VMEM((rows, feat), F32)],
        compiler_params=params(),
        name="leave",
        cost_estimate=cost(7),
    )(after, active, down, vecs, behind)


def fall_kernel(
    info,
    grad_y,
    slope,
    up,
    after,
    vecs,
    proj,
    low,
    high,
    low_o,
    high_o,
    kept,
    theirs,
    mine,
    bias_sum,
    grad_after,
    attn_theirs,
    attn_mine,
    grad_mixed,
    sums,
    weights,
    grad_second,
    sems,
    sem,
):
    step, steps = pl.program_id(0), pl.num_programs(0)
    core = info[CORE]
    feat = grad_y.shape[1]
    tile = slope.shape[1]
    per = steps // 2
    keeping = pltpu.make_async_copy(weights, kept, sem)

    @pl.when(step == 0)
    def _():
        for copy in fetch(info, (low, high, low_o, high_o), weights, sems, False):
            copy.wait()
        keeping.start()
        grad_second[...] = jnp.zeros_like(grad_second)

    half = jnp.where(step < per, 1 - core, core)
    at = half * per + lax.rem(step, per)
    count = tile * weights.shape[0] // (steps * tile)
    down = weights[pl.ds(count * at, count)].reshape(tile, feat)
    grad = (dot_last(grad_y[...], down) * slope[...].astype(F32)).astype(BF16)
    bias_sum[...] = jnp.sum(grad.astype(F32), axis=0, keepdims=True)
    grad_second[...] += dot_last(grad, up[0])

    @pl.when(step < per)
    def _():
        theirs[...] = grad

    @pl.when(step >= per)
    def _():
        mine[...] = grad

    @pl.when(step == steps - 1)
    def _():
        normed, inverse = centre(after[...])
        second = grad_second[...]
        live = grad_y[...].astype(F32)
        sums[0:1] = jnp.sum(second * normed, axis=0, keepdims=True)
        sums[1:2] = jnp.sum(second, axis=0, keepdims=True)
        total = live + layer_back(second * vecs[1:2], normed, inverse)
        grad_after[...] = total
        attn = total.astype(BF16)
        sums[2:3] = jnp.sum(attn.astype(F32), axis=0, keepdims=True)
        sums[3:4] = jnp.sum(live, axis=0, keepdims=True)
        sums[4:8] = jnp.zeros_like(sums[4:8])
        left, right = attn[:, : feat // 2], attn[:, feat // 2 :]
        attn_mine[...] = jnp.where(core == 0, left, right)
        attn_theirs[...] = jnp.where(core == 0, right, left)
        grad_mixed[...] = (dot_last(left, proj[0]) + dot_last(right, proj[1])).astype(BF16)
        keeping.wait()


def fall(info, grad_y, slope, up_set, after, vecs, pieces):
    rows, feat = grad_y.shape
    hidden = slope.shape[1]
    tile = 768
    steps = hidden // tile
    per = steps // 2

    def at(n, info):
        return jnp.where(n < per, 1 - info[CORE], info[CORE]) * per + n % per

    def whole(dims):
        return pl.BlockSpec(dims, lambda n, info: (0,) * len(dims))

    return pl.pallas_call(
        fall_kernel,
        grid_spec=pltpu.PrefetchScalarGridSpec(
            num_scalar_prefetch=1,
            grid=(steps,),
            in_specs=[
                whole((rows, feat)),
                pl.BlockSpec((rows, tile), lambda n, info: (0, at(n, info))),
                pl.BlockSpec(
                    (1, feat, tile), lambda n, info: (at(n, info) // per, 0, n % per)
                ),
                whole((rows, feat)),
                whole((8, feat)),
                pl.BlockSpec((2, feat, feat // 2), lambda n, info: (0, 0, 4)),
            ]
            + [ANY] * 4,
            out_specs=(
                ANY,
                pl.BlockSpec((rows, tile), lambda n, info: (0, jnp.minimum(n, per - 1))),
                pl.BlockSpec((rows, tile), lambda n, info: (0, jnp.maximum(n - per, 0))),
                pl.BlockSpec((1, tile), lambda n, info: (0, at(n, info))),
                whole((rows, feat)),
                whole((rows, feat // 2)),
                whole((rows, feat // 2)),
                whole((rows, feat)),
                whole((8, feat)),
            ),
            scratch_shapes=[
                pltpu.VMEM((16, 2, hidden // 32, feat), BF16),
                pltpu.VMEM((rows, feat), F32),
                pltpu.SemaphoreType.DMA((32,)),
                pltpu.SemaphoreType.DMA,
            ],
        ),
        out_shape=(
            shape((16, 2, hidden // 32, feat), BF16),
            shape((rows, hidden // 2), BF16),
            shape((rows, hidden // 2), BF16),
            shape((1, hidden), F32),
            shape((rows, feat), F32),
            shape((rows, feat // 2), BF16),
            shape((rows, feat // 2), BF16),
            shape((rows, feat), BF16),
            shape((8, feat), F32),
        ),
        compiler_params=params(),
        name="fall",
        cost_estimate=cost(18),
    )(info, grad_y, slope, up_set, after, vecs, up_set, *pieces)


def exit_kernel(
    info, tokens, mine, theirs, weights, grad_after, vecs, _, grad_tokens, sums, grad_first, joint
):
    step = pl.program_id(0)
    core = info[CORE]
    third = mine.shape[2]
    half = jnp.where(step == 0, core, 1 - core)
    spot = pl.ds(pl.multiple_of(half * third, third), third)

    def parts(source):
        for part in range(3):
            joint[:, part * third : (part + 1) * third] = source[part]
        sums[2:3, spot] = jnp.sum(source[0].astype(F32), axis=0, keepdims=True)
        sums[3:4, spot] = jnp.sum(source[2].astype(F32), axis=0, keepdims=True)
        return dot_last(joint[...], weights[0])

    @pl.when(step == 0)
    def _():
        grad_first[...] = parts(mine)

    @pl.when(step == 1)
    def _():
        grad = grad_first[...] + parts(theirs)
        normed, inverse = centre(tokens[...].astype(F32))
        sums[0:1] = jnp.sum(grad * normed, axis=0, keepdims=True)
        sums[1:2] = jnp.sum(grad, axis=0, keepdims=True)
        sums[4:8] = jnp.zeros_like(sums[4:8])
        back = layer_back(grad * vecs[0:1], normed, inverse)
        grad_tokens[...] = (grad_after[...] + back).astype(BF16)


def exit_back(info, tokens, mine, theirs, first_set, grad_after, vecs, behind):
    rows, feat = tokens.shape
    third = feat // 2

    def whole(dims):
        return pl.BlockSpec(dims, lambda n, info: (0,) * len(dims))

    return pl.pallas_call(
        exit_kernel,
        grid_spec=pltpu.PrefetchScalarGridSpec(
            num_scalar_prefetch=1,
            grid=(2,),
            in_specs=[
                whole((rows, feat)),
                whole((3, rows, third)),
                whole((3, rows, third)),
                pl.BlockSpec(
                    (1, feat, 3 * third),
                    lambda n, info: (jnp.where(n == 0, info[CORE], 1 - info[CORE]), 0, 0),
                ),
                whole((rows, feat)),
                whole((8, feat)),
                ANY,
            ],
            out_specs=(whole((rows, feat)), whole((8, feat))),
            scratch_shapes=[pltpu.VMEM((rows, feat), F32), pltpu.VMEM((rows, 3 * third), BF16)],
        ),
        out_shape=(shape((rows, feat), BF16), shape((8, feat), F32)),
        compiler_params=params(),
        name="exit_back",
        cost_estimate=cost(8),
    )(info, tokens, mine, theirs, first_set, grad_after, vecs, behind)


def line_up(info, left, left_o, turned):
    rows = left.shape[2]
    for chip in range(16):
        place = info[PLACE + chip]
        turned[place, :, :rows] = left[chip]
        turned[place, :, rows:] = left_o[chip]


def outer_tile(turned, right, right_o):
    rows = right.shape[0]
    both = turned[...].reshape(-1, turned.shape[2])
    total = dot(both[:, :rows], right) + dot(both[:, rows:], right_o)
    return total.reshape(16, -1, total.shape[1])


def outer_up_kernel(
    info, left, left_o, right, right_o, low, low_o, attn, attn_o, _, keep, away, turned
):
    step, last = pl.program_id(0), pl.num_programs(0) - 1

    @pl.when(step == 0)
    def _():
        line_up(info, left, left_o, turned)

    @pl.when(step < last)
    def _():
        total = outer_tile(turned, right[...], right_o[...])
        keep[...] = total[:8]
        away[...] = total[8:].astype(BF16)

    @pl.when(step == last)
    def _():
        line_up(info, low, low_o, turned)
        total = outer_tile(turned, attn[...], attn_o[...])
        keep[:, :, : attn.shape[1]] = total[:8]
        away[:, :, : attn.shape[1]] = total[8:].astype(BF16)


def outer_up(info, left, left_o, right, right_o, low, low_o, attn, attn_o, behind):
    _, block, rows = left.shape
    tile = 2 * attn.shape[1]
    n = right.shape[1] // tile
    cols = right.shape[1] + attn.shape[1]
    strip = pl.BlockSpec((rows, tile), lambda i: (0, jnp.minimum(i, n - 1)))
    out = pl.BlockSpec((8, block, tile), lambda i: (0, 0, i))
    return pl.pallas_call(
        outer_up_kernel,
        grid=(n + 1,),
        out_shape=(shape((8, block, cols), F32), shape((8, block, cols), BF16)),
        in_specs=[SMEM]
        + [full(left.shape)] * 2
        + [strip] * 2
        + [full(left.shape)] * 2
        + [full(attn.shape)] * 2
        + [ANY],
        out_specs=(out, out),
        scratch_shapes=[pltpu.VMEM((16, block, 2 * rows), BF16)],
        compiler_params=params(),
        name="outer_up",
        cost_estimate=cost(8),
    )(info, left, left_o, right, right_o, low, low_o, attn, attn_o, behind)


def outer_qkv_kernel(
    info, left, left_o, right, right_o, sums_a, sums_b, bias, _, keep, away, turned, extra
):
    feat, tile = sums_a.shape[1], right.shape[2]
    block = feat // 16
    line_up(info, left, left_o, turned)
    for part in range(3):
        cols = slice(part * tile, (part + 1) * tile)
        total = outer_tile(turned, right[part], right_o[part])
        keep[:, :, cols] = total[:8]
        away[:, :, cols] = total[8:].astype(BF16)
    ordered = [
        sums_b[0:1],
        sums_a[0:1],
        sums_b[1:4],
        sums_a[2:3],
        sums_a[1:2],
        sums_a[3:4],
        jnp.zeros((120, feat), F32),
    ]
    flipped = jnp.concatenate(ordered).T
    each = bias.shape[1] // 32
    for chip in range(16):
        place = info[PLACE + chip]
        extra[place] = flipped[chip * block : (chip + 1) * block]
        for core in (0, 1):
            at = (2 * chip + core) * each
            row = core * block // 2
            extra[place, row : row + 1, 128 - each :] = bias[:, at : at + each]
    keep[:, :, 3 * tile :] = extra[:8]
    away[:, :, 3 * tile :] = extra[8:].astype(BF16)


def outer_qkv(info, left, left_o, right, right_o, sums_a, sums_b, bias, behind):
    _, block, rows = left.shape
    cols = 3 * right.shape[2] + 128
    vmem = pl.BlockSpec(memory_space=pltpu.VMEM)
    return pl.pallas_call(
        outer_qkv_kernel,
        out_shape=(shape((8, block, cols), F32), shape((8, block, cols), BF16)),
        in_specs=[SMEM] + [vmem] * 7 + [ANY],
        out_specs=(vmem, vmem),
        scratch_shapes=[
            pltpu.VMEM((16, block, 2 * rows), BF16),
            pltpu.VMEM((16, block, 128), F32),
        ],
        compiler_params=params(),
        name="outer_qkv",
        cost_estimate=cost(8),
    )(info, left, left_o, right, right_o, sums_a, sums_b, bias, behind)


def outer_down_kernel(left, left_o, right, right_o, _, keep, away):
    def flat(blocks):
        return blocks[...].reshape(-1, blocks.shape[-1])

    total = dot(flat(left), right[...]) + dot(flat(left_o), right_o[...])
    total = total.reshape(keep.shape)

    @pl.when(pl.program_id(0) >= 2)
    def _():
        keep[...] = total

    @pl.when(pl.program_id(0) < 2)
    def _():
        away[...] = total.astype(BF16)


def outer_down(left, left_o, right, right_o, behind):
    _, block, rows = left.shape
    feat = right.shape[1]
    strip = pl.BlockSpec((4, block, rows), lambda j: ((j + 2) % 4, 0, 0))
    return pl.pallas_call(
        outer_down_kernel,
        grid=(4,),
        out_shape=(shape((8, block, feat), F32), shape((8, block, feat), BF16)),
        in_specs=[strip, strip, full((rows, feat)), full((rows, feat)), ANY],
        out_specs=(
            pl.BlockSpec((4, block, feat), lambda j: (jnp.maximum(j - 2, 0), 0, 0)),
            pl.BlockSpec((4, block, feat), lambda j: (jnp.minimum(j, 1), 0, 0)),
        ),
        compiler_params=params(),
        name="outer_down",
        cost_estimate=cost(8),
    )(left, left_o, right, right_o, behind)


def total_of(base, parts):
    return base[...] + parts[0][...].astype(F32) + (
        parts[1][...].astype(F32) + parts[2][...].astype(F32)
    )


def add_down_kernel(base, one, two, three, out):
    out[...] = total_of(base, (one, two, three))


def add_last_kernel(info, base, one, two, three, mine, theirs, total):
    core = info[CORE]
    half = mine.shape[0]
    total[...] = total_of(base, (one, two, three))
    mine[...] = total[pl.ds(pl.multiple_of(core * half, half), half)]
    theirs[...] = total[pl.ds(pl.multiple_of((1 - core) * half, half), half)]


def shift_first(keep, away, behind):
    got = gate(send(away, second_way), behind)
    return keep[:4] + got[:4].astype(F32), (keep[4:] + got[4:].astype(F32)).astype(BF16)


def shift_second(keep, away, behind):
    got = gate(send(away, first_way), behind)
    lows = [(keep[s] + got[s].astype(F32)).astype(BF16) for s in (1, 2, 3)]
    return keep[0] + got[0].astype(F32), [send(low, along_z(s)) for low, s in zip(lows, (1, 2, 3))]


def home_down(base, parts):
    vmem = pl.BlockSpec(memory_space=pltpu.VMEM)
    return pl.pallas_call(
        add_down_kernel,
        out_shape=shape(base.shape, F32),
        in_specs=[vmem] * 4,
        out_specs=vmem,
        compiler_params=params(),
        name="home_down",
        cost_estimate=cost(2),
    )(base, *parts)


def home(info, base, parts):
    rows, cols = base.shape
    vmem = pl.BlockSpec(memory_space=pltpu.VMEM)
    out = shape((rows // 2, cols), F32)
    mine, theirs = pl.pallas_call(
        add_last_kernel,
        out_shape=(out, out),
        in_specs=[SMEM] + [vmem] * 4,
        out_specs=(vmem, vmem),
        scratch_shapes=[pltpu.VMEM((rows, cols), F32)],
        compiler_params=params(),
        name="home",
        cost_estimate=cost(2),
    )(info, base, *parts)
    return mine, swap(theirs)


def finish_kernel(info, qkv, qkv_o, up, up_o, out_qkv, out_proj, out_up, gains, shifts, bias):
    rows, third = out_proj.shape[0], out_proj.shape[1] // 2
    wide = out_up.shape[1] // 2
    small = qkv[:, 3 * third :] + qkv_o[:, 3 * third :]
    flipped = jnp.concatenate([small, jnp.zeros((128 - rows, 128), F32)]).T
    gains[...] = flipped[0:2, :rows]
    shifts[...] = flipped[2:8, :rows]
    bias[...] = small[0:1, 128 - bias.shape[1] :]

    def lay(core):
        for half, (a, b) in ((core, (qkv, up)), (1 - core, (qkv_o, up_o))):
            for part in range(3):
                spot = part * 2 * third + half * third
                out_qkv[:, spot : spot + third] = a[:, part * third : (part + 1) * third]
            out_proj[:, half * third : (half + 1) * third] = b[:, wide:]
            out_up[:, half * wide : (half + 1) * wide] = b[:, :wide]

    @pl.when(info[CORE] == 0)
    def _():
        lay(0)

    @pl.when(info[CORE] == 1)
    def _():
        lay(1)


def finish(info, qkv, qkv_o, up, up_o):
    rows = qkv.shape[0]
    third = (qkv.shape[1] - 128) // 3
    vmem = pl.BlockSpec(memory_space=pltpu.VMEM)
    return pl.pallas_call(
        finish_kernel,
        out_shape=(
            shape((rows, 6 * third), F32),
            shape((rows, 2 * third), F32),
            shape((rows, 2 * (up.shape[1] - third)), F32),
            shape((2, rows), F32),
            shape((6, rows), F32),
            shape((1, 4 * rows), F32),
        ),
        in_specs=[SMEM] + [vmem] * 4,
        out_specs=(vmem,) * 6,
        compiler_params=params(),
        name="finish",
        cost_estimate=cost(2),
    )(info, qkv, qkv_o, up, up_o)


def local(
    tokens,
    upstream,
    lengths,
    qkv_weight,
    proj_weight,
    up_weight,
    down_weight,
    gains,
    shifts,
    up_bias,
):
    tok_rows, feat = tokens.shape
    rows = qkv_weight.shape[0]
    hidden = up_weight.shape[1]
    third, wide = feat // 2, hidden // 2
    chip, core = lax.axis_index("dp"), lax.axis_index("fsdp")
    info = facts(chip, core, lengths[0])

    live = lax.iota(jnp.int32, tok_rows) < lengths[0]
    grad_y = jnp.where(live[:, None], upstream, jnp.zeros_like(upstream))

    down = down_weight[None]
    down_z = near_z(down, (1, 2))
    small = jnp.concatenate([gains, shifts, up_bias.reshape(rows, -1)], axis=1)
    small = jnp.pad(small, ((0, 0), (0, 128 - small.shape[1])))
    mine, theirs = halves(info, qkv_weight, proj_weight, up_weight)
    one = 3 * third + 128
    piece, piece_up = pieces_of(info, mine, swap(theirs), small, 3 * third)
    zs, piece_up = gather([piece] + near_z(piece, (1, 2, 3)), (piece_up,), down_z)
    up_z = near_z(piece_up, (1, 2))
    low, piece_up = gather([zs, send(zs, first_way)], (piece_up,), up_z)
    up_z += near_z(piece_up, (3,))
    high = send(low, second_way)
    zs_up, down = gather([piece_up] + up_z, (down,))
    high = gate(high, zs_up)
    first_pieces = (low, high, swap(low), swap(high))
    grad_y_o = swap(grad_y)
    down_z += near_z(down, (3,))

    first_set, vecs, first, first_t, joint = enter(info, tokens, first_pieces)
    bias = first_set[0, :, :, one - 120 : one - 116] + first_set[1, :, :, one - 120 : one - 116]
    bias = bias.reshape(1, hidden).astype(F32)
    first_set = first_set.reshape(2, feat, one)
    first_o = swap(first_t)
    (low,) = gather([zs_up, send(zs_up, first_way)], (), (first,))
    (zs_down,) = gather([down] + down_z, (), (low,))
    mixed, mixed_t, stats = mix(info, joint, zs_down)
    high = gate(send(low, second_way), mixed)
    up_pieces = (low, high, swap(low), swap(high))
    mixed_t = mixed_t.reshape(first_t.shape)
    mixed_o = swap(mixed_t)
    (low,) = gather([zs_down, send(zs_down, first_way)], (), (mixed,))
    up_set, after, second, second_t, active, slope, turned, turned_t = rise(
        info, tokens, mixed, vecs, bias, up_pieces, low
    )
    up_set = up_set.reshape(2, feat, wide + third)
    high = gate(send(low, second_way), second)
    down_pieces = (low, high, swap(low), swap(high))
    second_o, turned_o = swap(second_t), swap(turned_t)
    down_set, hid_theirs, hid_mine, bias_sum, grad_after, at_theirs, at_mine, grad_mixed, sums_a = (
        fall(info, grad_y, slope, up_set, after, vecs, down_pieces)
    )
    hid_o, at_o = swap(hid_theirs), swap(at_theirs)
    down = outer_down(turned, turned_o, grad_y, grad_y_o, hid_theirs)
    up = outer_up(
        info, second_t, second_o, hid_mine, hid_o, mixed_t, mixed_o, at_mine, at_o, down[1]
    )
    theirs, mine = mix_back(info, joint, grad_mixed, stats, up[1])
    theirs_o = swap(theirs)
    down = shift_first(*down, theirs)
    up = shift_first(*up, down[1])
    grad_tokens, sums_b = exit_back(info, tokens, mine, theirs, first_set, grad_after, vecs, up[1])
    down = shift_second(*down, grad_tokens)
    qkv = outer_qkv(info, first_t, first_o, mine, theirs_o, sums_a, sums_b, bias_sum, down[0])
    up = shift_second(*up, qkv[1])
    output = leave(after, active, down_set.reshape(hidden, feat), vecs, up[0])
    base, parts = down
    own_down = home_down(base, parts[:2] + [gate(parts[2], output)])
    qkv = shift_first(*qkv, own_down)
    own_up = home(info, *up)
    own_qkv = home(info, *shift_second(*qkv, own_up[0]))
    out_qkv, out_proj, out_up, out_gains, out_shifts, out_bias = finish(info, *own_qkv, *own_up)
    return (
        output,
        grad_tokens,
        out_qkv,
        out_proj,
        out_up,
        own_down,
        out_gains.T,
        out_shifts.T,
        out_bias.reshape(-1),
    )


def solution(mesh):
    placed = (
        P(("dp", "fsdp"), None),
        P(("dp", "fsdp"), None),
        P(("dp", "fsdp")),
        P(("dp", "fsdp"), None),
        P(("dp", "fsdp"), None),
        P(("dp", "fsdp"), None),
        P(("dp", "fsdp"), None),
        P(("dp", "fsdp"), None),
        P(("dp", "fsdp"), None),
        P(("dp", "fsdp")),
    )
    sizes = (mesh.shape["dp"], mesh.shape["fsdp"])
    return jax.shard_map(
        local if sizes == (16, 2) else plain,
        mesh=mesh,
        in_specs=placed,
        out_specs=(
            P(("dp", "fsdp"), None),
            P(("dp", "fsdp"), None),
            P(("dp", "fsdp"), None),
            P(("dp", "fsdp"), None),
            P(("dp", "fsdp"), None),
            P(("dp", "fsdp"), None),
            P(("dp", "fsdp"), None),
            P(("dp", "fsdp"), None),
            P(("dp", "fsdp")),
        ),
        check_vma=False,
    )
```

```python
import math
from functools import partial

import jax
import jax.numpy as jnp
from jax import lax
from jax.experimental import pallas as pl
from jax.experimental.pallas import tpu as pltpu
from jax.sharding import PartitionSpec as P

HEADS = 12
EPS = 1e-06
NEG = -1e30
AXES = ("dp", "fsdp")
F32 = jnp.float32
BF16 = jnp.bfloat16
VMEM_LIMIT = 32 * 1024 * 1024


def collect(qkv_weight, proj_weight, up_weight, down_weight, gains, shifts, up_bias):
    gathered = (
        lax.all_gather(qkv_weight, ("dp", "fsdp"), axis=0, tiled=True),
        lax.all_gather(proj_weight, ("dp", "fsdp"), axis=0, tiled=True),
        lax.all_gather(up_weight, ("dp", "fsdp"), axis=0, tiled=True),
        lax.all_gather(down_weight, ("dp", "fsdp"), axis=0, tiled=True),
        lax.all_gather(gains, ("dp", "fsdp"), axis=0, tiled=True),
        lax.all_gather(shifts, ("dp", "fsdp"), axis=0, tiled=True),
        lax.all_gather(up_bias, ("dp", "fsdp"), axis=0, tiled=True),
    )
    return gathered


def give_back(grad_qkv, grad_proj, grad_up, grad_down, grad_gains, grad_shifts, grad_bias_up):
    owned = (
        lax.psum_scatter(grad_qkv, ("dp", "fsdp"), scatter_dimension=0, tiled=True),
        lax.psum_scatter(grad_proj, ("dp", "fsdp"), scatter_dimension=0, tiled=True),
        lax.psum_scatter(grad_up, ("dp", "fsdp"), scatter_dimension=0, tiled=True),
        lax.psum_scatter(grad_down, ("dp", "fsdp"), scatter_dimension=0, tiled=True),
        lax.psum_scatter(grad_gains, ("dp", "fsdp"), scatter_dimension=0, tiled=True),
        lax.psum_scatter(grad_shifts, ("dp", "fsdp"), scatter_dimension=0, tiled=True),
        lax.psum_scatter(grad_bias_up, ("dp", "fsdp"), scatter_dimension=0, tiled=True),
    )
    return owned


def normalize(values):
    centred = values - jnp.mean(values, axis=-1, keepdims=True)
    inverse = lax.rsqrt(jnp.mean(centred * centred, axis=-1, keepdims=True) + EPS)
    return (centred * inverse, inverse)


def norm_back(grad_norm, normed, inverse):
    return inverse * (
        grad_norm
        - jnp.mean(grad_norm, axis=-1, keepdims=True)
        - normed * jnp.mean(grad_norm * normed, axis=-1, keepdims=True)
    )


def block_scores(query_blk, key_rows, live_mask, scaling):
    raw = (
        jnp.einsum("qhd,khd->hqk", query_blk, key_rows, preferred_element_type=jnp.float32)
        * scaling
    )
    return jnp.where(live_mask[None, None, :], raw, NEG)


def plain(
    tokens,
    upstream,
    lengths,
    qkv_weight,
    proj_weight,
    up_weight,
    down_weight,
    gains,
    shifts,
    up_bias,
):
    tok_rows, feat_width = tokens.shape
    n_heads = HEADS
    head_size = feat_width // n_heads
    scaling = head_size ** (-0.5)
    block_rows = min(512, tok_rows)
    group_heads = 4
    head_starts = list(range(0, n_heads, group_heads))
    gathered = collect(qkv_weight, proj_weight, up_weight, down_weight, gains, shifts, up_bias)
    qkv_full, proj_full, up_full, down_full, gain_full, shift_full, bias_full = gathered
    gain_f = gain_full.astype(jnp.float32)
    shift_f = shift_full.astype(jnp.float32)
    bias_f = bias_full.astype(jnp.float32)
    live_mask = lax.iota(jnp.int32, tok_rows) < lengths[0]
    source = tokens.astype(jnp.float32)
    norm_one, inv_one = normalize(source)
    first = (norm_one * gain_f[:, 0] + shift_f[:, 0]).astype(jnp.bfloat16)
    joint_bias = jnp.concatenate([shift_f[:, 1], jnp.zeros_like(shift_f[:, 1]), shift_f[:, 2]])
    joint = (jnp.dot(first, qkv_full, preferred_element_type=jnp.float32) + joint_bias).astype(
        jnp.bfloat16
    )
    queries = joint[:, :feat_width].reshape(tok_rows, n_heads, head_size)
    key_rows = joint[:, feat_width : 2 * feat_width].reshape(tok_rows, n_heads, head_size)
    value_rows = joint[:, 2 * feat_width :].reshape(tok_rows, n_heads, head_size)
    log_sums = {}
    offset = 0
    group_parts = []
    for head_lo in head_starts:
        head_hi = head_lo + group_heads
        scores = block_scores(
            queries[offset : offset + block_rows, head_lo:head_hi],
            key_rows[:, head_lo:head_hi],
            live_mask,
            scaling,
        )
        row_max = jnp.max(scores, axis=-1, keepdims=True)
        expd = jnp.exp(scores - row_max)
        row_sum = jnp.sum(expd, axis=-1, keepdims=True)
        attn_low = (expd / row_sum).astype(jnp.bfloat16)
        log_sums[offset, head_lo] = row_max + jnp.log(row_sum)
        group_parts.append(
            jnp.einsum(
                "hqk,khd->qhd",
                attn_low,
                value_rows[:, head_lo:head_hi],
                preferred_element_type=jnp.float32,
            )
        )
    mixed_parts = jnp.concatenate(group_parts, axis=1)
    mixed = mixed_parts.reshape(tok_rows, feat_width).astype(jnp.bfloat16)
    after = source + jnp.dot(mixed, proj_full, preferred_element_type=jnp.float32) + shift_f[:, 3]
    norm_two, inv_two = normalize(after)
    second = (norm_two * gain_f[:, 1] + shift_f[:, 4]).astype(jnp.bfloat16)
    hidden = jnp.dot(second, up_full, preferred_element_type=jnp.float32) + bias_f
    gelu_exact = partial(jax.nn.gelu, approximate=False)
    active = gelu_exact(hidden).astype(jnp.bfloat16)
    output = (
        after + jnp.dot(active, down_full, preferred_element_type=jnp.float32) + shift_f[:, 5]
    ).astype(jnp.bfloat16)
    regathered = collect(qkv_weight, proj_weight, up_weight, down_weight, gains, shifts, up_bias)
    qkv_full, proj_full, up_full, down_full, gain_full, shift_full, bias_full = regathered
    grad_y = jnp.where(live_mask[:, None], upstream, jnp.zeros_like(upstream))
    sum_y = jnp.sum(grad_y, axis=0, dtype=jnp.float32)
    grad_down = jnp.einsum("tf,td->fd", active, grad_y, preferred_element_type=jnp.float32)
    grad_active = jnp.einsum("td,fd->tf", grad_y, down_full, preferred_element_type=jnp.float32)
    gelu_value, gelu_pull = jax.vjp(gelu_exact, hidden)
    grad_hidden = gelu_pull(grad_active)[0].astype(jnp.bfloat16)
    grad_bias_up = jnp.sum(grad_hidden, axis=0, dtype=jnp.float32)
    grad_up = jnp.einsum("td,tf->df", second, grad_hidden, preferred_element_type=jnp.float32)
    grad_second = jnp.einsum("tf,df->td", grad_hidden, up_full, preferred_element_type=jnp.float32)
    gain_two_grad = jnp.sum(grad_second * norm_two, axis=0)
    shift_two_grad = jnp.sum(grad_second, axis=0)
    grad_after = grad_y.astype(jnp.float32) + norm_back(
        grad_second * gain_f[:, 1], norm_two, inv_two
    )
    grad_attn = grad_after.astype(jnp.bfloat16)
    sum_attn = jnp.sum(grad_attn, axis=0, dtype=jnp.float32)
    grad_proj = jnp.einsum("td,te->de", mixed, grad_attn, preferred_element_type=jnp.float32)
    grad_mixed = jnp.einsum("te,de->td", grad_attn, proj_full, preferred_element_type=jnp.float32)
    grad_mixed = grad_mixed.astype(jnp.bfloat16).reshape(tok_rows, n_heads, head_size)
    key_groups = {}
    value_groups = {}
    for head_lo in head_starts:
        key_groups[head_lo] = jnp.zeros((tok_rows, group_heads, head_size), jnp.float32)
        value_groups[head_lo] = jnp.zeros((tok_rows, group_heads, head_size), jnp.float32)
    offset = 0
    query_groups = []
    for head_lo in head_starts:
        head_hi = head_lo + group_heads
        query_blk = queries[offset : offset + block_rows, head_lo:head_hi]
        grad_blk = grad_mixed[offset : offset + block_rows, head_lo:head_hi]
        key_part = key_rows[:, head_lo:head_hi]
        scores = block_scores(query_blk, key_part, live_mask, scaling)
        attn_p = jnp.exp(scores - log_sums[offset, head_lo])
        value_groups[head_lo] = jnp.einsum(
            "hqk,qhd->khd",
            attn_p.astype(jnp.bfloat16),
            grad_blk,
            preferred_element_type=jnp.float32,
        )
        grad_prob = jnp.einsum(
            "qhd,khd->hqk",
            grad_blk,
            value_rows[:, head_lo:head_hi],
            preferred_element_type=jnp.float32,
        )
        grad_score = attn_p * (grad_prob - jnp.sum(attn_p * grad_prob, axis=-1, keepdims=True))
        score_low = grad_score.astype(jnp.bfloat16)
        query_groups.append(
            jnp.einsum("hqk,khd->qhd", score_low, key_part, preferred_element_type=jnp.float32)
            * scaling
        )
        key_groups[head_lo] = (
            jnp.einsum("hqk,qhd->khd", score_low, query_blk, preferred_element_type=jnp.float32)
            * scaling
        )
    grad_query_parts = jnp.concatenate(query_groups, axis=1)
    grad_keys = jnp.concatenate([key_groups[head_lo] for head_lo in head_starts], axis=1)
    grad_vals = jnp.concatenate([value_groups[head_lo] for head_lo in head_starts], axis=1)
    grad_joint = jnp.concatenate(
        [
            grad_query_parts.reshape(tok_rows, feat_width),
            grad_keys.reshape(tok_rows, feat_width),
            grad_vals.reshape(tok_rows, feat_width),
        ],
        axis=1,
    ).astype(jnp.bfloat16)
    joint_sums = jnp.sum(grad_joint, axis=0, dtype=jnp.float32)
    grad_qkv = jnp.einsum("td,te->de", first, grad_joint, preferred_element_type=jnp.float32)
    grad_first = jnp.einsum("te,de->td", grad_joint, qkv_full, preferred_element_type=jnp.float32)
    gain_one_grad = jnp.sum(grad_first * norm_one, axis=0)
    shift_one_grad = jnp.sum(grad_first, axis=0)
    grad_tokens = (grad_after + norm_back(grad_first * gain_f[:, 0], norm_one, inv_one)).astype(
        jnp.bfloat16
    )
    grad_gains = jnp.stack([gain_one_grad, gain_two_grad], axis=1)
    grad_shifts = jnp.stack(
        [
            shift_one_grad,
            joint_sums[:feat_width],
            joint_sums[2 * feat_width :],
            sum_attn,
            shift_two_grad,
            sum_y,
        ],
        axis=1,
    )
    owned = give_back(
        grad_qkv, grad_proj, grad_up, grad_down, grad_gains, grad_shifts, grad_bias_up
    )
    own_qkv, own_proj, own_up, own_down, own_gains, own_shifts, own_bias = owned
    return (
        output,
        grad_tokens,
        own_qkv,
        own_proj,
        own_up,
        own_down,
        own_gains,
        own_shifts,
        own_bias,
    )


BOTH_LAST = (((1,), (1,)), ((), ()))
SMEM = pl.BlockSpec(memory_space=pltpu.SMEM)
ANY = pl.BlockSpec(memory_space=pl.ANY)
CORE, LENGTH, PLACE, PLACE_O = 32, 33, 34, 50


def pairs(move):
    return [(i, move(i)) for i in range(32)]


def first_way(i):
    return i ^ (2 if i % 2 == 0 else 4)


def second_way(i):
    return i ^ (4 if i % 2 == 0 else 2)


def along_z(step):
    return lambda i: i ^ (8 * step)


def send(array, move):
    return lax.ppermute(array, AXES, pairs(move))


def swap(array):
    return send(array, lambda i: i ^ 1)


def facts(chip, core, length):
    places = []
    for of_core in (core, 1 - core):
        for j in range(16):
            z, first, second = j % 4, (j // 4) % 2, j // 8
            mask = jnp.where(of_core == 0, first + 2 * second, second + 2 * first)
            places.append(jnp.bitwise_xor(chip, mask + 4 * z))
    spots = []
    for of_core in (core, 1 - core):
        for k in range(16):
            mask = jnp.bitwise_xor(chip, k)
            x, y, z = mask & 1, (mask >> 1) & 1, mask >> 2
            spots.append(z + jnp.where(of_core == 0, 4 * x + 8 * y, 4 * y + 8 * x))
    return jnp.stack(places + [core, length] + spots).astype(jnp.int32)


def params(mib):
    return pltpu.CompilerParams(vmem_limit_bytes=mib * 1024 * 1024)


def cost(micros):
    flops = int(micros * (3e10 if micros > 3 else 1e9))
    return pl.CostEstimate(flops=flops, bytes_accessed=1, transcendentals=0)


def shape(dims, dtype):
    return jax.ShapeDtypeStruct(dims, dtype)


def full(dims):
    return pl.BlockSpec(dims, lambda *_: (0,) * len(dims))


def dot(left, right):
    return jnp.dot(left, right, preferred_element_type=F32)


def dot_last(left, right):
    return lax.dot_general(left, right, BOTH_LAST, preferred_element_type=F32)


def fetch(info, pieces, dest, sems, by_half):
    copies = []
    cols = pl.ds(pieces[0].shape[-1] - dest.shape[-1], dest.shape[-1])
    for who in (0, 1):
        half = info[CORE] if who == 0 else 1 - info[CORE]
        for j in range(16):
            at = info[16 * who + j]
            src = pieces[2 * who + j // 8].at[j % 8, :, cols]
            dst = dest.at[half, at] if by_half else dest.at[at, half]
            copies.append(pltpu.make_async_copy(src, dst, sems.at[16 * who + j]))
    for copy in copies:
        copy.start()
    return copies


def settle(info, pieces, dest, cols):
    for who in (0, 1):
        half = info[CORE] if who == 0 else 1 - info[CORE]
        for j in range(16):
            dest[half, info[16 * who + j]] = pieces[2 * who + j // 8][j % 8, :, cols]


def centre(values):
    centred = values - jnp.mean(values, axis=-1, keepdims=True)
    inverse = lax.rsqrt(jnp.mean(centred * centred, axis=-1, keepdims=True) + EPS)
    return centred * inverse, inverse


def layer_back(grad, normed, inverse):
    return inverse * (
        grad
        - jnp.mean(grad, axis=-1, keepdims=True)
        - normed * jnp.mean(grad * normed, axis=-1, keepdims=True)
    )


def halves_kernel(info, qkv, proj, up, mine, theirs, sems):
    feat = proj.shape[1]
    third, wide = feat // 2, up.shape[1] // 2
    copies = []

    def copy(src, start, out, at, width):
        cols = pl.ds(pl.multiple_of(start, 128), width)
        sem = sems.at[len(copies)]
        copies.append(pltpu.make_async_copy(src.at[:, cols], out.at[:, pl.ds(at, width)], sem))

    for out, h in ((theirs, 1 - info[CORE]), (mine, info[CORE])):
        for i in range(3):
            copy(qkv, i * feat + h * third, out, i * third, third)
        copy(up, h * wide, out, 3 * third, wide)
        copy(proj, h * third, out, 3 * third + wide, third)
    for c in copies:
        c.start()
    for c in copies:
        c.wait()


def halves(info, qkv, proj, up):
    rows = qkv.shape[0]
    width = (qkv.shape[1] + proj.shape[1] + up.shape[1]) // 2
    vmem = pl.BlockSpec(memory_space=pltpu.VMEM)
    out = shape((rows, width), BF16)
    return pl.pallas_call(
        halves_kernel,
        out_shape=(out, out),
        in_specs=[SMEM] + [ANY] * 3,
        out_specs=(vmem, vmem),
        scratch_shapes=[pltpu.SemaphoreType.DMA((10,))],
        compiler_params=params(8),
        name="halves",
        cost_estimate=cost(0),
    )(info, qkv, proj, up)


def pieces_kernel(info, mine, given, small, one, two):
    ours, others = mine[...].astype(F32), given[...].astype(F32)
    few = small[...].astype(F32)
    none = jnp.zeros_like(few)
    first = info[CORE] == 0

    def stack(a, b):
        return jnp.concatenate([jnp.where(first, a, b), jnp.where(first, b, a)]).astype(BF16)

    split = one.shape[2] - few.shape[1]
    one[0, :, :split] = stack(ours[:, :split], others[:, :split])
    one[0, :, split:] = stack(few, none)
    two[0] = stack(ours[:, split:], others[:, split:])


def pieces_of(info, mine, given, small, split):
    rows, width = mine.shape
    one = split + small.shape[1]
    vmem = pl.BlockSpec(memory_space=pltpu.VMEM)
    return pl.pallas_call(
        pieces_kernel,
        out_shape=(
            shape((1, 2 * rows, one), BF16),
            shape((1, 2 * rows, width - split), BF16),
        ),
        in_specs=[SMEM] + [vmem] * 3,
        out_specs=(vmem,) * 2,
        compiler_params=params(8),
        name="pieces_of",
        cost_estimate=cost(0),
    )(info, mine, given, small)


def gather_kernel(n_in, n_held, *refs):
    parts = refs[:n_in]
    out = refs[n_in + n_held]
    at = 0
    for part in parts:
        out[at : at + part.shape[0]] = part[...]
        at += part.shape[0]


def gather(parts, held=(), behind=(), micros=0):
    vmem = pl.BlockSpec(memory_space=pltpu.VMEM)
    _, rows, cols = parts[0].shape
    count = sum(part.shape[0] for part in parts)
    n, n_held = len(parts), len(held)
    return pl.pallas_call(
        partial(gather_kernel, n, n_held + len(behind)),
        out_shape=(shape((count, rows, cols), BF16),) + tuple(shape(h.shape, h.dtype) for h in held),
        in_specs=[vmem] * n + [ANY] * (n_held + len(behind)),
        out_specs=(vmem,) + (ANY,) * n_held,
        input_output_aliases={n + i: 1 + i for i in range(n_held)},
        compiler_params=params(16),
        name="gather",
        cost_estimate=cost(micros),
    )(*parts, *held, *behind)


def gate_kernel(array, behind, out):
    pass


def gate(array, behind, micros=1):
    return pl.pallas_call(
        gate_kernel,
        out_shape=shape(array.shape, array.dtype),
        in_specs=[ANY, ANY],
        out_specs=ANY,
        input_output_aliases={0: 0},
        compiler_params=params(4),
        name="gate",
        cost_estimate=cost(micros),
    )(array, behind)


def near_z(piece, steps):
    return [send(piece, along_z(s)) for s in steps]


def enter_kernel(
    info,
    tokens,
    upstream,
    down,
    low,
    high,
    low_o,
    high_o,
    kept,
    vecs,
    bias,
    first,
    flipped,
    joint,
    grad_y,
    piece_down,
    weights,
    sem,
):
    feat = tokens.shape[1]
    third = feat // 2
    piece_down[0] = down[...]
    place = lax.broadcasted_iota(jnp.int32, upstream.shape, 0)
    grad_y[...] = jnp.where(place < info[LENGTH], upstream[...].astype(F32), 0.0).astype(BF16)
    settle(info, (low, high, low_o, high_o), weights, slice(None))
    normed, _ = centre(tokens[...].astype(F32))
    out = pltpu.make_async_copy(weights, kept, sem)
    out.start()
    split = 3 * third
    small = weights[0, :, :, split:] + weights[1, :, :, split:]
    small = small.reshape(feat, 128).astype(F32)
    each = bias.shape[1] // 32
    for device in range(32):
        row = device * feat // 32
        bias[:, device * each : (device + 1) * each] = small[row : row + 1, 128 - each :]
    small = small.T
    vecs[...] = small[:8]
    low_first = (normed * small[0:1] + small[2:3]).astype(BF16)
    first[...] = low_first
    flipped[...] = low_first.T.reshape(flipped.shape)
    for h in (0, 1):
        cols = slice(h * third, (h + 1) * third)
        bias = jnp.concatenate(
            [small[3:4, cols], jnp.zeros((1, third), F32), small[4:5, cols]], axis=1
        )
        w = weights[h, :, :, :split].reshape(feat, split)
        joint[h] = (dot(low_first, w) + bias).astype(BF16)
    out.wait()


def enter(info, tokens, upstream, down, hidden, pieces):
    rows, feat = tokens.shape
    width = pieces[0].shape[-1]
    vmem = pl.BlockSpec(memory_space=pltpu.VMEM)
    sets = (2, 16, feat // 16, width)
    return pl.pallas_call(
        enter_kernel,
        out_shape=(
            shape(sets, BF16),
            shape((8, feat), F32),
            shape((1, hidden), F32),
            shape((rows, feat), BF16),
            shape((16, feat // 16, rows), BF16),
            shape((2, rows, 3 * feat // 2), BF16),
            shape((rows, feat), BF16),
            shape((1,) + down.shape, BF16),
        ),
        in_specs=[SMEM] + [vmem] * 7,
        out_specs=(ANY,) + (vmem,) * 7,
        scratch_shapes=[pltpu.VMEM(sets, BF16), pltpu.SemaphoreType.DMA],
        compiler_params=params(20),
        name="enter",
        cost_estimate=cost(8),
    )(info, tokens, upstream, down, *pieces)


def scores_of(info, keys, queries):
    raw = dot_last(keys, queries)
    place = lax.broadcasted_iota(jnp.int32, raw.shape, 0)
    return jnp.where(place < info[LENGTH], raw, NEG)


def mix_kernel(info, q, k, v, _, mixed, flipped, stats):
    head = q.shape[-1] // 2
    scale = head**-0.5
    turned = v[0].T
    outs = []
    for h in (0, 1):
        cols = slice(h * head, (h + 1) * head)
        scores = scores_of(info, k[0, :, cols], q[0, :, cols] * scale)
        most = jnp.max(scores, axis=0, keepdims=True)
        expd = jnp.exp(scores - most)
        total = jnp.sum(expd, axis=0, keepdims=True)
        attn = (expd * (1.0 / total)).astype(BF16)
        stats[0, h : h + 1] = most + jnp.log(total)
        outs.append(dot(turned[cols], attn))
    both = jnp.concatenate(outs)
    flipped[...] = both.astype(BF16)
    mixed[...] = both.T.astype(BF16)


def mix(info, joint, behind):
    _, rows, width = joint.shape
    feat, pair = 2 * width // 3, 2 * width // 3 // HEADS * 2
    per = feat // 2 // pair
    spec = [
        pl.BlockSpec((1, rows, pair), lambda i, part=part: (i // per, 0, part * per + i % per))
        for part in range(3)
    ]
    n = HEADS // 2
    return pl.pallas_call(
        mix_kernel,
        grid=(n,),
        out_shape=(
            shape((rows, feat), BF16),
            shape((feat, rows), BF16),
            shape((n, 8, rows), F32),
        ),
        in_specs=[SMEM] + spec + [ANY],
        out_specs=(
            pl.BlockSpec((rows, pair), lambda i: (0, i)),
            pl.BlockSpec((pair, rows), lambda i: (i, 0)),
            pl.BlockSpec((1, 8, rows), lambda i: (i, 0, 0)),
        ),
        compiler_params=params(12),
        name="mix",
        cost_estimate=cost(10),
    )(info, joint, joint, joint, behind)


def mix_back_kernel(info, q, k, v, grad, stats, _, theirs, mine):
    head = q.shape[-1] // 2
    scale = head**-0.5
    turned = k[0].T
    parts = [[], [], []]
    for h in (0, 1):
        cols = slice(h * head, (h + 1) * head)
        queries = q[0, :, cols] * scale
        grad_h = grad[:, cols]
        attn = jnp.exp(scores_of(info, k[0, :, cols], queries) - stats[0, h : h + 1])
        grad_prob = dot_last(v[0, :, cols], grad_h)
        inner = jnp.sum(attn * grad_prob, axis=0, keepdims=True)
        low = (attn * (grad_prob - inner)).astype(BF16)
        parts[0].append(dot(turned[cols], low) * scale)
        parts[1].append(dot(low, queries))
        parts[2].append(dot(attn.astype(BF16), grad_h))
    out = [
        jnp.concatenate(parts[0]).T.astype(BF16),
        jnp.concatenate(parts[1], axis=1).astype(BF16),
        jnp.concatenate(parts[2], axis=1).astype(BF16),
    ]
    step, per = pl.program_id(0), pl.num_programs(0) // 2

    @pl.when(step < per)
    def _():
        for part in range(3):
            theirs[part] = out[part]

    @pl.when(step >= per)
    def _():
        for part in range(3):
            mine[part] = out[part]


def mix_back(info, joint, grad_mixed, stats, behind):
    _, rows, width = joint.shape
    feat, pair = 2 * width // 3, 2 * width // 3 // HEADS * 2
    per = feat // 2 // pair
    n = HEADS // 2

    def half(i, info):
        return jnp.where(i < per, 1 - info[CORE], info[CORE])

    spec = [
        pl.BlockSpec(
            (1, rows, pair), lambda i, info, part=part: (half(i, info), 0, part * per + i % per)
        )
        for part in range(3)
    ]
    out = shape((3, rows, feat // 2), BF16)
    return pl.pallas_call(
        mix_back_kernel,
        grid_spec=pltpu.PrefetchScalarGridSpec(
            num_scalar_prefetch=1,
            grid=(n,),
            in_specs=spec
            + [
                pl.BlockSpec((rows, pair), lambda i, info: (0, half(i, info) * per + i % per)),
                pl.BlockSpec(
                    (1, 8, rows), lambda i, info: (half(i, info) * per + i % per, 0, 0)
                ),
                ANY,
            ],
            out_specs=(
                pl.BlockSpec((3, rows, pair), lambda i, info: (0, 0, jnp.minimum(i, per - 1))),
                pl.BlockSpec((3, rows, pair), lambda i, info: (0, 0, jnp.maximum(i - per, 0))),
            ),
        ),
        out_shape=(out, out),
        compiler_params=params(12),
        name="mix_back",
        cost_estimate=cost(16),
    )(info, joint, joint, joint, grad_mixed, stats, behind)


GELU = (0.254829592, -0.284496736, 1.421413741, -1.453152027, 1.061405429)


def gelu_parts(x):
    bell = jnp.exp2(x * x * (-0.5 / math.log(2)))
    below = 1.0 + (0.3275911 * 0.5**0.5) * jnp.abs(x)
    t = pl.reciprocal(below, approx=True)
    t = t * (2.0 - below * t)
    poly = 0.5 * GELU[4]
    for c in GELU[3::-1]:
        poly = poly * t + 0.5 * c
    tail = poly * t * bell
    phi = jnp.where(x < 0, tail, 1.0 - tail)
    return x * phi, phi + x * (bell * (2 * math.pi) ** -0.5)


def rise_kernel(
    info, tokens, mixed, vecs, low, high, low_o, high_o, _, after, second, flipped, weights
):
    feat = tokens.shape[1]
    wide = low.shape[2] - feat // 2
    settle(info, (low, high, low_o, high_o), weights, slice(wide, None))
    start = tokens[...].astype(F32) + vecs[5:6]
    grown = [dot(mixed[...], weights[h].reshape(feat, feat // 2)) for h in (0, 1)]
    total = start + jnp.concatenate(grown, axis=1)
    after[...] = total
    normed, _ = centre(total)
    value = (normed * vecs[1:2] + vecs[6:7]).astype(BF16)
    second[...] = value
    flipped[...] = value.T.reshape(flipped.shape)


def rise(info, tokens, mixed, vecs, pieces, behind):
    rows, feat = tokens.shape
    vmem = pl.BlockSpec(memory_space=pltpu.VMEM)
    return pl.pallas_call(
        rise_kernel,
        out_shape=(
            shape((rows, feat), F32),
            shape((rows, feat), BF16),
            shape((16, feat // 16, rows), BF16),
        ),
        in_specs=[SMEM] + [vmem] * 7 + [ANY],
        out_specs=(vmem,) * 3,
        scratch_shapes=[pltpu.VMEM((2, 16, feat // 16, feat // 2), BF16)],
        compiler_params=params(20),
        name="rise",
        cost_estimate=cost(5),
    )(info, tokens, mixed, vecs, *pieces, behind)


def widen_kernel(
    info,
    second,
    bias,
    low,
    high,
    low_o,
    high_o,
    _,
    weights,
    active,
    slope,
    mine,
    theirs,
    turned,
    block_sems,
):
    step, steps = pl.program_id(0), pl.num_programs(0)
    core = info[CORE]
    feat = second.shape[1]
    tile = active.shape[1]
    wide = weights.shape[-1] - feat // 2
    per = wide // tile
    rows = mine.shape[1]
    count = tile // rows

    @pl.when(step == 0)
    def _():
        settle(info, (low, high, low_o, high_o), weights, slice(None))

    cols = pl.ds(pl.multiple_of(lax.rem(step, per) * tile, tile), tile)
    w = weights[step // per, :, :, cols].reshape(feat, tile)
    hidden = dot(second[...], w) + bias[...]
    value, grad = gelu_parts(hidden)
    value = value.astype(BF16)
    active[...] = value
    slope[...] = grad.astype(BF16)
    turned[pl.ds(step * count, count)] = value.T.reshape(count, rows, -1)
    for i in range(count):
        at = step * count + i
        chip = step * (count // 2) + i // 2

        @pl.when(core == i % 2)
        def _():
            dst = mine.at[info[PLACE + chip]]
            pltpu.make_async_copy(turned.at[at], dst, block_sems.at[at]).start()

        @pl.when(core != i % 2)
        def _():
            dst = theirs.at[info[PLACE_O + chip]]
            pltpu.make_async_copy(turned.at[at], dst, block_sems.at[at]).start()

    @pl.when(step == steps - 1)
    def _():
        for at in range(turned.shape[0]):
            pltpu.make_async_copy(turned.at[at], mine.at[0], block_sems.at[at]).wait()


def widen(info, second, bias, pieces, behind):
    rows, feat = second.shape
    width = pieces[0].shape[-1]
    hidden = 2 * width - feat
    tile, block = 768, hidden // 32
    turned = shape((16, block, rows), BF16)
    sets = (2, 16, feat // 16, width)
    strip = pl.BlockSpec((rows, tile), lambda n: (0, n))
    return pl.pallas_call(
        widen_kernel,
        grid=(hidden // tile,),
        out_shape=(
            shape(sets, BF16),
            shape((rows, hidden), BF16),
            shape((rows, hidden), BF16),
            turned,
            turned,
        ),
        in_specs=[SMEM, full((rows, feat)), pl.BlockSpec((1, tile), lambda n: (0, n))]
        + [full(pieces[0].shape)] * 4
        + [ANY],
        out_specs=(full(sets), strip, strip, ANY, ANY),
        scratch_shapes=[pltpu.VMEM((32, block, rows), BF16), pltpu.SemaphoreType.DMA((32,))],
        compiler_params=params(30),
        name="widen",
        cost_estimate=cost(18),
    )(info, second, bias, *pieces, behind)


def leave_kernel(after, active, down, vecs, _, output, total):
    step = pl.program_id(0)
    part = dot(active[...], down[...])

    @pl.when(step == 0)
    def _():
        total[...] = after[...] + vecs[7:8] + part

    @pl.when(step > 0)
    def _():
        total[...] += part

    @pl.when(step == pl.num_programs(0) - 1)
    def _():
        output[...] = total[...].astype(BF16)


def leave(after, active, down, vecs, behind):
    rows, feat = after.shape
    hidden = active.shape[1]
    tile = 768
    return pl.pallas_call(
        leave_kernel,
        grid=(hidden // tile,),
        out_shape=shape((rows, feat), BF16),
        in_specs=[
            full((rows, feat)),
            pl.BlockSpec((rows, tile), lambda n: (0, n)),
            pl.BlockSpec((tile, feat), lambda n: (n, 0)),
            full((8, feat)),
            ANY,
        ],
        out_specs=full((rows, feat)),
        scratch_shapes=[pltpu.VMEM((rows, feat), F32)],
        compiler_params=params(16),
        name="leave",
        cost_estimate=cost(7),
    )(after, active, down, vecs, behind)


def fall_kernel(
    info,
    grad_y,
    slope,
    up,
    after,
    vecs,
    proj,
    low,
    high,
    low_o,
    high_o,
    _,
    __,
    ___,
    kept,
    theirs,
    mine,
    bias_sum,
    grad_after,
    attn_theirs,
    attn_mine,
    grad_mixed,
    sums,
    weights,
    grad_second,
    sems,
    sem,
):
    step, steps = pl.program_id(0), pl.num_programs(0)
    core = info[CORE]
    feat = grad_y.shape[1]
    tile = slope.shape[1]
    per = steps // 2
    keeping = pltpu.make_async_copy(weights, kept, sem)

    @pl.when(step == 0)
    def _():
        for copy in fetch(info, (low, high, low_o, high_o), weights, sems, False):
            copy.wait()
        keeping.start()
        grad_second[...] = jnp.zeros_like(grad_second)

    half = jnp.where(step < per, 1 - core, core)
    at = half * per + lax.rem(step, per)
    count = tile * weights.shape[0] // (steps * tile)
    down = weights[pl.ds(count * at, count)].reshape(tile, feat)
    grad = (dot_last(grad_y[...], down) * slope[...].astype(F32)).astype(BF16)
    bias_sum[...] = jnp.sum(grad.astype(F32), axis=0, keepdims=True)
    grad_second[...] += dot_last(grad, up[0])

    @pl.when(step < per)
    def _():
        theirs[...] = grad

    @pl.when(step >= per)
    def _():
        mine[...] = grad

    @pl.when(step == steps - 1)
    def _():
        normed, inverse = centre(after[...])
        second = grad_second[...]
        live = grad_y[...].astype(F32)
        sums[0:1] = jnp.sum(second * normed, axis=0, keepdims=True)
        sums[1:2] = jnp.sum(second, axis=0, keepdims=True)
        total = live + layer_back(second * vecs[1:2], normed, inverse)
        grad_after[...] = total
        attn = total.astype(BF16)
        sums[2:3] = jnp.sum(attn.astype(F32), axis=0, keepdims=True)
        sums[3:4] = jnp.sum(live, axis=0, keepdims=True)
        sums[4:8] = jnp.zeros_like(sums[4:8])
        left, right = attn[:, : feat // 2], attn[:, feat // 2 :]
        attn_mine[...] = jnp.where(core == 0, left, right)
        attn_theirs[...] = jnp.where(core == 0, right, left)
        grad_mixed[...] = (dot_last(left, proj[0]) + dot_last(right, proj[1])).astype(BF16)
        keeping.wait()


def fall(info, grad_y, slope, up_set, after, vecs, pieces, behind):
    rows, feat = grad_y.shape
    hidden = slope.shape[1]
    tile = 768
    steps = hidden // tile
    per = steps // 2

    def at(n, info):
        return jnp.where(n < per, 1 - info[CORE], info[CORE]) * per + n % per

    def whole(dims):
        return pl.BlockSpec(dims, lambda n, info: (0,) * len(dims))

    return pl.pallas_call(
        fall_kernel,
        grid_spec=pltpu.PrefetchScalarGridSpec(
            num_scalar_prefetch=1,
            grid=(steps,),
            in_specs=[
                whole((rows, feat)),
                pl.BlockSpec((rows, tile), lambda n, info: (0, at(n, info))),
                pl.BlockSpec(
                    (1, feat, tile), lambda n, info: (at(n, info) // per, 0, n % per)
                ),
                whole((rows, feat)),
                whole((8, feat)),
                pl.BlockSpec((2, feat, feat // 2), lambda n, info: (0, 0, 4)),
            ]
            + [ANY] * 7,
            out_specs=(
                ANY,
                pl.BlockSpec((rows, tile), lambda n, info: (0, jnp.minimum(n, per - 1))),
                pl.BlockSpec((rows, tile), lambda n, info: (0, jnp.maximum(n - per, 0))),
                pl.BlockSpec((1, tile), lambda n, info: (0, at(n, info))),
                whole((rows, feat)),
                whole((rows, feat // 2)),
                whole((rows, feat // 2)),
                whole((rows, feat)),
                whole((8, feat)),
            ),
            scratch_shapes=[
                pltpu.VMEM((16, 2, hidden // 32, feat), BF16),
                pltpu.VMEM((rows, feat), F32),
                pltpu.SemaphoreType.DMA((32,)),
                pltpu.SemaphoreType.DMA,
            ],
        ),
        out_shape=(
            shape((16, 2, hidden // 32, feat), BF16),
            shape((rows, hidden // 2), BF16),
            shape((rows, hidden // 2), BF16),
            shape((1, hidden), F32),
            shape((rows, feat), F32),
            shape((rows, feat // 2), BF16),
            shape((rows, feat // 2), BF16),
            shape((rows, feat), BF16),
            shape((8, feat), F32),
        ),
        compiler_params=params(28),
        name="fall",
        cost_estimate=cost(18),
    )(info, grad_y, slope, up_set, after, vecs, up_set, *pieces, *behind)


def exit_kernel(
    info,
    tokens,
    mine,
    theirs,
    weights,
    grad_after,
    vecs,
    sums_a,
    bias,
    _,
    grad_tokens,
    keep,
    away,
    grad_first,
    joint,
    sums,
    extra,
):
    step = pl.program_id(0)
    core = info[CORE]
    third = mine.shape[2]
    half = jnp.where(step == 0, core, 1 - core)
    spot = pl.ds(pl.multiple_of(half * third, third), third)

    def parts(source):
        for part in range(3):
            joint[:, part * third : (part + 1) * third] = source[part]
        sums[3:4, spot] = jnp.sum(source[0].astype(F32), axis=0, keepdims=True)
        sums[4:5, spot] = jnp.sum(source[2].astype(F32), axis=0, keepdims=True)
        return dot_last(joint[...], weights[0])

    @pl.when(step == 0)
    def _():
        grad_first[...] = parts(mine)

    @pl.when(step == 1)
    def _():
        grad = grad_first[...] + parts(theirs)
        normed, inverse = centre(tokens[...].astype(F32))
        sums[0:1] = jnp.sum(grad * normed, axis=0, keepdims=True)
        sums[1:2] = sums_a[0:1]
        sums[2:3] = jnp.sum(grad, axis=0, keepdims=True)
        sums[5:6] = sums_a[2:3]
        sums[6:7] = sums_a[1:2]
        sums[7:8] = sums_a[3:4]
        sums[8:] = jnp.zeros_like(sums[8:])
        back = layer_back(grad * vecs[0:1], normed, inverse)
        grad_tokens[...] = (grad_after[...] + back).astype(BF16)
        flipped = sums[...].T
        block, each = extra.shape[1], bias.shape[1] // 32
        for chip in range(16):
            place = info[PLACE + chip]
            extra[place] = flipped[chip * block : (chip + 1) * block]
            for c in (0, 1):
                at = (2 * chip + c) * each
                row = c * block // 2
                extra[place, row : row + 1, 128 - each :] = bias[:, at : at + each]
        keep[...] = extra[:8]
        away[...] = extra[8:].astype(BF16)


def exit_back(info, tokens, mine, theirs, first_set, grad_after, vecs, sums_a, bias, behind):
    rows, feat = tokens.shape
    third = feat // 2
    block = feat // 16

    def whole(dims):
        return pl.BlockSpec(dims, lambda n, info: (0,) * len(dims))

    return pl.pallas_call(
        exit_kernel,
        grid_spec=pltpu.PrefetchScalarGridSpec(
            num_scalar_prefetch=1,
            grid=(2,),
            in_specs=[
                whole((rows, feat)),
                whole((3, rows, third)),
                whole((3, rows, third)),
                pl.BlockSpec(
                    (1, feat, 3 * third),
                    lambda n, info: (jnp.where(n == 0, info[CORE], 1 - info[CORE]), 0, 0),
                ),
                whole((rows, feat)),
                whole((8, feat)),
                whole((8, feat)),
                whole(bias.shape),
                ANY,
            ],
            out_specs=(whole((rows, feat)), whole((8, block, 128)), whole((8, block, 128))),
            scratch_shapes=[
                pltpu.VMEM((rows, feat), F32),
                pltpu.VMEM((rows, 3 * third), BF16),
                pltpu.VMEM((128, feat), F32),
                pltpu.VMEM((16, block, 128), F32),
            ],
        ),
        out_shape=(
            shape((rows, feat), BF16),
            shape((8, block, 128), F32),
            shape((8, block, 128), BF16),
        ),
        compiler_params=params(18),
        name="exit_back",
        cost_estimate=cost(8),
    )(info, tokens, mine, theirs, first_set, grad_after, vecs, sums_a, bias, behind)


def line_up(info, left, left_o, turned):
    rows = left.shape[2]
    for chip in range(16):
        place = info[PLACE + chip]
        turned[place, :, :rows] = left[chip]
        turned[place, :, rows:] = left_o[chip]


def outer_tile(turned, right, right_o):
    rows = right.shape[0]
    both = turned[...].reshape(-1, turned.shape[2])
    total = dot(both[:, :rows], right) + dot(both[:, rows:], right_o)
    return total.reshape(16, -1, total.shape[1])


def outer_up_kernel(
    info, left, left_o, right, right_o, low, low_o, attn, attn_o, _, keep, away, turned
):
    step, last = pl.program_id(0), pl.num_programs(0) - 1

    @pl.when(step == 0)
    def _():
        line_up(info, left, left_o, turned)

    @pl.when(step < last)
    def _():
        total = outer_tile(turned, right[...], right_o[...])
        keep[...] = total[:8]
        away[...] = total[8:].astype(BF16)

    @pl.when(step == last)
    def _():
        line_up(info, low, low_o, turned)
        total = outer_tile(turned, attn[...], attn_o[...])
        keep[:, :, : attn.shape[1]] = total[:8]
        away[:, :, : attn.shape[1]] = total[8:].astype(BF16)


def outer_up(info, left, left_o, right, right_o, low, low_o, attn, attn_o, behind):
    _, block, rows = left.shape
    tile = 2 * attn.shape[1]
    n = right.shape[1] // tile
    cols = right.shape[1] + attn.shape[1]
    strip = pl.BlockSpec((rows, tile), lambda i: (0, jnp.minimum(i, n - 1)))
    out = pl.BlockSpec((8, block, tile), lambda i: (0, 0, i))
    return pl.pallas_call(
        outer_up_kernel,
        grid=(n + 1,),
        out_shape=(shape((8, block, cols), F32), shape((8, block, cols), BF16)),
        in_specs=[SMEM]
        + [full(left.shape)] * 2
        + [strip] * 2
        + [full(left.shape)] * 2
        + [full(attn.shape)] * 2
        + [ANY],
        out_specs=(out, out),
        scratch_shapes=[pltpu.VMEM((16, block, 2 * rows), BF16)],
        compiler_params=params(20),
        name="outer_up",
        cost_estimate=cost(8),
    )(info, left, left_o, right, right_o, low, low_o, attn, attn_o, behind)


def outer_qkv_kernel(info, left, left_o, right, right_o, _, keep, away, turned):
    tile = right.shape[2]
    line_up(info, left, left_o, turned)
    for part in range(3):
        cols = slice(part * tile, (part + 1) * tile)
        total = outer_tile(turned, right[part], right_o[part])
        keep[:, :, cols] = total[:8]
        away[:, :, cols] = total[8:].astype(BF16)


def outer_qkv(info, left, left_o, right, right_o, behind):
    _, block, rows = left.shape
    cols = 3 * right.shape[2]
    vmem = pl.BlockSpec(memory_space=pltpu.VMEM)
    return pl.pallas_call(
        outer_qkv_kernel,
        out_shape=(shape((8, block, cols), F32), shape((8, block, cols), BF16)),
        in_specs=[SMEM] + [vmem] * 4 + [ANY],
        out_specs=(vmem, vmem),
        scratch_shapes=[pltpu.VMEM((16, block, 2 * rows), BF16)],
        compiler_params=params(20),
        name="outer_qkv",
        cost_estimate=cost(8),
    )(info, left, left_o, right, right_o, behind)


def outer_down_kernel(left, left_o, right, right_o, _, keep, away):
    def flat(blocks):
        return blocks[...].reshape(-1, blocks.shape[-1])

    total = dot(flat(left), right[...]) + dot(flat(left_o), right_o[...])
    total = total.reshape(keep.shape)

    @pl.when(pl.program_id(0) >= 2)
    def _():
        keep[...] = total

    @pl.when(pl.program_id(0) < 2)
    def _():
        away[...] = total.astype(BF16)


def outer_down(left, left_o, right, right_o, behind):
    _, block, rows = left.shape
    feat = right.shape[1]
    strip = pl.BlockSpec((4, block, rows), lambda j: ((j + 2) % 4, 0, 0))
    return pl.pallas_call(
        outer_down_kernel,
        grid=(4,),
        out_shape=(shape((8, block, feat), F32), shape((8, block, feat), BF16)),
        in_specs=[strip, strip, full((rows, feat)), full((rows, feat)), ANY],
        out_specs=(
            pl.BlockSpec((4, block, feat), lambda j: (jnp.maximum(j - 2, 0), 0, 0)),
            pl.BlockSpec((4, block, feat), lambda j: (jnp.minimum(j, 1), 0, 0)),
        ),
        compiler_params=params(16),
        name="outer_down",
        cost_estimate=cost(8),
    )(left, left_o, right, right_o, behind)


def add_first_kernel(keep, got, _, kept, away):
    kept[...] = keep[:4] + got[:4].astype(F32)
    away[...] = (keep[4:] + got[4:].astype(F32)).astype(BF16)


def shift_first(keep, away, behind, micros=0):
    _, rows, cols = keep.shape
    vmem = pl.BlockSpec(memory_space=pltpu.VMEM)
    return pl.pallas_call(
        add_first_kernel,
        out_shape=(shape((4, rows, cols), F32), shape((4, rows, cols), BF16)),
        in_specs=[vmem, vmem, ANY],
        out_specs=(vmem, vmem),
        compiler_params=params(12),
        name="shift_first",
        cost_estimate=cost(micros),
    )(keep, send(away, second_way), behind)


def add_both_kernel(keep, got, few_keep, few_got, _, kept, away):
    split = keep.shape[2]
    kept[:, :, :split] = keep[:4] + got[:4].astype(F32)
    kept[:, :, split:] = few_keep[:4] + few_got[:4].astype(F32)
    away[:, :, :split] = (keep[4:] + got[4:].astype(F32)).astype(BF16)
    away[:, :, split:] = (few_keep[4:] + few_got[4:].astype(F32)).astype(BF16)


def shift_both(keep, away, few_keep, few_away, behind):
    _, rows, cols = keep.shape
    cols += few_keep.shape[2]
    vmem = pl.BlockSpec(memory_space=pltpu.VMEM)
    return pl.pallas_call(
        add_both_kernel,
        out_shape=(shape((4, rows, cols), F32), shape((4, rows, cols), BF16)),
        in_specs=[vmem] * 4 + [ANY],
        out_specs=(vmem, vmem),
        compiler_params=params(12),
        name="shift_both",
        cost_estimate=cost(0),
    )(keep, send(away, second_way), few_keep, send(few_away, second_way), behind)


def add_second_kernel(keep, got, _, base, one, two, three):
    base[...] = keep[0] + got[0].astype(F32)
    for s, out in ((1, one), (2, two), (3, three)):
        out[...] = (keep[s] + got[s].astype(F32)).astype(BF16)


def shift_second(keep, away, behind):
    _, rows, cols = keep.shape
    vmem = pl.BlockSpec(memory_space=pltpu.VMEM)
    base, *lows = pl.pallas_call(
        add_second_kernel,
        out_shape=(shape((rows, cols), F32),) + (shape((rows, cols), BF16),) * 3,
        in_specs=[vmem, vmem, ANY],
        out_specs=(vmem,) * 4,
        compiler_params=params(8),
        name="shift_second",
        cost_estimate=cost(0),
    )(keep, send(away, first_way), behind)
    return base, [send(low, along_z(s)) for low, s in zip(lows, (1, 2, 3))]


def total_of(base, parts):
    return base[...] + parts[0][...].astype(F32) + (
        parts[1][...].astype(F32) + parts[2][...].astype(F32)
    )


def add_down_kernel(base, one, two, three, _, out):
    out[...] = total_of(base, (one, two, three))


def home_down(base, parts, behind):
    vmem = pl.BlockSpec(memory_space=pltpu.VMEM)
    return pl.pallas_call(
        add_down_kernel,
        out_shape=shape(base.shape, F32),
        in_specs=[vmem] * 4 + [ANY],
        out_specs=vmem,
        compiler_params=params(8),
        name="home_down",
        cost_estimate=cost(0),
    )(base, *parts, behind)


def add_last_kernel(info, base, one, two, three, _, mine, theirs, total):
    core = info[CORE]
    half = mine.shape[0]
    total[...] = total_of(base, (one, two, three))
    mine[...] = total[pl.ds(pl.multiple_of(core * half, half), half)]
    theirs[...] = total[pl.ds(pl.multiple_of((1 - core) * half, half), half)]


def home(info, base, parts, behind):
    rows, cols = base.shape
    vmem = pl.BlockSpec(memory_space=pltpu.VMEM)
    out = shape((rows // 2, cols), F32)
    mine, theirs = pl.pallas_call(
        add_last_kernel,
        out_shape=(out, out),
        in_specs=[SMEM] + [vmem] * 4 + [ANY],
        out_specs=(vmem, vmem),
        scratch_shapes=[pltpu.VMEM((rows, cols), F32)],
        compiler_params=params(8),
        name="home",
        cost_estimate=cost(0),
    )(info, base, *parts, behind)
    return mine, swap(theirs)


def finish_kernel(info, qkv, qkv_o, up, up_o, out_qkv, out_proj, out_up, gains, shifts, bias):
    rows, third = out_proj.shape[0], out_proj.shape[1] // 2
    wide = out_up.shape[1] // 2
    small = qkv[:, 3 * third :] + qkv_o[:, 3 * third :]
    flipped = jnp.concatenate([small, jnp.zeros((128 - rows, 128), F32)]).T
    gains[...] = flipped[0:2, :rows]
    shifts[...] = flipped[2:8, :rows]
    bias[...] = small[0:1, 128 - bias.shape[1] :]

    def lay(core):
        for half, (a, b) in ((core, (qkv, up)), (1 - core, (qkv_o, up_o))):
            for part in range(3):
                spot = part * 2 * third + half * third
                out_qkv[:, spot : spot + third] = a[:, part * third : (part + 1) * third]
            out_proj[:, half * third : (half + 1) * third] = b[:, wide:]
            out_up[:, half * wide : (half + 1) * wide] = b[:, :wide]

    @pl.when(info[CORE] == 0)
    def _():
        lay(0)

    @pl.when(info[CORE] == 1)
    def _():
        lay(1)


def finish(info, qkv, qkv_o, up, up_o):
    rows = qkv.shape[0]
    third = (qkv.shape[1] - 128) // 3
    vmem = pl.BlockSpec(memory_space=pltpu.VMEM)
    return pl.pallas_call(
        finish_kernel,
        out_shape=(
            shape((rows, 6 * third), F32),
            shape((rows, 2 * third), F32),
            shape((rows, 2 * (up.shape[1] - third)), F32),
            shape((2, rows), F32),
            shape((6, rows), F32),
            shape((1, 4 * rows), F32),
        ),
        in_specs=[SMEM] + [vmem] * 4,
        out_specs=(vmem,) * 6,
        compiler_params=params(8),
        name="finish",
        cost_estimate=cost(0),
    )(info, qkv, qkv_o, up, up_o)


def local(
    tokens,
    upstream,
    lengths,
    qkv_weight,
    proj_weight,
    up_weight,
    down_weight,
    gains,
    shifts,
    up_bias,
):
    tok_rows, feat = tokens.shape
    rows = qkv_weight.shape[0]
    hidden = up_weight.shape[1]
    third, wide = feat // 2, hidden // 2
    chip, core = lax.axis_index("dp"), lax.axis_index("fsdp")
    info = facts(chip, core, lengths[0])

    small = jnp.concatenate([gains, shifts], axis=1)
    small = jnp.pad(small, ((0, 0), (0, 128 - small.shape[1])))
    small = small + jnp.pad(up_bias[None], ((0, rows - 1), (128 - up_bias.shape[0], 0)))
    mine, theirs = halves(info, qkv_weight, proj_weight, up_weight)
    one = 3 * third + 128
    piece, piece_up = pieces_of(info, mine, swap(theirs), small, 3 * third)
    zs, piece_up = gather([piece] + near_z(piece, (1, 2, 3)), (piece_up,))
    up_z = near_z(piece_up, (1, 2))
    low, piece_up = gather([zs, send(zs, first_way)], (piece_up,), up_z)
    up_z += near_z(piece_up, (3,))
    high = send(low, second_way)
    (zs_up,) = gather([piece_up] + up_z)
    high = gate(high, zs_up)
    first_pieces = (low, high, swap(low), swap(high))

    first_set, vecs, bias, first, first_t, joint, grad_y, down = enter(
        info, tokens, upstream, down_weight, hidden, first_pieces
    )
    grad_y_o = swap(grad_y)
    first_set = first_set.reshape(2, feat, one)
    first_o = swap(first_t)
    (low,) = gather([zs_up, send(zs_up, first_way)], (), (vecs,))
    down_z = near_z(down, (1, 2, 3))
    mixed, mixed_t, stats = mix(info, joint, low)
    high = gate(send(low, second_way), mixed)
    up_pieces = (low, high, swap(low), swap(high))
    (zs_down,) = gather([down] + down_z, (), (high,), 5)
    mixed_t = mixed_t.reshape(first_t.shape)
    mixed_o = swap(mixed_t)
    after, second, second_t = rise(info, tokens, mixed, vecs, up_pieces, zs_down)
    second_o = swap(second_t)
    (low,) = gather([zs_down, send(zs_down, first_way)], (), (second,))
    up_set, active, slope, turned, turned_t = widen(info, second, bias, up_pieces, low)
    up_set = up_set.reshape(2, feat, wide + third)
    high = gate(send(low, second_way), slope, 5)
    down_pieces = (low, high, swap(low), swap(high))
    down = outer_down(turned, swap(turned_t), grad_y, grad_y_o, slope)
    down_set, hid_theirs, hid_mine, bias_sum, grad_after, at_theirs, at_mine, grad_mixed, sums_a = (
        fall(
            info, grad_y, slope, up_set, after, vecs, down_pieces, (down[1], second_o, mixed_o)
        )
    )
    hid_o, at_o = swap(hid_theirs), swap(at_theirs)
    down = shift_first(*down, hid_theirs, 5)
    up = outer_up(
        info, second_t, second_o, hid_mine, hid_o, mixed_t, mixed_o, at_mine, at_o, down[1]
    )
    down = shift_second(*down, up[1])
    theirs, mine = mix_back(info, joint, grad_mixed, stats, down[0])
    theirs_o = swap(theirs)
    own_down = home_down(*down, theirs)
    up = shift_first(*up, own_down, 5)
    qkv = outer_qkv(info, first_t, first_o, mine, theirs_o, up[1])
    grad_tokens, few_keep, few_away = exit_back(
        info, tokens, mine, theirs, first_set, grad_after, vecs, sums_a, bias_sum, qkv[1]
    )
    up = shift_second(*up, grad_tokens)
    qkv = shift_both(*qkv, few_keep, few_away, up[0])
    output = leave(after, active, down_set.reshape(hidden, feat), vecs, qkv[1])
    base, parts = shift_second(*qkv, output)
    own_up = home(info, *up, base)
    own_qkv = home(info, base, parts, own_up[0])
    out_qkv, out_proj, out_up, out_gains, out_shifts, out_bias = finish(info, *own_qkv, *own_up)
    return (
        output,
        grad_tokens,
        out_qkv,
        out_proj,
        out_up,
        own_down,
        out_gains.T,
        out_shifts.T,
        out_bias.reshape(-1),
    )


def solution(mesh):
    placed = (
        P(("dp", "fsdp"), None),
        P(("dp", "fsdp"), None),
        P(("dp", "fsdp")),
        P(("dp", "fsdp"), None),
        P(("dp", "fsdp"), None),
        P(("dp", "fsdp"), None),
        P(("dp", "fsdp"), None),
        P(("dp", "fsdp"), None),
        P(("dp", "fsdp"), None),
        P(("dp", "fsdp")),
    )
    sizes = (mesh.shape["dp"], mesh.shape["fsdp"])
    return jax.shard_map(
        local if sizes == (16, 2) else plain,
        mesh=mesh,
        in_specs=placed,
        out_specs=(
            P(("dp", "fsdp"), None),
            P(("dp", "fsdp"), None),
            P(("dp", "fsdp"), None),
            P(("dp", "fsdp"), None),
            P(("dp", "fsdp"), None),
            P(("dp", "fsdp"), None),
            P(("dp", "fsdp"), None),
            P(("dp", "fsdp"), None),
            P(("dp", "fsdp")),
        ),
        check_vma=False,
    )
```

```python
import math
from functools import partial

import jax
import jax.numpy as jnp
from jax import lax
from jax.experimental import pallas as pl
from jax.experimental.pallas import tpu as pltpu
from jax.sharding import PartitionSpec as P

HEADS = 12
EPS = 1e-06
NEG = -1e30
AXES = ("dp", "fsdp")
F32 = jnp.float32
BF16 = jnp.bfloat16
VMEM_LIMIT = 32 * 1024 * 1024


def collect(qkv_weight, proj_weight, up_weight, down_weight, gains, shifts, up_bias):
    gathered = (
        lax.all_gather(qkv_weight, ("dp", "fsdp"), axis=0, tiled=True),
        lax.all_gather(proj_weight, ("dp", "fsdp"), axis=0, tiled=True),
        lax.all_gather(up_weight, ("dp", "fsdp"), axis=0, tiled=True),
        lax.all_gather(down_weight, ("dp", "fsdp"), axis=0, tiled=True),
        lax.all_gather(gains, ("dp", "fsdp"), axis=0, tiled=True),
        lax.all_gather(shifts, ("dp", "fsdp"), axis=0, tiled=True),
        lax.all_gather(up_bias, ("dp", "fsdp"), axis=0, tiled=True),
    )
    return gathered


def give_back(grad_qkv, grad_proj, grad_up, grad_down, grad_gains, grad_shifts, grad_bias_up):
    owned = (
        lax.psum_scatter(grad_qkv, ("dp", "fsdp"), scatter_dimension=0, tiled=True),
        lax.psum_scatter(grad_proj, ("dp", "fsdp"), scatter_dimension=0, tiled=True),
        lax.psum_scatter(grad_up, ("dp", "fsdp"), scatter_dimension=0, tiled=True),
        lax.psum_scatter(grad_down, ("dp", "fsdp"), scatter_dimension=0, tiled=True),
        lax.psum_scatter(grad_gains, ("dp", "fsdp"), scatter_dimension=0, tiled=True),
        lax.psum_scatter(grad_shifts, ("dp", "fsdp"), scatter_dimension=0, tiled=True),
        lax.psum_scatter(grad_bias_up, ("dp", "fsdp"), scatter_dimension=0, tiled=True),
    )
    return owned


def normalize(values):
    centred = values - jnp.mean(values, axis=-1, keepdims=True)
    inverse = lax.rsqrt(jnp.mean(centred * centred, axis=-1, keepdims=True) + EPS)
    return (centred * inverse, inverse)


def norm_back(grad_norm, normed, inverse):
    return inverse * (
        grad_norm
        - jnp.mean(grad_norm, axis=-1, keepdims=True)
        - normed * jnp.mean(grad_norm * normed, axis=-1, keepdims=True)
    )


def block_scores(query_blk, key_rows, live_mask, scaling):
    raw = (
        jnp.einsum("qhd,khd->hqk", query_blk, key_rows, preferred_element_type=jnp.float32)
        * scaling
    )
    return jnp.where(live_mask[None, None, :], raw, NEG)


def plain(
    tokens,
    upstream,
    lengths,
    qkv_weight,
    proj_weight,
    up_weight,
    down_weight,
    gains,
    shifts,
    up_bias,
):
    tok_rows, feat_width = tokens.shape
    n_heads = HEADS
    head_size = feat_width // n_heads
    scaling = head_size ** (-0.5)
    block_rows = min(512, tok_rows)
    group_heads = 4
    head_starts = list(range(0, n_heads, group_heads))
    gathered = collect(qkv_weight, proj_weight, up_weight, down_weight, gains, shifts, up_bias)
    qkv_full, proj_full, up_full, down_full, gain_full, shift_full, bias_full = gathered
    gain_f = gain_full.astype(jnp.float32)
    shift_f = shift_full.astype(jnp.float32)
    bias_f = bias_full.astype(jnp.float32)
    live_mask = lax.iota(jnp.int32, tok_rows) < lengths[0]
    source = tokens.astype(jnp.float32)
    norm_one, inv_one = normalize(source)
    first = (norm_one * gain_f[:, 0] + shift_f[:, 0]).astype(jnp.bfloat16)
    joint_bias = jnp.concatenate([shift_f[:, 1], jnp.zeros_like(shift_f[:, 1]), shift_f[:, 2]])
    joint = (jnp.dot(first, qkv_full, preferred_element_type=jnp.float32) + joint_bias).astype(
        jnp.bfloat16
    )
    queries = joint[:, :feat_width].reshape(tok_rows, n_heads, head_size)
    key_rows = joint[:, feat_width : 2 * feat_width].reshape(tok_rows, n_heads, head_size)
    value_rows = joint[:, 2 * feat_width :].reshape(tok_rows, n_heads, head_size)
    log_sums = {}
    offset = 0
    group_parts = []
    for head_lo in head_starts:
        head_hi = head_lo + group_heads
        scores = block_scores(
            queries[offset : offset + block_rows, head_lo:head_hi],
            key_rows[:, head_lo:head_hi],
            live_mask,
            scaling,
        )
        row_max = jnp.max(scores, axis=-1, keepdims=True)
        expd = jnp.exp(scores - row_max)
        row_sum = jnp.sum(expd, axis=-1, keepdims=True)
        attn_low = (expd / row_sum).astype(jnp.bfloat16)
        log_sums[offset, head_lo] = row_max + jnp.log(row_sum)
        group_parts.append(
            jnp.einsum(
                "hqk,khd->qhd",
                attn_low,
                value_rows[:, head_lo:head_hi],
                preferred_element_type=jnp.float32,
            )
        )
    mixed_parts = jnp.concatenate(group_parts, axis=1)
    mixed = mixed_parts.reshape(tok_rows, feat_width).astype(jnp.bfloat16)
    after = source + jnp.dot(mixed, proj_full, preferred_element_type=jnp.float32) + shift_f[:, 3]
    norm_two, inv_two = normalize(after)
    second = (norm_two * gain_f[:, 1] + shift_f[:, 4]).astype(jnp.bfloat16)
    hidden = jnp.dot(second, up_full, preferred_element_type=jnp.float32) + bias_f
    gelu_exact = partial(jax.nn.gelu, approximate=False)
    active = gelu_exact(hidden).astype(jnp.bfloat16)
    output = (
        after + jnp.dot(active, down_full, preferred_element_type=jnp.float32) + shift_f[:, 5]
    ).astype(jnp.bfloat16)
    regathered = collect(qkv_weight, proj_weight, up_weight, down_weight, gains, shifts, up_bias)
    qkv_full, proj_full, up_full, down_full, gain_full, shift_full, bias_full = regathered
    grad_y = jnp.where(live_mask[:, None], upstream, jnp.zeros_like(upstream))
    sum_y = jnp.sum(grad_y, axis=0, dtype=jnp.float32)
    grad_down = jnp.einsum("tf,td->fd", active, grad_y, preferred_element_type=jnp.float32)
    grad_active = jnp.einsum("td,fd->tf", grad_y, down_full, preferred_element_type=jnp.float32)
    gelu_value, gelu_pull = jax.vjp(gelu_exact, hidden)
    grad_hidden = gelu_pull(grad_active)[0].astype(jnp.bfloat16)
    grad_bias_up = jnp.sum(grad_hidden, axis=0, dtype=jnp.float32)
    grad_up = jnp.einsum("td,tf->df", second, grad_hidden, preferred_element_type=jnp.float32)
    grad_second = jnp.einsum("tf,df->td", grad_hidden, up_full, preferred_element_type=jnp.float32)
    gain_two_grad = jnp.sum(grad_second * norm_two, axis=0)
    shift_two_grad = jnp.sum(grad_second, axis=0)
    grad_after = grad_y.astype(jnp.float32) + norm_back(
        grad_second * gain_f[:, 1], norm_two, inv_two
    )
    grad_attn = grad_after.astype(jnp.bfloat16)
    sum_attn = jnp.sum(grad_attn, axis=0, dtype=jnp.float32)
    grad_proj = jnp.einsum("td,te->de", mixed, grad_attn, preferred_element_type=jnp.float32)
    grad_mixed = jnp.einsum("te,de->td", grad_attn, proj_full, preferred_element_type=jnp.float32)
    grad_mixed = grad_mixed.astype(jnp.bfloat16).reshape(tok_rows, n_heads, head_size)
    key_groups = {}
    value_groups = {}
    for head_lo in head_starts:
        key_groups[head_lo] = jnp.zeros((tok_rows, group_heads, head_size), jnp.float32)
        value_groups[head_lo] = jnp.zeros((tok_rows, group_heads, head_size), jnp.float32)
    offset = 0
    query_groups = []
    for head_lo in head_starts:
        head_hi = head_lo + group_heads
        query_blk = queries[offset : offset + block_rows, head_lo:head_hi]
        grad_blk = grad_mixed[offset : offset + block_rows, head_lo:head_hi]
        key_part = key_rows[:, head_lo:head_hi]
        scores = block_scores(query_blk, key_part, live_mask, scaling)
        attn_p = jnp.exp(scores - log_sums[offset, head_lo])
        value_groups[head_lo] = jnp.einsum(
            "hqk,qhd->khd",
            attn_p.astype(jnp.bfloat16),
            grad_blk,
            preferred_element_type=jnp.float32,
        )
        grad_prob = jnp.einsum(
            "qhd,khd->hqk",
            grad_blk,
            value_rows[:, head_lo:head_hi],
            preferred_element_type=jnp.float32,
        )
        grad_score = attn_p * (grad_prob - jnp.sum(attn_p * grad_prob, axis=-1, keepdims=True))
        score_low = grad_score.astype(jnp.bfloat16)
        query_groups.append(
            jnp.einsum("hqk,khd->qhd", score_low, key_part, preferred_element_type=jnp.float32)
            * scaling
        )
        key_groups[head_lo] = (
            jnp.einsum("hqk,qhd->khd", score_low, query_blk, preferred_element_type=jnp.float32)
            * scaling
        )
    grad_query_parts = jnp.concatenate(query_groups, axis=1)
    grad_keys = jnp.concatenate([key_groups[head_lo] for head_lo in head_starts], axis=1)
    grad_vals = jnp.concatenate([value_groups[head_lo] for head_lo in head_starts], axis=1)
    grad_joint = jnp.concatenate(
        [
            grad_query_parts.reshape(tok_rows, feat_width),
            grad_keys.reshape(tok_rows, feat_width),
            grad_vals.reshape(tok_rows, feat_width),
        ],
        axis=1,
    ).astype(jnp.bfloat16)
    joint_sums = jnp.sum(grad_joint, axis=0, dtype=jnp.float32)
    grad_qkv = jnp.einsum("td,te->de", first, grad_joint, preferred_element_type=jnp.float32)
    grad_first = jnp.einsum("te,de->td", grad_joint, qkv_full, preferred_element_type=jnp.float32)
    gain_one_grad = jnp.sum(grad_first * norm_one, axis=0)
    shift_one_grad = jnp.sum(grad_first, axis=0)
    grad_tokens = (grad_after + norm_back(grad_first * gain_f[:, 0], norm_one, inv_one)).astype(
        jnp.bfloat16
    )
    grad_gains = jnp.stack([gain_one_grad, gain_two_grad], axis=1)
    grad_shifts = jnp.stack(
        [
            shift_one_grad,
            joint_sums[:feat_width],
            joint_sums[2 * feat_width :],
            sum_attn,
            shift_two_grad,
            sum_y,
        ],
        axis=1,
    )
    owned = give_back(
        grad_qkv, grad_proj, grad_up, grad_down, grad_gains, grad_shifts, grad_bias_up
    )
    own_qkv, own_proj, own_up, own_down, own_gains, own_shifts, own_bias = owned
    return (
        output,
        grad_tokens,
        own_qkv,
        own_proj,
        own_up,
        own_down,
        own_gains,
        own_shifts,
        own_bias,
    )


BOTH_LAST = (((1,), (1,)), ((), ()))
SMEM = pl.BlockSpec(memory_space=pltpu.SMEM)
ANY = pl.BlockSpec(memory_space=pl.ANY)
CORE, LENGTH, PLACE, PLACE_O = 32, 33, 34, 50


def pairs(move):
    return [(i, move(i)) for i in range(32)]


def first_way(i):
    return i ^ (2 if i % 2 == 0 else 4)


def second_way(i):
    return i ^ (4 if i % 2 == 0 else 2)


def along_z(step):
    return lambda i: i ^ (8 * step)


def send(array, move):
    return lax.ppermute(array, AXES, pairs(move))


def swap(array):
    return send(array, lambda i: i ^ 1)


def facts(chip, core, length):
    places = []
    for of_core in (core, 1 - core):
        for j in range(16):
            z, first, second = j % 4, (j // 4) % 2, j // 8
            mask = jnp.where(of_core == 0, first + 2 * second, second + 2 * first)
            places.append(jnp.bitwise_xor(chip, mask + 4 * z))
    spots = []
    for of_core in (core, 1 - core):
        for k in range(16):
            mask = jnp.bitwise_xor(chip, k)
            x, y, z = mask & 1, (mask >> 1) & 1, mask >> 2
            spots.append(z + jnp.where(of_core == 0, 4 * x + 8 * y, 4 * y + 8 * x))
    return jnp.stack(places + [core, length] + spots).astype(jnp.int32)


def params(mib):
    return pltpu.CompilerParams(vmem_limit_bytes=mib * 1024 * 1024)


def cost(micros):
    flops = int(micros * (3e10 if micros > 3 else 1e9))
    return pl.CostEstimate(flops=flops, bytes_accessed=1, transcendentals=0)


def shape(dims, dtype):
    return jax.ShapeDtypeStruct(dims, dtype)


def full(dims):
    return pl.BlockSpec(dims, lambda *_: (0,) * len(dims))


class Chain:
    def __init__(self):
        self.token, self.extra = None, ()

    def near(self, *arrays):
        self.extra = arrays

    def call(
        self, kernel, *, out_shape, in_specs, out_specs, grid=(), prefetch=0, aliases={}, **options
    ):
        single = not isinstance(out_shape, tuple)
        if single:
            out_shape, out_specs = (out_shape,), (out_specs,)
        held = 0 if self.token is None else 1
        extra, self.extra = self.extra, ()
        n_in, n_out = prefetch + len(in_specs), len(out_shape)
        at_token = n_in + len(extra)

        def body(*refs):
            skip = at_token + held
            return kernel(*refs[:n_in], *refs[skip : skip + n_out], *refs[skip + n_out + 1 :])

        token = shape((8, 128), F32)
        specs = pltpu.PrefetchScalarGridSpec(
            num_scalar_prefetch=prefetch,
            grid=grid,
            in_specs=list(in_specs) + [ANY] * (len(extra) + held),
            out_specs=tuple(out_specs) + (ANY,),
            scratch_shapes=options.pop("scratch_shapes", ()),
        )
        run = pl.pallas_call(
            body,
            grid_spec=specs,
            out_shape=tuple(out_shape) + (token,),
            input_output_aliases=aliases | ({at_token: n_out} if held else {}),
            **options,
        )

        def with_token(*args):
            *outs, self.token = run(*args, *extra, *([self.token] if held else []))
            return outs[0] if single else tuple(outs)

        return with_token


def dot(left, right):
    return jnp.dot(left, right, preferred_element_type=F32)


def dot_last(left, right):
    return lax.dot_general(left, right, BOTH_LAST, preferred_element_type=F32)


def settle(info, pieces, dest, who=(0, 1)):
    for w in who:
        half = info[CORE] if w == 0 else 1 - info[CORE]
        for j in range(16):
            dest[half, info[16 * w + j]] = pieces[2 * w + j // 8][j % 8]


def bring(pieces, raw, sems, start):
    cols = pl.ds(start, raw.shape[-1])
    return [
        pltpu.make_async_copy(piece.at[:, :, cols], raw.at[i], sems.at[i])
        for i, piece in enumerate(pieces)
    ]


def centre(values):
    centred = values - jnp.mean(values, axis=-1, keepdims=True)
    inverse = lax.rsqrt(jnp.mean(centred * centred, axis=-1, keepdims=True) + EPS)
    return centred * inverse, inverse


def layer_back(grad, normed, inverse):
    return inverse * (
        grad
        - jnp.mean(grad, axis=-1, keepdims=True)
        - normed * jnp.mean(grad * normed, axis=-1, keepdims=True)
    )


def stacked(core, mine, others):
    pair = (mine, others) if core == 0 else (others, mine)
    return jnp.concatenate([part.astype(F32) for part in pair]).astype(BF16)


def by_core(info, lay):
    for core in (0, 1):
        pl.when(info[CORE] == core)(partial(lay, core))


def first_piece_kernel(info, qkv, qkv_o, small, out):
    third = qkv.shape[1] // 6

    def lay(core):
        for i in range(3):
            cols = slice((2 * i + core) * third, (2 * i + core + 1) * third)
            out[0, :, i * third : (i + 1) * third] = stacked(core, qkv[:, cols], qkv_o[:, cols])
        out[0, :, 3 * third :] = stacked(core, small[...], jnp.zeros_like(small))

    by_core(info, lay)


def first_piece(chain, info, qkv, qkv_o, small):
    rows, cols = qkv.shape
    vmem = pl.BlockSpec(memory_space=pltpu.VMEM)
    return chain.call(
        first_piece_kernel,
        out_shape=shape((1, 2 * rows, cols // 2 + small.shape[1]), BF16),
        in_specs=[SMEM] + [vmem] * 3,
        out_specs=vmem,
        compiler_params=params(8),
        name="first_piece",
        cost_estimate=cost(0),
    )(info, qkv, qkv_o, small)


def up_piece_kernel(info, up, up_o, proj, proj_o, out):
    wide, third = up.shape[1] // 2, proj.shape[1] // 2

    def lay(core):
        for whole, other, at, width in ((up, up_o, 0, wide), (proj, proj_o, wide, third)):
            cols = slice(core * width, (core + 1) * width)
            out[0, :, at : at + width] = stacked(core, whole[:, cols], other[:, cols])

    by_core(info, lay)


def up_piece(chain, info, up, up_o, proj, proj_o):
    rows = up.shape[0]
    vmem = pl.BlockSpec(memory_space=pltpu.VMEM)
    return chain.call(
        up_piece_kernel,
        out_shape=shape((1, 2 * rows, (up.shape[1] + proj.shape[1]) // 2), BF16),
        in_specs=[SMEM] + [vmem] * 4,
        out_specs=vmem,
        compiler_params=params(8),
        name="up_piece",
        cost_estimate=cost(0),
    )(info, up, up_o, proj, proj_o)


def gather_kernel(n_in, n_held, *refs):
    out, at = refs[n_in + n_held], 0
    for part in refs[:n_in]:
        out[at : at + part.shape[0]] = part[...]
        at += part.shape[0]
    for i in range(n_held):
        refs[n_in + n_held + 1 + i][...] = refs[n_in + i][...]


def gather(chain, parts, held=(), micros=0):
    vmem = pl.BlockSpec(memory_space=pltpu.VMEM)
    _, rows, cols = parts[0].shape
    count = sum(part.shape[0] for part in parts)
    n, n_held = len(parts), len(held)
    return chain.call(
        partial(gather_kernel, n, n_held),
        out_shape=(shape((count, rows, cols), BF16),) + tuple(shape(h.shape, h.dtype) for h in held),
        in_specs=[vmem] * (n + n_held),
        out_specs=(vmem,) * (1 + n_held),
        compiler_params=params(16),
        name="gather",
        cost_estimate=cost(micros),
    )(*parts, *held)


def gate_kernel(array, out):
    pass


def gate(chain, array, micros):
    return chain.call(
        gate_kernel,
        out_shape=shape(array.shape, array.dtype),
        in_specs=[ANY],
        out_specs=ANY,
        aliases={0: 0},
        compiler_params=params(4),
        name="gate",
        cost_estimate=cost(micros),
    )(array)


def near_z(piece, steps):
    return [send(piece, along_z(s)) for s in steps]


def enter_kernel(
    info,
    tokens,
    upstream,
    down,
    low,
    high,
    low_o,
    high_o,
    kept,
    vecs,
    bias,
    first,
    flipped,
    joint,
    grad_y,
    piece_down,
    weights,
    sem,
):
    feat = tokens.shape[1]
    third = feat // 2
    piece_down[0] = down[...]
    place = lax.broadcasted_iota(jnp.int32, upstream.shape, 0)
    grad_y[...] = jnp.where(place < info[LENGTH], upstream[...].astype(F32), 0.0).astype(BF16)
    settle(info, (low, high, low_o, high_o), weights)
    normed, _ = centre(tokens[...].astype(F32))
    out = pltpu.make_async_copy(weights, kept, sem)
    out.start()
    split = 3 * third
    small = weights[0, :, :, split:] + weights[1, :, :, split:]
    small = small.reshape(feat, 128).astype(F32)
    each = bias.shape[1] // 32
    for device in range(32):
        row = device * feat // 32
        bias[:, device * each : (device + 1) * each] = small[row : row + 1, 128 - each :]
    small = small.T
    vecs[...] = small[:8]
    low_first = (normed * small[0:1] + small[2:3]).astype(BF16)
    first[...] = low_first
    flipped[...] = low_first.T.reshape(flipped.shape)
    for h in (0, 1):
        cols = slice(h * third, (h + 1) * third)
        bias = jnp.concatenate(
            [small[3:4, cols], jnp.zeros((1, third), F32), small[4:5, cols]], axis=1
        )
        w = weights[h, :, :, :split].reshape(feat, split)
        joint[h] = (dot(low_first, w) + bias).astype(BF16)
    out.wait()


def enter(chain, info, tokens, upstream, down, hidden, pieces):
    rows, feat = tokens.shape
    width = pieces[0].shape[-1]
    vmem = pl.BlockSpec(memory_space=pltpu.VMEM)
    sets = (2, 16, feat // 16, width)
    return chain.call(
        enter_kernel,
        out_shape=(
            shape(sets, BF16),
            shape((8, feat), F32),
            shape((1, hidden), F32),
            shape((rows, feat), BF16),
            shape((16, feat // 16, rows), BF16),
            shape((2, rows, 3 * feat // 2), BF16),
            shape((rows, feat), BF16),
            shape((1,) + down.shape, BF16),
        ),
        in_specs=[SMEM] + [vmem] * 7,
        out_specs=(ANY,) + (vmem,) * 7,
        scratch_shapes=[pltpu.VMEM(sets, BF16), pltpu.SemaphoreType.DMA],
        compiler_params=params(20),
        name="enter",
        cost_estimate=cost(8),
    )(info, tokens, upstream, down, *pieces)


def scores_of(info, keys, queries):
    raw = dot_last(keys, queries)
    place = lax.broadcasted_iota(jnp.int32, raw.shape, 0)
    return jnp.where(place < info[LENGTH], raw, NEG)


def mix_kernel(info, q, k, v, mixed, flipped, stats):
    head = mixed.shape[1] // (HEADS // 2)
    count = q.shape[-1] // head
    scale = head**-0.5
    turned = v[0].T

    def start(h):
        cols = slice(h * head, (h + 1) * head)
        return scores_of(info, k[0, :, cols], q[0, :, cols] * scale)

    def finish(h, scores):
        cols = slice(h * head, (h + 1) * head)
        most = jnp.max(scores, axis=0, keepdims=True)
        expd = jnp.exp(scores - most)
        total = jnp.sum(expd, axis=0, keepdims=True)
        attn = (expd * (1.0 / total)).astype(BF16)
        stats[h // 2, h % 2 : h % 2 + 1] = most + jnp.log(total)
        return dot(turned[cols], attn)

    ready = [start(h) for h in range(2)]
    outs = []
    for h in range(count):
        if h + 2 < count:
            ready.append(start(h + 2))
        outs.append(finish(h, ready[h]))
    both = jnp.concatenate(outs)
    flipped[...] = both.astype(BF16)
    mixed[...] = both.T.astype(BF16)


def mix(chain, info, joint):
    _, rows, width = joint.shape
    feat = 2 * width // 3
    wide = feat // 2
    spec = [pl.BlockSpec((1, rows, wide), lambda i, part=part: (i, 0, part)) for part in range(3)]
    pairs_in_half = HEADS // 4
    return chain.call(
        mix_kernel,
        grid=(2,),
        out_shape=(
            shape((rows, feat), BF16),
            shape((feat, rows), BF16),
            shape((HEADS // 2, 8, rows), F32),
        ),
        in_specs=[SMEM] + spec,
        out_specs=(
            pl.BlockSpec((rows, wide), lambda i: (0, i)),
            pl.BlockSpec((wide, rows), lambda i: (i, 0)),
            pl.BlockSpec((pairs_in_half, 8, rows), lambda i: (i, 0, 0)),
        ),
        compiler_params=params(24),
        name="mix",
        cost_estimate=cost(10),
    )(info, joint, joint, joint)


def mix_back_kernel(info, q, k, v, grad, stats, theirs, mine):
    head = theirs.shape[2] // (HEADS // 2)
    count = q.shape[-1] // head
    scale = head**-0.5
    turned = k[0].T

    def start(h):
        cols = slice(h * head, (h + 1) * head)
        queries = q[0, :, cols] * scale
        scores = scores_of(info, k[0, :, cols], queries)
        return cols, queries, scores, dot_last(v[0, :, cols], grad[:, cols])

    def finish(h, cols, queries, scores, grad_prob):
        attn = jnp.exp(scores - stats[h // 2, h % 2 : h % 2 + 1])
        inner = jnp.sum(attn * grad_prob, axis=0, keepdims=True)
        low = (attn * (grad_prob - inner)).astype(BF16)
        return (
            dot(turned[cols], low) * scale,
            dot(low, queries),
            dot(attn.astype(BF16), grad[:, cols]),
        )

    ready = [start(h) for h in range(2)]
    done = []
    for h in range(count):
        if h + 2 < count:
            ready.append(start(h + 2))
        done.append(finish(h, *ready[h]))
    out = [
        jnp.concatenate([d[0] for d in done]).T.astype(BF16),
        jnp.concatenate([d[1] for d in done], axis=1).astype(BF16),
        jnp.concatenate([d[2] for d in done], axis=1).astype(BF16),
    ]

    @pl.when(pl.program_id(0) == 0)
    def _():
        for part in range(3):
            theirs[part] = out[part]

    @pl.when(pl.program_id(0) == 1)
    def _():
        for part in range(3):
            mine[part] = out[part]


def mix_back(chain, info, joint, grad_mixed, stats):
    _, rows, width = joint.shape
    feat = 2 * width // 3
    wide = feat // 2

    def half(i, info):
        return jnp.where(i == 0, 1 - info[CORE], info[CORE])

    spec = [
        pl.BlockSpec((1, rows, wide), lambda i, info, part=part: (half(i, info), 0, part))
        for part in range(3)
    ]
    out = shape((3, rows, feat // 2), BF16)
    return chain.call(
        mix_back_kernel,
        prefetch=1,
        grid=(2,),
        in_specs=spec
        + [
            pl.BlockSpec((rows, wide), lambda i, info: (0, half(i, info))),
            pl.BlockSpec((HEADS // 4, 8, rows), lambda i, info: (half(i, info), 0, 0)),
        ],
        out_specs=(
            pl.BlockSpec((3, rows, wide), lambda i, info: (0, 0, 0)),
            pl.BlockSpec((3, rows, wide), lambda i, info: (0, 0, 0)),
        ),
        out_shape=(out, out),
        compiler_params=params(30),
        name="mix_back",
        cost_estimate=cost(16),
    )(info, joint, joint, joint, grad_mixed, stats)


GELU = (0.254829592, -0.284496736, 1.421413741, -1.453152027, 1.061405429)


def gelu_parts(x):
    bell = jnp.exp2(x * x * (-0.5 / math.log(2)))
    below = 1.0 + (0.3275911 * 0.5**0.5) * jnp.abs(x)
    t = pl.reciprocal(below, approx=True)
    t = t * (2.0 - below * t)
    poly = 0.5 * GELU[4]
    for c in GELU[3::-1]:
        poly = poly * t + 0.5 * c
    tail = poly * t * bell
    phi = jnp.where(x < 0, tail, 1.0 - tail)
    return x * phi, phi + x * (bell * (2 * math.pi) ** -0.5)


def rise_kernel(
    info, tokens, mixed, vecs, low, high, low_o, high_o, weights, after, second, flipped, raw, sems
):
    feat = tokens.shape[1]
    copies = bring((low, high, low_o, high_o), raw, sems, low.shape[2] - raw.shape[-1])
    for copy in copies:
        copy.start()
    start = tokens[...].astype(F32) + vecs[5:6]
    for copy in copies:
        copy.wait()
    settle(info, raw, weights)
    grown = [dot(mixed[...], weights[h].reshape(feat, feat // 2)) for h in (0, 1)]
    total = start + jnp.concatenate(grown, axis=1)
    after[...] = total
    normed, _ = centre(total)
    value = (normed * vecs[1:2] + vecs[6:7]).astype(BF16)
    second[...] = value
    flipped[...] = value.T.reshape(flipped.shape)


def rise(chain, info, tokens, mixed, vecs, pieces):
    rows, feat = tokens.shape
    vmem = pl.BlockSpec(memory_space=pltpu.VMEM)
    block = feat // 16
    return chain.call(
        rise_kernel,
        out_shape=(
            shape((2, 16, block, feat // 2), BF16),
            shape((rows, feat), F32),
            shape((rows, feat), BF16),
            shape((16, block, rows), BF16),
        ),
        in_specs=[SMEM] + [vmem] * 3 + [ANY] * 4,
        out_specs=(vmem,) * 4,
        scratch_shapes=[
            pltpu.VMEM((4, 8, block, feat // 2), BF16),
            pltpu.SemaphoreType.DMA((4,)),
        ],
        compiler_params=params(16),
        name="rise",
        cost_estimate=cost(5),
    )(info, tokens, mixed, vecs, *pieces)


def widen_kernel(
    info,
    second,
    bias,
    low,
    high,
    low_o,
    high_o,
    weights,
    active,
    slope,
    mine,
    theirs,
    raw,
    sems,
):
    step, per = pl.program_id(0), pl.num_programs(0) // 2
    core = info[CORE]
    feat = second.shape[1]
    tile = active.shape[1]
    rows = mine.shape[1]
    count = tile // rows
    copies = bring((low, high, low_o, high_o), raw, sems, 0)

    @pl.when(step == 0)
    def _():
        for copy in copies:
            copy.start()

    for who in (0, 1):

        @pl.when(step == who * per)
        def _():
            for copy in copies[2 * who : 2 * who + 2]:
                copy.wait()
            settle(info, raw, weights, (who,))

    half = jnp.where(step < per, core, 1 - core)
    cols = pl.ds(pl.multiple_of(lax.rem(step, per) * tile, tile), tile)
    w = weights[half, :, :, cols].reshape(feat, tile)
    hidden = dot(second[...], w) + bias[...]
    value, grad = gelu_parts(hidden)
    value = value.astype(BF16)
    active[...] = value
    slope[...] = grad.astype(BF16)
    flipped = value.T.reshape(count, rows, -1)
    first_chip = (half * per + lax.rem(step, per)) * (count // 2)
    for c in (0, 1):

        @pl.when(core == c)
        def _():
            for i in range(count):
                chip = first_chip + i // 2
                if i % 2 == c:
                    mine[info[PLACE + chip]] = flipped[i]
                else:
                    theirs[info[PLACE_O + chip]] = flipped[i]


def widen(chain, info, second, bias, pieces):
    rows, feat = second.shape
    wide = pieces[0].shape[-1] - feat // 2
    hidden = 2 * wide
    tile, block = 768, hidden // 32
    per = wide // tile
    turned = shape((16, block, rows), BF16)
    sets = (2, 16, feat // 16, wide)

    def at(n, info):
        return jnp.where(n < per, info[CORE], 1 - info[CORE]) * per + n % per

    def whole(dims):
        return pl.BlockSpec(dims, lambda n, info: (0,) * len(dims))

    strip = pl.BlockSpec((rows, tile), lambda n, info: (0, at(n, info)))
    return chain.call(
        widen_kernel,
        prefetch=1,
        grid=(2 * per,),
        out_shape=(
            shape(sets, BF16),
            shape((rows, hidden), BF16),
            shape((rows, hidden), BF16),
            turned,
            turned,
        ),
        in_specs=[
            whole((rows, feat)),
            pl.BlockSpec((1, tile), lambda n, info: (0, at(n, info))),
        ]
        + [ANY] * 4,
        out_specs=(whole(sets), strip, strip, whole(turned.shape), whole(turned.shape)),
        scratch_shapes=[
            pltpu.VMEM((4, 8, feat // 16, wide), BF16),
            pltpu.SemaphoreType.DMA((4,)),
        ],
        compiler_params=params(30),
        name="widen",
        cost_estimate=cost(18),
    )(info, second, bias, *pieces)


def leave_kernel(after, active, down, vecs, output, total):
    step = pl.program_id(0)
    part = dot(active[...], down[...])

    @pl.when(step == 0)
    def _():
        total[...] = after[...] + vecs[7:8] + part

    @pl.when(step > 0)
    def _():
        total[...] += part

    @pl.when(step == pl.num_programs(0) - 1)
    def _():
        output[...] = total[...].astype(BF16)


def leave(chain, after, active, down, vecs):
    rows, feat = after.shape
    hidden = active.shape[1]
    tile = 768
    return chain.call(
        leave_kernel,
        grid=(hidden // tile,),
        out_shape=shape((rows, feat), BF16),
        in_specs=[
            full((rows, feat)),
            pl.BlockSpec((rows, tile), lambda n: (0, n)),
            pl.BlockSpec((tile, feat), lambda n: (n, 0)),
            full((8, feat)),
        ],
        out_specs=full((rows, feat)),
        scratch_shapes=[pltpu.VMEM((rows, feat), F32)],
        compiler_params=params(16),
        name="leave",
        cost_estimate=cost(7),
    )(after, active, down, vecs)


def fall_kernel(
    info,
    grad_y,
    slope,
    up,
    after,
    vecs,
    proj,
    low,
    high,
    low_o,
    high_o,
    kept,
    theirs,
    mine,
    bias_sum,
    grad_after,
    attn_theirs,
    attn_mine,
    grad_mixed,
    sums,
    weights,
    grad_second,
    normed,
    inverse,
    raw,
    sems,
    sem,
):
    step, steps = pl.program_id(0), pl.num_programs(0)
    core = info[CORE]
    feat = grad_y.shape[1]
    tile = slope.shape[1]
    per = steps // 2
    keeping = pltpu.make_async_copy(weights, kept, sem)

    @pl.when(step == 0)
    def _():
        copies = bring((low, high, low_o, high_o), raw, sems, 0)
        for copy in copies:
            copy.start()
        normed[...], inverse[...] = centre(after[...])
        grad_second[...] = jnp.zeros_like(grad_second)
        for copy in copies:
            copy.wait()
        for who in (0, 1):
            c = core if who == 0 else 1 - core
            for j in range(16):
                weights[info[16 * who + j], c] = raw[2 * who + j // 8, j % 8]
        keeping.start()

    half = jnp.where(step < per, 1 - core, core)
    at = half * per + lax.rem(step, per)
    count = tile * weights.shape[0] // (steps * tile)
    down = weights[pl.ds(count * at, count)].reshape(tile, feat)
    grad = (dot_last(grad_y[...], down) * slope[...].astype(F32)).astype(BF16)
    bias_sum[...] = jnp.sum(grad.astype(F32), axis=0, keepdims=True)
    grad_second[...] += dot_last(grad, up[0])

    @pl.when(step < per)
    def _():
        theirs[...] = grad

    @pl.when(step >= per)
    def _():
        mine[...] = grad

    @pl.when(step == steps - 1)
    def _():
        second = grad_second[...]
        live = grad_y[...].astype(F32)
        sums[0:1] = jnp.sum(second * normed[...], axis=0, keepdims=True)
        sums[1:2] = jnp.sum(second, axis=0, keepdims=True)
        total = live + layer_back(second * vecs[1:2], normed[...], inverse[...])
        grad_after[...] = total
        attn = total.astype(BF16)
        sums[2:3] = jnp.sum(attn.astype(F32), axis=0, keepdims=True)
        sums[3:4] = jnp.sum(live, axis=0, keepdims=True)
        sums[4:8] = jnp.zeros_like(sums[4:8])
        left, right = attn[:, : feat // 2], attn[:, feat // 2 :]
        attn_mine[...] = jnp.where(core == 0, left, right)
        attn_theirs[...] = jnp.where(core == 0, right, left)
        grad_mixed[...] = (dot_last(left, proj[0]) + dot_last(right, proj[1])).astype(BF16)
        keeping.wait()


def fall(chain, info, grad_y, slope, up_set, after, vecs, proj_set, pieces):
    rows, feat = grad_y.shape
    hidden = slope.shape[1]
    tile = 768
    steps = hidden // tile
    per = steps // 2

    def at(n, info):
        return jnp.where(n < per, 1 - info[CORE], info[CORE]) * per + n % per

    def whole(dims):
        return pl.BlockSpec(dims, lambda n, info: (0,) * len(dims))

    return chain.call(
        fall_kernel,
        prefetch=1,
        grid=(steps,),
        in_specs=[
            whole((rows, feat)),
            pl.BlockSpec((rows, tile), lambda n, info: (0, at(n, info))),
            pl.BlockSpec(
                (1, feat, tile), lambda n, info: (at(n, info) // per, 0, n % per)
            ),
            whole((rows, feat)),
            whole((8, feat)),
            whole((2, feat, feat // 2)),
        ]
        + [ANY] * 4,
        out_specs=(
            ANY,
            pl.BlockSpec((rows, tile), lambda n, info: (0, jnp.minimum(n, per - 1))),
            pl.BlockSpec((rows, tile), lambda n, info: (0, jnp.maximum(n - per, 0))),
            pl.BlockSpec((1, tile), lambda n, info: (0, at(n, info))),
            whole((rows, feat)),
            whole((rows, feat // 2)),
            whole((rows, feat // 2)),
            whole((rows, feat)),
            whole((8, feat)),
        ),
        scratch_shapes=[
            pltpu.VMEM((16, 2, hidden // 32, feat), BF16),
            pltpu.VMEM((rows, feat), F32),
            pltpu.VMEM((rows, feat), F32),
            pltpu.VMEM((rows, 1), F32),
            pltpu.VMEM((4,) + pieces[0].shape, BF16),
            pltpu.SemaphoreType.DMA((4,)),
            pltpu.SemaphoreType.DMA,
        ],
        out_shape=(
            shape((16, 2, hidden // 32, feat), BF16),
            shape((rows, hidden // 2), BF16),
            shape((rows, hidden // 2), BF16),
            shape((1, hidden), F32),
            shape((rows, feat), F32),
            shape((rows, feat // 2), BF16),
            shape((rows, feat // 2), BF16),
            shape((rows, feat), BF16),
            shape((8, feat), F32),
        ),
        compiler_params=params(32),
        name="fall",
        cost_estimate=cost(18),
    )(info, grad_y, slope, up_set, after, vecs, proj_set, *pieces)


def exit_kernel(
    info,
    tokens,
    mine,
    theirs,
    weights,
    grad_after,
    vecs,
    sums_a,
    bias,
    grad_tokens,
    keep,
    away,
    grad_first,
    joint,
    sums,
    extra,
):
    step = pl.program_id(0)
    core = info[CORE]
    third = mine.shape[2]
    half = jnp.where(step == 0, core, 1 - core)
    spot = pl.ds(pl.multiple_of(half * third, third), third)

    def parts(source):
        for part in range(3):
            joint[:, part * third : (part + 1) * third] = source[part]
        sums[3:4, spot] = jnp.sum(source[0].astype(F32), axis=0, keepdims=True)
        sums[4:5, spot] = jnp.sum(source[2].astype(F32), axis=0, keepdims=True)
        return dot_last(joint[...], weights[0])

    @pl.when(step == 0)
    def _():
        grad_first[...] = parts(mine)

    @pl.when(step == 1)
    def _():
        grad = grad_first[...] + parts(theirs)
        normed, inverse = centre(tokens[...].astype(F32))
        sums[0:1] = jnp.sum(grad * normed, axis=0, keepdims=True)
        sums[1:2] = sums_a[0:1]
        sums[2:3] = jnp.sum(grad, axis=0, keepdims=True)
        sums[5:6] = sums_a[2:3]
        sums[6:7] = sums_a[1:2]
        sums[7:8] = sums_a[3:4]
        sums[8:] = jnp.zeros_like(sums[8:])
        back = layer_back(grad * vecs[0:1], normed, inverse)
        grad_tokens[...] = (grad_after[...] + back).astype(BF16)
        flipped = sums[...].T
        block, each = extra.shape[1], bias.shape[1] // 32
        for chip in range(16):
            place = info[PLACE + chip]
            extra[place] = flipped[chip * block : (chip + 1) * block]
            for c in (0, 1):
                at = (2 * chip + c) * each
                row = c * block // 2
                extra[place, row : row + 1, 128 - each :] = bias[:, at : at + each]
        keep[...] = extra[:8]
        away[...] = extra[8:].astype(BF16)


def exit_back(chain, info, tokens, mine, theirs, first_set, grad_after, vecs, sums_a, bias):
    rows, feat = tokens.shape
    third = feat // 2
    block = feat // 16

    def whole(dims):
        return pl.BlockSpec(dims, lambda n, info: (0,) * len(dims))

    return chain.call(
        exit_kernel,
        prefetch=1,
        grid=(2,),
        in_specs=[
            whole((rows, feat)),
            whole((3, rows, third)),
            whole((3, rows, third)),
            pl.BlockSpec(
                (1, feat, 3 * third),
                lambda n, info: (jnp.where(n == 0, info[CORE], 1 - info[CORE]), 0, 0),
            ),
            whole((rows, feat)),
            whole((8, feat)),
            whole((8, feat)),
            whole(bias.shape),
        ],
        out_specs=(whole((rows, feat)), whole((8, block, 128)), whole((8, block, 128))),
        scratch_shapes=[
            pltpu.VMEM((rows, feat), F32),
            pltpu.VMEM((rows, 3 * third), BF16),
            pltpu.VMEM((128, feat), F32),
            pltpu.VMEM((16, block, 128), F32),
        ],
        out_shape=(
            shape((rows, feat), BF16),
            shape((8, block, 128), F32),
            shape((8, block, 128), BF16),
        ),
        compiler_params=params(18),
        name="exit_back",
        cost_estimate=cost(8),
    )(info, tokens, mine, theirs, first_set, grad_after, vecs, sums_a, bias)


def line_up(info, left, left_o, turned):
    rows = left.shape[2]
    for chip in range(16):
        place = info[PLACE + chip]
        turned[place, :, :rows] = left[chip]
        turned[place, :, rows:] = left_o[chip]


def outer_tile(turned, right, right_o):
    rows = right.shape[0]
    both = turned[...].reshape(-1, turned.shape[2])
    total = dot(both[:, :rows], right) + dot(both[:, rows:], right_o)
    return total.reshape(16, -1, total.shape[1])


def outer_up_kernel(
    info, left, left_o, right, right_o, low, low_o, attn, attn_o, keep, away, turned
):
    step, last = pl.program_id(0), pl.num_programs(0) - 1

    @pl.when(step == 0)
    def _():
        line_up(info, left, left_o, turned)

    @pl.when(step < last)
    def _():
        total = outer_tile(turned, right[...], right_o[...])
        keep[...] = total[:8]
        away[...] = total[8:].astype(BF16)

    @pl.when(step == last)
    def _():
        line_up(info, low, low_o, turned)
        total = outer_tile(turned, attn[...], attn_o[...])
        keep[:, :, : attn.shape[1]] = total[:8]
        away[:, :, : attn.shape[1]] = total[8:].astype(BF16)


def outer_up(chain, info, left, left_o, right, right_o, low, low_o, attn, attn_o):
    _, block, rows = left.shape
    tile = 2 * attn.shape[1]
    n = right.shape[1] // tile
    cols = right.shape[1] + attn.shape[1]
    strip = pl.BlockSpec((rows, tile), lambda i: (0, jnp.minimum(i, n - 1)))
    out = pl.BlockSpec((8, block, tile), lambda i: (0, 0, i))
    return chain.call(
        outer_up_kernel,
        grid=(n + 1,),
        out_shape=(shape((8, block, cols), F32), shape((8, block, cols), BF16)),
        in_specs=[SMEM]
        + [full(left.shape)] * 2
        + [strip] * 2
        + [full(left.shape)] * 2
        + [full(attn.shape)] * 2,
        out_specs=(out, out),
        scratch_shapes=[pltpu.VMEM((16, block, 2 * rows), BF16)],
        compiler_params=params(20),
        name="outer_up",
        cost_estimate=cost(8),
    )(info, left, left_o, right, right_o, low, low_o, attn, attn_o)


def outer_qkv_kernel(info, left, left_o, right, right_o, keep, away, turned):
    tile = right.shape[2]
    line_up(info, left, left_o, turned)
    for part in range(3):
        cols = slice(part * tile, (part + 1) * tile)
        total = outer_tile(turned, right[part], right_o[part])
        keep[:, :, cols] = total[:8]
        away[:, :, cols] = total[8:].astype(BF16)


def outer_qkv(chain, info, left, left_o, right, right_o):
    _, block, rows = left.shape
    cols = 3 * right.shape[2]
    vmem = pl.BlockSpec(memory_space=pltpu.VMEM)
    return chain.call(
        outer_qkv_kernel,
        out_shape=(shape((8, block, cols), F32), shape((8, block, cols), BF16)),
        in_specs=[SMEM] + [vmem] * 4,
        out_specs=(vmem, vmem),
        scratch_shapes=[pltpu.VMEM((16, block, 2 * rows), BF16)],
        compiler_params=params(20),
        name="outer_qkv",
        cost_estimate=cost(8),
    )(info, left, left_o, right, right_o)


def outer_down_kernel(left, left_o, right, right_o, keep, away):
    def flat(blocks):
        return blocks[...].reshape(-1, blocks.shape[-1])

    total = dot(flat(left), right[...]) + dot(flat(left_o), right_o[...])
    total = total.reshape(keep.shape)

    @pl.when(pl.program_id(0) >= 2)
    def _():
        keep[...] = total

    @pl.when(pl.program_id(0) < 2)
    def _():
        away[...] = total.astype(BF16)


def outer_down(chain, left, left_o, right, right_o):
    _, block, rows = left.shape
    feat = right.shape[1]
    strip = pl.BlockSpec((4, block, rows), lambda j: ((j + 2) % 4, 0, 0))
    return chain.call(
        outer_down_kernel,
        grid=(4,),
        out_shape=(shape((8, block, feat), F32), shape((8, block, feat), BF16)),
        in_specs=[strip, strip, full((rows, feat)), full((rows, feat))],
        out_specs=(
            pl.BlockSpec((4, block, feat), lambda j: (jnp.maximum(j - 2, 0), 0, 0)),
            pl.BlockSpec((4, block, feat), lambda j: (jnp.minimum(j, 1), 0, 0)),
        ),
        compiler_params=params(16),
        name="outer_down",
        cost_estimate=cost(8),
    )(left, left_o, right, right_o)


def add_first_kernel(keep, got, kept, away):
    kept[...] = keep[:4] + got[:4].astype(F32)
    away[...] = (keep[4:] + got[4:].astype(F32)).astype(BF16)


def shift_first(chain, keep, away, micros=0):
    _, rows, cols = keep.shape
    vmem = pl.BlockSpec(memory_space=pltpu.VMEM)
    return chain.call(
        add_first_kernel,
        out_shape=(shape((4, rows, cols), F32), shape((4, rows, cols), BF16)),
        in_specs=[vmem, vmem],
        out_specs=(vmem, vmem),
        compiler_params=params(12),
        name="shift_first",
        cost_estimate=cost(micros),
    )(keep, send(away, second_way))


def add_both_kernel(keep, got, few_keep, few_got, kept, away):
    split = keep.shape[2]
    kept[:, :, :split] = keep[:4] + got[:4].astype(F32)
    kept[:, :, split:] = few_keep[:4] + few_got[:4].astype(F32)
    away[:, :, :split] = (keep[4:] + got[4:].astype(F32)).astype(BF16)
    away[:, :, split:] = (few_keep[4:] + few_got[4:].astype(F32)).astype(BF16)


def shift_both(chain, keep, away, few_keep, few_away):
    _, rows, cols = keep.shape
    cols += few_keep.shape[2]
    vmem = pl.BlockSpec(memory_space=pltpu.VMEM)
    return chain.call(
        add_both_kernel,
        out_shape=(shape((4, rows, cols), F32), shape((4, rows, cols), BF16)),
        in_specs=[vmem] * 4,
        out_specs=(vmem, vmem),
        compiler_params=params(12),
        name="shift_both",
        cost_estimate=cost(0),
    )(keep, send(away, second_way), few_keep, send(few_away, second_way))


def add_second_kernel(keep, got, base, one, two, three):
    base[...] = keep[0] + got[0].astype(F32)
    for s, out in ((1, one), (2, two), (3, three)):
        out[...] = (keep[s] + got[s].astype(F32)).astype(BF16)


def shift_second(chain, keep, away):
    _, rows, cols = keep.shape
    vmem = pl.BlockSpec(memory_space=pltpu.VMEM)
    base, *lows = chain.call(
        add_second_kernel,
        out_shape=(shape((rows, cols), F32),) + (shape((rows, cols), BF16),) * 3,
        in_specs=[vmem, vmem],
        out_specs=(vmem,) * 4,
        compiler_params=params(8),
        name="shift_second",
        cost_estimate=cost(0),
    )(keep, send(away, first_way))
    return base, [send(low, along_z(s)) for low, s in zip(lows, (1, 2, 3))]


def total_of(base, parts):
    return base[...] + parts[0][...].astype(F32) + (
        parts[1][...].astype(F32) + parts[2][...].astype(F32)
    )


def add_down_kernel(base, one, two, three, out):
    out[...] = total_of(base, (one, two, three))


def home_down(chain, base, parts):
    vmem = pl.BlockSpec(memory_space=pltpu.VMEM)
    return chain.call(
        add_down_kernel,
        out_shape=shape(base.shape, F32),
        in_specs=[vmem] * 4,
        out_specs=vmem,
        compiler_params=params(8),
        name="home_down",
        cost_estimate=cost(0),
    )(base, *parts)


def add_last_kernel(info, base, one, two, three, mine, theirs, total):
    core = info[CORE]
    half = mine.shape[0]
    total[...] = total_of(base, (one, two, three))
    mine[...] = total[pl.ds(pl.multiple_of(core * half, half), half)]
    theirs[...] = total[pl.ds(pl.multiple_of((1 - core) * half, half), half)]


def home(chain, info, base, parts):
    rows, cols = base.shape
    vmem = pl.BlockSpec(memory_space=pltpu.VMEM)
    out = shape((rows // 2, cols), F32)
    mine, theirs = chain.call(
        add_last_kernel,
        out_shape=(out, out),
        in_specs=[SMEM] + [vmem] * 4,
        out_specs=(vmem, vmem),
        scratch_shapes=[pltpu.VMEM((rows, cols), F32)],
        compiler_params=params(8),
        name="home",
        cost_estimate=cost(0),
    )(info, base, *parts)
    return mine, swap(theirs)


def finish_kernel(info, qkv, qkv_o, up, up_o, out_qkv, out_proj, out_up, gains, shifts, bias):
    rows, third = out_proj.shape[0], out_proj.shape[1] // 2
    wide = out_up.shape[1] // 2
    small = qkv[:, 3 * third :] + qkv_o[:, 3 * third :]
    flipped = jnp.concatenate([small, jnp.zeros((128 - rows, 128), F32)]).T
    gains[...] = flipped[0:2, :rows]
    shifts[...] = flipped[2:8, :rows]
    bias[...] = small[0:1, 128 - bias.shape[1] :]

    def lay(core):
        for half, (a, b) in ((core, (qkv, up)), (1 - core, (qkv_o, up_o))):
            for part in range(3):
                spot = part * 2 * third + half * third
                out_qkv[:, spot : spot + third] = a[:, part * third : (part + 1) * third]
            out_proj[:, half * third : (half + 1) * third] = b[:, wide:]
            out_up[:, half * wide : (half + 1) * wide] = b[:, :wide]

    @pl.when(info[CORE] == 0)
    def _():
        lay(0)

    @pl.when(info[CORE] == 1)
    def _():
        lay(1)


def finish(chain, info, qkv, qkv_o, up, up_o):
    rows = qkv.shape[0]
    third = (qkv.shape[1] - 128) // 3
    vmem = pl.BlockSpec(memory_space=pltpu.VMEM)
    return chain.call(
        finish_kernel,
        out_shape=(
            shape((rows, 6 * third), F32),
            shape((rows, 2 * third), F32),
            shape((rows, 2 * (up.shape[1] - third)), F32),
            shape((2, rows), F32),
            shape((6, rows), F32),
            shape((1, 4 * rows), F32),
        ),
        in_specs=[SMEM] + [vmem] * 4,
        out_specs=(vmem,) * 6,
        compiler_params=params(8),
        name="finish",
        cost_estimate=cost(0),
    )(info, qkv, qkv_o, up, up_o)


def local(
    tokens,
    upstream,
    lengths,
    qkv_weight,
    proj_weight,
    up_weight,
    down_weight,
    gains,
    shifts,
    up_bias,
):
    tok_rows, feat = tokens.shape
    rows = qkv_weight.shape[0]
    hidden = up_weight.shape[1]
    third, wide = feat // 2, hidden // 2
    chip, core = lax.axis_index("dp"), lax.axis_index("fsdp")
    info = facts(chip, core, lengths[0])

    chain = Chain()

    small = jnp.concatenate([gains, shifts], axis=1)
    small = jnp.pad(small, ((0, 0), (0, 128 - small.shape[1])))
    small = small + jnp.pad(up_bias[None], ((0, rows - 1), (128 - up_bias.shape[0], 0)))
    piece = first_piece(chain, info, qkv_weight, swap(qkv_weight), small)
    piece_up = up_piece(chain, info, up_weight, swap(up_weight), proj_weight, swap(proj_weight))
    zs, piece_up = gather(chain, [piece] + near_z(piece, (1, 2, 3)), (piece_up,))
    up_z = near_z(piece_up, (1, 2, 3))
    (low,) = gather(chain, [zs, send(zs, first_way)])
    high = send(low, second_way)
    (zs_up,) = gather(chain, [piece_up] + up_z, (), 5)
    high = gate(chain, high, 0)
    pieces = (low, high, swap(low), swap(high))
    first_set, vecs, bias, first, first_t, joint, grad_y, down = enter(
        chain, info, tokens, upstream, down_weight, hidden, pieces
    )
    grad_y_o, first_o = swap(grad_y), swap(first_t)
    first_set = first_set.reshape(2, feat, 3 * third + 128)
    (low,) = gather(chain, [zs_up, send(zs_up, first_way)])
    down_z = near_z(down, (1, 2, 3))
    mixed, mixed_t, stats = mix(chain, info, joint)
    mixed_t = mixed_t.reshape(first_t.shape)
    mixed_o = swap(mixed_t)
    high = send(low, second_way)
    pieces = (low, high, swap(low), swap(high))
    (zs_down,) = gather(chain, [down] + down_z, (), 5)
    proj_set, after, second, second_t = rise(chain, info, tokens, mixed, vecs, pieces)
    second_o = swap(second_t)
    (low,) = gather(chain, [zs_down, send(zs_down, first_way)])
    up_set, active, slope, turned, turned_t = widen(chain, info, second, bias, pieces)
    up_set = up_set.reshape(2, feat, wide)
    proj_set = proj_set.reshape(2, feat, third)
    high = gate(chain, send(low, second_way), 5)
    pieces = (low, high, swap(low), swap(high))
    down = outer_down(chain, turned, swap(turned_t), grad_y, grad_y_o)
    down_set, hid_theirs, hid_mine, bias_sum, grad_after, at_theirs, at_mine, grad_mixed, sums_a = (
        fall(chain, info, grad_y, slope, up_set, after, vecs, proj_set, pieces)
    )
    hid_o, at_o = swap(hid_theirs), swap(at_theirs)
    down = shift_first(chain, *down, 5)
    up = outer_up(chain, info, second_t, second_o, hid_mine, hid_o, mixed_t, mixed_o, at_mine, at_o)
    down = shift_second(chain, *down)
    theirs, mine = mix_back(chain, info, joint, grad_mixed, stats)
    theirs_o = swap(theirs)
    own_down = home_down(chain, *down)
    up = shift_first(chain, *up, 5)
    chain.near(up[1])
    qkv = outer_qkv(chain, info, first_t, first_o, mine, theirs_o)
    grad_tokens, few_keep, few_away = exit_back(
        chain, info, tokens, mine, theirs, first_set, grad_after, vecs, sums_a, bias_sum
    )
    up = shift_second(chain, *up)
    qkv = shift_both(chain, *qkv, few_keep, few_away)
    output = leave(chain, after, active, down_set.reshape(hidden, feat), vecs)
    qkv = shift_second(chain, *qkv)
    own_up = home(chain, info, *up)
    own_qkv = home(chain, info, *qkv)
    out_qkv, out_proj, out_up, out_gains, out_shifts, out_bias = finish(
        chain, info, *own_qkv, *own_up
    )
    return (
        output,
        grad_tokens,
        out_qkv,
        out_proj,
        out_up,
        own_down,
        out_gains.T,
        out_shifts.T,
        out_bias.reshape(-1),
    )


def solution(mesh):
    placed = (
        P(("dp", "fsdp"), None),
        P(("dp", "fsdp"), None),
        P(("dp", "fsdp")),
        P(("dp", "fsdp"), None),
        P(("dp", "fsdp"), None),
        P(("dp", "fsdp"), None),
        P(("dp", "fsdp"), None),
        P(("dp", "fsdp"), None),
        P(("dp", "fsdp"), None),
        P(("dp", "fsdp")),
    )
    sizes = (mesh.shape["dp"], mesh.shape["fsdp"])
    return jax.shard_map(
        local if sizes == (16, 2) else plain,
        mesh=mesh,
        in_specs=placed,
        out_specs=(
            P(("dp", "fsdp"), None),
            P(("dp", "fsdp"), None),
            P(("dp", "fsdp"), None),
            P(("dp", "fsdp"), None),
            P(("dp", "fsdp"), None),
            P(("dp", "fsdp"), None),
            P(("dp", "fsdp"), None),
            P(("dp", "fsdp"), None),
            P(("dp", "fsdp")),
        ),
        check_vma=False,
    )
```

```python
import math
from functools import partial

import jax
import jax.numpy as jnp
from jax import lax
from jax.experimental import pallas as pl
from jax.experimental.pallas import tpu as pltpu
from jax.sharding import PartitionSpec as P

HEADS = 12
EPS = 1e-06
NEG = -1e30
AXES = ("dp", "fsdp")
F32 = jnp.float32
BF16 = jnp.bfloat16
VMEM_LIMIT = 32 * 1024 * 1024


def collect(qkv_weight, proj_weight, up_weight, down_weight, gains, shifts, up_bias):
    gathered = (
        lax.all_gather(qkv_weight, ("dp", "fsdp"), axis=0, tiled=True),
        lax.all_gather(proj_weight, ("dp", "fsdp"), axis=0, tiled=True),
        lax.all_gather(up_weight, ("dp", "fsdp"), axis=0, tiled=True),
        lax.all_gather(down_weight, ("dp", "fsdp"), axis=0, tiled=True),
        lax.all_gather(gains, ("dp", "fsdp"), axis=0, tiled=True),
        lax.all_gather(shifts, ("dp", "fsdp"), axis=0, tiled=True),
        lax.all_gather(up_bias, ("dp", "fsdp"), axis=0, tiled=True),
    )
    return gathered


def give_back(grad_qkv, grad_proj, grad_up, grad_down, grad_gains, grad_shifts, grad_bias_up):
    owned = (
        lax.psum_scatter(grad_qkv, ("dp", "fsdp"), scatter_dimension=0, tiled=True),
        lax.psum_scatter(grad_proj, ("dp", "fsdp"), scatter_dimension=0, tiled=True),
        lax.psum_scatter(grad_up, ("dp", "fsdp"), scatter_dimension=0, tiled=True),
        lax.psum_scatter(grad_down, ("dp", "fsdp"), scatter_dimension=0, tiled=True),
        lax.psum_scatter(grad_gains, ("dp", "fsdp"), scatter_dimension=0, tiled=True),
        lax.psum_scatter(grad_shifts, ("dp", "fsdp"), scatter_dimension=0, tiled=True),
        lax.psum_scatter(grad_bias_up, ("dp", "fsdp"), scatter_dimension=0, tiled=True),
    )
    return owned


def normalize(values):
    centred = values - jnp.mean(values, axis=-1, keepdims=True)
    inverse = lax.rsqrt(jnp.mean(centred * centred, axis=-1, keepdims=True) + EPS)
    return (centred * inverse, inverse)


def norm_back(grad_norm, normed, inverse):
    return inverse * (
        grad_norm
        - jnp.mean(grad_norm, axis=-1, keepdims=True)
        - normed * jnp.mean(grad_norm * normed, axis=-1, keepdims=True)
    )


def block_scores(query_blk, key_rows, live_mask, scaling):
    raw = (
        jnp.einsum("qhd,khd->hqk", query_blk, key_rows, preferred_element_type=jnp.float32)
        * scaling
    )
    return jnp.where(live_mask[None, None, :], raw, NEG)


def plain(
    tokens,
    upstream,
    lengths,
    qkv_weight,
    proj_weight,
    up_weight,
    down_weight,
    gains,
    shifts,
    up_bias,
):
    tok_rows, feat_width = tokens.shape
    n_heads = HEADS
    head_size = feat_width // n_heads
    scaling = head_size ** (-0.5)
    block_rows = min(512, tok_rows)
    group_heads = 4
    head_starts = list(range(0, n_heads, group_heads))
    gathered = collect(qkv_weight, proj_weight, up_weight, down_weight, gains, shifts, up_bias)
    qkv_full, proj_full, up_full, down_full, gain_full, shift_full, bias_full = gathered
    gain_f = gain_full.astype(jnp.float32)
    shift_f = shift_full.astype(jnp.float32)
    bias_f = bias_full.astype(jnp.float32)
    live_mask = lax.iota(jnp.int32, tok_rows) < lengths[0]
    source = tokens.astype(jnp.float32)
    norm_one, inv_one = normalize(source)
    first = (norm_one * gain_f[:, 0] + shift_f[:, 0]).astype(jnp.bfloat16)
    joint_bias = jnp.concatenate([shift_f[:, 1], jnp.zeros_like(shift_f[:, 1]), shift_f[:, 2]])
    joint = (jnp.dot(first, qkv_full, preferred_element_type=jnp.float32) + joint_bias).astype(
        jnp.bfloat16
    )
    queries = joint[:, :feat_width].reshape(tok_rows, n_heads, head_size)
    key_rows = joint[:, feat_width : 2 * feat_width].reshape(tok_rows, n_heads, head_size)
    value_rows = joint[:, 2 * feat_width :].reshape(tok_rows, n_heads, head_size)
    log_sums = {}
    offset = 0
    group_parts = []
    for head_lo in head_starts:
        head_hi = head_lo + group_heads
        scores = block_scores(
            queries[offset : offset + block_rows, head_lo:head_hi],
            key_rows[:, head_lo:head_hi],
            live_mask,
            scaling,
        )
        row_max = jnp.max(scores, axis=-1, keepdims=True)
        expd = jnp.exp(scores - row_max)
        row_sum = jnp.sum(expd, axis=-1, keepdims=True)
        attn_low = (expd / row_sum).astype(jnp.bfloat16)
        log_sums[offset, head_lo] = row_max + jnp.log(row_sum)
        group_parts.append(
            jnp.einsum(
                "hqk,khd->qhd",
                attn_low,
                value_rows[:, head_lo:head_hi],
                preferred_element_type=jnp.float32,
            )
        )
    mixed_parts = jnp.concatenate(group_parts, axis=1)
    mixed = mixed_parts.reshape(tok_rows, feat_width).astype(jnp.bfloat16)
    after = source + jnp.dot(mixed, proj_full, preferred_element_type=jnp.float32) + shift_f[:, 3]
    norm_two, inv_two = normalize(after)
    second = (norm_two * gain_f[:, 1] + shift_f[:, 4]).astype(jnp.bfloat16)
    hidden = jnp.dot(second, up_full, preferred_element_type=jnp.float32) + bias_f
    gelu_exact = partial(jax.nn.gelu, approximate=False)
    active = gelu_exact(hidden).astype(jnp.bfloat16)
    output = (
        after + jnp.dot(active, down_full, preferred_element_type=jnp.float32) + shift_f[:, 5]
    ).astype(jnp.bfloat16)
    regathered = collect(qkv_weight, proj_weight, up_weight, down_weight, gains, shifts, up_bias)
    qkv_full, proj_full, up_full, down_full, gain_full, shift_full, bias_full = regathered
    grad_y = jnp.where(live_mask[:, None], upstream, jnp.zeros_like(upstream))
    sum_y = jnp.sum(grad_y, axis=0, dtype=jnp.float32)
    grad_down = jnp.einsum("tf,td->fd", active, grad_y, preferred_element_type=jnp.float32)
    grad_active = jnp.einsum("td,fd->tf", grad_y, down_full, preferred_element_type=jnp.float32)
    gelu_value, gelu_pull = jax.vjp(gelu_exact, hidden)
    grad_hidden = gelu_pull(grad_active)[0].astype(jnp.bfloat16)
    grad_bias_up = jnp.sum(grad_hidden, axis=0, dtype=jnp.float32)
    grad_up = jnp.einsum("td,tf->df", second, grad_hidden, preferred_element_type=jnp.float32)
    grad_second = jnp.einsum("tf,df->td", grad_hidden, up_full, preferred_element_type=jnp.float32)
    gain_two_grad = jnp.sum(grad_second * norm_two, axis=0)
    shift_two_grad = jnp.sum(grad_second, axis=0)
    grad_after = grad_y.astype(jnp.float32) + norm_back(
        grad_second * gain_f[:, 1], norm_two, inv_two
    )
    grad_attn = grad_after.astype(jnp.bfloat16)
    sum_attn = jnp.sum(grad_attn, axis=0, dtype=jnp.float32)
    grad_proj = jnp.einsum("td,te->de", mixed, grad_attn, preferred_element_type=jnp.float32)
    grad_mixed = jnp.einsum("te,de->td", grad_attn, proj_full, preferred_element_type=jnp.float32)
    grad_mixed = grad_mixed.astype(jnp.bfloat16).reshape(tok_rows, n_heads, head_size)
    key_groups = {}
    value_groups = {}
    for head_lo in head_starts:
        key_groups[head_lo] = jnp.zeros((tok_rows, group_heads, head_size), jnp.float32)
        value_groups[head_lo] = jnp.zeros((tok_rows, group_heads, head_size), jnp.float32)
    offset = 0
    query_groups = []
    for head_lo in head_starts:
        head_hi = head_lo + group_heads
        query_blk = queries[offset : offset + block_rows, head_lo:head_hi]
        grad_blk = grad_mixed[offset : offset + block_rows, head_lo:head_hi]
        key_part = key_rows[:, head_lo:head_hi]
        scores = block_scores(query_blk, key_part, live_mask, scaling)
        attn_p = jnp.exp(scores - log_sums[offset, head_lo])
        value_groups[head_lo] = jnp.einsum(
            "hqk,qhd->khd",
            attn_p.astype(jnp.bfloat16),
            grad_blk,
            preferred_element_type=jnp.float32,
        )
        grad_prob = jnp.einsum(
            "qhd,khd->hqk",
            grad_blk,
            value_rows[:, head_lo:head_hi],
            preferred_element_type=jnp.float32,
        )
        grad_score = attn_p * (grad_prob - jnp.sum(attn_p * grad_prob, axis=-1, keepdims=True))
        score_low = grad_score.astype(jnp.bfloat16)
        query_groups.append(
            jnp.einsum("hqk,khd->qhd", score_low, key_part, preferred_element_type=jnp.float32)
            * scaling
        )
        key_groups[head_lo] = (
            jnp.einsum("hqk,qhd->khd", score_low, query_blk, preferred_element_type=jnp.float32)
            * scaling
        )
    grad_query_parts = jnp.concatenate(query_groups, axis=1)
    grad_keys = jnp.concatenate([key_groups[head_lo] for head_lo in head_starts], axis=1)
    grad_vals = jnp.concatenate([value_groups[head_lo] for head_lo in head_starts], axis=1)
    grad_joint = jnp.concatenate(
        [
            grad_query_parts.reshape(tok_rows, feat_width),
            grad_keys.reshape(tok_rows, feat_width),
            grad_vals.reshape(tok_rows, feat_width),
        ],
        axis=1,
    ).astype(jnp.bfloat16)
    joint_sums = jnp.sum(grad_joint, axis=0, dtype=jnp.float32)
    grad_qkv = jnp.einsum("td,te->de", first, grad_joint, preferred_element_type=jnp.float32)
    grad_first = jnp.einsum("te,de->td", grad_joint, qkv_full, preferred_element_type=jnp.float32)
    gain_one_grad = jnp.sum(grad_first * norm_one, axis=0)
    shift_one_grad = jnp.sum(grad_first, axis=0)
    grad_tokens = (grad_after + norm_back(grad_first * gain_f[:, 0], norm_one, inv_one)).astype(
        jnp.bfloat16
    )
    grad_gains = jnp.stack([gain_one_grad, gain_two_grad], axis=1)
    grad_shifts = jnp.stack(
        [
            shift_one_grad,
            joint_sums[:feat_width],
            joint_sums[2 * feat_width :],
            sum_attn,
            shift_two_grad,
            sum_y,
        ],
        axis=1,
    )
    owned = give_back(
        grad_qkv, grad_proj, grad_up, grad_down, grad_gains, grad_shifts, grad_bias_up
    )
    own_qkv, own_proj, own_up, own_down, own_gains, own_shifts, own_bias = owned
    return (
        output,
        grad_tokens,
        own_qkv,
        own_proj,
        own_up,
        own_down,
        own_gains,
        own_shifts,
        own_bias,
    )


BOTH_LAST = (((1,), (1,)), ((), ()))
SMEM = pl.BlockSpec(memory_space=pltpu.SMEM)
ANY = pl.BlockSpec(memory_space=pl.ANY)
CORE, LENGTH, PLACE, PLACE_O = 32, 33, 34, 50


def pairs(move):
    return [(i, move(i)) for i in range(32)]


def first_way(i):
    return i ^ (2 if i % 2 == 0 else 4)


def second_way(i):
    return i ^ (4 if i % 2 == 0 else 2)


def along_z(step):
    return lambda i: i ^ (8 * step)


def send(array, move):
    return lax.ppermute(array, AXES, pairs(move))


def swap(array):
    return send(array, lambda i: i ^ 1)


def facts(chip, core, length):
    places = []
    for of_core in (core, 1 - core):
        for j in range(16):
            z, first, second = j % 4, (j // 4) % 2, j // 8
            mask = jnp.where(of_core == 0, first + 2 * second, second + 2 * first)
            places.append(jnp.bitwise_xor(chip, mask + 4 * z))
    spots = []
    for of_core in (core, 1 - core):
        for k in range(16):
            mask = jnp.bitwise_xor(chip, k)
            x, y, z = mask & 1, (mask >> 1) & 1, mask >> 2
            spots.append(z + jnp.where(of_core == 0, 4 * x + 8 * y, 4 * y + 8 * x))
    return jnp.stack(places + [core, length] + spots).astype(jnp.int32)


def params(mib):
    return pltpu.CompilerParams(vmem_limit_bytes=mib * 1024 * 1024)


def cost(micros):
    flops = int(micros * (3e10 if micros > 3 else 1e9))
    return pl.CostEstimate(flops=flops, bytes_accessed=1, transcendentals=0)


def shape(dims, dtype):
    return jax.ShapeDtypeStruct(dims, dtype)


def full(dims):
    return pl.BlockSpec(dims, lambda *_: (0,) * len(dims))


class Chain:
    def __init__(self):
        self.token, self.extra = None, ()

    def near(self, *arrays):
        self.extra = arrays

    def call(
        self, kernel, *, out_shape, in_specs, out_specs, grid=(), prefetch=0, aliases={}, **options
    ):
        single = not isinstance(out_shape, tuple)
        if single:
            out_shape, out_specs = (out_shape,), (out_specs,)
        held = 0 if self.token is None else 1
        extra, self.extra = self.extra, ()
        n_in, n_out = prefetch + len(in_specs), len(out_shape)
        at_token = n_in + len(extra)

        def body(*refs):
            skip = at_token + held
            return kernel(*refs[:n_in], *refs[skip : skip + n_out], *refs[skip + n_out + 1 :])

        token = shape((8, 128), F32)
        specs = pltpu.PrefetchScalarGridSpec(
            num_scalar_prefetch=prefetch,
            grid=grid,
            in_specs=list(in_specs) + [ANY] * (len(extra) + held),
            out_specs=tuple(out_specs) + (ANY,),
            scratch_shapes=options.pop("scratch_shapes", ()),
        )
        run = pl.pallas_call(
            body,
            grid_spec=specs,
            out_shape=tuple(out_shape) + (token,),
            input_output_aliases=aliases | ({at_token: n_out} if held else {}),
            **options,
        )

        def with_token(*args):
            *outs, self.token = run(*args, *extra, *([self.token] if held else []))
            return outs[0] if single else tuple(outs)

        return with_token


def dot(left, right):
    return jnp.dot(left, right, preferred_element_type=F32)


def dot_last(left, right):
    return lax.dot_general(left, right, BOTH_LAST, preferred_element_type=F32)


def settle(info, pieces, dest, who=(0, 1)):
    few = pieces[0].shape[0]
    for w in who:
        half = info[CORE] if w == 0 else 1 - info[CORE]
        for j in range(16):
            dest[half, info[16 * w + j]] = pieces[(16 * w + j) // few][j % few]


def bring(pieces, raw, sems, start):
    cols = pl.ds(start, raw.shape[-1])
    return [
        pltpu.make_async_copy(piece.at[:, :, cols], raw.at[i], sems.at[i])
        for i, piece in enumerate(pieces)
    ]


def centre(values):
    centred = values - jnp.mean(values, axis=-1, keepdims=True)
    inverse = lax.rsqrt(jnp.mean(centred * centred, axis=-1, keepdims=True) + EPS)
    return centred * inverse, inverse


def layer_back(grad, normed, inverse):
    return inverse * (
        grad
        - jnp.mean(grad, axis=-1, keepdims=True)
        - normed * jnp.mean(grad * normed, axis=-1, keepdims=True)
    )


def stacked(core, mine, others):
    pair = (mine, others) if core == 0 else (others, mine)
    return jnp.concatenate([part.astype(F32) for part in pair]).astype(BF16)


def by_core(info, lay):
    for core in (0, 1):
        pl.when(info[CORE] == core)(partial(lay, core))


def first_piece_kernel(info, qkv, qkv_o, small, out):
    third = qkv.shape[1] // 6

    def lay(core):
        for i in range(3):
            cols = slice((2 * i + core) * third, (2 * i + core + 1) * third)
            out[0, :, i * third : (i + 1) * third] = stacked(core, qkv[:, cols], qkv_o[:, cols])
        out[0, :, 3 * third :] = stacked(core, small[...], jnp.zeros_like(small))

    by_core(info, lay)


def first_piece(chain, info, qkv, qkv_o, small):
    rows, cols = qkv.shape
    vmem = pl.BlockSpec(memory_space=pltpu.VMEM)
    return chain.call(
        first_piece_kernel,
        out_shape=shape((1, 2 * rows, cols // 2 + small.shape[1]), BF16),
        in_specs=[SMEM] + [vmem] * 3,
        out_specs=vmem,
        compiler_params=params(8),
        name="first_piece",
        cost_estimate=cost(0),
    )(info, qkv, qkv_o, small)


def up_piece_kernel(info, up, up_o, proj, proj_o, out):
    wide, third = up.shape[1] // 2, proj.shape[1] // 2

    def lay(core):
        for whole, other, at, width in ((up, up_o, 0, wide), (proj, proj_o, wide, third)):
            cols = slice(core * width, (core + 1) * width)
            out[0, :, at : at + width] = stacked(core, whole[:, cols], other[:, cols])

    by_core(info, lay)


def up_piece(chain, info, up, up_o, proj, proj_o):
    rows = up.shape[0]
    vmem = pl.BlockSpec(memory_space=pltpu.VMEM)
    return chain.call(
        up_piece_kernel,
        out_shape=shape((1, 2 * rows, (up.shape[1] + proj.shape[1]) // 2), BF16),
        in_specs=[SMEM] + [vmem] * 4,
        out_specs=vmem,
        compiler_params=params(8),
        name="up_piece",
        cost_estimate=cost(0),
    )(info, up, up_o, proj, proj_o)


def gather_kernel(n_in, n_held, *refs):
    out, at = refs[n_in + n_held], 0
    for part in refs[:n_in]:
        out[at : at + part.shape[0]] = part[...]
        at += part.shape[0]
    for i in range(n_held):
        refs[n_in + n_held + 1 + i][...] = refs[n_in + i][...]


def gather(chain, parts, held=(), micros=0):
    vmem = pl.BlockSpec(memory_space=pltpu.VMEM)
    _, rows, cols = parts[0].shape
    count = sum(part.shape[0] for part in parts)
    n, n_held = len(parts), len(held)
    return chain.call(
        partial(gather_kernel, n, n_held),
        out_shape=(shape((count, rows, cols), BF16),) + tuple(shape(h.shape, h.dtype) for h in held),
        in_specs=[vmem] * (n + n_held),
        out_specs=(vmem,) * (1 + n_held),
        compiler_params=params(16),
        name="gather",
        cost_estimate=cost(micros),
    )(*parts, *held)


def gate_kernel(array, out):
    pass


def gate(chain, array, micros):
    return chain.call(
        gate_kernel,
        out_shape=shape(array.shape, array.dtype),
        in_specs=[ANY],
        out_specs=ANY,
        aliases={0: 0},
        compiler_params=params(4),
        name="gate",
        cost_estimate=cost(micros),
    )(array)


def both_cores(*own):
    return own + tuple(swap(blocks) for blocks in own)


def near_z(piece, steps):
    return [send(piece, along_z(s)) for s in steps]


def enter_kernel(
    info,
    tokens,
    upstream,
    down,
    *refs,
):
    pieces = refs[:4]
    kept, vecs, bias, flipped, joint, grad_y, piece_down, weights, sem = refs[4:]
    feat = tokens.shape[1]
    third = feat // 2
    piece_down[0] = down[...]
    place = lax.broadcasted_iota(jnp.int32, upstream.shape, 0)
    grad_y[...] = jnp.where(place < info[LENGTH], upstream[...].astype(F32), 0.0).astype(BF16)
    settle(info, pieces, weights)
    normed, _ = centre(tokens[...].astype(F32))
    out = pltpu.make_async_copy(weights, kept, sem)
    out.start()
    split = 3 * third
    small = weights[0, :, :, split:] + weights[1, :, :, split:]
    small = small.reshape(feat, 128).astype(F32)
    each = bias.shape[1] // 32
    for device in range(32):
        row = device * feat // 32
        bias[:, device * each : (device + 1) * each] = small[row : row + 1, 128 - each :]
    small = small.T
    vecs[...] = small[:8]
    low_first = (normed * small[0:1] + small[2:3]).astype(BF16)
    flipped[...] = low_first.T.reshape(flipped.shape)
    for h in (0, 1):
        cols = slice(h * third, (h + 1) * third)
        bias = jnp.concatenate(
            [small[3:4, cols], jnp.zeros((1, third), F32), small[4:5, cols]], axis=1
        )
        w = weights[h, :, :, :split].reshape(feat, split)
        joint[h] = (dot(low_first, w) + bias).astype(BF16)
    out.wait()


def enter(chain, info, tokens, upstream, down, hidden, pieces):
    rows, feat = tokens.shape
    width = pieces[0].shape[-1]
    vmem = pl.BlockSpec(memory_space=pltpu.VMEM)
    sets = (2, 16, feat // 16, width)
    return chain.call(
        enter_kernel,
        out_shape=(
            shape(sets, BF16),
            shape((8, feat), F32),
            shape((1, hidden), F32),
            shape((16, feat // 16, rows), BF16),
            shape((2, rows, 3 * feat // 2), BF16),
            shape((rows, feat), BF16),
            shape((1,) + down.shape, BF16),
        ),
        in_specs=[SMEM] + [vmem] * 7,
        out_specs=(ANY,) + (vmem,) * 6,
        scratch_shapes=[pltpu.VMEM(sets, BF16), pltpu.SemaphoreType.DMA],
        compiler_params=params(20),
        name="enter",
        cost_estimate=cost(8),
    )(info, tokens, upstream, down, *pieces)


def scores_of(info, keys, queries):
    raw = dot_last(keys, queries)
    place = lax.broadcasted_iota(jnp.int32, raw.shape, 0)
    return jnp.where(place < info[LENGTH], raw, NEG)


def mix_kernel(info, q, k, v, mixed, flipped, stats):
    head = mixed.shape[1] // (HEADS // 2)
    count = q.shape[-1] // head
    scale = head**-0.5
    turned = v[0].T

    def start(h):
        cols = slice(h * head, (h + 1) * head)
        return scores_of(info, k[0, :, cols], q[0, :, cols] * scale)

    def finish(h, scores):
        cols = slice(h * head, (h + 1) * head)
        most = jnp.max(scores, axis=0, keepdims=True)
        expd = jnp.exp(scores - most)
        total = jnp.sum(expd, axis=0, keepdims=True)
        attn = (expd * (1.0 / total)).astype(BF16)
        stats[h // 2, h % 2 : h % 2 + 1] = most + jnp.log(total)
        return dot(turned[cols], attn)

    ready = [start(h) for h in range(2)]
    outs = []
    for h in range(count):
        if h + 2 < count:
            ready.append(start(h + 2))
        outs.append(finish(h, ready[h]))
    both = jnp.concatenate(outs)
    flipped[...] = both.astype(BF16)
    mixed[...] = both.T.astype(BF16)


def mix(chain, info, joint):
    _, rows, width = joint.shape
    feat = 2 * width // 3
    wide = feat // 2
    spec = [pl.BlockSpec((1, rows, wide), lambda i, part=part: (i, 0, part)) for part in range(3)]
    pairs_in_half = HEADS // 4
    return chain.call(
        mix_kernel,
        grid=(2,),
        out_shape=(
            shape((rows, feat), BF16),
            shape((feat, rows), BF16),
            shape((HEADS // 2, 8, rows), F32),
        ),
        in_specs=[SMEM] + spec,
        out_specs=(
            pl.BlockSpec((rows, wide), lambda i: (0, i)),
            pl.BlockSpec((wide, rows), lambda i: (i, 0)),
            pl.BlockSpec((pairs_in_half, 8, rows), lambda i: (i, 0, 0)),
        ),
        compiler_params=params(24),
        name="mix",
        cost_estimate=cost(10),
    )(info, joint, joint, joint)


def mix_back_kernel(info, q, k, v, grad, stats, theirs, mine):
    head = theirs.shape[2] // (HEADS // 2)
    count = q.shape[-1] // head
    scale = head**-0.5
    turned = k[0].T

    def start(h):
        cols = slice(h * head, (h + 1) * head)
        queries = q[0, :, cols] * scale
        scores = scores_of(info, k[0, :, cols], queries)
        return cols, queries, scores, dot_last(v[0, :, cols], grad[:, cols])

    def finish(h, cols, queries, scores, grad_prob):
        attn = jnp.exp(scores - stats[h // 2, h % 2 : h % 2 + 1])
        inner = jnp.sum(attn * grad_prob, axis=0, keepdims=True)
        low = (attn * (grad_prob - inner)).astype(BF16)
        return (
            dot(turned[cols], low) * scale,
            dot(low, queries),
            dot(attn.astype(BF16), grad[:, cols]),
        )

    ready = [start(h) for h in range(2)]
    done = []
    for h in range(count):
        if h + 2 < count:
            ready.append(start(h + 2))
        done.append(finish(h, *ready[h]))
    out = [
        jnp.concatenate([d[0] for d in done]).T.astype(BF16),
        jnp.concatenate([d[1] for d in done], axis=1).astype(BF16),
        jnp.concatenate([d[2] for d in done], axis=1).astype(BF16),
    ]

    @pl.when(pl.program_id(0) == 0)
    def _():
        for part in range(3):
            theirs[part] = out[part]

    @pl.when(pl.program_id(0) == 1)
    def _():
        for part in range(3):
            mine[part] = out[part]


def mix_back(chain, info, joint, grad_mixed, stats):
    _, rows, width = joint.shape
    feat = 2 * width // 3
    wide = feat // 2

    def half(i, info):
        return jnp.where(i == 0, 1 - info[CORE], info[CORE])

    spec = [
        pl.BlockSpec((1, rows, wide), lambda i, info, part=part: (half(i, info), 0, part))
        for part in range(3)
    ]
    out = shape((3, rows, feat // 2), BF16)
    return chain.call(
        mix_back_kernel,
        prefetch=1,
        grid=(2,),
        in_specs=spec
        + [
            pl.BlockSpec((rows, wide), lambda i, info: (0, half(i, info))),
            pl.BlockSpec((HEADS // 4, 8, rows), lambda i, info: (half(i, info), 0, 0)),
        ],
        out_specs=(
            pl.BlockSpec((3, rows, wide), lambda i, info: (0, 0, 0)),
            pl.BlockSpec((3, rows, wide), lambda i, info: (0, 0, 0)),
        ),
        out_shape=(out, out),
        compiler_params=params(30),
        name="mix_back",
        cost_estimate=cost(16),
    )(info, joint, joint, joint, grad_mixed, stats)


GELU = (0.254829592, -0.284496736, 1.421413741, -1.453152027, 1.061405429)


def gelu_parts(x):
    bell = jnp.exp2(x * x * (-0.5 / math.log(2)))
    below = 1.0 + (0.3275911 * 0.5**0.5) * jnp.abs(x)
    t = pl.reciprocal(below, approx=True)
    t = t * (2.0 - below * t)
    poly = 0.5 * GELU[4]
    for c in GELU[3::-1]:
        poly = poly * t + 0.5 * c
    tail = poly * t * bell
    phi = jnp.where(x < 0, tail, 1.0 - tail)
    return x * phi, phi + x * (bell * (2 * math.pi) ** -0.5)


def rise_kernel(info, tokens, mixed, vecs, *refs):
    pieces = refs[:8]
    weights, after, second, flipped, raw, sems = refs[8:]
    feat = tokens.shape[1]
    copies = bring(pieces, raw, sems, pieces[0].shape[2] - raw.shape[-1])
    for copy in copies:
        copy.start()
    start = tokens[...].astype(F32) + vecs[5:6]
    for copy in copies:
        copy.wait()
    settle(info, [raw.at[i] for i in range(8)], weights)
    grown = [dot(mixed[...], weights[h].reshape(feat, feat // 2)) for h in (0, 1)]
    total = start + jnp.concatenate(grown, axis=1)
    after[...] = total
    normed, _ = centre(total)
    value = (normed * vecs[1:2] + vecs[6:7]).astype(BF16)
    second[...] = value
    flipped[...] = value.T.reshape(flipped.shape)


def rise(chain, info, tokens, mixed, vecs, pieces):
    rows, feat = tokens.shape
    vmem = pl.BlockSpec(memory_space=pltpu.VMEM)
    block = feat // 16
    return chain.call(
        rise_kernel,
        out_shape=(
            shape((2, 16, block, feat // 2), BF16),
            shape((rows, feat), F32),
            shape((rows, feat), BF16),
            shape((16, block, rows), BF16),
        ),
        in_specs=[SMEM] + [vmem] * 3 + [ANY] * 8,
        out_specs=(vmem,) * 4,
        scratch_shapes=[
            pltpu.VMEM((8, 4, block, feat // 2), BF16),
            pltpu.SemaphoreType.DMA((8,)),
        ],
        compiler_params=params(16),
        name="rise",
        cost_estimate=cost(5),
    )(info, tokens, mixed, vecs, *pieces)


def widen_kernel(which, info, second, bias, *refs):
    pieces = refs[:4]
    weights, active, slope, mine, theirs, raw, sems = refs[4:]
    step = pl.program_id(0)
    core = info[CORE]
    feat = second.shape[1]
    tile = active.shape[1]
    rows = mine.shape[1]
    count = tile // rows

    @pl.when(step == 0)
    def _():
        copies = bring(pieces, raw, sems, 0)
        for copy in copies:
            copy.start()
        for copy in copies:
            copy.wait()
        for j in range(16):
            weights[info[16 * which + j]] = raw[j // 4, j % 4]

    cols = pl.ds(pl.multiple_of(step * tile, tile), tile)
    w = weights[:, :, cols].reshape(feat, tile)
    hidden = dot(second[...], w) + bias[...]
    value, grad = gelu_parts(hidden)
    value = value.astype(BF16)
    active[...] = value
    slope[...] = grad.astype(BF16)
    flipped = value.T.reshape(count // 2, 2, rows, -1)
    mine[...] = jnp.where(core == 0, flipped[:, 0], flipped[:, 1])
    theirs[...] = jnp.where(core == 0, flipped[:, 1], flipped[:, 0])


def widen(chain, which, info, second, bias, pieces):
    rows, feat = second.shape
    wide = pieces[0].shape[-1] - feat // 2
    tile, block = 768, wide // 16
    per = wide // tile
    turned = shape((8, block, rows), BF16)

    def whole(dims):
        return pl.BlockSpec(dims, lambda n, info: (0,) * len(dims))

    def bias_at(n, info):
        half = info[CORE] if which == 0 else 1 - info[CORE]
        return (0, half * per + n)

    strip = pl.BlockSpec((rows, tile), lambda n, info: (0, n))
    part = pl.BlockSpec((tile // block // 2, block, rows), lambda n, info: (n, 0, 0))
    return chain.call(
        partial(widen_kernel, which),
        prefetch=1,
        grid=(per,),
        out_shape=(
            shape((16, feat // 16, wide), BF16),
            shape((rows, wide), BF16),
            shape((rows, wide), BF16),
            turned,
            turned,
        ),
        in_specs=[whole((rows, feat)), pl.BlockSpec((1, tile), bias_at)] + [ANY] * 4,
        out_specs=(whole((16, feat // 16, wide)), strip, strip, part, part),
        scratch_shapes=[
            pltpu.VMEM((4, 4, feat // 16, wide), BF16),
            pltpu.SemaphoreType.DMA((4,)),
        ],
        compiler_params=params(24),
        name="widen",
        cost_estimate=cost(18),
    )(info, second, bias, *pieces)


def leave_kernel(info, after, first, second, down, vecs, output, total):
    step, per = pl.program_id(0), pl.num_programs(0) // 2

    @pl.when(step == 0)
    def _():
        total[...] = after[...] + vecs[7:8] + dot(first[...], down[...])

    @pl.when((step > 0) & (step < per))
    def _():
        total[...] += dot(first[...], down[...])

    @pl.when(step >= per)
    def _():
        total[...] += dot(second[...], down[...])

    @pl.when(step == 2 * per - 1)
    def _():
        output[...] = total[...].astype(BF16)


def leave(chain, info, after, first, second, down, vecs):
    rows, feat = after.shape
    tile = 768
    per = first.shape[1] // tile

    def whole(dims):
        return pl.BlockSpec(dims, lambda n, info: (0,) * len(dims))

    def down_at(n, info):
        half = jnp.where(n < per, info[CORE], 1 - info[CORE])
        return (half * per + n % per, 0)

    return chain.call(
        leave_kernel,
        prefetch=1,
        grid=(2 * per,),
        out_shape=shape((rows, feat), BF16),
        in_specs=[
            whole((rows, feat)),
            pl.BlockSpec((rows, tile), lambda n, info: (0, jnp.minimum(n, per - 1))),
            pl.BlockSpec((rows, tile), lambda n, info: (0, jnp.maximum(n - per, 0))),
            pl.BlockSpec((tile, feat), down_at),
            whole((8, feat)),
        ],
        out_specs=whole((rows, feat)),
        scratch_shapes=[pltpu.VMEM((rows, feat), F32)],
        compiler_params=params(16),
        name="leave",
        cost_estimate=cost(7),
    )(info, after, first, second, down, vecs)


def fall_kernel(info, grad_y, slope, slope_o, up, up_o, after, vecs, proj, *refs):
    pieces = refs[:4]
    kept, theirs, mine, bias_sum, grad_after, attn_theirs, attn_mine, grad_mixed, sums = refs[4:13]
    weights, grad_second, normed, inverse, raw, sems, sem = refs[13:]
    step, steps = pl.program_id(0), pl.num_programs(0)
    core = info[CORE]
    feat = grad_y.shape[1]
    tile = slope.shape[1]
    per = steps // 2
    keeping = pltpu.make_async_copy(weights, kept, sem)

    @pl.when(step == 0)
    def _():
        copies = bring(pieces, raw, sems, 0)
        for copy in copies:
            copy.start()
        normed[...], inverse[...] = centre(after[...])
        grad_second[...] = jnp.zeros_like(grad_second)
        for copy in copies:
            copy.wait()
        for who in (0, 1):
            c = core if who == 0 else 1 - core
            for j in range(16):
                weights[info[16 * who + j], c] = raw[2 * who + j // 8, j % 8]
        keeping.start()

    half = jnp.where(step < per, 1 - core, core)
    at = half * per + lax.rem(step, per)
    count = tile * weights.shape[0] // (steps * tile)
    down = weights[pl.ds(count * at, count)].reshape(tile, feat)
    raw_grad = dot_last(grad_y[...], down)

    def tell(slope_ref, up_ref, out):
        grad = (raw_grad * slope_ref[...].astype(F32)).astype(BF16)
        bias_sum[...] = jnp.sum(grad.astype(F32), axis=0, keepdims=True)
        grad_second[...] += dot_last(grad, up_ref[...])
        out[...] = grad

    pl.when(step < per)(lambda: tell(slope_o, up_o, theirs))
    pl.when(step >= per)(lambda: tell(slope, up, mine))

    @pl.when(step == steps - 1)
    def _():
        second = grad_second[...]
        live = grad_y[...].astype(F32)
        sums[0:1] = jnp.sum(second * normed[...], axis=0, keepdims=True)
        sums[1:2] = jnp.sum(second, axis=0, keepdims=True)
        total = live + layer_back(second * vecs[1:2], normed[...], inverse[...])
        grad_after[...] = total
        attn = total.astype(BF16)
        sums[2:3] = jnp.sum(attn.astype(F32), axis=0, keepdims=True)
        sums[3:4] = jnp.sum(live, axis=0, keepdims=True)
        sums[4:8] = jnp.zeros_like(sums[4:8])
        left, right = attn[:, : feat // 2], attn[:, feat // 2 :]
        attn_mine[...] = jnp.where(core == 0, left, right)
        attn_theirs[...] = jnp.where(core == 0, right, left)
        grad_mixed[...] = (dot_last(left, proj[0]) + dot_last(right, proj[1])).astype(BF16)
        keeping.wait()


def fall(chain, info, grad_y, slopes, up_sets, after, vecs, proj_set, pieces):
    rows, feat = grad_y.shape
    hidden = 2 * slopes[0].shape[1]
    tile = 768
    steps = hidden // tile
    per = steps // 2

    def at(n, info):
        return jnp.where(n < per, 1 - info[CORE], info[CORE]) * per + n % per

    def whole(dims):
        return pl.BlockSpec(dims, lambda n, info: (0,) * len(dims))

    return chain.call(
        fall_kernel,
        prefetch=1,
        grid=(steps,),
        in_specs=[
            whole((rows, feat)),
            pl.BlockSpec((rows, tile), lambda n, info: (0, jnp.maximum(n - per, 0))),
            pl.BlockSpec((rows, tile), lambda n, info: (0, jnp.minimum(n, per - 1))),
            pl.BlockSpec((feat, tile), lambda n, info: (0, jnp.maximum(n - per, 0))),
            pl.BlockSpec((feat, tile), lambda n, info: (0, jnp.minimum(n, per - 1))),
            whole((rows, feat)),
            whole((8, feat)),
            whole((2, feat, feat // 2)),
        ]
        + [ANY] * 4,
        out_specs=(
            ANY,
            pl.BlockSpec((rows, tile), lambda n, info: (0, jnp.minimum(n, per - 1))),
            pl.BlockSpec((rows, tile), lambda n, info: (0, jnp.maximum(n - per, 0))),
            pl.BlockSpec((1, tile), lambda n, info: (0, at(n, info))),
            whole((rows, feat)),
            whole((rows, feat // 2)),
            whole((rows, feat // 2)),
            whole((rows, feat)),
            whole((8, feat)),
        ),
        scratch_shapes=[
            pltpu.VMEM((16, 2, hidden // 32, feat), BF16),
            pltpu.VMEM((rows, feat), F32),
            pltpu.VMEM((rows, feat), F32),
            pltpu.VMEM((rows, 1), F32),
            pltpu.VMEM((4,) + pieces[0].shape, BF16),
            pltpu.SemaphoreType.DMA((4,)),
            pltpu.SemaphoreType.DMA,
        ],
        out_shape=(
            shape((16, 2, hidden // 32, feat), BF16),
            shape((rows, hidden // 2), BF16),
            shape((rows, hidden // 2), BF16),
            shape((1, hidden), F32),
            shape((rows, feat), F32),
            shape((rows, feat // 2), BF16),
            shape((rows, feat // 2), BF16),
            shape((rows, feat), BF16),
            shape((8, feat), F32),
        ),
        compiler_params=params(32),
        name="fall",
        cost_estimate=cost(18),
    )(info, grad_y, *slopes, *up_sets, after, vecs, proj_set, *pieces)


def exit_kernel(
    info,
    tokens,
    mine,
    theirs,
    weights,
    grad_after,
    vecs,
    sums_a,
    bias,
    grad_tokens,
    keep,
    away,
    grad_first,
    joint,
    sums,
    extra,
):
    step = pl.program_id(0)
    core = info[CORE]
    third = mine.shape[2]
    half = jnp.where(step == 0, core, 1 - core)
    spot = pl.ds(pl.multiple_of(half * third, third), third)

    def parts(source):
        for part in range(3):
            joint[:, part * third : (part + 1) * third] = source[part]
        sums[3:4, spot] = jnp.sum(source[0].astype(F32), axis=0, keepdims=True)
        sums[4:5, spot] = jnp.sum(source[2].astype(F32), axis=0, keepdims=True)
        return dot_last(joint[...], weights[0])

    @pl.when(step == 0)
    def _():
        grad_first[...] = parts(mine)

    @pl.when(step == 1)
    def _():
        grad = grad_first[...] + parts(theirs)
        normed, inverse = centre(tokens[...].astype(F32))
        sums[0:1] = jnp.sum(grad * normed, axis=0, keepdims=True)
        sums[1:2] = sums_a[0:1]
        sums[2:3] = jnp.sum(grad, axis=0, keepdims=True)
        sums[5:6] = sums_a[2:3]
        sums[6:7] = sums_a[1:2]
        sums[7:8] = sums_a[3:4]
        sums[8:] = jnp.zeros_like(sums[8:])
        back = layer_back(grad * vecs[0:1], normed, inverse)
        grad_tokens[...] = (grad_after[...] + back).astype(BF16)
        flipped = sums[...].T
        block, each = extra.shape[1], bias.shape[1] // 32
        for chip in range(16):
            place = info[PLACE + chip]
            extra[place] = flipped[chip * block : (chip + 1) * block]
            for c in (0, 1):
                at = (2 * chip + c) * each
                row = c * block // 2
                extra[place, row : row + 1, 128 - each :] = bias[:, at : at + each]
        keep[...] = extra[:8]
        away[...] = extra[8:].astype(BF16)


def exit_back(chain, info, tokens, mine, theirs, first_set, grad_after, vecs, sums_a, bias):
    rows, feat = tokens.shape
    third = feat // 2
    block = feat // 16

    def whole(dims):
        return pl.BlockSpec(dims, lambda n, info: (0,) * len(dims))

    return chain.call(
        exit_kernel,
        prefetch=1,
        grid=(2,),
        in_specs=[
            whole((rows, feat)),
            whole((3, rows, third)),
            whole((3, rows, third)),
            pl.BlockSpec(
                (1, feat, 3 * third),
                lambda n, info: (jnp.where(n == 0, info[CORE], 1 - info[CORE]), 0, 0),
            ),
            whole((rows, feat)),
            whole((8, feat)),
            whole((8, feat)),
            whole(bias.shape),
        ],
        out_specs=(whole((rows, feat)), whole((8, block, 128)), whole((8, block, 128))),
        scratch_shapes=[
            pltpu.VMEM((rows, feat), F32),
            pltpu.VMEM((rows, 3 * third), BF16),
            pltpu.VMEM((128, feat), F32),
            pltpu.VMEM((16, block, 128), F32),
        ],
        out_shape=(
            shape((rows, feat), BF16),
            shape((8, block, 128), F32),
            shape((8, block, 128), BF16),
        ),
        compiler_params=params(18),
        name="exit_back",
        cost_estimate=cost(8),
    )(info, tokens, mine, theirs, first_set, grad_after, vecs, sums_a, bias)


def line_up(info, left, left_o, turned):
    rows = left.shape[2]
    for chip in range(16):
        place = info[PLACE + chip]
        turned[place, :, :rows] = left[chip]
        turned[place, :, rows:] = left_o[chip]


def outer_tile(turned, right, right_o):
    rows = right.shape[0]
    both = turned[...].reshape(-1, turned.shape[2])
    total = dot(both[:, :rows], right) + dot(both[:, rows:], right_o)
    return total.reshape(16, -1, total.shape[1])


def outer_up_kernel(
    info, left, left_o, right, right_o, low, low_o, attn, attn_o, keep, away, turned
):
    step, last = pl.program_id(0), pl.num_programs(0) - 1

    @pl.when(step == 0)
    def _():
        line_up(info, left, left_o, turned)

    @pl.when(step < last)
    def _():
        total = outer_tile(turned, right[...], right_o[...])
        keep[...] = total[:8]
        away[...] = total[8:].astype(BF16)

    @pl.when(step == last)
    def _():
        line_up(info, low, low_o, turned)
        total = outer_tile(turned, attn[...], attn_o[...])
        keep[:, :, : attn.shape[1]] = total[:8]
        away[:, :, : attn.shape[1]] = total[8:].astype(BF16)


def outer_up(chain, info, left, left_o, right, right_o, low, low_o, attn, attn_o):
    _, block, rows = left.shape
    tile = 2 * attn.shape[1]
    n = right.shape[1] // tile
    cols = right.shape[1] + attn.shape[1]
    strip = pl.BlockSpec((rows, tile), lambda i: (0, jnp.minimum(i, n - 1)))
    out = pl.BlockSpec((8, block, tile), lambda i: (0, 0, i))
    return chain.call(
        outer_up_kernel,
        grid=(n + 1,),
        out_shape=(shape((8, block, cols), F32), shape((8, block, cols), BF16)),
        in_specs=[SMEM]
        + [full(left.shape)] * 2
        + [strip] * 2
        + [full(left.shape)] * 2
        + [full(attn.shape)] * 2,
        out_specs=(out, out),
        scratch_shapes=[pltpu.VMEM((16, block, 2 * rows), BF16)],
        compiler_params=params(20),
        name="outer_up",
        cost_estimate=cost(8),
    )(info, left, left_o, right, right_o, low, low_o, attn, attn_o)


def outer_qkv_kernel(info, left, left_o, right, right_o, keep, away, turned):
    tile = right.shape[2]
    line_up(info, left, left_o, turned)
    for part in range(3):
        cols = slice(part * tile, (part + 1) * tile)
        total = outer_tile(turned, right[part], right_o[part])
        keep[:, :, cols] = total[:8]
        away[:, :, cols] = total[8:].astype(BF16)


def outer_qkv(chain, info, left, left_o, right, right_o):
    _, block, rows = left.shape
    cols = 3 * right.shape[2]
    vmem = pl.BlockSpec(memory_space=pltpu.VMEM)
    return chain.call(
        outer_qkv_kernel,
        out_shape=(shape((8, block, cols), F32), shape((8, block, cols), BF16)),
        in_specs=[SMEM] + [vmem] * 4,
        out_specs=(vmem, vmem),
        scratch_shapes=[pltpu.VMEM((16, block, 2 * rows), BF16)],
        compiler_params=params(20),
        name="outer_qkv",
        cost_estimate=cost(8),
    )(info, left, left_o, right, right_o)


def outer_down_kernel(
    info, first, second, first_o, second_o, right, right_o, keep, away, turned
):
    rows = right.shape[0]
    core = info[CORE]
    for r in range(8):
        place = info[PLACE + 8 * core + r]
        turned[place, :, :rows] = first[r]
        turned[place, :, rows:] = second_o[r]
        place = info[PLACE + 8 * (1 - core) + r]
        turned[place, :, :rows] = second[r]
        turned[place, :, rows:] = first_o[r]
    for out, spots in ((away, slice(8, 16)), (keep, slice(0, 8))):
        left = turned[spots].reshape(-1, turned.shape[2])
        total = dot(left[:, :rows], right[...]) + dot(left[:, rows:], right_o[...])
        out[...] = total.reshape(out.shape).astype(out.dtype)


def outer_down(chain, info, first, second, first_o, second_o, right, right_o):
    _, block, rows = first.shape
    feat = right.shape[1]
    vmem = pl.BlockSpec(memory_space=pltpu.VMEM)
    return chain.call(
        outer_down_kernel,
        out_shape=(shape((8, block, feat), F32), shape((8, block, feat), BF16)),
        in_specs=[SMEM] + [vmem] * 6,
        out_specs=(vmem, vmem),
        scratch_shapes=[pltpu.VMEM((16, block, 2 * rows), BF16)],
        compiler_params=params(24),
        name="outer_down",
        cost_estimate=cost(0),
    )(info, first, second, first_o, second_o, right, right_o)


def add_first_kernel(keep, got, kept, away):
    kept[...] = keep[:4] + got[:4].astype(F32)
    away[...] = (keep[4:] + got[4:].astype(F32)).astype(BF16)


def shift_first(chain, keep, away, micros=0):
    _, rows, cols = keep.shape
    vmem = pl.BlockSpec(memory_space=pltpu.VMEM)
    return chain.call(
        add_first_kernel,
        out_shape=(shape((4, rows, cols), F32), shape((4, rows, cols), BF16)),
        in_specs=[vmem, vmem],
        out_specs=(vmem, vmem),
        compiler_params=params(12),
        name="shift_first",
        cost_estimate=cost(micros),
    )(keep, send(away, second_way))


def add_both_kernel(keep, got, few_keep, few_got, kept, away):
    split = keep.shape[2]
    kept[:, :, :split] = keep[:4] + got[:4].astype(F32)
    kept[:, :, split:] = few_keep[:4] + few_got[:4].astype(F32)
    away[:, :, :split] = (keep[4:] + got[4:].astype(F32)).astype(BF16)
    away[:, :, split:] = (few_keep[4:] + few_got[4:].astype(F32)).astype(BF16)


def shift_both(chain, keep, away, few_keep, few_away):
    _, rows, cols = keep.shape
    cols += few_keep.shape[2]
    vmem = pl.BlockSpec(memory_space=pltpu.VMEM)
    return chain.call(
        add_both_kernel,
        out_shape=(shape((4, rows, cols), F32), shape((4, rows, cols), BF16)),
        in_specs=[vmem] * 4,
        out_specs=(vmem, vmem),
        compiler_params=params(12),
        name="shift_both",
        cost_estimate=cost(0),
    )(keep, send(away, second_way), few_keep, send(few_away, second_way))


def add_second_kernel(keep, got, base, one, two, three):
    base[...] = keep[0] + got[0].astype(F32)
    for s, out in ((1, one), (2, two), (3, three)):
        out[...] = (keep[s] + got[s].astype(F32)).astype(BF16)


def shift_second(chain, keep, away):
    _, rows, cols = keep.shape
    vmem = pl.BlockSpec(memory_space=pltpu.VMEM)
    base, *lows = chain.call(
        add_second_kernel,
        out_shape=(shape((rows, cols), F32),) + (shape((rows, cols), BF16),) * 3,
        in_specs=[vmem, vmem],
        out_specs=(vmem,) * 4,
        compiler_params=params(8),
        name="shift_second",
        cost_estimate=cost(0),
    )(keep, send(away, first_way))
    return base, [send(low, along_z(s)) for low, s in zip(lows, (1, 2, 3))]


def total_of(base, parts):
    return base[...] + parts[0][...].astype(F32) + (
        parts[1][...].astype(F32) + parts[2][...].astype(F32)
    )


def add_down_kernel(base, one, two, three, out):
    out[...] = total_of(base, (one, two, three))


def home_down(chain, base, parts):
    vmem = pl.BlockSpec(memory_space=pltpu.VMEM)
    return chain.call(
        add_down_kernel,
        out_shape=shape(base.shape, F32),
        in_specs=[vmem] * 4,
        out_specs=vmem,
        compiler_params=params(8),
        name="home_down",
        cost_estimate=cost(0),
    )(base, *parts)


def add_last_kernel(info, base, one, two, three, mine, theirs, total):
    core = info[CORE]
    half = mine.shape[0]
    total[...] = total_of(base, (one, two, three))
    mine[...] = total[pl.ds(pl.multiple_of(core * half, half), half)]
    theirs[...] = total[pl.ds(pl.multiple_of((1 - core) * half, half), half)]


def home(chain, info, base, parts):
    rows, cols = base.shape
    vmem = pl.BlockSpec(memory_space=pltpu.VMEM)
    out = shape((rows // 2, cols), F32)
    mine, theirs = chain.call(
        add_last_kernel,
        out_shape=(out, out),
        in_specs=[SMEM] + [vmem] * 4,
        out_specs=(vmem, vmem),
        scratch_shapes=[pltpu.VMEM((rows, cols), F32)],
        compiler_params=params(8),
        name="home",
        cost_estimate=cost(0),
    )(info, base, *parts)
    return mine, swap(theirs)


def finish_kernel(info, qkv, qkv_o, up, up_o, out_qkv, out_proj, out_up, gains, shifts, bias):
    rows, third = out_proj.shape[0], out_proj.shape[1] // 2
    wide = out_up.shape[1] // 2
    small = qkv[:, 3 * third :] + qkv_o[:, 3 * third :]
    flipped = jnp.concatenate([small, jnp.zeros((128 - rows, 128), F32)]).T
    gains[...] = flipped[0:2, :rows]
    shifts[...] = flipped[2:8, :rows]
    bias[...] = small[0:1, 128 - bias.shape[1] :]

    def lay(core):
        for half, (a, b) in ((core, (qkv, up)), (1 - core, (qkv_o, up_o))):
            for part in range(3):
                spot = part * 2 * third + half * third
                out_qkv[:, spot : spot + third] = a[:, part * third : (part + 1) * third]
            out_proj[:, half * third : (half + 1) * third] = b[:, wide:]
            out_up[:, half * wide : (half + 1) * wide] = b[:, :wide]

    @pl.when(info[CORE] == 0)
    def _():
        lay(0)

    @pl.when(info[CORE] == 1)
    def _():
        lay(1)


def finish(chain, info, qkv, qkv_o, up, up_o):
    rows = qkv.shape[0]
    third = (qkv.shape[1] - 128) // 3
    vmem = pl.BlockSpec(memory_space=pltpu.VMEM)
    return chain.call(
        finish_kernel,
        out_shape=(
            shape((rows, 6 * third), F32),
            shape((rows, 2 * third), F32),
            shape((rows, 2 * (up.shape[1] - third)), F32),
            shape((2, rows), F32),
            shape((6, rows), F32),
            shape((1, 4 * rows), F32),
        ),
        in_specs=[SMEM] + [vmem] * 4,
        out_specs=(vmem,) * 6,
        compiler_params=params(8),
        name="finish",
        cost_estimate=cost(0),
    )(info, qkv, qkv_o, up, up_o)


def local(
    tokens,
    upstream,
    lengths,
    qkv_weight,
    proj_weight,
    up_weight,
    down_weight,
    gains,
    shifts,
    up_bias,
):
    tok_rows, feat = tokens.shape
    rows = qkv_weight.shape[0]
    hidden = up_weight.shape[1]
    third, wide = feat // 2, hidden // 2
    chip, core = lax.axis_index("dp"), lax.axis_index("fsdp")
    info = facts(chip, core, lengths[0])

    chain = Chain()

    small = jnp.concatenate([gains, shifts], axis=1)
    small = jnp.pad(small, ((0, 0), (0, 128 - small.shape[1])))
    small = small + jnp.pad(up_bias[None], ((0, rows - 1), (128 - up_bias.shape[0], 0)))
    piece = first_piece(chain, info, qkv_weight, swap(qkv_weight), small)
    piece_up = up_piece(chain, info, up_weight, swap(up_weight), proj_weight, swap(proj_weight))
    zs, piece_up = gather(chain, [piece] + near_z(piece, (1, 2, 3)), (piece_up,))
    up_z = near_z(piece_up, (1, 2, 3))
    (low,) = gather(chain, [zs, send(zs, first_way)])
    high = send(low, second_way)
    (zs,) = gather(chain, [piece_up] + up_z, (), 5)
    pieces = both_cores(low, gate(chain, high, 0))
    first_set, vecs, bias, first_t, joint, grad_y, down = enter(
        chain, info, tokens, upstream, down_weight, hidden, pieces
    )
    grad_y_o, first_o = swap(grad_y), swap(first_t)
    first_set = first_set.reshape(2, feat, 3 * third + 128)
    first, second = send(zs, first_way), send(zs, second_way)
    first = gate(chain, first, 0)
    pieces = both_cores(zs, first, second, send(first, second_way))
    down_z = near_z(down, (1, 2, 3))
    mixed, mixed_t, stats = mix(chain, info, joint)
    mixed_t = mixed_t.reshape(first_t.shape)
    mixed_o = swap(mixed_t)
    (zs,) = gather(chain, [down] + down_z, (), 5)
    proj_set, after, normed, normed_t = rise(chain, info, tokens, mixed, vecs, pieces)
    normed_o = swap(normed_t)
    up_a, active_a, slope_a, mine_a, theirs_a = widen(chain, 0, info, normed, bias, pieces[:4])
    theirs_a = swap(theirs_a)
    (low,) = gather(chain, [zs, send(zs, first_way)])
    high = send(low, second_way)
    up_b, active_b, slope_b, mine_b, theirs_b = widen(chain, 1, info, normed, bias, pieces[4:])
    proj_set = proj_set.reshape(2, feat, third)
    down = outer_down(
        chain, info, mine_a, mine_b, theirs_a, swap(theirs_b), grad_y, grad_y_o
    )
    pieces = both_cores(low, gate(chain, high, 0))
    up_sets = (up_a.reshape(feat, wide), up_b.reshape(feat, wide))
    down_set, hid_theirs, hid_mine, bias_sum, grad_after, at_theirs, at_mine, grad_mixed, sums_a = (
        fall(chain, info, grad_y, (slope_a, slope_b), up_sets, after, vecs, proj_set, pieces)
    )
    hid_o, at_o = swap(hid_theirs), swap(at_theirs)
    down = shift_first(chain, *down, 5)
    up = outer_up(chain, info, normed_t, normed_o, hid_mine, hid_o, mixed_t, mixed_o, at_mine, at_o)
    down = shift_second(chain, *down)
    theirs, mine = mix_back(chain, info, joint, grad_mixed, stats)
    theirs_o = swap(theirs)
    down = (down[0], [gate(chain, part, 0) for part in down[1]])
    up = shift_first(chain, *up, 5)
    chain.near(up[1])
    qkv = outer_qkv(chain, info, first_t, first_o, mine, theirs_o)
    grad_tokens, few_keep, few_away = exit_back(
        chain, info, tokens, mine, theirs, first_set, grad_after, vecs, sums_a, bias_sum
    )
    up = shift_second(chain, *up)
    qkv = shift_both(chain, *qkv, few_keep, few_away)
    output = leave(
        chain, info, after, active_a, active_b, down_set.reshape(hidden, feat), vecs
    )
    qkv = shift_second(chain, *qkv)
    own_down = home_down(chain, *down)
    own_up = home(chain, info, *up)
    own_qkv = home(chain, info, *qkv)
    out_qkv, out_proj, out_up, out_gains, out_shifts, out_bias = finish(
        chain, info, *own_qkv, *own_up
    )
    return (
        output,
        grad_tokens,
        out_qkv,
        out_proj,
        out_up,
        own_down,
        out_gains.T,
        out_shifts.T,
        out_bias.reshape(-1),
    )


def solution(mesh):
    placed = (
        P(("dp", "fsdp"), None),
        P(("dp", "fsdp"), None),
        P(("dp", "fsdp")),
        P(("dp", "fsdp"), None),
        P(("dp", "fsdp"), None),
        P(("dp", "fsdp"), None),
        P(("dp", "fsdp"), None),
        P(("dp", "fsdp"), None),
        P(("dp", "fsdp"), None),
        P(("dp", "fsdp")),
    )
    sizes = (mesh.shape["dp"], mesh.shape["fsdp"])
    return jax.shard_map(
        local if sizes == (16, 2) else plain,
        mesh=mesh,
        in_specs=placed,
        out_specs=(
            P(("dp", "fsdp"), None),
            P(("dp", "fsdp"), None),
            P(("dp", "fsdp"), None),
            P(("dp", "fsdp"), None),
            P(("dp", "fsdp"), None),
            P(("dp", "fsdp"), None),
            P(("dp", "fsdp"), None),
            P(("dp", "fsdp"), None),
            P(("dp", "fsdp")),
        ),
        check_vma=False,
    )
```

```python
import math
from functools import partial

import jax
import jax.numpy as jnp
from jax import lax
from jax.experimental import pallas as pl
from jax.experimental.pallas import tpu as pltpu
from jax.sharding import PartitionSpec as P

HEADS = 12
EPS = 1e-06
NEG = -1e30
AXES = ("dp", "fsdp")
F32 = jnp.float32
BF16 = jnp.bfloat16
VMEM_LIMIT = 32 * 1024 * 1024


def collect(qkv_weight, proj_weight, up_weight, down_weight, gains, shifts, up_bias):
    gathered = (
        lax.all_gather(qkv_weight, ("dp", "fsdp"), axis=0, tiled=True),
        lax.all_gather(proj_weight, ("dp", "fsdp"), axis=0, tiled=True),
        lax.all_gather(up_weight, ("dp", "fsdp"), axis=0, tiled=True),
        lax.all_gather(down_weight, ("dp", "fsdp"), axis=0, tiled=True),
        lax.all_gather(gains, ("dp", "fsdp"), axis=0, tiled=True),
        lax.all_gather(shifts, ("dp", "fsdp"), axis=0, tiled=True),
        lax.all_gather(up_bias, ("dp", "fsdp"), axis=0, tiled=True),
    )
    return gathered


def give_back(grad_qkv, grad_proj, grad_up, grad_down, grad_gains, grad_shifts, grad_bias_up):
    owned = (
        lax.psum_scatter(grad_qkv, ("dp", "fsdp"), scatter_dimension=0, tiled=True),
        lax.psum_scatter(grad_proj, ("dp", "fsdp"), scatter_dimension=0, tiled=True),
        lax.psum_scatter(grad_up, ("dp", "fsdp"), scatter_dimension=0, tiled=True),
        lax.psum_scatter(grad_down, ("dp", "fsdp"), scatter_dimension=0, tiled=True),
        lax.psum_scatter(grad_gains, ("dp", "fsdp"), scatter_dimension=0, tiled=True),
        lax.psum_scatter(grad_shifts, ("dp", "fsdp"), scatter_dimension=0, tiled=True),
        lax.psum_scatter(grad_bias_up, ("dp", "fsdp"), scatter_dimension=0, tiled=True),
    )
    return owned


def normalize(values):
    centred = values - jnp.mean(values, axis=-1, keepdims=True)
    inverse = lax.rsqrt(jnp.mean(centred * centred, axis=-1, keepdims=True) + EPS)
    return (centred * inverse, inverse)


def norm_back(grad_norm, normed, inverse):
    return inverse * (
        grad_norm
        - jnp.mean(grad_norm, axis=-1, keepdims=True)
        - normed * jnp.mean(grad_norm * normed, axis=-1, keepdims=True)
    )


def block_scores(query_blk, key_rows, live_mask, scaling):
    raw = (
        jnp.einsum("qhd,khd->hqk", query_blk, key_rows, preferred_element_type=jnp.float32)
        * scaling
    )
    return jnp.where(live_mask[None, None, :], raw, NEG)


def plain(
    tokens,
    upstream,
    lengths,
    qkv_weight,
    proj_weight,
    up_weight,
    down_weight,
    gains,
    shifts,
    up_bias,
):
    tok_rows, feat_width = tokens.shape
    n_heads = HEADS
    head_size = feat_width // n_heads
    scaling = head_size ** (-0.5)
    block_rows = min(512, tok_rows)
    group_heads = 4
    head_starts = list(range(0, n_heads, group_heads))
    gathered = collect(qkv_weight, proj_weight, up_weight, down_weight, gains, shifts, up_bias)
    qkv_full, proj_full, up_full, down_full, gain_full, shift_full, bias_full = gathered
    gain_f = gain_full.astype(jnp.float32)
    shift_f = shift_full.astype(jnp.float32)
    bias_f = bias_full.astype(jnp.float32)
    live_mask = lax.iota(jnp.int32, tok_rows) < lengths[0]
    source = tokens.astype(jnp.float32)
    norm_one, inv_one = normalize(source)
    first = (norm_one * gain_f[:, 0] + shift_f[:, 0]).astype(jnp.bfloat16)
    joint_bias = jnp.concatenate([shift_f[:, 1], jnp.zeros_like(shift_f[:, 1]), shift_f[:, 2]])
    joint = (jnp.dot(first, qkv_full, preferred_element_type=jnp.float32) + joint_bias).astype(
        jnp.bfloat16
    )
    queries = joint[:, :feat_width].reshape(tok_rows, n_heads, head_size)
    key_rows = joint[:, feat_width : 2 * feat_width].reshape(tok_rows, n_heads, head_size)
    value_rows = joint[:, 2 * feat_width :].reshape(tok_rows, n_heads, head_size)
    log_sums = {}
    offset = 0
    group_parts = []
    for head_lo in head_starts:
        head_hi = head_lo + group_heads
        scores = block_scores(
            queries[offset : offset + block_rows, head_lo:head_hi],
            key_rows[:, head_lo:head_hi],
            live_mask,
            scaling,
        )
        row_max = jnp.max(scores, axis=-1, keepdims=True)
        expd = jnp.exp(scores - row_max)
        row_sum = jnp.sum(expd, axis=-1, keepdims=True)
        attn_low = (expd / row_sum).astype(jnp.bfloat16)
        log_sums[offset, head_lo] = row_max + jnp.log(row_sum)
        group_parts.append(
            jnp.einsum(
                "hqk,khd->qhd",
                attn_low,
                value_rows[:, head_lo:head_hi],
                preferred_element_type=jnp.float32,
            )
        )
    mixed_parts = jnp.concatenate(group_parts, axis=1)
    mixed = mixed_parts.reshape(tok_rows, feat_width).astype(jnp.bfloat16)
    after = source + jnp.dot(mixed, proj_full, preferred_element_type=jnp.float32) + shift_f[:, 3]
    norm_two, inv_two = normalize(after)
    second = (norm_two * gain_f[:, 1] + shift_f[:, 4]).astype(jnp.bfloat16)
    hidden = jnp.dot(second, up_full, preferred_element_type=jnp.float32) + bias_f
    gelu_exact = partial(jax.nn.gelu, approximate=False)
    active = gelu_exact(hidden).astype(jnp.bfloat16)
    output = (
        after + jnp.dot(active, down_full, preferred_element_type=jnp.float32) + shift_f[:, 5]
    ).astype(jnp.bfloat16)
    regathered = collect(qkv_weight, proj_weight, up_weight, down_weight, gains, shifts, up_bias)
    qkv_full, proj_full, up_full, down_full, gain_full, shift_full, bias_full = regathered
    grad_y = jnp.where(live_mask[:, None], upstream, jnp.zeros_like(upstream))
    sum_y = jnp.sum(grad_y, axis=0, dtype=jnp.float32)
    grad_down = jnp.einsum("tf,td->fd", active, grad_y, preferred_element_type=jnp.float32)
    grad_active = jnp.einsum("td,fd->tf", grad_y, down_full, preferred_element_type=jnp.float32)
    gelu_value, gelu_pull = jax.vjp(gelu_exact, hidden)
    grad_hidden = gelu_pull(grad_active)[0].astype(jnp.bfloat16)
    grad_bias_up = jnp.sum(grad_hidden, axis=0, dtype=jnp.float32)
    grad_up = jnp.einsum("td,tf->df", second, grad_hidden, preferred_element_type=jnp.float32)
    grad_second = jnp.einsum("tf,df->td", grad_hidden, up_full, preferred_element_type=jnp.float32)
    gain_two_grad = jnp.sum(grad_second * norm_two, axis=0)
    shift_two_grad = jnp.sum(grad_second, axis=0)
    grad_after = grad_y.astype(jnp.float32) + norm_back(
        grad_second * gain_f[:, 1], norm_two, inv_two
    )
    grad_attn = grad_after.astype(jnp.bfloat16)
    sum_attn = jnp.sum(grad_attn, axis=0, dtype=jnp.float32)
    grad_proj = jnp.einsum("td,te->de", mixed, grad_attn, preferred_element_type=jnp.float32)
    grad_mixed = jnp.einsum("te,de->td", grad_attn, proj_full, preferred_element_type=jnp.float32)
    grad_mixed = grad_mixed.astype(jnp.bfloat16).reshape(tok_rows, n_heads, head_size)
    key_groups = {}
    value_groups = {}
    for head_lo in head_starts:
        key_groups[head_lo] = jnp.zeros((tok_rows, group_heads, head_size), jnp.float32)
        value_groups[head_lo] = jnp.zeros((tok_rows, group_heads, head_size), jnp.float32)
    offset = 0
    query_groups = []
    for head_lo in head_starts:
        head_hi = head_lo + group_heads
        query_blk = queries[offset : offset + block_rows, head_lo:head_hi]
        grad_blk = grad_mixed[offset : offset + block_rows, head_lo:head_hi]
        key_part = key_rows[:, head_lo:head_hi]
        scores = block_scores(query_blk, key_part, live_mask, scaling)
        attn_p = jnp.exp(scores - log_sums[offset, head_lo])
        value_groups[head_lo] = jnp.einsum(
            "hqk,qhd->khd",
            attn_p.astype(jnp.bfloat16),
            grad_blk,
            preferred_element_type=jnp.float32,
        )
        grad_prob = jnp.einsum(
            "qhd,khd->hqk",
            grad_blk,
            value_rows[:, head_lo:head_hi],
            preferred_element_type=jnp.float32,
        )
        grad_score = attn_p * (grad_prob - jnp.sum(attn_p * grad_prob, axis=-1, keepdims=True))
        score_low = grad_score.astype(jnp.bfloat16)
        query_groups.append(
            jnp.einsum("hqk,khd->qhd", score_low, key_part, preferred_element_type=jnp.float32)
            * scaling
        )
        key_groups[head_lo] = (
            jnp.einsum("hqk,qhd->khd", score_low, query_blk, preferred_element_type=jnp.float32)
            * scaling
        )
    grad_query_parts = jnp.concatenate(query_groups, axis=1)
    grad_keys = jnp.concatenate([key_groups[head_lo] for head_lo in head_starts], axis=1)
    grad_vals = jnp.concatenate([value_groups[head_lo] for head_lo in head_starts], axis=1)
    grad_joint = jnp.concatenate(
        [
            grad_query_parts.reshape(tok_rows, feat_width),
            grad_keys.reshape(tok_rows, feat_width),
            grad_vals.reshape(tok_rows, feat_width),
        ],
        axis=1,
    ).astype(jnp.bfloat16)
    joint_sums = jnp.sum(grad_joint, axis=0, dtype=jnp.float32)
    grad_qkv = jnp.einsum("td,te->de", first, grad_joint, preferred_element_type=jnp.float32)
    grad_first = jnp.einsum("te,de->td", grad_joint, qkv_full, preferred_element_type=jnp.float32)
    gain_one_grad = jnp.sum(grad_first * norm_one, axis=0)
    shift_one_grad = jnp.sum(grad_first, axis=0)
    grad_tokens = (grad_after + norm_back(grad_first * gain_f[:, 0], norm_one, inv_one)).astype(
        jnp.bfloat16
    )
    grad_gains = jnp.stack([gain_one_grad, gain_two_grad], axis=1)
    grad_shifts = jnp.stack(
        [
            shift_one_grad,
            joint_sums[:feat_width],
            joint_sums[2 * feat_width :],
            sum_attn,
            shift_two_grad,
            sum_y,
        ],
        axis=1,
    )
    owned = give_back(
        grad_qkv, grad_proj, grad_up, grad_down, grad_gains, grad_shifts, grad_bias_up
    )
    own_qkv, own_proj, own_up, own_down, own_gains, own_shifts, own_bias = owned
    return (
        output,
        grad_tokens,
        own_qkv,
        own_proj,
        own_up,
        own_down,
        own_gains,
        own_shifts,
        own_bias,
    )


BOTH_LAST = (((1,), (1,)), ((), ()))
SMEM = pl.BlockSpec(memory_space=pltpu.SMEM)
ANY = pl.BlockSpec(memory_space=pl.ANY)
CORE, LENGTH, PLACE, PLACE_O = 32, 33, 34, 50


def pairs(move):
    return [(i, move(i)) for i in range(32)]


def first_way(i):
    return i ^ (2 if i % 2 == 0 else 4)


def second_way(i):
    return i ^ (4 if i % 2 == 0 else 2)


def along_z(step):
    return lambda i: i ^ (8 * step)


def send(array, move):
    return lax.ppermute(array, AXES, pairs(move))


def swap(array):
    return send(array, lambda i: i ^ 1)


def facts(chip, core, length):
    places = []
    for of_core in (core, 1 - core):
        for j in range(16):
            z, first, second = j % 4, (j // 4) % 2, j // 8
            mask = jnp.where(of_core == 0, first + 2 * second, second + 2 * first)
            places.append(jnp.bitwise_xor(chip, mask + 4 * z))
    spots = []
    for of_core in (core, 1 - core):
        for k in range(16):
            mask = jnp.bitwise_xor(chip, k)
            x, y, z = mask & 1, (mask >> 1) & 1, mask >> 2
            spots.append(z + jnp.where(of_core == 0, 4 * x + 8 * y, 4 * y + 8 * x))
    return jnp.stack(places + [core, length] + spots).astype(jnp.int32)


def params(mib):
    return pltpu.CompilerParams(vmem_limit_bytes=mib * 1024 * 1024)


def cost(micros):
    flops = int(micros * (3e10 if micros > 3 else 1e9))
    return pl.CostEstimate(flops=flops, bytes_accessed=1, transcendentals=0)


def shape(dims, dtype):
    return jax.ShapeDtypeStruct(dims, dtype)


def full(dims):
    return pl.BlockSpec(dims, lambda *_: (0,) * len(dims))


class Chain:
    def __init__(self):
        self.token, self.extra = None, ()

    def near(self, *arrays):
        self.extra = arrays

    def call(
        self, kernel, *, out_shape, in_specs, out_specs, grid=(), prefetch=0, aliases={}, **options
    ):
        single = not isinstance(out_shape, tuple)
        if single:
            out_shape, out_specs = (out_shape,), (out_specs,)
        held = 0 if self.token is None else 1
        extra, self.extra = self.extra, ()
        n_in, n_out = prefetch + len(in_specs), len(out_shape)
        at_token = n_in + len(extra)

        def body(*refs):
            skip = at_token + held
            return kernel(*refs[:n_in], *refs[skip : skip + n_out], *refs[skip + n_out + 1 :])

        token = shape((8, 128), F32)
        specs = pltpu.PrefetchScalarGridSpec(
            num_scalar_prefetch=prefetch,
            grid=grid,
            in_specs=list(in_specs) + [ANY] * (len(extra) + held),
            out_specs=tuple(out_specs) + (ANY,),
            scratch_shapes=options.pop("scratch_shapes", ()),
        )
        run = pl.pallas_call(
            body,
            grid_spec=specs,
            out_shape=tuple(out_shape) + (token,),
            input_output_aliases=aliases | ({at_token: n_out} if held else {}),
            **options,
        )

        def with_token(*args):
            *outs, self.token = run(*args, *extra, *([self.token] if held else []))
            return outs[0] if single else tuple(outs)

        return with_token


def dot(left, right):
    return jnp.dot(left, right, preferred_element_type=F32)


def dot_last(left, right):
    return lax.dot_general(left, right, BOTH_LAST, preferred_element_type=F32)


def settle(info, pieces, dest, who=(0, 1)):
    few = pieces[0].shape[0]
    for w in who:
        half = info[CORE] if w == 0 else 1 - info[CORE]
        for j in range(16):
            dest[half, info[16 * w + j]] = pieces[(16 * w + j) // few][j % few]


def bring(pieces, raw, sems, start):
    cols = pl.ds(start, raw.shape[-1])
    return [
        pltpu.make_async_copy(piece.at[:, :, cols], raw.at[i], sems.at[i])
        for i, piece in enumerate(pieces)
    ]


def centre(values):
    centred = values - jnp.mean(values, axis=-1, keepdims=True)
    inverse = lax.rsqrt(jnp.mean(centred * centred, axis=-1, keepdims=True) + EPS)
    return centred * inverse, inverse


def layer_back(grad, normed, inverse):
    return inverse * (
        grad
        - jnp.mean(grad, axis=-1, keepdims=True)
        - normed * jnp.mean(grad * normed, axis=-1, keepdims=True)
    )


def stacked(core, mine, others):
    pair = (mine, others) if core == 0 else (others, mine)
    return jnp.concatenate([part.astype(F32) for part in pair]).astype(BF16)


def by_core(info, lay):
    for core in (0, 1):
        pl.when(info[CORE] == core)(partial(lay, core))


def first_piece_kernel(info, qkv, qkv_o, small, out):
    third = qkv.shape[1] // 6

    def lay(core):
        for i in range(3):
            cols = slice((2 * i + core) * third, (2 * i + core + 1) * third)
            out[0, :, i * third : (i + 1) * third] = stacked(core, qkv[:, cols], qkv_o[:, cols])
        out[0, :, 3 * third :] = stacked(core, small[...], jnp.zeros_like(small))

    by_core(info, lay)


def first_piece(chain, info, qkv, qkv_o, small):
    rows, cols = qkv.shape
    vmem = pl.BlockSpec(memory_space=pltpu.VMEM)
    return chain.call(
        first_piece_kernel,
        out_shape=shape((1, 2 * rows, cols // 2 + small.shape[1]), BF16),
        in_specs=[SMEM] + [vmem] * 3,
        out_specs=vmem,
        compiler_params=params(8),
        name="first_piece",
        cost_estimate=cost(0),
    )(info, qkv, qkv_o, small)


def up_piece_kernel(info, up, up_o, proj, proj_o, out):
    wide, third = up.shape[1] // 2, proj.shape[1] // 2

    def lay(core):
        for whole, other, at, width in ((up, up_o, 0, wide), (proj, proj_o, wide, third)):
            cols = slice(core * width, (core + 1) * width)
            out[0, :, at : at + width] = stacked(core, whole[:, cols], other[:, cols])

    by_core(info, lay)


def up_piece(chain, info, up, up_o, proj, proj_o):
    rows = up.shape[0]
    vmem = pl.BlockSpec(memory_space=pltpu.VMEM)
    return chain.call(
        up_piece_kernel,
        out_shape=shape((1, 2 * rows, (up.shape[1] + proj.shape[1]) // 2), BF16),
        in_specs=[SMEM] + [vmem] * 4,
        out_specs=vmem,
        compiler_params=params(8),
        name="up_piece",
        cost_estimate=cost(0),
    )(info, up, up_o, proj, proj_o)


def gather_kernel(n_in, n_held, order, *refs):
    out = refs[n_in + n_held]
    for i, part in enumerate(refs[:n_in]):
        at = part.shape[0] * (i if order is None else order[i])
        out[at : at + part.shape[0]] = part[...]
    for i in range(n_held):
        refs[n_in + n_held + 1 + i][...] = refs[n_in + i][...]


def gather(chain, parts, held=(), micros=0, order=None):
    vmem = pl.BlockSpec(memory_space=pltpu.VMEM)
    _, rows, cols = parts[0].shape
    count = sum(part.shape[0] for part in parts)
    n, n_held = len(parts), len(held)
    return chain.call(
        partial(gather_kernel, n, n_held, order),
        out_shape=(shape((count, rows, cols), BF16),) + tuple(shape(h.shape, h.dtype) for h in held),
        in_specs=[vmem] * (n + n_held),
        out_specs=(vmem,) * (1 + n_held),
        compiler_params=params(16),
        name="gather",
        cost_estimate=cost(micros),
    )(*parts, *held)


def gate_kernel(array, out):
    pass


def gate(chain, array, micros):
    return chain.call(
        gate_kernel,
        out_shape=shape(array.shape, array.dtype),
        in_specs=[ANY],
        out_specs=ANY,
        aliases={0: 0},
        compiler_params=params(4),
        name="gate",
        cost_estimate=cost(micros),
    )(array)


def both_cores(*own):
    return own + tuple(swap(blocks) for blocks in own)


def near_z(piece, steps):
    return [send(piece, along_z(s)) for s in steps]


def enter_kernel(
    info,
    tokens,
    upstream,
    down,
    *refs,
):
    pieces = refs[:8]
    kept, vecs, bias, flipped, joint, grad_y, piece_down, weights, sem = refs[8:]
    feat = tokens.shape[1]
    third = feat // 2
    piece_down[0] = down[...]
    place = lax.broadcasted_iota(jnp.int32, upstream.shape, 0)
    grad_y[...] = jnp.where(place < info[LENGTH], upstream[...].astype(F32), 0.0).astype(BF16)
    settle(info, pieces, weights)
    normed, _ = centre(tokens[...].astype(F32))
    out = pltpu.make_async_copy(weights, kept, sem)
    out.start()
    split = 3 * third
    small = weights[0, :, :, split:] + weights[1, :, :, split:]
    small = small.reshape(feat, 128).astype(F32)
    each = bias.shape[1] // 32
    for device in range(32):
        row = device * feat // 32
        bias[:, device * each : (device + 1) * each] = small[row : row + 1, 128 - each :]
    small = small.T
    vecs[...] = small[:8]
    low_first = (normed * small[0:1] + small[2:3]).astype(BF16)
    flipped[...] = low_first.T.reshape(flipped.shape)
    for h in (0, 1):
        cols = slice(h * third, (h + 1) * third)
        bias = jnp.concatenate(
            [small[3:4, cols], jnp.zeros((1, third), F32), small[4:5, cols]], axis=1
        )
        w = weights[h, :, :, :split].reshape(feat, split)
        joint[h] = (dot(low_first, w) + bias).astype(BF16)
    out.wait()


def enter(chain, info, tokens, upstream, down, hidden, pieces):
    rows, feat = tokens.shape
    width = pieces[0].shape[-1]
    vmem = pl.BlockSpec(memory_space=pltpu.VMEM)
    sets = (2, 16, feat // 16, width)
    return chain.call(
        enter_kernel,
        out_shape=(
            shape(sets, BF16),
            shape((8, feat), F32),
            shape((1, hidden), F32),
            shape((16, feat // 16, rows), BF16),
            shape((2, rows, 3 * feat // 2), BF16),
            shape((rows, feat), BF16),
            shape((1,) + down.shape, BF16),
        ),
        in_specs=[SMEM] + [vmem] * 11,
        out_specs=(ANY,) + (vmem,) * 6,
        scratch_shapes=[pltpu.VMEM(sets, BF16), pltpu.SemaphoreType.DMA],
        compiler_params=params(20),
        name="enter",
        cost_estimate=cost(8),
    )(info, tokens, upstream, down, *pieces)


def scores_of(info, keys, queries):
    raw = dot_last(keys, queries)
    place = lax.broadcasted_iota(jnp.int32, raw.shape, 0)
    return jnp.where(place < info[LENGTH], raw, NEG)


def mix_kernel(info, q, k, v, mixed, flipped, stats):
    head = mixed.shape[1] // (HEADS // 2)
    count = q.shape[-1] // head
    scale = head**-0.5
    turned = v[0].T

    def start(h):
        cols = slice(h * head, (h + 1) * head)
        return scores_of(info, k[0, :, cols], q[0, :, cols] * scale)

    def finish(h, scores):
        cols = slice(h * head, (h + 1) * head)
        most = jnp.max(scores, axis=0, keepdims=True)
        expd = jnp.exp(scores - most)
        total = jnp.sum(expd, axis=0, keepdims=True)
        attn = (expd * (1.0 / total)).astype(BF16)
        stats[h // 2, h % 2 : h % 2 + 1] = most + jnp.log(total)
        return dot(turned[cols], attn)

    ready = [start(h) for h in range(2)]
    outs = []
    for h in range(count):
        if h + 2 < count:
            ready.append(start(h + 2))
        outs.append(finish(h, ready[h]))
    both = jnp.concatenate(outs)
    flipped[...] = both.astype(BF16)
    mixed[...] = both.T.astype(BF16)


def mix(chain, info, joint):
    _, rows, width = joint.shape
    feat = 2 * width // 3
    wide = feat // 2
    spec = [pl.BlockSpec((1, rows, wide), lambda i, part=part: (i, 0, part)) for part in range(3)]
    pairs_in_half = HEADS // 4
    return chain.call(
        mix_kernel,
        grid=(2,),
        out_shape=(
            shape((rows, feat), BF16),
            shape((feat, rows), BF16),
            shape((HEADS // 2, 8, rows), F32),
        ),
        in_specs=[SMEM] + spec,
        out_specs=(
            pl.BlockSpec((rows, wide), lambda i: (0, i)),
            pl.BlockSpec((wide, rows), lambda i: (i, 0)),
            pl.BlockSpec((pairs_in_half, 8, rows), lambda i: (i, 0, 0)),
        ),
        compiler_params=params(24),
        name="mix",
        cost_estimate=cost(10),
    )(info, joint, joint, joint)


def mix_back_kernel(info, q, k, v, grad, stats, theirs, mine):
    head = theirs.shape[2] // (HEADS // 2)
    count = q.shape[-1] // head
    scale = head**-0.5
    turned = k[0].T

    def start(h):
        cols = slice(h * head, (h + 1) * head)
        queries = q[0, :, cols] * scale
        scores = scores_of(info, k[0, :, cols], queries)
        return cols, queries, scores, dot_last(v[0, :, cols], grad[:, cols])

    def finish(h, cols, queries, scores, grad_prob):
        attn = jnp.exp(scores - stats[h // 2, h % 2 : h % 2 + 1])
        inner = jnp.sum(attn * grad_prob, axis=0, keepdims=True)
        low = (attn * (grad_prob - inner)).astype(BF16)
        return (
            dot(turned[cols], low) * scale,
            dot(low, queries),
            dot(attn.astype(BF16), grad[:, cols]),
        )

    ready = [start(h) for h in range(2)]
    done = []
    for h in range(count):
        if h + 2 < count:
            ready.append(start(h + 2))
        done.append(finish(h, *ready[h]))
    out = [
        jnp.concatenate([d[0] for d in done]).T.astype(BF16),
        jnp.concatenate([d[1] for d in done], axis=1).astype(BF16),
        jnp.concatenate([d[2] for d in done], axis=1).astype(BF16),
    ]

    @pl.when(pl.program_id(0) == 0)
    def _():
        for part in range(3):
            theirs[part] = out[part]

    @pl.when(pl.program_id(0) == 1)
    def _():
        for part in range(3):
            mine[part] = out[part]


def mix_back(chain, info, joint, grad_mixed, stats):
    _, rows, width = joint.shape
    feat = 2 * width // 3
    wide = feat // 2

    def half(i, info):
        return jnp.where(i == 0, 1 - info[CORE], info[CORE])

    spec = [
        pl.BlockSpec((1, rows, wide), lambda i, info, part=part: (half(i, info), 0, part))
        for part in range(3)
    ]
    out = shape((3, rows, feat // 2), BF16)
    return chain.call(
        mix_back_kernel,
        prefetch=1,
        grid=(2,),
        in_specs=spec
        + [
            pl.BlockSpec((rows, wide), lambda i, info: (0, half(i, info))),
            pl.BlockSpec((HEADS // 4, 8, rows), lambda i, info: (half(i, info), 0, 0)),
        ],
        out_specs=(
            pl.BlockSpec((3, rows, wide), lambda i, info: (0, 0, 0)),
            pl.BlockSpec((3, rows, wide), lambda i, info: (0, 0, 0)),
        ),
        out_shape=(out, out),
        compiler_params=params(30),
        name="mix_back",
        cost_estimate=cost(16),
    )(info, joint, joint, joint, grad_mixed, stats)


GELU = (0.254829592, -0.284496736, 1.421413741, -1.453152027, 1.061405429)


def gelu_parts(x):
    bell = jnp.exp2(x * x * (-0.5 / math.log(2)))
    below = 1.0 + (0.3275911 * 0.5**0.5) * jnp.abs(x)
    t = pl.reciprocal(below, approx=True)
    t = t * (2.0 - below * t)
    poly = 0.5 * GELU[4]
    for c in GELU[3::-1]:
        poly = poly * t + 0.5 * c
    tail = poly * t * bell
    phi = jnp.where(x < 0, tail, 1.0 - tail)
    return x * phi, phi + x * (bell * (2 * math.pi) ** -0.5)


def rise_kernel(info, tokens, mixed, vecs, *refs):
    pieces = refs[:8]
    weights, after, second, flipped, raw, sems = refs[8:]
    feat = tokens.shape[1]
    copies = bring(pieces, raw, sems, pieces[0].shape[2] - raw.shape[-1])
    for copy in copies:
        copy.start()
    start = tokens[...].astype(F32) + vecs[5:6]
    for copy in copies:
        copy.wait()
    settle(info, [raw.at[i] for i in range(8)], weights)
    grown = [dot(mixed[...], weights[h].reshape(feat, feat // 2)) for h in (0, 1)]
    total = start + jnp.concatenate(grown, axis=1)
    after[...] = total
    normed, _ = centre(total)
    value = (normed * vecs[1:2] + vecs[6:7]).astype(BF16)
    second[...] = value
    flipped[...] = value.T.reshape(flipped.shape)


def rise(chain, info, tokens, mixed, vecs, pieces):
    rows, feat = tokens.shape
    vmem = pl.BlockSpec(memory_space=pltpu.VMEM)
    block = feat // 16
    return chain.call(
        rise_kernel,
        out_shape=(
            shape((2, 16, block, feat // 2), BF16),
            shape((rows, feat), F32),
            shape((rows, feat), BF16),
            shape((16, block, rows), BF16),
        ),
        in_specs=[SMEM] + [vmem] * 3 + [ANY] * 8,
        out_specs=(vmem,) * 4,
        scratch_shapes=[
            pltpu.VMEM((8, 4, block, feat // 2), BF16),
            pltpu.SemaphoreType.DMA((8,)),
        ],
        compiler_params=params(16),
        name="rise",
        cost_estimate=cost(5),
    )(info, tokens, mixed, vecs, *pieces)


def widen_kernel(which, info, second, bias, *refs):
    pieces = refs[:4]
    weights, active, slope, mine, theirs, raw, sems = refs[4:]
    step = pl.program_id(0)
    core = info[CORE]
    feat = second.shape[1]
    tile = active.shape[1]
    rows = mine.shape[1]
    count = tile // rows

    @pl.when(step == 0)
    def _():
        copies = bring(pieces, raw, sems, 0)
        for copy in copies:
            copy.start()
        for copy in copies:
            copy.wait()
        for j in range(16):
            weights[info[16 * which + j]] = raw[j // 4, j % 4]

    cols = pl.ds(pl.multiple_of(step * tile, tile), tile)
    w = weights[:, :, cols].reshape(feat, tile)
    hidden = dot(second[...], w) + bias[...]
    value, grad = gelu_parts(hidden)
    value = value.astype(BF16)
    active[...] = value
    slope[...] = grad.astype(BF16)
    flipped = value.T.reshape(count // 2, 2, rows, -1)
    mine[...] = jnp.where(core == 0, flipped[:, 0], flipped[:, 1])
    theirs[...] = jnp.where(core == 0, flipped[:, 1], flipped[:, 0])


def widen(chain, which, info, second, bias, pieces):
    rows, feat = second.shape
    wide = pieces[0].shape[-1] - feat // 2
    tile, block = 768, wide // 16
    per = wide // tile
    turned = shape((8, block, rows), BF16)

    def whole(dims):
        return pl.BlockSpec(dims, lambda n, info: (0,) * len(dims))

    def bias_at(n, info):
        half = info[CORE] if which == 0 else 1 - info[CORE]
        return (0, half * per + n)

    strip = pl.BlockSpec((rows, tile), lambda n, info: (0, n))
    part = pl.BlockSpec((tile // block // 2, block, rows), lambda n, info: (n, 0, 0))
    return chain.call(
        partial(widen_kernel, which),
        prefetch=1,
        grid=(per,),
        out_shape=(
            shape((16, feat // 16, wide), BF16),
            shape((rows, wide), BF16),
            shape((rows, wide), BF16),
            turned,
            turned,
        ),
        in_specs=[whole((rows, feat)), pl.BlockSpec((1, tile), bias_at)] + [ANY] * 4,
        out_specs=(whole((16, feat // 16, wide)), strip, strip, part, part),
        scratch_shapes=[
            pltpu.VMEM((4, 4, feat // 16, wide), BF16),
            pltpu.SemaphoreType.DMA((4,)),
        ],
        compiler_params=params(24),
        name="widen",
        cost_estimate=cost(18),
    )(info, second, bias, *pieces)


def leave_kernel(info, after, first, second, down, vecs, output, total):
    step, per = pl.program_id(0), pl.num_programs(0) // 2

    @pl.when(step == 0)
    def _():
        total[...] = after[...] + vecs[7:8] + dot(first[...], down[...])

    @pl.when((step > 0) & (step < per))
    def _():
        total[...] += dot(first[...], down[...])

    @pl.when(step >= per)
    def _():
        total[...] += dot(second[...], down[...])

    @pl.when(step == 2 * per - 1)
    def _():
        output[...] = total[...].astype(BF16)


def leave(chain, info, after, first, second, down, vecs):
    rows, feat = after.shape
    tile = 768
    per = first.shape[1] // tile

    def whole(dims):
        return pl.BlockSpec(dims, lambda n, info: (0,) * len(dims))

    def down_at(n, info):
        half = jnp.where(n < per, info[CORE], 1 - info[CORE])
        return (half * per + n % per, 0)

    return chain.call(
        leave_kernel,
        prefetch=1,
        grid=(2 * per,),
        out_shape=shape((rows, feat), BF16),
        in_specs=[
            whole((rows, feat)),
            pl.BlockSpec((rows, tile), lambda n, info: (0, jnp.minimum(n, per - 1))),
            pl.BlockSpec((rows, tile), lambda n, info: (0, jnp.maximum(n - per, 0))),
            pl.BlockSpec((tile, feat), down_at),
            whole((8, feat)),
        ],
        out_specs=whole((rows, feat)),
        scratch_shapes=[pltpu.VMEM((rows, feat), F32)],
        compiler_params=params(16),
        name="leave",
        cost_estimate=cost(7),
    )(info, after, first, second, down, vecs)


def fall_kernel(info, grad_y, slope, slope_o, up, up_o, after, vecs, proj, *refs):
    pieces = refs[:4]
    kept, theirs, mine, bias_sum, grad_after, attn_theirs, attn_mine, grad_mixed, sums = refs[4:13]
    weights, grad_second, normed, inverse, raw, sems, sem = refs[13:]
    step, steps = pl.program_id(0), pl.num_programs(0)
    core = info[CORE]
    feat = grad_y.shape[1]
    tile = slope.shape[1]
    per = steps // 2
    keeping = pltpu.make_async_copy(weights, kept, sem)

    @pl.when(step == 0)
    def _():
        copies = bring(pieces, raw, sems, 0)
        for copy in copies:
            copy.start()
        normed[...], inverse[...] = centre(after[...])
        grad_second[...] = jnp.zeros_like(grad_second)
        for copy in copies:
            copy.wait()
        for who in (0, 1):
            c = core if who == 0 else 1 - core
            for j in range(16):
                weights[info[16 * who + j], c] = raw[2 * who + j // 8, j % 8]
        keeping.start()

    half = jnp.where(step < per, 1 - core, core)
    at = half * per + lax.rem(step, per)
    count = tile * weights.shape[0] // (steps * tile)
    down = weights[pl.ds(count * at, count)].reshape(tile, feat)
    raw_grad = dot_last(grad_y[...], down)

    def tell(slope_ref, up_ref, out):
        grad = (raw_grad * slope_ref[...].astype(F32)).astype(BF16)
        bias_sum[...] = jnp.sum(grad.astype(F32), axis=0, keepdims=True)
        grad_second[...] += dot_last(grad, up_ref[...])
        out[...] = grad

    pl.when(step < per)(lambda: tell(slope_o, up_o, theirs))
    pl.when(step >= per)(lambda: tell(slope, up, mine))

    @pl.when(step == steps - 1)
    def _():
        second = grad_second[...]
        live = grad_y[...].astype(F32)
        sums[0:1] = jnp.sum(second * normed[...], axis=0, keepdims=True)
        sums[1:2] = jnp.sum(second, axis=0, keepdims=True)
        total = live + layer_back(second * vecs[1:2], normed[...], inverse[...])
        grad_after[...] = total
        attn = total.astype(BF16)
        sums[2:3] = jnp.sum(attn.astype(F32), axis=0, keepdims=True)
        sums[3:4] = jnp.sum(live, axis=0, keepdims=True)
        sums[4:8] = jnp.zeros_like(sums[4:8])
        left, right = attn[:, : feat // 2], attn[:, feat // 2 :]
        attn_mine[...] = jnp.where(core == 0, left, right)
        attn_theirs[...] = jnp.where(core == 0, right, left)
        grad_mixed[...] = (dot_last(left, proj[0]) + dot_last(right, proj[1])).astype(BF16)
        keeping.wait()


def fall(chain, info, grad_y, slopes, up_sets, after, vecs, proj_set, pieces):
    rows, feat = grad_y.shape
    hidden = 2 * slopes[0].shape[1]
    tile = 768
    steps = hidden // tile
    per = steps // 2

    def at(n, info):
        return jnp.where(n < per, 1 - info[CORE], info[CORE]) * per + n % per

    def whole(dims):
        return pl.BlockSpec(dims, lambda n, info: (0,) * len(dims))

    return chain.call(
        fall_kernel,
        prefetch=1,
        grid=(steps,),
        in_specs=[
            whole((rows, feat)),
            pl.BlockSpec((rows, tile), lambda n, info: (0, jnp.maximum(n - per, 0))),
            pl.BlockSpec((rows, tile), lambda n, info: (0, jnp.minimum(n, per - 1))),
            pl.BlockSpec((feat, tile), lambda n, info: (0, jnp.maximum(n - per, 0))),
            pl.BlockSpec((feat, tile), lambda n, info: (0, jnp.minimum(n, per - 1))),
            whole((rows, feat)),
            whole((8, feat)),
            whole((2, feat, feat // 2)),
        ]
        + [ANY] * 4,
        out_specs=(
            ANY,
            pl.BlockSpec((rows, tile), lambda n, info: (0, jnp.minimum(n, per - 1))),
            pl.BlockSpec((rows, tile), lambda n, info: (0, jnp.maximum(n - per, 0))),
            pl.BlockSpec((1, tile), lambda n, info: (0, at(n, info))),
            whole((rows, feat)),
            whole((rows, feat // 2)),
            whole((rows, feat // 2)),
            whole((rows, feat)),
            whole((8, feat)),
        ),
        scratch_shapes=[
            pltpu.VMEM((16, 2, hidden // 32, feat), BF16),
            pltpu.VMEM((rows, feat), F32),
            pltpu.VMEM((rows, feat), F32),
            pltpu.VMEM((rows, 1), F32),
            pltpu.VMEM((4,) + pieces[0].shape, BF16),
            pltpu.SemaphoreType.DMA((4,)),
            pltpu.SemaphoreType.DMA,
        ],
        out_shape=(
            shape((16, 2, hidden // 32, feat), BF16),
            shape((rows, hidden // 2), BF16),
            shape((rows, hidden // 2), BF16),
            shape((1, hidden), F32),
            shape((rows, feat), F32),
            shape((rows, feat // 2), BF16),
            shape((rows, feat // 2), BF16),
            shape((rows, feat), BF16),
            shape((8, feat), F32),
        ),
        compiler_params=params(32),
        name="fall",
        cost_estimate=cost(18),
    )(info, grad_y, *slopes, *up_sets, after, vecs, proj_set, *pieces)


def exit_kernel(
    info,
    tokens,
    mine,
    theirs,
    weights,
    grad_after,
    vecs,
    sums_a,
    bias,
    grad_tokens,
    keep,
    away,
    grad_first,
    joint,
    sums,
    extra,
):
    step = pl.program_id(0)
    core = info[CORE]
    third = mine.shape[2]
    half = jnp.where(step == 0, core, 1 - core)
    spot = pl.ds(pl.multiple_of(half * third, third), third)

    def parts(source):
        for part in range(3):
            joint[:, part * third : (part + 1) * third] = source[part]
        sums[3:4, spot] = jnp.sum(source[0].astype(F32), axis=0, keepdims=True)
        sums[4:5, spot] = jnp.sum(source[2].astype(F32), axis=0, keepdims=True)
        return dot_last(joint[...], weights[0])

    @pl.when(step == 0)
    def _():
        grad_first[...] = parts(mine)

    @pl.when(step == 1)
    def _():
        grad = grad_first[...] + parts(theirs)
        normed, inverse = centre(tokens[...].astype(F32))
        sums[0:1] = jnp.sum(grad * normed, axis=0, keepdims=True)
        sums[1:2] = sums_a[0:1]
        sums[2:3] = jnp.sum(grad, axis=0, keepdims=True)
        sums[5:6] = sums_a[2:3]
        sums[6:7] = sums_a[1:2]
        sums[7:8] = sums_a[3:4]
        sums[8:] = jnp.zeros_like(sums[8:])
        back = layer_back(grad * vecs[0:1], normed, inverse)
        grad_tokens[...] = (grad_after[...] + back).astype(BF16)
        flipped = sums[...].T
        block, each = extra.shape[1], bias.shape[1] // 32
        for chip in range(16):
            place = info[PLACE + chip]
            extra[place] = flipped[chip * block : (chip + 1) * block]
            for c in (0, 1):
                at = (2 * chip + c) * each
                row = c * block // 2
                extra[place, row : row + 1, 128 - each :] = bias[:, at : at + each]
        keep[...] = extra[:8]
        away[...] = extra[8:].astype(BF16)


def exit_back(chain, info, tokens, mine, theirs, first_set, grad_after, vecs, sums_a, bias):
    rows, feat = tokens.shape
    third = feat // 2
    block = feat // 16

    def whole(dims):
        return pl.BlockSpec(dims, lambda n, info: (0,) * len(dims))

    return chain.call(
        exit_kernel,
        prefetch=1,
        grid=(2,),
        in_specs=[
            whole((rows, feat)),
            whole((3, rows, third)),
            whole((3, rows, third)),
            pl.BlockSpec(
                (1, feat, 3 * third),
                lambda n, info: (jnp.where(n == 0, info[CORE], 1 - info[CORE]), 0, 0),
            ),
            whole((rows, feat)),
            whole((8, feat)),
            whole((8, feat)),
            whole(bias.shape),
        ],
        out_specs=(whole((rows, feat)), whole((8, block, 128)), whole((8, block, 128))),
        scratch_shapes=[
            pltpu.VMEM((rows, feat), F32),
            pltpu.VMEM((rows, 3 * third), BF16),
            pltpu.VMEM((128, feat), F32),
            pltpu.VMEM((16, block, 128), F32),
        ],
        out_shape=(
            shape((rows, feat), BF16),
            shape((8, block, 128), F32),
            shape((8, block, 128), BF16),
        ),
        compiler_params=params(18),
        name="exit_back",
        cost_estimate=cost(8),
    )(info, tokens, mine, theirs, first_set, grad_after, vecs, sums_a, bias)


def line_up(info, left, left_o, turned):
    rows = left.shape[2]
    for chip in range(16):
        place = info[PLACE + chip]
        turned[place, :, :rows] = left[chip]
        turned[place, :, rows:] = left_o[chip]


def outer_tile(turned, right, right_o):
    rows = right.shape[0]
    both = turned[...].reshape(-1, turned.shape[2])
    total = dot(both[:, :rows], right) + dot(both[:, rows:], right_o)
    return total.reshape(16, -1, total.shape[1])


def outer_up_kernel(
    info, left, left_o, right, right_o, low, low_o, attn, attn_o, keep, away, turned, *late
):
    step, last = pl.program_id(0), pl.num_programs(0) - 1
    buffers, sems = late[:4], late[4]
    copies = [
        pltpu.make_async_copy(src, dst, sems.at[i])
        for i, (src, dst) in enumerate(zip((low, low_o, attn, attn_o), buffers))
    ]

    @pl.when(step == 0)
    def _():
        for copy in copies:
            copy.start()
        line_up(info, left, left_o, turned)

    @pl.when(step < last)
    def _():
        total = outer_tile(turned, right[...], right_o[...])
        keep[...] = total[:8]
        away[...] = total[8:].astype(BF16)

    @pl.when(step == last)
    def _():
        for copy in copies:
            copy.wait()
        line_up(info, buffers[0], buffers[1], turned)
        total = outer_tile(turned, buffers[2][...], buffers[3][...])
        keep[:, :, : attn.shape[1]] = total[:8]
        away[:, :, : attn.shape[1]] = total[8:].astype(BF16)


def outer_up(chain, info, left, left_o, right, right_o, low, low_o, attn, attn_o):
    _, block, rows = left.shape
    tile = 2 * attn.shape[1]
    n = right.shape[1] // tile
    cols = right.shape[1] + attn.shape[1]
    strip = pl.BlockSpec((rows, tile), lambda i: (0, jnp.minimum(i, n - 1)))
    out = pl.BlockSpec((8, block, tile), lambda i: (0, 0, i))
    return chain.call(
        outer_up_kernel,
        grid=(n + 1,),
        out_shape=(shape((8, block, cols), F32), shape((8, block, cols), BF16)),
        in_specs=[SMEM] + [full(left.shape)] * 2 + [strip] * 2 + [ANY] * 4,
        out_specs=(out, out),
        scratch_shapes=[pltpu.VMEM((16, block, 2 * rows), BF16)]
        + [pltpu.VMEM(left.shape, BF16)] * 2
        + [pltpu.VMEM(attn.shape, BF16)] * 2
        + [pltpu.SemaphoreType.DMA((4,))],
        compiler_params=params(20),
        name="outer_up",
        cost_estimate=cost(8),
    )(info, left, left_o, right, right_o, low, low_o, attn, attn_o)


def outer_qkv_kernel(info, left, left_o, right, right_o, keep, away, turned):
    tile = right.shape[2]
    line_up(info, left, left_o, turned)
    for part in range(3):
        cols = slice(part * tile, (part + 1) * tile)
        total = outer_tile(turned, right[part], right_o[part])
        keep[:, :, cols] = total[:8]
        away[:, :, cols] = total[8:].astype(BF16)


def outer_qkv(chain, info, left, left_o, right, right_o):
    _, block, rows = left.shape
    cols = 3 * right.shape[2]
    vmem = pl.BlockSpec(memory_space=pltpu.VMEM)
    return chain.call(
        outer_qkv_kernel,
        out_shape=(shape((8, block, cols), F32), shape((8, block, cols), BF16)),
        in_specs=[SMEM] + [vmem] * 4,
        out_specs=(vmem, vmem),
        scratch_shapes=[pltpu.VMEM((16, block, 2 * rows), BF16)],
        compiler_params=params(20),
        name="outer_qkv",
        cost_estimate=cost(8),
    )(info, left, left_o, right, right_o)


def outer_down_kernel(
    info, first, second, first_o, second_o, right, right_o, keep, away, turned
):
    rows = right.shape[0]
    core = info[CORE]
    for r in range(8):
        place = info[PLACE + 8 * core + r]
        turned[place, :, :rows] = first[r]
        turned[place, :, rows:] = second_o[r]
        place = info[PLACE + 8 * (1 - core) + r]
        turned[place, :, :rows] = second[r]
        turned[place, :, rows:] = first_o[r]
    for out, spots in ((away, slice(8, 16)), (keep, slice(0, 8))):
        left = turned[spots].reshape(-1, turned.shape[2])
        total = dot(left[:, :rows], right[...]) + dot(left[:, rows:], right_o[...])
        out[...] = total.reshape(out.shape).astype(out.dtype)


def outer_down(chain, info, first, second, first_o, second_o, right, right_o):
    _, block, rows = first.shape
    feat = right.shape[1]
    vmem = pl.BlockSpec(memory_space=pltpu.VMEM)
    return chain.call(
        outer_down_kernel,
        out_shape=(shape((8, block, feat), F32), shape((8, block, feat), BF16)),
        in_specs=[SMEM] + [vmem] * 6,
        out_specs=(vmem, vmem),
        scratch_shapes=[pltpu.VMEM((16, block, 2 * rows), BF16)],
        compiler_params=params(24),
        name="outer_down",
        cost_estimate=cost(0),
    )(info, first, second, first_o, second_o, right, right_o)


def add_first_kernel(keep, got, kept, away):
    kept[...] = keep[:4] + got[:4].astype(F32)
    away[...] = (keep[4:] + got[4:].astype(F32)).astype(BF16)


def shift_first(chain, keep, away, micros=0):
    _, rows, cols = keep.shape
    vmem = pl.BlockSpec(memory_space=pltpu.VMEM)
    return chain.call(
        add_first_kernel,
        out_shape=(shape((4, rows, cols), F32), shape((4, rows, cols), BF16)),
        in_specs=[vmem, vmem],
        out_specs=(vmem, vmem),
        compiler_params=params(12),
        name="shift_first",
        cost_estimate=cost(micros),
    )(keep, send(away, second_way))


def add_both_kernel(keep, got, few_keep, few_got, kept, away):
    split = keep.shape[2]
    kept[:, :, :split] = keep[:4] + got[:4].astype(F32)
    kept[:, :, split:] = few_keep[:4] + few_got[:4].astype(F32)
    away[:, :, :split] = (keep[4:] + got[4:].astype(F32)).astype(BF16)
    away[:, :, split:] = (few_keep[4:] + few_got[4:].astype(F32)).astype(BF16)


def shift_both(chain, keep, away, few_keep, few_away):
    _, rows, cols = keep.shape
    cols += few_keep.shape[2]
    vmem = pl.BlockSpec(memory_space=pltpu.VMEM)
    return chain.call(
        add_both_kernel,
        out_shape=(shape((4, rows, cols), F32), shape((4, rows, cols), BF16)),
        in_specs=[vmem] * 4,
        out_specs=(vmem, vmem),
        compiler_params=params(12),
        name="shift_both",
        cost_estimate=cost(0),
    )(keep, send(away, second_way), few_keep, send(few_away, second_way))


def add_second_kernel(keep, got, base, one, two, three):
    base[...] = keep[0] + got[0].astype(F32)
    for s, out in ((1, one), (2, two), (3, three)):
        out[...] = (keep[s] + got[s].astype(F32)).astype(BF16)


def shift_second(chain, keep, away):
    _, rows, cols = keep.shape
    vmem = pl.BlockSpec(memory_space=pltpu.VMEM)
    base, *lows = chain.call(
        add_second_kernel,
        out_shape=(shape((rows, cols), F32),) + (shape((rows, cols), BF16),) * 3,
        in_specs=[vmem, vmem],
        out_specs=(vmem,) * 4,
        compiler_params=params(8),
        name="shift_second",
        cost_estimate=cost(0),
    )(keep, send(away, first_way))
    return base, [send(low, along_z(s)) for low, s in zip(lows, (1, 2, 3))]


def total_of(base, parts):
    return base[...] + parts[0][...].astype(F32) + (
        parts[1][...].astype(F32) + parts[2][...].astype(F32)
    )


def add_down_kernel(base, one, two, three, out):
    out[...] = total_of(base, (one, two, three))


def home_down(chain, base, parts):
    vmem = pl.BlockSpec(memory_space=pltpu.VMEM)
    return chain.call(
        add_down_kernel,
        out_shape=shape(base.shape, F32),
        in_specs=[vmem] * 4,
        out_specs=vmem,
        compiler_params=params(8),
        name="home_down",
        cost_estimate=cost(0),
    )(base, *parts)


def add_last_kernel(info, base, one, two, three, mine, theirs, total):
    core = info[CORE]
    half = mine.shape[0]
    total[...] = total_of(base, (one, two, three))
    mine[...] = total[pl.ds(pl.multiple_of(core * half, half), half)]
    theirs[...] = total[pl.ds(pl.multiple_of((1 - core) * half, half), half)]


def home(chain, info, base, parts):
    rows, cols = base.shape
    vmem = pl.BlockSpec(memory_space=pltpu.VMEM)
    out = shape((rows // 2, cols), F32)
    mine, theirs = chain.call(
        add_last_kernel,
        out_shape=(out, out),
        in_specs=[SMEM] + [vmem] * 4,
        out_specs=(vmem, vmem),
        scratch_shapes=[pltpu.VMEM((rows, cols), F32)],
        compiler_params=params(8),
        name="home",
        cost_estimate=cost(0),
    )(info, base, *parts)
    return mine, swap(theirs)


def finish_kernel(info, qkv, qkv_o, up, up_o, out_qkv, out_proj, out_up, gains, shifts, bias):
    rows, third = out_proj.shape[0], out_proj.shape[1] // 2
    wide = out_up.shape[1] // 2
    small = qkv[:, 3 * third :] + qkv_o[:, 3 * third :]
    flipped = jnp.concatenate([small, jnp.zeros((128 - rows, 128), F32)]).T
    gains[...] = flipped[0:2, :rows]
    shifts[...] = flipped[2:8, :rows]
    bias[...] = small[0:1, 128 - bias.shape[1] :]

    def lay(core):
        for half, (a, b) in ((core, (qkv, up)), (1 - core, (qkv_o, up_o))):
            for part in range(3):
                spot = part * 2 * third + half * third
                out_qkv[:, spot : spot + third] = a[:, part * third : (part + 1) * third]
            out_proj[:, half * third : (half + 1) * third] = b[:, wide:]
            out_up[:, half * wide : (half + 1) * wide] = b[:, :wide]

    @pl.when(info[CORE] == 0)
    def _():
        lay(0)

    @pl.when(info[CORE] == 1)
    def _():
        lay(1)


def finish(chain, info, qkv, qkv_o, up, up_o):
    rows = qkv.shape[0]
    third = (qkv.shape[1] - 128) // 3
    vmem = pl.BlockSpec(memory_space=pltpu.VMEM)
    return chain.call(
        finish_kernel,
        out_shape=(
            shape((rows, 6 * third), F32),
            shape((rows, 2 * third), F32),
            shape((rows, 2 * (up.shape[1] - third)), F32),
            shape((2, rows), F32),
            shape((6, rows), F32),
            shape((1, 4 * rows), F32),
        ),
        in_specs=[SMEM] + [vmem] * 4,
        out_specs=(vmem,) * 6,
        compiler_params=params(8),
        name="finish",
        cost_estimate=cost(0),
    )(info, qkv, qkv_o, up, up_o)


def local(
    tokens,
    upstream,
    lengths,
    qkv_weight,
    proj_weight,
    up_weight,
    down_weight,
    gains,
    shifts,
    up_bias,
):
    tok_rows, feat = tokens.shape
    rows = qkv_weight.shape[0]
    hidden = up_weight.shape[1]
    third, wide = feat // 2, hidden // 2
    chip, core = lax.axis_index("dp"), lax.axis_index("fsdp")
    info = facts(chip, core, lengths[0])

    chain = Chain()

    small = jnp.concatenate([gains, shifts], axis=1)
    small = jnp.pad(small, ((0, 0), (0, 128 - small.shape[1])))
    small = small + jnp.pad(up_bias[None], ((0, rows - 1), (128 - up_bias.shape[0], 0)))
    piece = first_piece(chain, info, qkv_weight, swap(qkv_weight), small)
    piece_up = up_piece(chain, info, up_weight, swap(up_weight), proj_weight, swap(proj_weight))
    zs, piece_up = gather(chain, [piece] + near_z(piece, (3, 2, 1)), (piece_up,), 0, (0, 3, 2, 1))
    up_z = near_z(piece_up, (1, 2, 3))
    first = gate(chain, send(zs, first_way), 0)
    second, both = send(zs, second_way), send(first, second_way)
    (zs_up,) = gather(chain, [piece_up] + up_z, (), 5)
    pieces = both_cores(zs, first, gate(chain, second, 0), gate(chain, both, 0))
    zs = zs_up
    first_set, vecs, bias, first_t, joint, grad_y, down = enter(
        chain, info, tokens, upstream, down_weight, hidden, pieces
    )
    grad_y_o, first_o = swap(grad_y), swap(first_t)
    first_set = first_set.reshape(2, feat, 3 * third + 128)
    first, second = send(zs, first_way), send(zs, second_way)
    first = gate(chain, first, 0)
    pieces = both_cores(zs, first, second, send(first, second_way))
    down_z = near_z(down, (1, 2, 3))
    mixed, mixed_t, stats = mix(chain, info, joint)
    mixed_t = mixed_t.reshape(first_t.shape)
    mixed_o = swap(mixed_t)
    (zs,) = gather(chain, [down] + down_z, (), 5)
    proj_set, after, normed, normed_t = rise(chain, info, tokens, mixed, vecs, pieces)
    normed_o = swap(normed_t)
    up_a, active_a, slope_a, mine_a, theirs_a = widen(chain, 0, info, normed, bias, pieces[:4])
    theirs_a = swap(theirs_a)
    (low,) = gather(chain, [zs, send(zs, first_way)])
    high = send(low, second_way)
    up_b, active_b, slope_b, mine_b, theirs_b = widen(chain, 1, info, normed, bias, pieces[4:])
    proj_set = proj_set.reshape(2, feat, third)
    down = outer_down(
        chain, info, mine_a, mine_b, theirs_a, swap(theirs_b), grad_y, grad_y_o
    )
    pieces = both_cores(low, gate(chain, high, 0))
    up_sets = (up_a.reshape(feat, wide), up_b.reshape(feat, wide))
    down_set, hid_theirs, hid_mine, bias_sum, grad_after, at_theirs, at_mine, grad_mixed, sums_a = (
        fall(chain, info, grad_y, (slope_a, slope_b), up_sets, after, vecs, proj_set, pieces)
    )
    hid_o, at_o = swap(hid_theirs), swap(at_theirs)
    down = shift_first(chain, *down, 5)
    up = outer_up(chain, info, normed_t, normed_o, hid_mine, hid_o, mixed_t, mixed_o, at_mine, at_o)
    down = shift_second(chain, *down)
    theirs, mine = mix_back(chain, info, joint, grad_mixed, stats)
    theirs_o = swap(theirs)
    down = (down[0], [gate(chain, part, 0) for part in down[1]])
    up = shift_first(chain, *up, 5)
    chain.near(up[1])
    qkv = outer_qkv(chain, info, first_t, first_o, mine, theirs_o)
    grad_tokens, few_keep, few_away = exit_back(
        chain, info, tokens, mine, theirs, first_set, grad_after, vecs, sums_a, bias_sum
    )
    up = shift_second(chain, *up)
    qkv = shift_both(chain, *qkv, few_keep, few_away)
    output = leave(
        chain, info, after, active_a, active_b, down_set.reshape(hidden, feat), vecs
    )
    qkv = shift_second(chain, *qkv)
    own_down = home_down(chain, *down)
    own_up = home(chain, info, *up)
    own_qkv = home(chain, info, *qkv)
    out_qkv, out_proj, out_up, out_gains, out_shifts, out_bias = finish(
        chain, info, *own_qkv, *own_up
    )
    return (
        output,
        grad_tokens,
        out_qkv,
        out_proj,
        out_up,
        own_down,
        out_gains.T,
        out_shifts.T,
        out_bias.reshape(-1),
    )


def solution(mesh):
    placed = (
        P(("dp", "fsdp"), None),
        P(("dp", "fsdp"), None),
        P(("dp", "fsdp")),
        P(("dp", "fsdp"), None),
        P(("dp", "fsdp"), None),
        P(("dp", "fsdp"), None),
        P(("dp", "fsdp"), None),
        P(("dp", "fsdp"), None),
        P(("dp", "fsdp"), None),
        P(("dp", "fsdp")),
    )
    sizes = (mesh.shape["dp"], mesh.shape["fsdp"])
    return jax.shard_map(
        local if sizes == (16, 2) else plain,
        mesh=mesh,
        in_specs=placed,
        out_specs=(
            P(("dp", "fsdp"), None),
            P(("dp", "fsdp"), None),
            P(("dp", "fsdp"), None),
            P(("dp", "fsdp"), None),
            P(("dp", "fsdp"), None),
            P(("dp", "fsdp"), None),
            P(("dp", "fsdp"), None),
            P(("dp", "fsdp"), None),
            P(("dp", "fsdp")),
        ),
        check_vma=False,
    )
```

```python
import math
from functools import partial

import jax
import jax.numpy as jnp
from jax import lax
from jax.experimental import pallas as pl
from jax.experimental.pallas import tpu as pltpu
from jax.sharding import PartitionSpec as P

HEADS = 12
EPS = 1e-06
NEG = -1e30
AXES = ("dp", "fsdp")
F32 = jnp.float32
BF16 = jnp.bfloat16
VMEM_LIMIT = 32 * 1024 * 1024


def collect(qkv_weight, proj_weight, up_weight, down_weight, gains, shifts, up_bias):
    gathered = (
        lax.all_gather(qkv_weight, ("dp", "fsdp"), axis=0, tiled=True),
        lax.all_gather(proj_weight, ("dp", "fsdp"), axis=0, tiled=True),
        lax.all_gather(up_weight, ("dp", "fsdp"), axis=0, tiled=True),
        lax.all_gather(down_weight, ("dp", "fsdp"), axis=0, tiled=True),
        lax.all_gather(gains, ("dp", "fsdp"), axis=0, tiled=True),
        lax.all_gather(shifts, ("dp", "fsdp"), axis=0, tiled=True),
        lax.all_gather(up_bias, ("dp", "fsdp"), axis=0, tiled=True),
    )
    return gathered


def give_back(grad_qkv, grad_proj, grad_up, grad_down, grad_gains, grad_shifts, grad_bias_up):
    owned = (
        lax.psum_scatter(grad_qkv, ("dp", "fsdp"), scatter_dimension=0, tiled=True),
        lax.psum_scatter(grad_proj, ("dp", "fsdp"), scatter_dimension=0, tiled=True),
        lax.psum_scatter(grad_up, ("dp", "fsdp"), scatter_dimension=0, tiled=True),
        lax.psum_scatter(grad_down, ("dp", "fsdp"), scatter_dimension=0, tiled=True),
        lax.psum_scatter(grad_gains, ("dp", "fsdp"), scatter_dimension=0, tiled=True),
        lax.psum_scatter(grad_shifts, ("dp", "fsdp"), scatter_dimension=0, tiled=True),
        lax.psum_scatter(grad_bias_up, ("dp", "fsdp"), scatter_dimension=0, tiled=True),
    )
    return owned


def normalize(values):
    centred = values - jnp.mean(values, axis=-1, keepdims=True)
    inverse = lax.rsqrt(jnp.mean(centred * centred, axis=-1, keepdims=True) + EPS)
    return (centred * inverse, inverse)


def norm_back(grad_norm, normed, inverse):
    return inverse * (
        grad_norm
        - jnp.mean(grad_norm, axis=-1, keepdims=True)
        - normed * jnp.mean(grad_norm * normed, axis=-1, keepdims=True)
    )


def block_scores(query_blk, key_rows, live_mask, scaling):
    raw = (
        jnp.einsum("qhd,khd->hqk", query_blk, key_rows, preferred_element_type=jnp.float32)
        * scaling
    )
    return jnp.where(live_mask[None, None, :], raw, NEG)


def plain(
    tokens,
    upstream,
    lengths,
    qkv_weight,
    proj_weight,
    up_weight,
    down_weight,
    gains,
    shifts,
    up_bias,
):
    tok_rows, feat_width = tokens.shape
    n_heads = HEADS
    head_size = feat_width // n_heads
    scaling = head_size ** (-0.5)
    block_rows = min(512, tok_rows)
    group_heads = 4
    head_starts = list(range(0, n_heads, group_heads))
    gathered = collect(qkv_weight, proj_weight, up_weight, down_weight, gains, shifts, up_bias)
    qkv_full, proj_full, up_full, down_full, gain_full, shift_full, bias_full = gathered
    gain_f = gain_full.astype(jnp.float32)
    shift_f = shift_full.astype(jnp.float32)
    bias_f = bias_full.astype(jnp.float32)
    live_mask = lax.iota(jnp.int32, tok_rows) < lengths[0]
    source = tokens.astype(jnp.float32)
    norm_one, inv_one = normalize(source)
    first = (norm_one * gain_f[:, 0] + shift_f[:, 0]).astype(jnp.bfloat16)
    joint_bias = jnp.concatenate([shift_f[:, 1], jnp.zeros_like(shift_f[:, 1]), shift_f[:, 2]])
    joint = (jnp.dot(first, qkv_full, preferred_element_type=jnp.float32) + joint_bias).astype(
        jnp.bfloat16
    )
    queries = joint[:, :feat_width].reshape(tok_rows, n_heads, head_size)
    key_rows = joint[:, feat_width : 2 * feat_width].reshape(tok_rows, n_heads, head_size)
    value_rows = joint[:, 2 * feat_width :].reshape(tok_rows, n_heads, head_size)
    log_sums = {}
    offset = 0
    group_parts = []
    for head_lo in head_starts:
        head_hi = head_lo + group_heads
        scores = block_scores(
            queries[offset : offset + block_rows, head_lo:head_hi],
            key_rows[:, head_lo:head_hi],
            live_mask,
            scaling,
        )
        row_max = jnp.max(scores, axis=-1, keepdims=True)
        expd = jnp.exp(scores - row_max)
        row_sum = jnp.sum(expd, axis=-1, keepdims=True)
        attn_low = (expd / row_sum).astype(jnp.bfloat16)
        log_sums[offset, head_lo] = row_max + jnp.log(row_sum)
        group_parts.append(
            jnp.einsum(
                "hqk,khd->qhd",
                attn_low,
                value_rows[:, head_lo:head_hi],
                preferred_element_type=jnp.float32,
            )
        )
    mixed_parts = jnp.concatenate(group_parts, axis=1)
    mixed = mixed_parts.reshape(tok_rows, feat_width).astype(jnp.bfloat16)
    after = source + jnp.dot(mixed, proj_full, preferred_element_type=jnp.float32) + shift_f[:, 3]
    norm_two, inv_two = normalize(after)
    second = (norm_two * gain_f[:, 1] + shift_f[:, 4]).astype(jnp.bfloat16)
    hidden = jnp.dot(second, up_full, preferred_element_type=jnp.float32) + bias_f
    gelu_exact = partial(jax.nn.gelu, approximate=False)
    active = gelu_exact(hidden).astype(jnp.bfloat16)
    output = (
        after + jnp.dot(active, down_full, preferred_element_type=jnp.float32) + shift_f[:, 5]
    ).astype(jnp.bfloat16)
    regathered = collect(qkv_weight, proj_weight, up_weight, down_weight, gains, shifts, up_bias)
    qkv_full, proj_full, up_full, down_full, gain_full, shift_full, bias_full = regathered
    grad_y = jnp.where(live_mask[:, None], upstream, jnp.zeros_like(upstream))
    sum_y = jnp.sum(grad_y, axis=0, dtype=jnp.float32)
    grad_down = jnp.einsum("tf,td->fd", active, grad_y, preferred_element_type=jnp.float32)
    grad_active = jnp.einsum("td,fd->tf", grad_y, down_full, preferred_element_type=jnp.float32)
    gelu_value, gelu_pull = jax.vjp(gelu_exact, hidden)
    grad_hidden = gelu_pull(grad_active)[0].astype(jnp.bfloat16)
    grad_bias_up = jnp.sum(grad_hidden, axis=0, dtype=jnp.float32)
    grad_up = jnp.einsum("td,tf->df", second, grad_hidden, preferred_element_type=jnp.float32)
    grad_second = jnp.einsum("tf,df->td", grad_hidden, up_full, preferred_element_type=jnp.float32)
    gain_two_grad = jnp.sum(grad_second * norm_two, axis=0)
    shift_two_grad = jnp.sum(grad_second, axis=0)
    grad_after = grad_y.astype(jnp.float32) + norm_back(
        grad_second * gain_f[:, 1], norm_two, inv_two
    )
    grad_attn = grad_after.astype(jnp.bfloat16)
    sum_attn = jnp.sum(grad_attn, axis=0, dtype=jnp.float32)
    grad_proj = jnp.einsum("td,te->de", mixed, grad_attn, preferred_element_type=jnp.float32)
    grad_mixed = jnp.einsum("te,de->td", grad_attn, proj_full, preferred_element_type=jnp.float32)
    grad_mixed = grad_mixed.astype(jnp.bfloat16).reshape(tok_rows, n_heads, head_size)
    key_groups = {}
    value_groups = {}
    for head_lo in head_starts:
        key_groups[head_lo] = jnp.zeros((tok_rows, group_heads, head_size), jnp.float32)
        value_groups[head_lo] = jnp.zeros((tok_rows, group_heads, head_size), jnp.float32)
    offset = 0
    query_groups = []
    for head_lo in head_starts:
        head_hi = head_lo + group_heads
        query_blk = queries[offset : offset + block_rows, head_lo:head_hi]
        grad_blk = grad_mixed[offset : offset + block_rows, head_lo:head_hi]
        key_part = key_rows[:, head_lo:head_hi]
        scores = block_scores(query_blk, key_part, live_mask, scaling)
        attn_p = jnp.exp(scores - log_sums[offset, head_lo])
        value_groups[head_lo] = jnp.einsum(
            "hqk,qhd->khd",
            attn_p.astype(jnp.bfloat16),
            grad_blk,
            preferred_element_type=jnp.float32,
        )
        grad_prob = jnp.einsum(
            "qhd,khd->hqk",
            grad_blk,
            value_rows[:, head_lo:head_hi],
            preferred_element_type=jnp.float32,
        )
        grad_score = attn_p * (grad_prob - jnp.sum(attn_p * grad_prob, axis=-1, keepdims=True))
        score_low = grad_score.astype(jnp.bfloat16)
        query_groups.append(
            jnp.einsum("hqk,khd->qhd", score_low, key_part, preferred_element_type=jnp.float32)
            * scaling
        )
        key_groups[head_lo] = (
            jnp.einsum("hqk,qhd->khd", score_low, query_blk, preferred_element_type=jnp.float32)
            * scaling
        )
    grad_query_parts = jnp.concatenate(query_groups, axis=1)
    grad_keys = jnp.concatenate([key_groups[head_lo] for head_lo in head_starts], axis=1)
    grad_vals = jnp.concatenate([value_groups[head_lo] for head_lo in head_starts], axis=1)
    grad_joint = jnp.concatenate(
        [
            grad_query_parts.reshape(tok_rows, feat_width),
            grad_keys.reshape(tok_rows, feat_width),
            grad_vals.reshape(tok_rows, feat_width),
        ],
        axis=1,
    ).astype(jnp.bfloat16)
    joint_sums = jnp.sum(grad_joint, axis=0, dtype=jnp.float32)
    grad_qkv = jnp.einsum("td,te->de", first, grad_joint, preferred_element_type=jnp.float32)
    grad_first = jnp.einsum("te,de->td", grad_joint, qkv_full, preferred_element_type=jnp.float32)
    gain_one_grad = jnp.sum(grad_first * norm_one, axis=0)
    shift_one_grad = jnp.sum(grad_first, axis=0)
    grad_tokens = (grad_after + norm_back(grad_first * gain_f[:, 0], norm_one, inv_one)).astype(
        jnp.bfloat16
    )
    grad_gains = jnp.stack([gain_one_grad, gain_two_grad], axis=1)
    grad_shifts = jnp.stack(
        [
            shift_one_grad,
            joint_sums[:feat_width],
            joint_sums[2 * feat_width :],
            sum_attn,
            shift_two_grad,
            sum_y,
        ],
        axis=1,
    )
    owned = give_back(
        grad_qkv, grad_proj, grad_up, grad_down, grad_gains, grad_shifts, grad_bias_up
    )
    own_qkv, own_proj, own_up, own_down, own_gains, own_shifts, own_bias = owned
    return (
        output,
        grad_tokens,
        own_qkv,
        own_proj,
        own_up,
        own_down,
        own_gains,
        own_shifts,
        own_bias,
    )


BOTH_LAST = (((1,), (1,)), ((), ()))
SMEM = pl.BlockSpec(memory_space=pltpu.SMEM)
ANY = pl.BlockSpec(memory_space=pl.ANY)
CORE, LENGTH, PLACE, PLACE_O = 32, 33, 34, 50


def pairs(move):
    return [(i, move(i)) for i in range(32)]


def first_way(i):
    return i ^ (2 if i % 2 == 0 else 4)


def second_way(i):
    return i ^ (4 if i % 2 == 0 else 2)


def along_z(step):
    return lambda i: i ^ (8 * step)


def send(array, move):
    return lax.ppermute(array, AXES, pairs(move))


def swap(array):
    return send(array, lambda i: i ^ 1)


def facts(chip, core, length):
    places = []
    for of_core in (core, 1 - core):
        for j in range(16):
            z, first, second = j % 4, (j // 4) % 2, j // 8
            mask = jnp.where(of_core == 0, first + 2 * second, second + 2 * first)
            places.append(jnp.bitwise_xor(chip, mask + 4 * z))
    spots = []
    for of_core in (core, 1 - core):
        for k in range(16):
            mask = jnp.bitwise_xor(chip, k)
            x, y, z = mask & 1, (mask >> 1) & 1, mask >> 2
            spots.append(z + jnp.where(of_core == 0, 4 * x + 8 * y, 4 * y + 8 * x))
    return jnp.stack(places + [core, length] + spots).astype(jnp.int32)


def params(mib):
    return pltpu.CompilerParams(vmem_limit_bytes=mib * 1024 * 1024)


def cost(micros):
    flops = int(micros * (3e10 if micros > 3 else 1e9))
    return pl.CostEstimate(flops=flops, bytes_accessed=1, transcendentals=0)


def shape(dims, dtype):
    return jax.ShapeDtypeStruct(dims, dtype)


def full(dims):
    return pl.BlockSpec(dims, lambda *_: (0,) * len(dims))


class Chain:
    def __init__(self):
        self.token, self.extra = None, ()

    def near(self, *arrays):
        self.extra = arrays

    def call(
        self, kernel, *, out_shape, in_specs, out_specs, grid=(), prefetch=0, aliases={}, **options
    ):
        single = not isinstance(out_shape, tuple)
        if single:
            out_shape, out_specs = (out_shape,), (out_specs,)
        held = 0 if self.token is None else 1
        extra, self.extra = self.extra, ()
        n_in, n_out = prefetch + len(in_specs), len(out_shape)
        at_token = n_in + len(extra)

        def body(*refs):
            skip = at_token + held
            return kernel(*refs[:n_in], *refs[skip : skip + n_out], *refs[skip + n_out + 1 :])

        token = shape((8, 128), F32)
        specs = pltpu.PrefetchScalarGridSpec(
            num_scalar_prefetch=prefetch,
            grid=grid,
            in_specs=list(in_specs) + [ANY] * (len(extra) + held),
            out_specs=tuple(out_specs) + (ANY,),
            scratch_shapes=options.pop("scratch_shapes", ()),
        )
        run = pl.pallas_call(
            body,
            grid_spec=specs,
            out_shape=tuple(out_shape) + (token,),
            input_output_aliases=aliases | ({at_token: n_out} if held else {}),
            **options,
        )

        def with_token(*args):
            *outs, self.token = run(*args, *extra, *([self.token] if held else []))
            return outs[0] if single else tuple(outs)

        return with_token


def dot(left, right):
    return jnp.dot(left, right, preferred_element_type=F32)


def dot_last(left, right):
    return lax.dot_general(left, right, BOTH_LAST, preferred_element_type=F32)


def settle(info, pieces, dest, who=(0, 1)):
    few = pieces[0].shape[0]
    for w in who:
        half = info[CORE] if w == 0 else 1 - info[CORE]
        for j in range(16):
            dest[half, info[16 * w + j]] = pieces[(16 * w + j) // few][j % few]


def bring(pieces, raw, sems, start):
    cols = pl.ds(start, raw.shape[-1])
    return [
        pltpu.make_async_copy(piece.at[:, :, cols], raw.at[i], sems.at[i])
        for i, piece in enumerate(pieces)
    ]


def centre(values):
    centred = values - jnp.mean(values, axis=-1, keepdims=True)
    inverse = lax.rsqrt(jnp.mean(centred * centred, axis=-1, keepdims=True) + EPS)
    return centred * inverse, inverse


def layer_back(grad, normed, inverse):
    return inverse * (
        grad
        - jnp.mean(grad, axis=-1, keepdims=True)
        - normed * jnp.mean(grad * normed, axis=-1, keepdims=True)
    )


def stacked(core, mine, others):
    pair = (mine, others) if core == 0 else (others, mine)
    return jnp.concatenate([part.astype(F32) for part in pair]).astype(BF16)


def by_core(info, lay):
    for core in (0, 1):
        pl.when(info[CORE] == core)(partial(lay, core))


def first_piece_kernel(info, qkv, qkv_o, small, out):
    third = qkv.shape[1] // 6

    def lay(core):
        for i in range(3):
            cols = slice((2 * i + core) * third, (2 * i + core + 1) * third)
            out[0, :, i * third : (i + 1) * third] = stacked(core, qkv[:, cols], qkv_o[:, cols])
        out[0, :, 3 * third :] = stacked(core, small[...], jnp.zeros_like(small))

    by_core(info, lay)


def first_piece(chain, info, qkv, qkv_o, small):
    rows, cols = qkv.shape
    vmem = pl.BlockSpec(memory_space=pltpu.VMEM)
    return chain.call(
        first_piece_kernel,
        out_shape=shape((1, 2 * rows, cols // 2 + small.shape[1]), BF16),
        in_specs=[SMEM] + [vmem] * 3,
        out_specs=vmem,
        compiler_params=params(8),
        name="first_piece",
        cost_estimate=cost(0),
    )(info, qkv, qkv_o, small)


def up_piece_kernel(info, up, up_o, proj, proj_o, out):
    wide, third = up.shape[1] // 2, proj.shape[1] // 2

    def lay(core):
        for whole, other, at, width in ((up, up_o, 0, wide), (proj, proj_o, wide, third)):
            cols = slice(core * width, (core + 1) * width)
            out[0, :, at : at + width] = stacked(core, whole[:, cols], other[:, cols])

    by_core(info, lay)


def up_piece(chain, info, up, up_o, proj, proj_o):
    rows = up.shape[0]
    vmem = pl.BlockSpec(memory_space=pltpu.VMEM)
    return chain.call(
        up_piece_kernel,
        out_shape=shape((1, 2 * rows, (up.shape[1] + proj.shape[1]) // 2), BF16),
        in_specs=[SMEM] + [vmem] * 4,
        out_specs=vmem,
        compiler_params=params(8),
        name="up_piece",
        cost_estimate=cost(0),
    )(info, up, up_o, proj, proj_o)


def gather_kernel(n_in, n_held, order, *refs):
    out = refs[n_in + n_held]
    for i, part in enumerate(refs[:n_in]):
        at = part.shape[0] * (i if order is None else order[i])
        out[at : at + part.shape[0]] = part[...]
    for i in range(n_held):
        refs[n_in + n_held + 1 + i][...] = refs[n_in + i][...]


def gather(chain, parts, held=(), micros=0, order=None):
    vmem = pl.BlockSpec(memory_space=pltpu.VMEM)
    _, rows, cols = parts[0].shape
    count = sum(part.shape[0] for part in parts)
    n, n_held = len(parts), len(held)
    return chain.call(
        partial(gather_kernel, n, n_held, order),
        out_shape=(shape((count, rows, cols), BF16),) + tuple(shape(h.shape, h.dtype) for h in held),
        in_specs=[vmem] * (n + n_held),
        out_specs=(vmem,) * (1 + n_held),
        compiler_params=params(16),
        name="gather",
        cost_estimate=cost(micros),
    )(*parts, *held)


def gate_kernel(array, out):
    pass


def gate(chain, array, micros):
    return chain.call(
        gate_kernel,
        out_shape=shape(array.shape, array.dtype),
        in_specs=[ANY],
        out_specs=ANY,
        aliases={0: 0},
        compiler_params=params(4),
        name="gate",
        cost_estimate=cost(micros),
    )(array)


def both_cores(*own):
    return own + tuple(swap(blocks) for blocks in own)


def near_z(piece, steps):
    return [send(piece, along_z(s)) for s in steps]


def enter_kernel(
    info,
    tokens,
    upstream,
    down,
    *refs,
):
    pieces = refs[:8]
    kept, vecs, bias, flipped, joint, grad_y, piece_down, weights, sem = refs[8:]
    feat = tokens.shape[1]
    third = feat // 2
    piece_down[0] = down[...]
    place = lax.broadcasted_iota(jnp.int32, upstream.shape, 0)
    grad_y[...] = jnp.where(place < info[LENGTH], upstream[...].astype(F32), 0.0).astype(BF16)
    settle(info, pieces, weights)
    normed, _ = centre(tokens[...].astype(F32))
    out = pltpu.make_async_copy(weights, kept, sem)
    out.start()
    split = 3 * third
    small = weights[0, :, :, split:] + weights[1, :, :, split:]
    small = small.reshape(feat, 128).astype(F32)
    each = bias.shape[1] // 32
    for device in range(32):
        row = device * feat // 32
        bias[:, device * each : (device + 1) * each] = small[row : row + 1, 128 - each :]
    small = small.T
    vecs[...] = small[:8]
    low_first = (normed * small[0:1] + small[2:3]).astype(BF16)
    flipped[...] = low_first.T.reshape(flipped.shape)
    for h in (0, 1):
        cols = slice(h * third, (h + 1) * third)
        bias = jnp.concatenate(
            [small[3:4, cols], jnp.zeros((1, third), F32), small[4:5, cols]], axis=1
        )
        w = weights[h, :, :, :split].reshape(feat, split)
        joint[h] = (dot(low_first, w) + bias).astype(BF16)
    out.wait()


def enter(chain, info, tokens, upstream, down, hidden, pieces):
    rows, feat = tokens.shape
    width = pieces[0].shape[-1]
    vmem = pl.BlockSpec(memory_space=pltpu.VMEM)
    sets = (2, 16, feat // 16, width)
    return chain.call(
        enter_kernel,
        out_shape=(
            shape(sets, BF16),
            shape((8, feat), F32),
            shape((1, hidden), F32),
            shape((16, feat // 16, rows), BF16),
            shape((2, rows, 3 * feat // 2), BF16),
            shape((rows, feat), BF16),
            shape((1,) + down.shape, BF16),
        ),
        in_specs=[SMEM] + [vmem] * 11,
        out_specs=(ANY,) + (vmem,) * 6,
        scratch_shapes=[pltpu.VMEM(sets, BF16), pltpu.SemaphoreType.DMA],
        compiler_params=params(20),
        name="enter",
        cost_estimate=cost(8),
    )(info, tokens, upstream, down, *pieces)


def scores_of(info, keys, queries):
    raw = dot_last(keys, queries)
    place = lax.broadcasted_iota(jnp.int32, raw.shape, 0)
    return jnp.where(place < info[LENGTH], raw, NEG)


def mix_kernel(info, q, k, v, mixed, flipped, stats):
    head = mixed.shape[1] // (HEADS // 2)
    count = q.shape[-1] // head
    scale = head**-0.5
    turned = v[0].T

    def start(h):
        cols = slice(h * head, (h + 1) * head)
        return scores_of(info, k[0, :, cols], q[0, :, cols] * scale)

    def finish(h, scores):
        cols = slice(h * head, (h + 1) * head)
        most = jnp.max(scores, axis=0, keepdims=True)
        expd = jnp.exp(scores - most)
        total = jnp.sum(expd, axis=0, keepdims=True)
        attn = (expd * (1.0 / total)).astype(BF16)
        stats[h // 2, h % 2 : h % 2 + 1] = most + jnp.log(total)
        return dot(turned[cols], attn)

    ready = [start(h) for h in range(2)]
    outs = []
    for h in range(count):
        if h + 2 < count:
            ready.append(start(h + 2))
        outs.append(finish(h, ready[h]))
    both = jnp.concatenate(outs)
    flipped[...] = both.astype(BF16)
    mixed[...] = both.T.astype(BF16)


def mix(chain, info, joint):
    _, rows, width = joint.shape
    feat = 2 * width // 3
    wide = feat // 2
    spec = [pl.BlockSpec((1, rows, wide), lambda i, part=part: (i, 0, part)) for part in range(3)]
    pairs_in_half = HEADS // 4
    return chain.call(
        mix_kernel,
        grid=(2,),
        out_shape=(
            shape((rows, feat), BF16),
            shape((feat, rows), BF16),
            shape((HEADS // 2, 8, rows), F32),
        ),
        in_specs=[SMEM] + spec,
        out_specs=(
            pl.BlockSpec((rows, wide), lambda i: (0, i)),
            pl.BlockSpec((wide, rows), lambda i: (i, 0)),
            pl.BlockSpec((pairs_in_half, 8, rows), lambda i: (i, 0, 0)),
        ),
        compiler_params=params(24),
        name="mix",
        cost_estimate=cost(10),
    )(info, joint, joint, joint)


def mix_back_kernel(info, q, k, v, grad, stats, theirs, mine):
    head = theirs.shape[2] // (HEADS // 2)
    count = q.shape[-1] // head
    scale = head**-0.5
    turned = k[0].T

    def start(h):
        cols = slice(h * head, (h + 1) * head)
        queries = q[0, :, cols] * scale
        scores = scores_of(info, k[0, :, cols], queries)
        return cols, queries, scores, dot_last(v[0, :, cols], grad[:, cols])

    def finish(h, cols, queries, scores, grad_prob):
        attn = jnp.exp(scores - stats[h // 2, h % 2 : h % 2 + 1])
        inner = jnp.sum(attn * grad_prob, axis=0, keepdims=True)
        low = (attn * (grad_prob - inner)).astype(BF16)
        return (
            dot(turned[cols], low) * scale,
            dot(low, queries),
            dot(attn.astype(BF16), grad[:, cols]),
        )

    ready = [start(h) for h in range(2)]
    done = []
    for h in range(count):
        if h + 2 < count:
            ready.append(start(h + 2))
        done.append(finish(h, *ready[h]))
    out = [
        jnp.concatenate([d[0] for d in done]).T.astype(BF16),
        jnp.concatenate([d[1] for d in done], axis=1).astype(BF16),
        jnp.concatenate([d[2] for d in done], axis=1).astype(BF16),
    ]

    @pl.when(pl.program_id(0) == 0)
    def _():
        for part in range(3):
            theirs[part] = out[part]

    @pl.when(pl.program_id(0) == 1)
    def _():
        for part in range(3):
            mine[part] = out[part]


def mix_back(chain, info, joint, grad_mixed, stats):
    _, rows, width = joint.shape
    feat = 2 * width // 3
    wide = feat // 2

    def half(i, info):
        return jnp.where(i == 0, 1 - info[CORE], info[CORE])

    spec = [
        pl.BlockSpec((1, rows, wide), lambda i, info, part=part: (half(i, info), 0, part))
        for part in range(3)
    ]
    out = shape((3, rows, feat // 2), BF16)
    return chain.call(
        mix_back_kernel,
        prefetch=1,
        grid=(2,),
        in_specs=spec
        + [
            pl.BlockSpec((rows, wide), lambda i, info: (0, half(i, info))),
            pl.BlockSpec((HEADS // 4, 8, rows), lambda i, info: (half(i, info), 0, 0)),
        ],
        out_specs=(
            pl.BlockSpec((3, rows, wide), lambda i, info: (0, 0, 0)),
            pl.BlockSpec((3, rows, wide), lambda i, info: (0, 0, 0)),
        ),
        out_shape=(out, out),
        compiler_params=params(30),
        name="mix_back",
        cost_estimate=cost(16),
    )(info, joint, joint, joint, grad_mixed, stats)


GELU = (0.254829592, -0.284496736, 1.421413741, -1.453152027, 1.061405429)


def gelu_parts(x):
    bell = jnp.exp2(x * x * (-0.5 / math.log(2)))
    below = 1.0 + (0.3275911 * 0.5**0.5) * jnp.abs(x)
    t = pl.reciprocal(below, approx=True)
    t = t * (2.0 - below * t)
    poly = 0.5 * GELU[4]
    for c in GELU[3::-1]:
        poly = poly * t + 0.5 * c
    tail = poly * t * bell
    phi = jnp.where(x < 0, tail, 1.0 - tail)
    return x * phi, phi + x * (bell * (2 * math.pi) ** -0.5)


def rise_kernel(info, tokens, mixed, vecs, *refs):
    pieces = refs[:8]
    weights, after, second, flipped, raw, sems = refs[8:]
    feat = tokens.shape[1]
    copies = bring(pieces, raw, sems, pieces[0].shape[2] - raw.shape[-1])
    for copy in copies:
        copy.start()
    start = tokens[...].astype(F32) + vecs[5:6]
    for copy in copies:
        copy.wait()
    settle(info, [raw.at[i] for i in range(8)], weights)
    grown = [dot(mixed[...], weights[h].reshape(feat, feat // 2)) for h in (0, 1)]
    total = start + jnp.concatenate(grown, axis=1)
    after[...] = total
    normed, _ = centre(total)
    value = (normed * vecs[1:2] + vecs[6:7]).astype(BF16)
    second[...] = value
    flipped[...] = value.T.reshape(flipped.shape)


def rise(chain, info, tokens, mixed, vecs, pieces):
    rows, feat = tokens.shape
    vmem = pl.BlockSpec(memory_space=pltpu.VMEM)
    block = feat // 16
    return chain.call(
        rise_kernel,
        out_shape=(
            shape((2, 16, block, feat // 2), BF16),
            shape((rows, feat), F32),
            shape((rows, feat), BF16),
            shape((16, block, rows), BF16),
        ),
        in_specs=[SMEM] + [vmem] * 3 + [ANY] * 8,
        out_specs=(vmem,) * 4,
        scratch_shapes=[
            pltpu.VMEM((8, 4, block, feat // 2), BF16),
            pltpu.SemaphoreType.DMA((8,)),
        ],
        compiler_params=params(16),
        name="rise",
        cost_estimate=cost(5),
    )(info, tokens, mixed, vecs, *pieces)


def widen_kernel(which, info, second, bias, *refs):
    pieces = refs[:4]
    weights, active, slope, mine, theirs, raw, sems = refs[4:]
    step = pl.program_id(0)
    core = info[CORE]
    feat = second.shape[1]
    tile = active.shape[1]
    rows = mine.shape[1]
    count = tile // rows

    @pl.when(step == 0)
    def _():
        copies = bring(pieces, raw, sems, 0)
        for copy in copies:
            copy.start()
        for copy in copies:
            copy.wait()
        for j in range(16):
            weights[info[16 * which + j]] = raw[j // 4, j % 4]

    cols = pl.ds(pl.multiple_of(step * tile, tile), tile)
    w = weights[:, :, cols].reshape(feat, tile)
    hidden = dot(second[...], w) + bias[...]
    value, grad = gelu_parts(hidden)
    value = value.astype(BF16)
    active[...] = value
    slope[...] = grad.astype(BF16)
    flipped = value.T.reshape(count // 2, 2, rows, -1)
    mine[...] = jnp.where(core == 0, flipped[:, 0], flipped[:, 1])
    theirs[...] = jnp.where(core == 0, flipped[:, 1], flipped[:, 0])


def widen(chain, which, info, second, bias, pieces):
    rows, feat = second.shape
    wide = pieces[0].shape[-1] - feat // 2
    tile, block = 768, wide // 16
    per = wide // tile
    turned = shape((8, block, rows), BF16)

    def whole(dims):
        return pl.BlockSpec(dims, lambda n, info: (0,) * len(dims))

    def bias_at(n, info):
        half = info[CORE] if which == 0 else 1 - info[CORE]
        return (0, half * per + n)

    strip = pl.BlockSpec((rows, tile), lambda n, info: (0, n))
    part = pl.BlockSpec((tile // block // 2, block, rows), lambda n, info: (n, 0, 0))
    return chain.call(
        partial(widen_kernel, which),
        prefetch=1,
        grid=(per,),
        out_shape=(
            shape((16, feat // 16, wide), BF16),
            shape((rows, wide), BF16),
            shape((rows, wide), BF16),
            turned,
            turned,
        ),
        in_specs=[whole((rows, feat)), pl.BlockSpec((1, tile), bias_at)] + [ANY] * 4,
        out_specs=(whole((16, feat // 16, wide)), strip, strip, part, part),
        scratch_shapes=[
            pltpu.VMEM((4, 4, feat // 16, wide), BF16),
            pltpu.SemaphoreType.DMA((4,)),
        ],
        compiler_params=params(24),
        name="widen",
        cost_estimate=cost(18),
    )(info, second, bias, *pieces)


def leave_kernel(info, after, first, second, down, vecs, output, total):
    step, per = pl.program_id(0), pl.num_programs(0) // 2

    @pl.when(step == 0)
    def _():
        total[...] = after[...] + vecs[7:8] + dot(first[...], down[...])

    @pl.when((step > 0) & (step < per))
    def _():
        total[...] += dot(first[...], down[...])

    @pl.when(step >= per)
    def _():
        total[...] += dot(second[...], down[...])

    @pl.when(step == 2 * per - 1)
    def _():
        output[...] = total[...].astype(BF16)


def leave(chain, info, after, first, second, down, vecs):
    rows, feat = after.shape
    tile = 768
    per = first.shape[1] // tile

    def whole(dims):
        return pl.BlockSpec(dims, lambda n, info: (0,) * len(dims))

    def down_at(n, info):
        half = jnp.where(n < per, info[CORE], 1 - info[CORE])
        return (half * per + n % per, 0)

    return chain.call(
        leave_kernel,
        prefetch=1,
        grid=(2 * per,),
        out_shape=shape((rows, feat), BF16),
        in_specs=[
            whole((rows, feat)),
            pl.BlockSpec((rows, tile), lambda n, info: (0, jnp.minimum(n, per - 1))),
            pl.BlockSpec((rows, tile), lambda n, info: (0, jnp.maximum(n - per, 0))),
            pl.BlockSpec((tile, feat), down_at),
            whole((8, feat)),
        ],
        out_specs=whole((rows, feat)),
        scratch_shapes=[pltpu.VMEM((rows, feat), F32)],
        compiler_params=params(16),
        name="leave",
        cost_estimate=cost(7),
    )(info, after, first, second, down, vecs)


def fall_kernel(info, grad_y, slope, slope_o, up, up_o, after, vecs, proj, *refs):
    pieces = refs[:4]
    kept, theirs, mine, bias_sum, grad_after, attn_theirs, attn_mine, grad_mixed, sums = refs[4:13]
    weights, grad_second, normed, inverse, raw, sems, sem = refs[13:]
    step, steps = pl.program_id(0), pl.num_programs(0)
    core = info[CORE]
    feat = grad_y.shape[1]
    tile = slope.shape[1]
    per = steps // 2
    keeping = pltpu.make_async_copy(weights, kept, sem)

    @pl.when(step == 0)
    def _():
        copies = bring(pieces, raw, sems, 0)
        for copy in copies:
            copy.start()
        normed[...], inverse[...] = centre(after[...])
        grad_second[...] = jnp.zeros_like(grad_second)
        for copy in copies:
            copy.wait()
        for who in (0, 1):
            c = core if who == 0 else 1 - core
            for j in range(16):
                weights[info[16 * who + j], c] = raw[2 * who + j // 8, j % 8]
        keeping.start()

    half = jnp.where(step < per, 1 - core, core)
    at = half * per + lax.rem(step, per)
    count = tile * weights.shape[0] // (steps * tile)
    down = weights[pl.ds(count * at, count)].reshape(tile, feat)
    raw_grad = dot_last(grad_y[...], down)

    def tell(slope_ref, up_ref, out):
        grad = (raw_grad * slope_ref[...].astype(F32)).astype(BF16)
        bias_sum[...] = jnp.sum(grad.astype(F32), axis=0, keepdims=True)
        grad_second[...] += dot_last(grad, up_ref[...])
        out[...] = grad

    pl.when(step < per)(lambda: tell(slope_o, up_o, theirs))
    pl.when(step >= per)(lambda: tell(slope, up, mine))

    @pl.when(step == steps - 1)
    def _():
        second = grad_second[...]
        live = grad_y[...].astype(F32)
        sums[0:1] = jnp.sum(second * normed[...], axis=0, keepdims=True)
        sums[1:2] = jnp.sum(second, axis=0, keepdims=True)
        total = live + layer_back(second * vecs[1:2], normed[...], inverse[...])
        grad_after[...] = total
        attn = total.astype(BF16)
        sums[2:3] = jnp.sum(attn.astype(F32), axis=0, keepdims=True)
        sums[3:4] = jnp.sum(live, axis=0, keepdims=True)
        sums[4:8] = jnp.zeros_like(sums[4:8])
        left, right = attn[:, : feat // 2], attn[:, feat // 2 :]
        attn_mine[...] = jnp.where(core == 0, left, right)
        attn_theirs[...] = jnp.where(core == 0, right, left)
        grad_mixed[...] = (dot_last(left, proj[0]) + dot_last(right, proj[1])).astype(BF16)
        keeping.wait()


def fall(chain, info, grad_y, slopes, up_sets, after, vecs, proj_set, pieces):
    rows, feat = grad_y.shape
    hidden = 2 * slopes[0].shape[1]
    tile = 768
    steps = hidden // tile
    per = steps // 2

    def at(n, info):
        return jnp.where(n < per, 1 - info[CORE], info[CORE]) * per + n % per

    def whole(dims):
        return pl.BlockSpec(dims, lambda n, info: (0,) * len(dims))

    return chain.call(
        fall_kernel,
        prefetch=1,
        grid=(steps,),
        in_specs=[
            whole((rows, feat)),
            pl.BlockSpec((rows, tile), lambda n, info: (0, jnp.maximum(n - per, 0))),
            pl.BlockSpec((rows, tile), lambda n, info: (0, jnp.minimum(n, per - 1))),
            pl.BlockSpec((feat, tile), lambda n, info: (0, jnp.maximum(n - per, 0))),
            pl.BlockSpec((feat, tile), lambda n, info: (0, jnp.minimum(n, per - 1))),
            whole((rows, feat)),
            whole((8, feat)),
            whole((2, feat, feat // 2)),
        ]
        + [ANY] * 4,
        out_specs=(
            ANY,
            pl.BlockSpec((rows, tile), lambda n, info: (0, jnp.minimum(n, per - 1))),
            pl.BlockSpec((rows, tile), lambda n, info: (0, jnp.maximum(n - per, 0))),
            pl.BlockSpec((1, tile), lambda n, info: (0, at(n, info))),
            whole((rows, feat)),
            whole((rows, feat // 2)),
            whole((rows, feat // 2)),
            whole((rows, feat)),
            whole((8, feat)),
        ),
        scratch_shapes=[
            pltpu.VMEM((16, 2, hidden // 32, feat), BF16),
            pltpu.VMEM((rows, feat), F32),
            pltpu.VMEM((rows, feat), F32),
            pltpu.VMEM((rows, 1), F32),
            pltpu.VMEM((4,) + pieces[0].shape, BF16),
            pltpu.SemaphoreType.DMA((4,)),
            pltpu.SemaphoreType.DMA,
        ],
        out_shape=(
            shape((16, 2, hidden // 32, feat), BF16),
            shape((rows, hidden // 2), BF16),
            shape((rows, hidden // 2), BF16),
            shape((1, hidden), F32),
            shape((rows, feat), F32),
            shape((rows, feat // 2), BF16),
            shape((rows, feat // 2), BF16),
            shape((rows, feat), BF16),
            shape((8, feat), F32),
        ),
        compiler_params=params(32),
        name="fall",
        cost_estimate=cost(18),
    )(info, grad_y, *slopes, *up_sets, after, vecs, proj_set, *pieces)


def exit_kernel(
    info,
    tokens,
    mine,
    theirs,
    weights,
    grad_after,
    vecs,
    sums_a,
    bias,
    grad_tokens,
    keep,
    away,
    grad_first,
    joint,
    sums,
    extra,
):
    step = pl.program_id(0)
    core = info[CORE]
    third = mine.shape[2]
    half = jnp.where(step == 0, core, 1 - core)
    spot = pl.ds(pl.multiple_of(half * third, third), third)

    def parts(source):
        for part in range(3):
            joint[:, part * third : (part + 1) * third] = source[part]
        sums[3:4, spot] = jnp.sum(source[0].astype(F32), axis=0, keepdims=True)
        sums[4:5, spot] = jnp.sum(source[2].astype(F32), axis=0, keepdims=True)
        return dot_last(joint[...], weights[0])

    @pl.when(step == 0)
    def _():
        grad_first[...] = parts(mine)

    @pl.when(step == 1)
    def _():
        grad = grad_first[...] + parts(theirs)
        normed, inverse = centre(tokens[...].astype(F32))
        sums[0:1] = jnp.sum(grad * normed, axis=0, keepdims=True)
        sums[1:2] = sums_a[0:1]
        sums[2:3] = jnp.sum(grad, axis=0, keepdims=True)
        sums[5:6] = sums_a[2:3]
        sums[6:7] = sums_a[1:2]
        sums[7:8] = sums_a[3:4]
        sums[8:] = jnp.zeros_like(sums[8:])
        back = layer_back(grad * vecs[0:1], normed, inverse)
        grad_tokens[...] = (grad_after[...] + back).astype(BF16)
        flipped = sums[...].T
        block, each = extra.shape[1], bias.shape[1] // 32
        for chip in range(16):
            place = info[PLACE + chip]
            extra[place] = flipped[chip * block : (chip + 1) * block]
            for c in (0, 1):
                at = (2 * chip + c) * each
                row = c * block // 2
                extra[place, row : row + 1, 128 - each :] = bias[:, at : at + each]
        keep[...] = extra[:8]
        away[...] = extra[8:].astype(BF16)


def exit_back(chain, info, tokens, mine, theirs, first_set, grad_after, vecs, sums_a, bias):
    rows, feat = tokens.shape
    third = feat // 2
    block = feat // 16

    def whole(dims):
        return pl.BlockSpec(dims, lambda n, info: (0,) * len(dims))

    return chain.call(
        exit_kernel,
        prefetch=1,
        grid=(2,),
        in_specs=[
            whole((rows, feat)),
            whole((3, rows, third)),
            whole((3, rows, third)),
            pl.BlockSpec(
                (1, feat, 3 * third),
                lambda n, info: (jnp.where(n == 0, info[CORE], 1 - info[CORE]), 0, 0),
            ),
            whole((rows, feat)),
            whole((8, feat)),
            whole((8, feat)),
            whole(bias.shape),
        ],
        out_specs=(whole((rows, feat)), whole((8, block, 128)), whole((8, block, 128))),
        scratch_shapes=[
            pltpu.VMEM((rows, feat), F32),
            pltpu.VMEM((rows, 3 * third), BF16),
            pltpu.VMEM((128, feat), F32),
            pltpu.VMEM((16, block, 128), F32),
        ],
        out_shape=(
            shape((rows, feat), BF16),
            shape((8, block, 128), F32),
            shape((8, block, 128), BF16),
        ),
        compiler_params=params(18),
        name="exit_back",
        cost_estimate=cost(8),
    )(info, tokens, mine, theirs, first_set, grad_after, vecs, sums_a, bias)


def line_up(info, left, left_o, turned):
    rows = left.shape[2]
    for chip in range(16):
        place = info[PLACE + chip]
        turned[place, :, :rows] = left[chip]
        turned[place, :, rows:] = left_o[chip]


def outer_tile(turned, right, right_o):
    rows = right.shape[0]
    both = turned[...].reshape(-1, turned.shape[2])
    total = dot(both[:, :rows], right) + dot(both[:, rows:], right_o)
    return total.reshape(16, -1, total.shape[1])


def outer_up_kernel(
    info, left, left_o, right, right_o, low, low_o, attn, attn_o, keep, away, turned, *late
):
    step, last = pl.program_id(0), pl.num_programs(0) - 1
    buffers, sems = late[:4], late[4]
    copies = [
        pltpu.make_async_copy(src, dst, sems.at[i])
        for i, (src, dst) in enumerate(zip((low, low_o, attn, attn_o), buffers))
    ]

    @pl.when(step == 0)
    def _():
        for copy in copies:
            copy.start()
        line_up(info, left, left_o, turned)

    @pl.when(step < last)
    def _():
        total = outer_tile(turned, right[...], right_o[...])
        keep[...] = total[:8].astype(BF16)
        away[...] = total[8:].astype(BF16)

    @pl.when(step == last)
    def _():
        for copy in copies:
            copy.wait()
        line_up(info, buffers[0], buffers[1], turned)
        total = outer_tile(turned, buffers[2][...], buffers[3][...])
        keep[:, :, : attn.shape[1]] = total[:8].astype(BF16)
        away[:, :, : attn.shape[1]] = total[8:].astype(BF16)


def outer_up(chain, info, left, left_o, right, right_o, low, low_o, attn, attn_o):
    _, block, rows = left.shape
    tile = 2 * attn.shape[1]
    n = right.shape[1] // tile
    cols = right.shape[1] + attn.shape[1]
    strip = pl.BlockSpec((rows, tile), lambda i: (0, jnp.minimum(i, n - 1)))
    out = pl.BlockSpec((8, block, tile), lambda i: (0, 0, i))
    return chain.call(
        outer_up_kernel,
        grid=(n + 1,),
        out_shape=(shape((8, block, cols), BF16), shape((8, block, cols), BF16)),
        in_specs=[SMEM] + [full(left.shape)] * 2 + [strip] * 2 + [ANY] * 4,
        out_specs=(out, out),
        scratch_shapes=[pltpu.VMEM((16, block, 2 * rows), BF16)]
        + [pltpu.VMEM(left.shape, BF16)] * 2
        + [pltpu.VMEM(attn.shape, BF16)] * 2
        + [pltpu.SemaphoreType.DMA((4,))],
        compiler_params=params(20),
        name="outer_up",
        cost_estimate=cost(8),
    )(info, left, left_o, right, right_o, low, low_o, attn, attn_o)


def outer_qkv_kernel(info, left, left_o, right, right_o, keep, away, turned):
    tile = right.shape[2]
    line_up(info, left, left_o, turned)
    for part in range(3):
        cols = slice(part * tile, (part + 1) * tile)
        total = outer_tile(turned, right[part], right_o[part])
        keep[:, :, cols] = total[:8]
        away[:, :, cols] = total[8:].astype(BF16)


def outer_qkv(chain, info, left, left_o, right, right_o):
    _, block, rows = left.shape
    cols = 3 * right.shape[2]
    vmem = pl.BlockSpec(memory_space=pltpu.VMEM)
    return chain.call(
        outer_qkv_kernel,
        out_shape=(shape((8, block, cols), F32), shape((8, block, cols), BF16)),
        in_specs=[SMEM] + [vmem] * 4,
        out_specs=(vmem, vmem),
        scratch_shapes=[pltpu.VMEM((16, block, 2 * rows), BF16)],
        compiler_params=params(20),
        name="outer_qkv",
        cost_estimate=cost(8),
    )(info, left, left_o, right, right_o)


def outer_down_kernel(
    info, first, second, first_o, second_o, right, right_o, keep, away, turned
):
    rows = right.shape[0]
    core = info[CORE]
    for r in range(8):
        place = info[PLACE + 8 * core + r]
        turned[place, :, :rows] = first[r]
        turned[place, :, rows:] = second_o[r]
        place = info[PLACE + 8 * (1 - core) + r]
        turned[place, :, :rows] = second[r]
        turned[place, :, rows:] = first_o[r]
    for out, spots in ((away, slice(8, 16)), (keep, slice(0, 8))):
        left = turned[spots].reshape(-1, turned.shape[2])
        total = dot(left[:, :rows], right[...]) + dot(left[:, rows:], right_o[...])
        out[...] = total.reshape(out.shape).astype(out.dtype)


def outer_down(chain, info, first, second, first_o, second_o, right, right_o):
    _, block, rows = first.shape
    feat = right.shape[1]
    vmem = pl.BlockSpec(memory_space=pltpu.VMEM)
    return chain.call(
        outer_down_kernel,
        out_shape=(shape((8, block, feat), BF16), shape((8, block, feat), BF16)),
        in_specs=[SMEM] + [vmem] * 6,
        out_specs=(vmem, vmem),
        scratch_shapes=[pltpu.VMEM((16, block, 2 * rows), BF16)],
        compiler_params=params(24),
        name="outer_down",
        cost_estimate=cost(0),
    )(info, first, second, first_o, second_o, right, right_o)


def add_first_kernel(keep, got, kept, away, raw, low, sems):
    far = pltpu.make_async_copy(got.at[pl.ds(4, 4)], raw.at[1], sems.at[0])
    near = pltpu.make_async_copy(got.at[pl.ds(0, 4)], raw.at[0], sems.at[1])
    out = pltpu.make_async_copy(low, away, sems.at[2])
    far.start()
    near.start()
    far.wait()
    low[...] = (keep[4:].astype(F32) + raw[1].astype(F32)).astype(BF16)
    out.start()
    near.wait()
    kept[...] = keep[:4].astype(F32) + raw[0].astype(F32)
    out.wait()


def shift_first(chain, keep, away, micros=0):
    _, rows, cols = keep.shape
    vmem = pl.BlockSpec(memory_space=pltpu.VMEM)
    return chain.call(
        add_first_kernel,
        out_shape=(shape((4, rows, cols), F32), shape((4, rows, cols), BF16)),
        in_specs=[vmem, ANY],
        out_specs=(vmem, ANY),
        scratch_shapes=[
            pltpu.VMEM((2, 4, rows, cols), BF16),
            pltpu.VMEM((4, rows, cols), BF16),
            pltpu.SemaphoreType.DMA((3,)),
        ],
        compiler_params=params(12),
        name="shift_first",
        cost_estimate=cost(micros),
    )(keep, send(away, second_way))


def add_both_kernel(keep, got, few_keep, few_got, kept, away):
    split = keep.shape[2]
    kept[:, :, :split] = keep[:4] + got[:4].astype(F32)
    kept[:, :, split:] = few_keep[:4] + few_got[:4].astype(F32)
    away[:, :, :split] = (keep[4:] + got[4:].astype(F32)).astype(BF16)
    away[:, :, split:] = (few_keep[4:] + few_got[4:].astype(F32)).astype(BF16)


def shift_both(chain, keep, away, few_keep, few_away):
    _, rows, cols = keep.shape
    cols += few_keep.shape[2]
    vmem = pl.BlockSpec(memory_space=pltpu.VMEM)
    return chain.call(
        add_both_kernel,
        out_shape=(shape((4, rows, cols), F32), shape((4, rows, cols), BF16)),
        in_specs=[vmem] * 4,
        out_specs=(vmem, vmem),
        compiler_params=params(12),
        name="shift_both",
        cost_estimate=cost(0),
    )(keep, send(away, second_way), few_keep, send(few_away, second_way))


def add_second_kernel(keep, got, base, one, two, three):
    base[...] = keep[0] + got[0].astype(F32)
    for s, out in ((1, one), (2, two), (3, three)):
        out[...] = (keep[s] + got[s].astype(F32)).astype(BF16)


def shift_second(chain, keep, away):
    _, rows, cols = keep.shape
    vmem = pl.BlockSpec(memory_space=pltpu.VMEM)
    base, *lows = chain.call(
        add_second_kernel,
        out_shape=(shape((rows, cols), F32),) + (shape((rows, cols), BF16),) * 3,
        in_specs=[vmem, vmem],
        out_specs=(vmem,) * 4,
        compiler_params=params(8),
        name="shift_second",
        cost_estimate=cost(0),
    )(keep, send(away, first_way))
    return base, [send(low, along_z(s)) for low, s in zip(lows, (1, 2, 3))]


def total_of(base, parts):
    return base[...] + parts[0][...].astype(F32) + (
        parts[1][...].astype(F32) + parts[2][...].astype(F32)
    )


def add_down_kernel(base, one, two, three, out):
    out[...] = total_of(base, (one, two, three))


def home_down(chain, base, parts):
    vmem = pl.BlockSpec(memory_space=pltpu.VMEM)
    return chain.call(
        add_down_kernel,
        out_shape=shape(base.shape, F32),
        in_specs=[vmem] * 4,
        out_specs=vmem,
        compiler_params=params(8),
        name="home_down",
        cost_estimate=cost(0),
    )(base, *parts)


def add_last_kernel(info, base, one, two, three, mine, theirs, total):
    core = info[CORE]
    half = mine.shape[0]
    total[...] = total_of(base, (one, two, three))
    mine[...] = total[pl.ds(pl.multiple_of(core * half, half), half)]
    theirs[...] = total[pl.ds(pl.multiple_of((1 - core) * half, half), half)]


def home(chain, info, base, parts):
    rows, cols = base.shape
    vmem = pl.BlockSpec(memory_space=pltpu.VMEM)
    out = shape((rows // 2, cols), F32)
    mine, theirs = chain.call(
        add_last_kernel,
        out_shape=(out, out),
        in_specs=[SMEM] + [vmem] * 4,
        out_specs=(vmem, vmem),
        scratch_shapes=[pltpu.VMEM((rows, cols), F32)],
        compiler_params=params(8),
        name="home",
        cost_estimate=cost(0),
    )(info, base, *parts)
    return mine, swap(theirs)


def finish_kernel(info, qkv, qkv_o, up, up_o, out_qkv, out_proj, out_up, gains, shifts, bias):
    rows, third = out_proj.shape[0], out_proj.shape[1] // 2
    wide = out_up.shape[1] // 2
    small = qkv[:, 3 * third :] + qkv_o[:, 3 * third :]
    flipped = jnp.concatenate([small, jnp.zeros((128 - rows, 128), F32)]).T
    gains[...] = flipped[0:2, :rows]
    shifts[...] = flipped[2:8, :rows]
    bias[...] = small[0:1, 128 - bias.shape[1] :]

    def lay(core):
        for half, (a, b) in ((core, (qkv, up)), (1 - core, (qkv_o, up_o))):
            for part in range(3):
                spot = part * 2 * third + half * third
                out_qkv[:, spot : spot + third] = a[:, part * third : (part + 1) * third]
            out_proj[:, half * third : (half + 1) * third] = b[:, wide:]
            out_up[:, half * wide : (half + 1) * wide] = b[:, :wide]

    @pl.when(info[CORE] == 0)
    def _():
        lay(0)

    @pl.when(info[CORE] == 1)
    def _():
        lay(1)


def finish(chain, info, qkv, qkv_o, up, up_o):
    rows = qkv.shape[0]
    third = (qkv.shape[1] - 128) // 3
    vmem = pl.BlockSpec(memory_space=pltpu.VMEM)
    return chain.call(
        finish_kernel,
        out_shape=(
            shape((rows, 6 * third), F32),
            shape((rows, 2 * third), F32),
            shape((rows, 2 * (up.shape[1] - third)), F32),
            shape((2, rows), F32),
            shape((6, rows), F32),
            shape((1, 4 * rows), F32),
        ),
        in_specs=[SMEM] + [vmem] * 4,
        out_specs=(vmem,) * 6,
        compiler_params=params(8),
        name="finish",
        cost_estimate=cost(0),
    )(info, qkv, qkv_o, up, up_o)


def local(
    tokens,
    upstream,
    lengths,
    qkv_weight,
    proj_weight,
    up_weight,
    down_weight,
    gains,
    shifts,
    up_bias,
):
    tok_rows, feat = tokens.shape
    rows = qkv_weight.shape[0]
    hidden = up_weight.shape[1]
    third, wide = feat // 2, hidden // 2
    chip, core = lax.axis_index("dp"), lax.axis_index("fsdp")
    info = facts(chip, core, lengths[0])

    chain = Chain()

    small = jnp.concatenate([gains, shifts], axis=1)
    small = jnp.pad(small, ((0, 0), (0, 128 - small.shape[1])))
    small = small + jnp.pad(up_bias[None], ((0, rows - 1), (128 - up_bias.shape[0], 0)))
    piece = first_piece(chain, info, qkv_weight, swap(qkv_weight), small)
    piece_up = up_piece(chain, info, up_weight, swap(up_weight), proj_weight, swap(proj_weight))
    zs, piece_up = gather(chain, [piece] + near_z(piece, (3, 2, 1)), (piece_up,), 0, (0, 3, 2, 1))
    up_z = near_z(piece_up, (1, 2, 3))
    first = gate(chain, send(zs, first_way), 0)
    second, both = send(zs, second_way), send(first, second_way)
    (zs_up,) = gather(chain, [piece_up] + up_z, (), 5)
    pieces = both_cores(zs, first, gate(chain, second, 0), gate(chain, both, 0))
    zs = zs_up
    first_set, vecs, bias, first_t, joint, grad_y, down = enter(
        chain, info, tokens, upstream, down_weight, hidden, pieces
    )
    grad_y_o, first_o = swap(grad_y), swap(first_t)
    first_set = first_set.reshape(2, feat, 3 * third + 128)
    first, second = send(zs, first_way), send(zs, second_way)
    first = gate(chain, first, 0)
    pieces = both_cores(zs, first, second, send(first, second_way))
    down_z = near_z(down, (1, 2, 3))
    mixed, mixed_t, stats = mix(chain, info, joint)
    mixed_t = mixed_t.reshape(first_t.shape)
    mixed_o = swap(mixed_t)
    (zs,) = gather(chain, [down] + down_z, (), 5)
    proj_set, after, normed, normed_t = rise(chain, info, tokens, mixed, vecs, pieces)
    normed_o = swap(normed_t)
    up_a, active_a, slope_a, mine_a, theirs_a = widen(chain, 0, info, normed, bias, pieces[:4])
    theirs_a = swap(theirs_a)
    (low,) = gather(chain, [zs, send(zs, first_way)])
    high = send(low, second_way)
    up_b, active_b, slope_b, mine_b, theirs_b = widen(chain, 1, info, normed, bias, pieces[4:])
    proj_set = proj_set.reshape(2, feat, third)
    down = outer_down(
        chain, info, mine_a, mine_b, theirs_a, swap(theirs_b), grad_y, grad_y_o
    )
    pieces = both_cores(low, gate(chain, high, 0))
    up_sets = (up_a.reshape(feat, wide), up_b.reshape(feat, wide))
    down_set, hid_theirs, hid_mine, bias_sum, grad_after, at_theirs, at_mine, grad_mixed, sums_a = (
        fall(chain, info, grad_y, (slope_a, slope_b), up_sets, after, vecs, proj_set, pieces)
    )
    hid_o, at_o = swap(hid_theirs), swap(at_theirs)
    down = shift_first(chain, *down, 5)
    up = outer_up(chain, info, normed_t, normed_o, hid_mine, hid_o, mixed_t, mixed_o, at_mine, at_o)
    down = shift_second(chain, *down)
    theirs, mine = mix_back(chain, info, joint, grad_mixed, stats)
    theirs_o = swap(theirs)
    down = (down[0], [gate(chain, part, 0) for part in down[1]])
    up = shift_first(chain, *up, 5)
    chain.near(up[1])
    qkv = outer_qkv(chain, info, first_t, first_o, mine, theirs_o)
    grad_tokens, few_keep, few_away = exit_back(
        chain, info, tokens, mine, theirs, first_set, grad_after, vecs, sums_a, bias_sum
    )
    up = shift_second(chain, *up)
    qkv = shift_both(chain, *qkv, few_keep, few_away)
    output = leave(
        chain, info, after, active_a, active_b, down_set.reshape(hidden, feat), vecs
    )
    qkv = shift_second(chain, *qkv)
    own_down = home_down(chain, *down)
    own_up = home(chain, info, *up)
    own_qkv = home(chain, info, *qkv)
    out_qkv, out_proj, out_up, out_gains, out_shifts, out_bias = finish(
        chain, info, *own_qkv, *own_up
    )
    return (
        output,
        grad_tokens,
        out_qkv,
        out_proj,
        out_up,
        own_down,
        out_gains.T,
        out_shifts.T,
        out_bias.reshape(-1),
    )


def solution(mesh):
    placed = (
        P(("dp", "fsdp"), None),
        P(("dp", "fsdp"), None),
        P(("dp", "fsdp")),
        P(("dp", "fsdp"), None),
        P(("dp", "fsdp"), None),
        P(("dp", "fsdp"), None),
        P(("dp", "fsdp"), None),
        P(("dp", "fsdp"), None),
        P(("dp", "fsdp"), None),
        P(("dp", "fsdp")),
    )
    sizes = (mesh.shape["dp"], mesh.shape["fsdp"])
    return jax.shard_map(
        local if sizes == (16, 2) else plain,
        mesh=mesh,
        in_specs=placed,
        out_specs=(
            P(("dp", "fsdp"), None),
            P(("dp", "fsdp"), None),
            P(("dp", "fsdp"), None),
            P(("dp", "fsdp"), None),
            P(("dp", "fsdp"), None),
            P(("dp", "fsdp"), None),
            P(("dp", "fsdp"), None),
            P(("dp", "fsdp"), None),
            P(("dp", "fsdp")),
        ),
        check_vma=False,
    )
```

```python
import math
from functools import partial

import jax
import jax.numpy as jnp
from jax import lax
from jax.experimental import pallas as pl
from jax.experimental.pallas import tpu as pltpu
from jax.sharding import PartitionSpec as P

HEADS = 12
EPS = 1e-06
NEG = -1e30
AXES = ("dp", "fsdp")
F32 = jnp.float32
BF16 = jnp.bfloat16
VMEM_LIMIT = 32 * 1024 * 1024


def collect(qkv_weight, proj_weight, up_weight, down_weight, gains, shifts, up_bias):
    gathered = (
        lax.all_gather(qkv_weight, ("dp", "fsdp"), axis=0, tiled=True),
        lax.all_gather(proj_weight, ("dp", "fsdp"), axis=0, tiled=True),
        lax.all_gather(up_weight, ("dp", "fsdp"), axis=0, tiled=True),
        lax.all_gather(down_weight, ("dp", "fsdp"), axis=0, tiled=True),
        lax.all_gather(gains, ("dp", "fsdp"), axis=0, tiled=True),
        lax.all_gather(shifts, ("dp", "fsdp"), axis=0, tiled=True),
        lax.all_gather(up_bias, ("dp", "fsdp"), axis=0, tiled=True),
    )
    return gathered


def give_back(grad_qkv, grad_proj, grad_up, grad_down, grad_gains, grad_shifts, grad_bias_up):
    owned = (
        lax.psum_scatter(grad_qkv, ("dp", "fsdp"), scatter_dimension=0, tiled=True),
        lax.psum_scatter(grad_proj, ("dp", "fsdp"), scatter_dimension=0, tiled=True),
        lax.psum_scatter(grad_up, ("dp", "fsdp"), scatter_dimension=0, tiled=True),
        lax.psum_scatter(grad_down, ("dp", "fsdp"), scatter_dimension=0, tiled=True),
        lax.psum_scatter(grad_gains, ("dp", "fsdp"), scatter_dimension=0, tiled=True),
        lax.psum_scatter(grad_shifts, ("dp", "fsdp"), scatter_dimension=0, tiled=True),
        lax.psum_scatter(grad_bias_up, ("dp", "fsdp"), scatter_dimension=0, tiled=True),
    )
    return owned


def normalize(values):
    centred = values - jnp.mean(values, axis=-1, keepdims=True)
    inverse = lax.rsqrt(jnp.mean(centred * centred, axis=-1, keepdims=True) + EPS)
    return (centred * inverse, inverse)


def norm_back(grad_norm, normed, inverse):
    return inverse * (
        grad_norm
        - jnp.mean(grad_norm, axis=-1, keepdims=True)
        - normed * jnp.mean(grad_norm * normed, axis=-1, keepdims=True)
    )


def block_scores(query_blk, key_rows, live_mask, scaling):
    raw = (
        jnp.einsum("qhd,khd->hqk", query_blk, key_rows, preferred_element_type=jnp.float32)
        * scaling
    )
    return jnp.where(live_mask[None, None, :], raw, NEG)


def plain(
    tokens,
    upstream,
    lengths,
    qkv_weight,
    proj_weight,
    up_weight,
    down_weight,
    gains,
    shifts,
    up_bias,
):
    tok_rows, feat_width = tokens.shape
    n_heads = HEADS
    head_size = feat_width // n_heads
    scaling = head_size ** (-0.5)
    block_rows = min(512, tok_rows)
    group_heads = 4
    head_starts = list(range(0, n_heads, group_heads))
    gathered = collect(qkv_weight, proj_weight, up_weight, down_weight, gains, shifts, up_bias)
    qkv_full, proj_full, up_full, down_full, gain_full, shift_full, bias_full = gathered
    gain_f = gain_full.astype(jnp.float32)
    shift_f = shift_full.astype(jnp.float32)
    bias_f = bias_full.astype(jnp.float32)
    live_mask = lax.iota(jnp.int32, tok_rows) < lengths[0]
    source = tokens.astype(jnp.float32)
    norm_one, inv_one = normalize(source)
    first = (norm_one * gain_f[:, 0] + shift_f[:, 0]).astype(jnp.bfloat16)
    joint_bias = jnp.concatenate([shift_f[:, 1], jnp.zeros_like(shift_f[:, 1]), shift_f[:, 2]])
    joint = (jnp.dot(first, qkv_full, preferred_element_type=jnp.float32) + joint_bias).astype(
        jnp.bfloat16
    )
    queries = joint[:, :feat_width].reshape(tok_rows, n_heads, head_size)
    key_rows = joint[:, feat_width : 2 * feat_width].reshape(tok_rows, n_heads, head_size)
    value_rows = joint[:, 2 * feat_width :].reshape(tok_rows, n_heads, head_size)
    log_sums = {}
    offset = 0
    group_parts = []
    for head_lo in head_starts:
        head_hi = head_lo + group_heads
        scores = block_scores(
            queries[offset : offset + block_rows, head_lo:head_hi],
            key_rows[:, head_lo:head_hi],
            live_mask,
            scaling,
        )
        row_max = jnp.max(scores, axis=-1, keepdims=True)
        expd = jnp.exp(scores - row_max)
        row_sum = jnp.sum(expd, axis=-1, keepdims=True)
        attn_low = (expd / row_sum).astype(jnp.bfloat16)
        log_sums[offset, head_lo] = row_max + jnp.log(row_sum)
        group_parts.append(
            jnp.einsum(
                "hqk,khd->qhd",
                attn_low,
                value_rows[:, head_lo:head_hi],
                preferred_element_type=jnp.float32,
            )
        )
    mixed_parts = jnp.concatenate(group_parts, axis=1)
    mixed = mixed_parts.reshape(tok_rows, feat_width).astype(jnp.bfloat16)
    after = source + jnp.dot(mixed, proj_full, preferred_element_type=jnp.float32) + shift_f[:, 3]
    norm_two, inv_two = normalize(after)
    second = (norm_two * gain_f[:, 1] + shift_f[:, 4]).astype(jnp.bfloat16)
    hidden = jnp.dot(second, up_full, preferred_element_type=jnp.float32) + bias_f
    gelu_exact = partial(jax.nn.gelu, approximate=False)
    active = gelu_exact(hidden).astype(jnp.bfloat16)
    output = (
        after + jnp.dot(active, down_full, preferred_element_type=jnp.float32) + shift_f[:, 5]
    ).astype(jnp.bfloat16)
    regathered = collect(qkv_weight, proj_weight, up_weight, down_weight, gains, shifts, up_bias)
    qkv_full, proj_full, up_full, down_full, gain_full, shift_full, bias_full = regathered
    grad_y = jnp.where(live_mask[:, None], upstream, jnp.zeros_like(upstream))
    sum_y = jnp.sum(grad_y, axis=0, dtype=jnp.float32)
    grad_down = jnp.einsum("tf,td->fd", active, grad_y, preferred_element_type=jnp.float32)
    grad_active = jnp.einsum("td,fd->tf", grad_y, down_full, preferred_element_type=jnp.float32)
    gelu_value, gelu_pull = jax.vjp(gelu_exact, hidden)
    grad_hidden = gelu_pull(grad_active)[0].astype(jnp.bfloat16)
    grad_bias_up = jnp.sum(grad_hidden, axis=0, dtype=jnp.float32)
    grad_up = jnp.einsum("td,tf->df", second, grad_hidden, preferred_element_type=jnp.float32)
    grad_second = jnp.einsum("tf,df->td", grad_hidden, up_full, preferred_element_type=jnp.float32)
    gain_two_grad = jnp.sum(grad_second * norm_two, axis=0)
    shift_two_grad = jnp.sum(grad_second, axis=0)
    grad_after = grad_y.astype(jnp.float32) + norm_back(
        grad_second * gain_f[:, 1], norm_two, inv_two
    )
    grad_attn = grad_after.astype(jnp.bfloat16)
    sum_attn = jnp.sum(grad_attn, axis=0, dtype=jnp.float32)
    grad_proj = jnp.einsum("td,te->de", mixed, grad_attn, preferred_element_type=jnp.float32)
    grad_mixed = jnp.einsum("te,de->td", grad_attn, proj_full, preferred_element_type=jnp.float32)
    grad_mixed = grad_mixed.astype(jnp.bfloat16).reshape(tok_rows, n_heads, head_size)
    key_groups = {}
    value_groups = {}
    for head_lo in head_starts:
        key_groups[head_lo] = jnp.zeros((tok_rows, group_heads, head_size), jnp.float32)
        value_groups[head_lo] = jnp.zeros((tok_rows, group_heads, head_size), jnp.float32)
    offset = 0
    query_groups = []
    for head_lo in head_starts:
        head_hi = head_lo + group_heads
        query_blk = queries[offset : offset + block_rows, head_lo:head_hi]
        grad_blk = grad_mixed[offset : offset + block_rows, head_lo:head_hi]
        key_part = key_rows[:, head_lo:head_hi]
        scores = block_scores(query_blk, key_part, live_mask, scaling)
        attn_p = jnp.exp(scores - log_sums[offset, head_lo])
        value_groups[head_lo] = jnp.einsum(
            "hqk,qhd->khd",
            attn_p.astype(jnp.bfloat16),
            grad_blk,
            preferred_element_type=jnp.float32,
        )
        grad_prob = jnp.einsum(
            "qhd,khd->hqk",
            grad_blk,
            value_rows[:, head_lo:head_hi],
            preferred_element_type=jnp.float32,
        )
        grad_score = attn_p * (grad_prob - jnp.sum(attn_p * grad_prob, axis=-1, keepdims=True))
        score_low = grad_score.astype(jnp.bfloat16)
        query_groups.append(
            jnp.einsum("hqk,khd->qhd", score_low, key_part, preferred_element_type=jnp.float32)
            * scaling
        )
        key_groups[head_lo] = (
            jnp.einsum("hqk,qhd->khd", score_low, query_blk, preferred_element_type=jnp.float32)
            * scaling
        )
    grad_query_parts = jnp.concatenate(query_groups, axis=1)
    grad_keys = jnp.concatenate([key_groups[head_lo] for head_lo in head_starts], axis=1)
    grad_vals = jnp.concatenate([value_groups[head_lo] for head_lo in head_starts], axis=1)
    grad_joint = jnp.concatenate(
        [
            grad_query_parts.reshape(tok_rows, feat_width),
            grad_keys.reshape(tok_rows, feat_width),
            grad_vals.reshape(tok_rows, feat_width),
        ],
        axis=1,
    ).astype(jnp.bfloat16)
    joint_sums = jnp.sum(grad_joint, axis=0, dtype=jnp.float32)
    grad_qkv = jnp.einsum("td,te->de", first, grad_joint, preferred_element_type=jnp.float32)
    grad_first = jnp.einsum("te,de->td", grad_joint, qkv_full, preferred_element_type=jnp.float32)
    gain_one_grad = jnp.sum(grad_first * norm_one, axis=0)
    shift_one_grad = jnp.sum(grad_first, axis=0)
    grad_tokens = (grad_after + norm_back(grad_first * gain_f[:, 0], norm_one, inv_one)).astype(
        jnp.bfloat16
    )
    grad_gains = jnp.stack([gain_one_grad, gain_two_grad], axis=1)
    grad_shifts = jnp.stack(
        [
            shift_one_grad,
            joint_sums[:feat_width],
            joint_sums[2 * feat_width :],
            sum_attn,
            shift_two_grad,
            sum_y,
        ],
        axis=1,
    )
    owned = give_back(
        grad_qkv, grad_proj, grad_up, grad_down, grad_gains, grad_shifts, grad_bias_up
    )
    own_qkv, own_proj, own_up, own_down, own_gains, own_shifts, own_bias = owned
    return (
        output,
        grad_tokens,
        own_qkv,
        own_proj,
        own_up,
        own_down,
        own_gains,
        own_shifts,
        own_bias,
    )


BOTH_LAST = (((1,), (1,)), ((), ()))
SMEM = pl.BlockSpec(memory_space=pltpu.SMEM)
ANY = pl.BlockSpec(memory_space=pl.ANY)
CORE, LENGTH, PLACE, PLACE_O = 32, 33, 34, 50


def pairs(move):
    return [(i, move(i)) for i in range(32)]


def first_way(i):
    return i ^ (2 if i % 2 == 0 else 4)


def second_way(i):
    return i ^ (4 if i % 2 == 0 else 2)


def along_z(step):
    return lambda i: i ^ (8 * step)


def send(array, move):
    return lax.ppermute(array, AXES, pairs(move))


def swap(array):
    return send(array, lambda i: i ^ 1)


def facts(chip, core, length):
    places = []
    for of_core in (core, 1 - core):
        for j in range(16):
            z, first, second = j % 4, (j // 4) % 2, j // 8
            mask = jnp.where(of_core == 0, first + 2 * second, second + 2 * first)
            places.append(jnp.bitwise_xor(chip, mask + 4 * z))
    spots = []
    for of_core in (core, 1 - core):
        for k in range(16):
            mask = jnp.bitwise_xor(chip, k)
            x, y, z = mask & 1, (mask >> 1) & 1, mask >> 2
            spots.append(z + jnp.where(of_core == 0, 4 * x + 8 * y, 4 * y + 8 * x))
    return jnp.stack(places + [core, length] + spots).astype(jnp.int32)


def params(mib):
    return pltpu.CompilerParams(vmem_limit_bytes=mib * 1024 * 1024)


def cost(micros):
    flops = int(micros * (3e10 if micros > 3 else 1e9))
    return pl.CostEstimate(flops=flops, bytes_accessed=1, transcendentals=0)


def shape(dims, dtype):
    return jax.ShapeDtypeStruct(dims, dtype)


def full(dims):
    return pl.BlockSpec(dims, lambda *_: (0,) * len(dims))


class Chain:
    def __init__(self):
        self.token, self.extra = None, ()

    def near(self, *arrays):
        self.extra = arrays

    def call(
        self, kernel, *, out_shape, in_specs, out_specs, grid=(), prefetch=0, aliases={}, **options
    ):
        single = not isinstance(out_shape, tuple)
        if single:
            out_shape, out_specs = (out_shape,), (out_specs,)
        held = 0 if self.token is None else 1
        extra, self.extra = self.extra, ()
        n_in, n_out = prefetch + len(in_specs), len(out_shape)
        at_token = n_in + len(extra)

        def body(*refs):
            skip = at_token + held
            return kernel(*refs[:n_in], *refs[skip : skip + n_out], *refs[skip + n_out + 1 :])

        token = shape((8, 128), F32)
        specs = pltpu.PrefetchScalarGridSpec(
            num_scalar_prefetch=prefetch,
            grid=grid,
            in_specs=list(in_specs) + [ANY] * (len(extra) + held),
            out_specs=tuple(out_specs) + (ANY,),
            scratch_shapes=options.pop("scratch_shapes", ()),
        )
        run = pl.pallas_call(
            body,
            grid_spec=specs,
            out_shape=tuple(out_shape) + (token,),
            input_output_aliases=aliases | ({at_token: n_out} if held else {}),
            **options,
        )

        def with_token(*args):
            *outs, self.token = run(*args, *extra, *([self.token] if held else []))
            return outs[0] if single else tuple(outs)

        return with_token


def dot(left, right):
    return jnp.dot(left, right, preferred_element_type=F32)


def dot_last(left, right):
    return lax.dot_general(left, right, BOTH_LAST, preferred_element_type=F32)


def settle(info, pieces, dest, who=(0, 1)):
    few = pieces[0].shape[0]
    for w in who:
        half = info[CORE] if w == 0 else 1 - info[CORE]
        for j in range(16):
            dest[half, info[16 * w + j]] = pieces[(16 * w + j) // few][j % few]


def bring(pieces, raw, sems, start):
    cols = pl.ds(start, raw.shape[-1])
    return [
        pltpu.make_async_copy(piece.at[:, :, cols], raw.at[i], sems.at[i])
        for i, piece in enumerate(pieces)
    ]


def centre(values):
    centred = values - jnp.mean(values, axis=-1, keepdims=True)
    inverse = lax.rsqrt(jnp.mean(centred * centred, axis=-1, keepdims=True) + EPS)
    return centred * inverse, inverse


def layer_back(grad, normed, inverse):
    return inverse * (
        grad
        - jnp.mean(grad, axis=-1, keepdims=True)
        - normed * jnp.mean(grad * normed, axis=-1, keepdims=True)
    )


def stacked(core, mine, others):
    pair = (mine, others) if core == 0 else (others, mine)
    return jnp.concatenate([part.astype(F32) for part in pair]).astype(BF16)


def by_core(info, lay):
    for core in (0, 1):
        pl.when(info[CORE] == core)(partial(lay, core))


def first_piece_kernel(info, qkv, qkv_o, small, out):
    third = qkv.shape[1] // 6

    def lay(core):
        for i in range(3):
            cols = slice((2 * i + core) * third, (2 * i + core + 1) * third)
            out[0, :, i * third : (i + 1) * third] = stacked(core, qkv[:, cols], qkv_o[:, cols])
        out[0, :, 3 * third :] = stacked(core, small[...], jnp.zeros_like(small))

    by_core(info, lay)


def first_piece(chain, info, qkv, qkv_o, small):
    rows, cols = qkv.shape
    vmem = pl.BlockSpec(memory_space=pltpu.VMEM)
    return chain.call(
        first_piece_kernel,
        out_shape=shape((1, 2 * rows, cols // 2 + small.shape[1]), BF16),
        in_specs=[SMEM] + [vmem] * 3,
        out_specs=vmem,
        compiler_params=params(8),
        name="first_piece",
        cost_estimate=cost(0),
    )(info, qkv, qkv_o, small)


def up_piece_kernel(info, up, up_o, proj, proj_o, out):
    wide, third = up.shape[1] // 2, proj.shape[1] // 2

    def lay(core):
        for whole, other, at, width in ((up, up_o, 0, wide), (proj, proj_o, wide, third)):
            cols = slice(core * width, (core + 1) * width)
            out[0, :, at : at + width] = stacked(core, whole[:, cols], other[:, cols])

    by_core(info, lay)


def up_piece(chain, info, up, up_o, proj, proj_o):
    rows = up.shape[0]
    vmem = pl.BlockSpec(memory_space=pltpu.VMEM)
    return chain.call(
        up_piece_kernel,
        out_shape=shape((1, 2 * rows, (up.shape[1] + proj.shape[1]) // 2), BF16),
        in_specs=[SMEM] + [vmem] * 4,
        out_specs=vmem,
        compiler_params=params(8),
        name="up_piece",
        cost_estimate=cost(0),
    )(info, up, up_o, proj, proj_o)


def gather_kernel(n_in, n_held, order, *refs):
    out = refs[n_in + n_held]
    for i, part in enumerate(refs[:n_in]):
        at = part.shape[0] * (i if order is None else order[i])
        out[at : at + part.shape[0]] = part[...]
    for i in range(n_held):
        refs[n_in + n_held + 1 + i][...] = refs[n_in + i][...]


def gather(chain, parts, held=(), micros=0, order=None):
    vmem = pl.BlockSpec(memory_space=pltpu.VMEM)
    _, rows, cols = parts[0].shape
    count = sum(part.shape[0] for part in parts)
    n, n_held = len(parts), len(held)
    return chain.call(
        partial(gather_kernel, n, n_held, order),
        out_shape=(shape((count, rows, cols), BF16),) + tuple(shape(h.shape, h.dtype) for h in held),
        in_specs=[vmem] * (n + n_held),
        out_specs=(vmem,) * (1 + n_held),
        compiler_params=params(16),
        name="gather",
        cost_estimate=cost(micros),
    )(*parts, *held)


def gate_kernel(array, out):
    pass


def gate(chain, array, micros):
    return chain.call(
        gate_kernel,
        out_shape=shape(array.shape, array.dtype),
        in_specs=[ANY],
        out_specs=ANY,
        aliases={0: 0},
        compiler_params=params(4),
        name="gate",
        cost_estimate=cost(micros),
    )(array)


def both_cores(*own):
    return own + tuple(swap(blocks) for blocks in own)


def near_z(piece, steps):
    return [send(piece, along_z(s)) for s in steps]


def enter_kernel(
    info,
    tokens,
    upstream,
    down,
    *refs,
):
    pieces = refs[:8]
    kept, vecs, bias, flipped, joint, grad_y, piece_down, weights, sem = refs[8:]
    feat = tokens.shape[1]
    third = feat // 2
    piece_down[0] = down[...]
    place = lax.broadcasted_iota(jnp.int32, upstream.shape, 0)
    grad_y[...] = jnp.where(place < info[LENGTH], upstream[...].astype(F32), 0.0).astype(BF16)
    settle(info, pieces, weights)
    normed, _ = centre(tokens[...].astype(F32))
    out = pltpu.make_async_copy(weights, kept, sem)
    out.start()
    split = 3 * third
    small = weights[0, :, :, split:] + weights[1, :, :, split:]
    small = small.reshape(feat, 128).astype(F32)
    each = bias.shape[1] // 32
    for device in range(32):
        row = device * feat // 32
        bias[:, device * each : (device + 1) * each] = small[row : row + 1, 128 - each :]
    small = small.T
    vecs[...] = small[:8]
    low_first = (normed * small[0:1] + small[2:3]).astype(BF16)
    flipped[...] = low_first.T.reshape(flipped.shape)
    for h in (0, 1):
        cols = slice(h * third, (h + 1) * third)
        bias = jnp.concatenate(
            [small[3:4, cols], jnp.zeros((1, third), F32), small[4:5, cols]], axis=1
        )
        w = weights[h, :, :, :split].reshape(feat, split)
        joint[h] = (dot(low_first, w) + bias).astype(BF16)
    out.wait()


def enter(chain, info, tokens, upstream, down, hidden, pieces):
    rows, feat = tokens.shape
    width = pieces[0].shape[-1]
    vmem = pl.BlockSpec(memory_space=pltpu.VMEM)
    sets = (2, 16, feat // 16, width)
    return chain.call(
        enter_kernel,
        out_shape=(
            shape(sets, BF16),
            shape((8, feat), F32),
            shape((1, hidden), F32),
            shape((16, feat // 16, rows), BF16),
            shape((2, rows, 3 * feat // 2), BF16),
            shape((rows, feat), BF16),
            shape((1,) + down.shape, BF16),
        ),
        in_specs=[SMEM] + [vmem] * 11,
        out_specs=(ANY,) + (vmem,) * 6,
        scratch_shapes=[pltpu.VMEM(sets, BF16), pltpu.SemaphoreType.DMA],
        compiler_params=params(20),
        name="enter",
        cost_estimate=cost(8),
    )(info, tokens, upstream, down, *pieces)


def scores_of(info, keys, queries):
    raw = dot_last(keys, queries)
    place = lax.broadcasted_iota(jnp.int32, raw.shape, 0)
    return jnp.where(place < info[LENGTH], raw, NEG)


def mix_kernel(info, q, k, v, mixed, flipped, stats):
    head = mixed.shape[1] // (HEADS // 2)
    count = q.shape[-1] // head
    scale = head**-0.5
    turned = v[0].T

    def start(h):
        cols = slice(h * head, (h + 1) * head)
        return scores_of(info, k[0, :, cols], q[0, :, cols] * scale)

    def finish(h, scores):
        cols = slice(h * head, (h + 1) * head)
        most = jnp.max(scores, axis=0, keepdims=True)
        expd = jnp.exp(scores - most)
        total = jnp.sum(expd, axis=0, keepdims=True)
        attn = (expd * (1.0 / total)).astype(BF16)
        stats[h // 2, h % 2 : h % 2 + 1] = most + jnp.log(total)
        return dot(turned[cols], attn)

    ready = [start(h) for h in range(2)]
    outs = []
    for h in range(count):
        if h + 2 < count:
            ready.append(start(h + 2))
        outs.append(finish(h, ready[h]))
    both = jnp.concatenate(outs)
    flipped[...] = both.astype(BF16)
    mixed[...] = both.T.astype(BF16)


def mix(chain, info, joint):
    _, rows, width = joint.shape
    feat = 2 * width // 3
    wide = feat // 2
    spec = [pl.BlockSpec((1, rows, wide), lambda i, part=part: (i, 0, part)) for part in range(3)]
    pairs_in_half = HEADS // 4
    return chain.call(
        mix_kernel,
        grid=(2,),
        out_shape=(
            shape((rows, feat), BF16),
            shape((feat, rows), BF16),
            shape((HEADS // 2, 8, rows), F32),
        ),
        in_specs=[SMEM] + spec,
        out_specs=(
            pl.BlockSpec((rows, wide), lambda i: (0, i)),
            pl.BlockSpec((wide, rows), lambda i: (i, 0)),
            pl.BlockSpec((pairs_in_half, 8, rows), lambda i: (i, 0, 0)),
        ),
        compiler_params=params(24),
        name="mix",
        cost_estimate=cost(10),
    )(info, joint, joint, joint)


def mix_back_kernel(info, q, k, v, grad, stats, theirs, mine):
    head = theirs.shape[2] // (HEADS // 2)
    count = q.shape[-1] // head
    scale = head**-0.5
    turned = k[0].T

    def start(h):
        cols = slice(h * head, (h + 1) * head)
        queries = q[0, :, cols] * scale
        scores = scores_of(info, k[0, :, cols], queries)
        return cols, queries, scores, dot_last(v[0, :, cols], grad[:, cols])

    def finish(h, cols, queries, scores, grad_prob):
        attn = jnp.exp(scores - stats[h // 2, h % 2 : h % 2 + 1])
        inner = jnp.sum(attn * grad_prob, axis=0, keepdims=True)
        low = (attn * (grad_prob - inner)).astype(BF16)
        return (
            dot(turned[cols], low) * scale,
            dot(low, queries),
            dot(attn.astype(BF16), grad[:, cols]),
        )

    ready = [start(h) for h in range(2)]
    done = []
    for h in range(count):
        if h + 2 < count:
            ready.append(start(h + 2))
        done.append(finish(h, *ready[h]))
    out = [
        jnp.concatenate([d[0] for d in done]).T.astype(BF16),
        jnp.concatenate([d[1] for d in done], axis=1).astype(BF16),
        jnp.concatenate([d[2] for d in done], axis=1).astype(BF16),
    ]

    @pl.when(pl.program_id(0) == 0)
    def _():
        for part in range(3):
            theirs[part] = out[part]

    @pl.when(pl.program_id(0) == 1)
    def _():
        for part in range(3):
            mine[part] = out[part]


def mix_back(chain, info, joint, grad_mixed, stats):
    _, rows, width = joint.shape
    feat = 2 * width // 3
    wide = feat // 2

    def half(i, info):
        return jnp.where(i == 0, 1 - info[CORE], info[CORE])

    spec = [
        pl.BlockSpec((1, rows, wide), lambda i, info, part=part: (half(i, info), 0, part))
        for part in range(3)
    ]
    out = shape((3, rows, feat // 2), BF16)
    return chain.call(
        mix_back_kernel,
        prefetch=1,
        grid=(2,),
        in_specs=spec
        + [
            pl.BlockSpec((rows, wide), lambda i, info: (0, half(i, info))),
            pl.BlockSpec((HEADS // 4, 8, rows), lambda i, info: (half(i, info), 0, 0)),
        ],
        out_specs=(
            pl.BlockSpec((3, rows, wide), lambda i, info: (0, 0, 0)),
            pl.BlockSpec((3, rows, wide), lambda i, info: (0, 0, 0)),
        ),
        out_shape=(out, out),
        compiler_params=params(30),
        name="mix_back",
        cost_estimate=cost(16),
    )(info, joint, joint, joint, grad_mixed, stats)


GELU = (0.254829592, -0.284496736, 1.421413741, -1.453152027, 1.061405429)


def gelu_parts(x):
    bell = jnp.exp2(x * x * (-0.5 / math.log(2)))
    below = 1.0 + (0.3275911 * 0.5**0.5) * jnp.abs(x)
    t = pl.reciprocal(below, approx=True)
    t = t * (2.0 - below * t)
    poly = 0.5 * GELU[4]
    for c in GELU[3::-1]:
        poly = poly * t + 0.5 * c
    tail = poly * t * bell
    phi = jnp.where(x < 0, tail, 1.0 - tail)
    return x * phi, phi + x * (bell * (2 * math.pi) ** -0.5)


def rise_kernel(info, tokens, mixed, vecs, *refs):
    pieces = refs[:8]
    weights, after, second, flipped, raw, sems = refs[8:]
    feat = tokens.shape[1]
    copies = bring(pieces, raw, sems, pieces[0].shape[2] - raw.shape[-1])
    for copy in copies:
        copy.start()
    start = tokens[...].astype(F32) + vecs[5:6]
    for copy in copies:
        copy.wait()
    settle(info, [raw.at[i] for i in range(8)], weights)
    grown = [dot(mixed[...], weights[h].reshape(feat, feat // 2)) for h in (0, 1)]
    total = start + jnp.concatenate(grown, axis=1)
    after[...] = total
    normed, _ = centre(total)
    value = (normed * vecs[1:2] + vecs[6:7]).astype(BF16)
    second[...] = value
    flipped[...] = value.T.reshape(flipped.shape)


def rise(chain, info, tokens, mixed, vecs, pieces):
    rows, feat = tokens.shape
    vmem = pl.BlockSpec(memory_space=pltpu.VMEM)
    block = feat // 16
    return chain.call(
        rise_kernel,
        out_shape=(
            shape((2, 16, block, feat // 2), BF16),
            shape((rows, feat), F32),
            shape((rows, feat), BF16),
            shape((16, block, rows), BF16),
        ),
        in_specs=[SMEM] + [vmem] * 3 + [ANY] * 8,
        out_specs=(vmem,) * 4,
        scratch_shapes=[
            pltpu.VMEM((8, 4, block, feat // 2), BF16),
            pltpu.SemaphoreType.DMA((8,)),
        ],
        compiler_params=params(16),
        name="rise",
        cost_estimate=cost(5),
    )(info, tokens, mixed, vecs, *pieces)


def widen_kernel(which, info, second, bias, *refs):
    pieces = refs[:4]
    weights, active, slope, mine, theirs, raw, sems = refs[4:]
    step = pl.program_id(0)
    core = info[CORE]
    feat = second.shape[1]
    tile = active.shape[1]
    rows = mine.shape[1]
    count = tile // rows

    @pl.when(step == 0)
    def _():
        copies = bring(pieces, raw, sems, 0)
        for copy in copies:
            copy.start()
        for copy in copies:
            copy.wait()
        for j in range(16):
            weights[info[16 * which + j]] = raw[j // 4, j % 4]

    cols = pl.ds(pl.multiple_of(step * tile, tile), tile)
    w = weights[:, :, cols].reshape(feat, tile)
    hidden = dot(second[...], w) + bias[...]
    value, grad = gelu_parts(hidden)
    value = value.astype(BF16)
    active[...] = value
    slope[...] = grad.astype(BF16)
    flipped = value.T.reshape(count // 2, 2, rows, -1)
    mine[...] = jnp.where(core == 0, flipped[:, 0], flipped[:, 1])
    theirs[...] = jnp.where(core == 0, flipped[:, 1], flipped[:, 0])


def widen(chain, which, info, second, bias, pieces):
    rows, feat = second.shape
    wide = pieces[0].shape[-1] - feat // 2
    tile, block = 768, wide // 16
    per = wide // tile
    turned = shape((8, block, rows), BF16)

    def whole(dims):
        return pl.BlockSpec(dims, lambda n, info: (0,) * len(dims))

    def bias_at(n, info):
        half = info[CORE] if which == 0 else 1 - info[CORE]
        return (0, half * per + n)

    strip = pl.BlockSpec((rows, tile), lambda n, info: (0, n))
    part = pl.BlockSpec((tile // block // 2, block, rows), lambda n, info: (n, 0, 0))
    return chain.call(
        partial(widen_kernel, which),
        prefetch=1,
        grid=(per,),
        out_shape=(
            shape((16, feat // 16, wide), BF16),
            shape((rows, wide), BF16),
            shape((rows, wide), BF16),
            turned,
            turned,
        ),
        in_specs=[whole((rows, feat)), pl.BlockSpec((1, tile), bias_at)] + [ANY] * 4,
        out_specs=(whole((16, feat // 16, wide)), strip, strip, part, part),
        scratch_shapes=[
            pltpu.VMEM((4, 4, feat // 16, wide), BF16),
            pltpu.SemaphoreType.DMA((4,)),
        ],
        compiler_params=params(24),
        name="widen",
        cost_estimate=cost(18),
    )(info, second, bias, *pieces)


def leave_kernel(info, after, first, second, down, vecs, output, total):
    step, per = pl.program_id(0), pl.num_programs(0) // 2

    @pl.when(step == 0)
    def _():
        total[...] = after[...] + vecs[7:8] + dot(first[...], down[...])

    @pl.when((step > 0) & (step < per))
    def _():
        total[...] += dot(first[...], down[...])

    @pl.when(step >= per)
    def _():
        total[...] += dot(second[...], down[...])

    @pl.when(step == 2 * per - 1)
    def _():
        output[...] = total[...].astype(BF16)


def leave(chain, info, after, first, second, down, vecs):
    rows, feat = after.shape
    tile = 768
    per = first.shape[1] // tile

    def whole(dims):
        return pl.BlockSpec(dims, lambda n, info: (0,) * len(dims))

    def down_at(n, info):
        half = jnp.where(n < per, info[CORE], 1 - info[CORE])
        return (half * per + n % per, 0)

    return chain.call(
        leave_kernel,
        prefetch=1,
        grid=(2 * per,),
        out_shape=shape((rows, feat), BF16),
        in_specs=[
            whole((rows, feat)),
            pl.BlockSpec((rows, tile), lambda n, info: (0, jnp.minimum(n, per - 1))),
            pl.BlockSpec((rows, tile), lambda n, info: (0, jnp.maximum(n - per, 0))),
            pl.BlockSpec((tile, feat), down_at),
            whole((8, feat)),
        ],
        out_specs=whole((rows, feat)),
        scratch_shapes=[pltpu.VMEM((rows, feat), F32)],
        compiler_params=params(16),
        name="leave",
        cost_estimate=cost(7),
    )(info, after, first, second, down, vecs)


def fall_kernel(info, grad_y, slope, slope_o, up, up_o, after, vecs, proj, *refs):
    pieces = refs[:4]
    kept, theirs, mine, bias_sum, grad_after, attn_theirs, attn_mine, grad_mixed, sums = refs[4:13]
    weights, grad_second, normed, inverse, raw, sems, sem = refs[13:]
    step, steps = pl.program_id(0), pl.num_programs(0)
    core = info[CORE]
    feat = grad_y.shape[1]
    tile = slope.shape[1]
    per = steps // 2
    keeping = pltpu.make_async_copy(weights, kept, sem)

    @pl.when(step == 0)
    def _():
        copies = bring(pieces, raw, sems, 0)
        for copy in copies:
            copy.start()
        normed[...], inverse[...] = centre(after[...])
        grad_second[...] = jnp.zeros_like(grad_second)
        for copy in copies:
            copy.wait()
        for who in (0, 1):
            c = core if who == 0 else 1 - core
            for j in range(16):
                weights[info[16 * who + j], c] = raw[2 * who + j // 8, j % 8]
        keeping.start()

    half = jnp.where(step < per, 1 - core, core)
    at = half * per + lax.rem(step, per)
    count = tile * weights.shape[0] // (steps * tile)
    down = weights[pl.ds(count * at, count)].reshape(tile, feat)
    raw_grad = dot_last(grad_y[...], down)

    def tell(slope_ref, up_ref, out):
        grad = (raw_grad * slope_ref[...].astype(F32)).astype(BF16)
        bias_sum[...] = jnp.sum(grad.astype(F32), axis=0, keepdims=True)
        grad_second[...] += dot_last(grad, up_ref[...])
        out[...] = grad

    pl.when(step < per)(lambda: tell(slope_o, up_o, theirs))
    pl.when(step >= per)(lambda: tell(slope, up, mine))

    @pl.when(step == steps - 1)
    def _():
        second = grad_second[...]
        live = grad_y[...].astype(F32)
        sums[0:1] = jnp.sum(second * normed[...], axis=0, keepdims=True)
        sums[1:2] = jnp.sum(second, axis=0, keepdims=True)
        total = live + layer_back(second * vecs[1:2], normed[...], inverse[...])
        grad_after[...] = total
        attn = total.astype(BF16)
        sums[2:3] = jnp.sum(attn.astype(F32), axis=0, keepdims=True)
        sums[3:4] = jnp.sum(live, axis=0, keepdims=True)
        sums[4:8] = jnp.zeros_like(sums[4:8])
        left, right = attn[:, : feat // 2], attn[:, feat // 2 :]
        attn_mine[...] = jnp.where(core == 0, left, right)
        attn_theirs[...] = jnp.where(core == 0, right, left)
        grad_mixed[...] = (dot_last(left, proj[0]) + dot_last(right, proj[1])).astype(BF16)
        keeping.wait()


def fall(chain, info, grad_y, slopes, up_sets, after, vecs, proj_set, pieces):
    rows, feat = grad_y.shape
    hidden = 2 * slopes[0].shape[1]
    tile = 768
    steps = hidden // tile
    per = steps // 2

    def at(n, info):
        return jnp.where(n < per, 1 - info[CORE], info[CORE]) * per + n % per

    def whole(dims):
        return pl.BlockSpec(dims, lambda n, info: (0,) * len(dims))

    return chain.call(
        fall_kernel,
        prefetch=1,
        grid=(steps,),
        in_specs=[
            whole((rows, feat)),
            pl.BlockSpec((rows, tile), lambda n, info: (0, jnp.maximum(n - per, 0))),
            pl.BlockSpec((rows, tile), lambda n, info: (0, jnp.minimum(n, per - 1))),
            pl.BlockSpec((feat, tile), lambda n, info: (0, jnp.maximum(n - per, 0))),
            pl.BlockSpec((feat, tile), lambda n, info: (0, jnp.minimum(n, per - 1))),
            whole((rows, feat)),
            whole((8, feat)),
            whole((2, feat, feat // 2)),
        ]
        + [ANY] * 4,
        out_specs=(
            ANY,
            pl.BlockSpec((rows, tile), lambda n, info: (0, jnp.minimum(n, per - 1))),
            pl.BlockSpec((rows, tile), lambda n, info: (0, jnp.maximum(n - per, 0))),
            pl.BlockSpec((1, tile), lambda n, info: (0, at(n, info))),
            whole((rows, feat)),
            whole((rows, feat // 2)),
            whole((rows, feat // 2)),
            whole((rows, feat)),
            whole((8, feat)),
        ),
        scratch_shapes=[
            pltpu.VMEM((16, 2, hidden // 32, feat), BF16),
            pltpu.VMEM((rows, feat), F32),
            pltpu.VMEM((rows, feat), F32),
            pltpu.VMEM((rows, 1), F32),
            pltpu.VMEM((4,) + pieces[0].shape, BF16),
            pltpu.SemaphoreType.DMA((4,)),
            pltpu.SemaphoreType.DMA,
        ],
        out_shape=(
            shape((16, 2, hidden // 32, feat), BF16),
            shape((rows, hidden // 2), BF16),
            shape((rows, hidden // 2), BF16),
            shape((1, hidden), F32),
            shape((rows, feat), F32),
            shape((rows, feat // 2), BF16),
            shape((rows, feat // 2), BF16),
            shape((rows, feat), BF16),
            shape((8, feat), F32),
        ),
        compiler_params=params(32),
        name="fall",
        cost_estimate=cost(18),
    )(info, grad_y, *slopes, *up_sets, after, vecs, proj_set, *pieces)


def exit_kernel(
    info,
    tokens,
    mine,
    theirs,
    weights,
    grad_after,
    vecs,
    sums_a,
    bias,
    grad_tokens,
    keep,
    away,
    grad_first,
    joint,
    sums,
    extra,
):
    step = pl.program_id(0)
    core = info[CORE]
    third = mine.shape[2]
    half = jnp.where(step == 0, core, 1 - core)
    spot = pl.ds(pl.multiple_of(half * third, third), third)

    def parts(source):
        for part in range(3):
            joint[:, part * third : (part + 1) * third] = source[part]
        sums[3:4, spot] = jnp.sum(source[0].astype(F32), axis=0, keepdims=True)
        sums[4:5, spot] = jnp.sum(source[2].astype(F32), axis=0, keepdims=True)
        return dot_last(joint[...], weights[0])

    @pl.when(step == 0)
    def _():
        grad_first[...] = parts(mine)

    @pl.when(step == 1)
    def _():
        grad = grad_first[...] + parts(theirs)
        normed, inverse = centre(tokens[...].astype(F32))
        sums[0:1] = jnp.sum(grad * normed, axis=0, keepdims=True)
        sums[1:2] = sums_a[0:1]
        sums[2:3] = jnp.sum(grad, axis=0, keepdims=True)
        sums[5:6] = sums_a[2:3]
        sums[6:7] = sums_a[1:2]
        sums[7:8] = sums_a[3:4]
        sums[8:] = jnp.zeros_like(sums[8:])
        back = layer_back(grad * vecs[0:1], normed, inverse)
        grad_tokens[...] = (grad_after[...] + back).astype(BF16)
        flipped = sums[...].T
        block, each = extra.shape[1], bias.shape[1] // 32
        for chip in range(16):
            place = info[PLACE + chip]
            extra[place] = flipped[chip * block : (chip + 1) * block]
            for c in (0, 1):
                at = (2 * chip + c) * each
                row = c * block // 2
                extra[place, row : row + 1, 128 - each :] = bias[:, at : at + each]
        keep[...] = extra[:8]
        away[...] = extra[8:].astype(BF16)


def exit_back(chain, info, tokens, mine, theirs, first_set, grad_after, vecs, sums_a, bias):
    rows, feat = tokens.shape
    third = feat // 2
    block = feat // 16

    def whole(dims):
        return pl.BlockSpec(dims, lambda n, info: (0,) * len(dims))

    return chain.call(
        exit_kernel,
        prefetch=1,
        grid=(2,),
        in_specs=[
            whole((rows, feat)),
            whole((3, rows, third)),
            whole((3, rows, third)),
            pl.BlockSpec(
                (1, feat, 3 * third),
                lambda n, info: (jnp.where(n == 0, info[CORE], 1 - info[CORE]), 0, 0),
            ),
            whole((rows, feat)),
            whole((8, feat)),
            whole((8, feat)),
            whole(bias.shape),
        ],
        out_specs=(whole((rows, feat)), whole((8, block, 128)), whole((8, block, 128))),
        scratch_shapes=[
            pltpu.VMEM((rows, feat), F32),
            pltpu.VMEM((rows, 3 * third), BF16),
            pltpu.VMEM((128, feat), F32),
            pltpu.VMEM((16, block, 128), F32),
        ],
        out_shape=(
            shape((rows, feat), BF16),
            shape((8, block, 128), F32),
            shape((8, block, 128), BF16),
        ),
        compiler_params=params(18),
        name="exit_back",
        cost_estimate=cost(8),
    )(info, tokens, mine, theirs, first_set, grad_after, vecs, sums_a, bias)


def line_up(info, left, left_o, turned):
    rows = left.shape[2]
    for chip in range(16):
        place = info[PLACE + chip]
        turned[place, :, :rows] = left[chip]
        turned[place, :, rows:] = left_o[chip]


def outer_tile(turned, right, right_o):
    rows = right.shape[0]
    both = turned[...].reshape(-1, turned.shape[2])
    total = dot(both[:, :rows], right) + dot(both[:, rows:], right_o)
    return total.reshape(16, -1, total.shape[1])


def outer_up_kernel(
    info, left, left_o, right, right_o, low, low_o, attn, attn_o, keep, away, turned, *late
):
    step, last = pl.program_id(0), pl.num_programs(0) - 1
    buffers, sems = late[:4], late[4]
    copies = [
        pltpu.make_async_copy(src, dst, sems.at[i])
        for i, (src, dst) in enumerate(zip((low, low_o, attn, attn_o), buffers))
    ]

    @pl.when(step == 0)
    def _():
        for copy in copies:
            copy.start()
        line_up(info, left, left_o, turned)

    @pl.when(step < last)
    def _():
        total = outer_tile(turned, right[...], right_o[...])
        keep[...] = total[:8].astype(BF16)
        away[...] = total[8:].astype(BF16)

    @pl.when(step == last)
    def _():
        for copy in copies:
            copy.wait()
        line_up(info, buffers[0], buffers[1], turned)
        total = outer_tile(turned, buffers[2][...], buffers[3][...])
        keep[:, :, : attn.shape[1]] = total[:8].astype(BF16)
        away[:, :, : attn.shape[1]] = total[8:].astype(BF16)


def outer_up(chain, info, left, left_o, right, right_o, low, low_o, attn, attn_o):
    _, block, rows = left.shape
    tile = 2 * attn.shape[1]
    n = right.shape[1] // tile
    cols = right.shape[1] + attn.shape[1]
    strip = pl.BlockSpec((rows, tile), lambda i: (0, jnp.minimum(i, n - 1)))
    out = pl.BlockSpec((8, block, tile), lambda i: (0, 0, i))
    return chain.call(
        outer_up_kernel,
        grid=(n + 1,),
        out_shape=(shape((8, block, cols), BF16), shape((8, block, cols), BF16)),
        in_specs=[SMEM] + [full(left.shape)] * 2 + [strip] * 2 + [ANY] * 4,
        out_specs=(out, out),
        scratch_shapes=[pltpu.VMEM((16, block, 2 * rows), BF16)]
        + [pltpu.VMEM(left.shape, BF16)] * 2
        + [pltpu.VMEM(attn.shape, BF16)] * 2
        + [pltpu.SemaphoreType.DMA((4,))],
        compiler_params=params(20),
        name="outer_up",
        cost_estimate=cost(8),
    )(info, left, left_o, right, right_o, low, low_o, attn, attn_o)


def outer_qkv_kernel(info, left, left_o, right, right_o, keep, away, turned):
    tile = right.shape[2]
    line_up(info, left, left_o, turned)
    for part in range(3):
        cols = slice(part * tile, (part + 1) * tile)
        total = outer_tile(turned, right[part], right_o[part])
        keep[:, :, cols] = total[:8]
        away[:, :, cols] = total[8:].astype(BF16)


def outer_qkv(chain, info, left, left_o, right, right_o):
    _, block, rows = left.shape
    cols = 3 * right.shape[2]
    vmem = pl.BlockSpec(memory_space=pltpu.VMEM)
    return chain.call(
        outer_qkv_kernel,
        out_shape=(shape((8, block, cols), F32), shape((8, block, cols), BF16)),
        in_specs=[SMEM] + [vmem] * 4,
        out_specs=(vmem, vmem),
        scratch_shapes=[pltpu.VMEM((16, block, 2 * rows), BF16)],
        compiler_params=params(20),
        name="outer_qkv",
        cost_estimate=cost(8),
    )(info, left, left_o, right, right_o)


def outer_down_kernel(
    info, first, second, first_o, second_o, right, right_o, keep, away, turned
):
    rows = right.shape[0]
    core = info[CORE]
    for r in range(8):
        place = info[PLACE + 8 * core + r]
        turned[place, :, :rows] = first[r]
        turned[place, :, rows:] = second_o[r]
        place = info[PLACE + 8 * (1 - core) + r]
        turned[place, :, :rows] = second[r]
        turned[place, :, rows:] = first_o[r]
    for out, spots in ((away, slice(8, 16)), (keep, slice(0, 8))):
        left = turned[spots].reshape(-1, turned.shape[2])
        total = dot(left[:, :rows], right[...]) + dot(left[:, rows:], right_o[...])
        out[...] = total.reshape(out.shape).astype(out.dtype)


def outer_down(chain, info, first, second, first_o, second_o, right, right_o):
    _, block, rows = first.shape
    feat = right.shape[1]
    vmem = pl.BlockSpec(memory_space=pltpu.VMEM)
    return chain.call(
        outer_down_kernel,
        out_shape=(shape((8, block, feat), BF16), shape((8, block, feat), BF16)),
        in_specs=[SMEM] + [vmem] * 6,
        out_specs=(vmem, vmem),
        scratch_shapes=[pltpu.VMEM((16, block, 2 * rows), BF16)],
        compiler_params=params(24),
        name="outer_down",
        cost_estimate=cost(0),
    )(info, first, second, first_o, second_o, right, right_o)


def add_first_kernel(keep, got, kept, away, raw, low, sems):
    far = pltpu.make_async_copy(got.at[pl.ds(4, 4)], raw.at[1], sems.at[0])
    near = pltpu.make_async_copy(got.at[pl.ds(0, 4)], raw.at[0], sems.at[1])
    out = pltpu.make_async_copy(low, away, sems.at[2])
    far.start()
    near.start()
    far.wait()
    low[...] = (keep[4:].astype(F32) + raw[1].astype(F32)).astype(BF16)
    out.start()
    near.wait()
    kept[...] = (keep[:4].astype(F32) + raw[0].astype(F32)).astype(BF16)
    out.wait()


def shift_first(chain, keep, away, micros=0):
    _, rows, cols = keep.shape
    vmem = pl.BlockSpec(memory_space=pltpu.VMEM)
    return chain.call(
        add_first_kernel,
        out_shape=(shape((4, rows, cols), BF16), shape((4, rows, cols), BF16)),
        in_specs=[vmem, ANY],
        out_specs=(vmem, ANY),
        scratch_shapes=[
            pltpu.VMEM((2, 4, rows, cols), BF16),
            pltpu.VMEM((4, rows, cols), BF16),
            pltpu.SemaphoreType.DMA((3,)),
        ],
        compiler_params=params(12),
        name="shift_first",
        cost_estimate=cost(micros),
    )(keep, send(away, second_way))


def add_both_kernel(keep, got, few_keep, few_got, kept, away):
    split = keep.shape[2]
    kept[:, :, :split] = keep[:4] + got[:4].astype(F32)
    kept[:, :, split:] = few_keep[:4] + few_got[:4].astype(F32)
    away[:, :, :split] = (keep[4:] + got[4:].astype(F32)).astype(BF16)
    away[:, :, split:] = (few_keep[4:] + few_got[4:].astype(F32)).astype(BF16)


def shift_both(chain, keep, away, few_keep, few_away):
    _, rows, cols = keep.shape
    cols += few_keep.shape[2]
    vmem = pl.BlockSpec(memory_space=pltpu.VMEM)
    return chain.call(
        add_both_kernel,
        out_shape=(shape((4, rows, cols), F32), shape((4, rows, cols), BF16)),
        in_specs=[vmem] * 4,
        out_specs=(vmem, vmem),
        compiler_params=params(12),
        name="shift_both",
        cost_estimate=cost(0),
    )(keep, send(away, second_way), few_keep, send(few_away, second_way))


def add_second_kernel(keep, got, base, one, two, three):
    base[...] = keep[0].astype(F32) + got[0].astype(F32)
    for s, out in ((1, one), (2, two), (3, three)):
        out[...] = (keep[s].astype(F32) + got[s].astype(F32)).astype(BF16)


def shift_second(chain, keep, away):
    _, rows, cols = keep.shape
    vmem = pl.BlockSpec(memory_space=pltpu.VMEM)
    base, *lows = chain.call(
        add_second_kernel,
        out_shape=(shape((rows, cols), F32),) + (shape((rows, cols), BF16),) * 3,
        in_specs=[vmem, vmem],
        out_specs=(vmem,) * 4,
        compiler_params=params(8),
        name="shift_second",
        cost_estimate=cost(0),
    )(keep, send(away, first_way))
    return base, [send(low, along_z(s)) for low, s in zip(lows, (1, 2, 3))]


def total_of(base, parts):
    return base[...] + parts[0][...].astype(F32) + (
        parts[1][...].astype(F32) + parts[2][...].astype(F32)
    )


def add_down_kernel(base, one, two, three, out):
    out[...] = total_of(base, (one, two, three))


def home_down(chain, base, parts):
    vmem = pl.BlockSpec(memory_space=pltpu.VMEM)
    return chain.call(
        add_down_kernel,
        out_shape=shape(base.shape, F32),
        in_specs=[vmem] * 4,
        out_specs=vmem,
        compiler_params=params(8),
        name="home_down",
        cost_estimate=cost(0),
    )(base, *parts)


def add_last_kernel(info, base, one, two, three, mine, theirs, total):
    core = info[CORE]
    half = mine.shape[0]
    total[...] = total_of(base, (one, two, three))
    mine[...] = total[pl.ds(pl.multiple_of(core * half, half), half)]
    theirs[...] = total[pl.ds(pl.multiple_of((1 - core) * half, half), half)]


def home(chain, info, base, parts):
    rows, cols = base.shape
    vmem = pl.BlockSpec(memory_space=pltpu.VMEM)
    out = shape((rows // 2, cols), F32)
    mine, theirs = chain.call(
        add_last_kernel,
        out_shape=(out, out),
        in_specs=[SMEM] + [vmem] * 4,
        out_specs=(vmem, vmem),
        scratch_shapes=[pltpu.VMEM((rows, cols), F32)],
        compiler_params=params(8),
        name="home",
        cost_estimate=cost(0),
    )(info, base, *parts)
    return mine, swap(theirs)


def finish_kernel(info, qkv, qkv_o, up, up_o, out_qkv, out_proj, out_up, gains, shifts, bias):
    rows, third = out_proj.shape[0], out_proj.shape[1] // 2
    wide = out_up.shape[1] // 2
    small = qkv[:, 3 * third :] + qkv_o[:, 3 * third :]
    flipped = jnp.concatenate([small, jnp.zeros((128 - rows, 128), F32)]).T
    gains[...] = flipped[0:2, :rows]
    shifts[...] = flipped[2:8, :rows]
    bias[...] = small[0:1, 128 - bias.shape[1] :]

    def lay(core):
        for half, (a, b) in ((core, (qkv, up)), (1 - core, (qkv_o, up_o))):
            for part in range(3):
                spot = part * 2 * third + half * third
                out_qkv[:, spot : spot + third] = a[:, part * third : (part + 1) * third]
            out_proj[:, half * third : (half + 1) * third] = b[:, wide:]
            out_up[:, half * wide : (half + 1) * wide] = b[:, :wide]

    @pl.when(info[CORE] == 0)
    def _():
        lay(0)

    @pl.when(info[CORE] == 1)
    def _():
        lay(1)


def finish(chain, info, qkv, qkv_o, up, up_o):
    rows = qkv.shape[0]
    third = (qkv.shape[1] - 128) // 3
    vmem = pl.BlockSpec(memory_space=pltpu.VMEM)
    return chain.call(
        finish_kernel,
        out_shape=(
            shape((rows, 6 * third), F32),
            shape((rows, 2 * third), F32),
            shape((rows, 2 * (up.shape[1] - third)), F32),
            shape((2, rows), F32),
            shape((6, rows), F32),
            shape((1, 4 * rows), F32),
        ),
        in_specs=[SMEM] + [vmem] * 4,
        out_specs=(vmem,) * 6,
        compiler_params=params(8),
        name="finish",
        cost_estimate=cost(0),
    )(info, qkv, qkv_o, up, up_o)


def local(
    tokens,
    upstream,
    lengths,
    qkv_weight,
    proj_weight,
    up_weight,
    down_weight,
    gains,
    shifts,
    up_bias,
):
    tok_rows, feat = tokens.shape
    rows = qkv_weight.shape[0]
    hidden = up_weight.shape[1]
    third, wide = feat // 2, hidden // 2
    chip, core = lax.axis_index("dp"), lax.axis_index("fsdp")
    info = facts(chip, core, lengths[0])

    chain = Chain()

    small = jnp.concatenate([gains, shifts], axis=1)
    small = jnp.pad(small, ((0, 0), (0, 128 - small.shape[1])))
    small = small + jnp.pad(up_bias[None], ((0, rows - 1), (128 - up_bias.shape[0], 0)))
    piece = first_piece(chain, info, qkv_weight, swap(qkv_weight), small)
    piece_up = up_piece(chain, info, up_weight, swap(up_weight), proj_weight, swap(proj_weight))
    zs, piece_up = gather(chain, [piece] + near_z(piece, (3, 2, 1)), (piece_up,), 0, (0, 3, 2, 1))
    up_z = near_z(piece_up, (1, 2, 3))
    first = gate(chain, send(zs, first_way), 0)
    second, both = send(zs, second_way), send(first, second_way)
    (zs_up,) = gather(chain, [piece_up] + up_z, (), 5)
    pieces = both_cores(zs, first, gate(chain, second, 0), gate(chain, both, 0))
    zs = zs_up
    first_set, vecs, bias, first_t, joint, grad_y, down = enter(
        chain, info, tokens, upstream, down_weight, hidden, pieces
    )
    grad_y_o, first_o = swap(grad_y), swap(first_t)
    first_set = first_set.reshape(2, feat, 3 * third + 128)
    first, second = send(zs, first_way), send(zs, second_way)
    first = gate(chain, first, 0)
    pieces = both_cores(zs, first, second, send(first, second_way))
    down_z = near_z(down, (1, 2, 3))
    mixed, mixed_t, stats = mix(chain, info, joint)
    mixed_t = mixed_t.reshape(first_t.shape)
    mixed_o = swap(mixed_t)
    (zs,) = gather(chain, [down] + down_z, (), 5)
    proj_set, after, normed, normed_t = rise(chain, info, tokens, mixed, vecs, pieces)
    normed_o = swap(normed_t)
    up_a, active_a, slope_a, mine_a, theirs_a = widen(chain, 0, info, normed, bias, pieces[:4])
    theirs_a = swap(theirs_a)
    (low,) = gather(chain, [zs, send(zs, first_way)])
    high = send(low, second_way)
    up_b, active_b, slope_b, mine_b, theirs_b = widen(chain, 1, info, normed, bias, pieces[4:])
    proj_set = proj_set.reshape(2, feat, third)
    down = outer_down(
        chain, info, mine_a, mine_b, theirs_a, swap(theirs_b), grad_y, grad_y_o
    )
    pieces = both_cores(low, gate(chain, high, 0))
    up_sets = (up_a.reshape(feat, wide), up_b.reshape(feat, wide))
    down_set, hid_theirs, hid_mine, bias_sum, grad_after, at_theirs, at_mine, grad_mixed, sums_a = (
        fall(chain, info, grad_y, (slope_a, slope_b), up_sets, after, vecs, proj_set, pieces)
    )
    hid_o, at_o = swap(hid_theirs), swap(at_theirs)
    down = shift_first(chain, *down, 5)
    up = outer_up(chain, info, normed_t, normed_o, hid_mine, hid_o, mixed_t, mixed_o, at_mine, at_o)
    down = shift_second(chain, *down)
    theirs, mine = mix_back(chain, info, joint, grad_mixed, stats)
    theirs_o = swap(theirs)
    down = (down[0], [gate(chain, part, 0) for part in down[1]])
    up = shift_first(chain, *up, 5)
    chain.near(up[1])
    qkv = outer_qkv(chain, info, first_t, first_o, mine, theirs_o)
    grad_tokens, few_keep, few_away = exit_back(
        chain, info, tokens, mine, theirs, first_set, grad_after, vecs, sums_a, bias_sum
    )
    up = shift_second(chain, *up)
    qkv = shift_both(chain, *qkv, few_keep, few_away)
    output = leave(
        chain, info, after, active_a, active_b, down_set.reshape(hidden, feat), vecs
    )
    qkv = shift_second(chain, *qkv)
    own_down = home_down(chain, *down)
    own_up = home(chain, info, *up)
    own_qkv = home(chain, info, *qkv)
    out_qkv, out_proj, out_up, out_gains, out_shifts, out_bias = finish(
        chain, info, *own_qkv, *own_up
    )
    return (
        output,
        grad_tokens,
        out_qkv,
        out_proj,
        out_up,
        own_down,
        out_gains.T,
        out_shifts.T,
        out_bias.reshape(-1),
    )


def solution(mesh):
    placed = (
        P(("dp", "fsdp"), None),
        P(("dp", "fsdp"), None),
        P(("dp", "fsdp")),
        P(("dp", "fsdp"), None),
        P(("dp", "fsdp"), None),
        P(("dp", "fsdp"), None),
        P(("dp", "fsdp"), None),
        P(("dp", "fsdp"), None),
        P(("dp", "fsdp"), None),
        P(("dp", "fsdp")),
    )
    sizes = (mesh.shape["dp"], mesh.shape["fsdp"])
    return jax.shard_map(
        local if sizes == (16, 2) else plain,
        mesh=mesh,
        in_specs=placed,
        out_specs=(
            P(("dp", "fsdp"), None),
            P(("dp", "fsdp"), None),
            P(("dp", "fsdp"), None),
            P(("dp", "fsdp"), None),
            P(("dp", "fsdp"), None),
            P(("dp", "fsdp"), None),
            P(("dp", "fsdp"), None),
            P(("dp", "fsdp"), None),
            P(("dp", "fsdp")),
        ),
        check_vma=False,
    )
```
